32 devices in a mesh: groups: 2 (over x), nodes: 16 (over z, y, core).
Axes of the slice: x: 2, y: 2, z: 4, core: 2. Of those that a mesh axis runs over, the one named last changes fastest.
Arguments:
- features: bfloat16 [65536, 128], P(('groups', 'nodes')), parts along dimension 0, may hold values from -6 to 6
- fine_cotangent: bfloat16 [65536, 128], P(('groups', 'nodes')), parts along dimension 0, may hold values from -6 to 6
- mid_cotangent: bfloat16 [16384, 128], P(('groups', 'nodes')), parts along dimension 0, may hold values from -6 to 6
- coarse_cotangent: bfloat16 [512, 128], P(('groups', 'nodes')), parts along dimension 0, may hold values from -6 to 6
- weights: bfloat16 [3, 4, 128, 128], replicated, may hold values from -0.5 to 0.5
- fine_offsets: int32 [16, 32768], P('groups', 'nodes'), parts along dimension 0, may hold values from -256 to 256
- fine_edge_w: float32 [16, 32768], P('groups', 'nodes'), parts along dimension 0, may hold values from -2 to 2
- pool_fine: bfloat16 [16, 32768], P('groups', 'nodes'), parts along dimension 0, may hold values from -1 to 1
- owner_dev: int32 [2048, 1], P(('groups', 'nodes')), parts along dimension 0, may hold values from 0 to 15; in each aligned block of 64 rows (0 to 63, 64 to 127, ...) at most 8 rows name the same one
- coarse_slot: int32 [2048], P(('groups', 'nodes')), parts along dimension 0, may hold values from 0 to 63
- mid_nbrs: int32 [16, 8192], P('groups', 'nodes'), parts along dimension 0, may hold values from 0 to 511
- mid_edge_w: float32 [16, 8192], P('groups', 'nodes'), parts along dimension 0, may hold values from -2 to 2
- pool_mid: bfloat16 [512, 512], P(('groups', 'nodes')), parts along dimension 0, may hold values from -0.25 to 0.25
- coarse_nbrs: int32 [16, 256], P('groups', 'nodes'), parts along dimension 0, may hold values from 0 to 255
- coarse_edge_w: float32 [16, 256], P('groups', 'nodes'), parts along dimension 0, may hold values from -2 to 2
Outputs:
- feature_grads: bfloat16 [65536, 128], P(('groups', 'nodes')), parts along dimension 0
- weight_grads: float32 [6, 4, 128, 128], P('groups'), parts along dimension 0
The draws below stay inside these ranges and needn't reach their ends.
There are 2 independent parts, one for each index of `groups`. The reference program is written for one: setup_inputs(seed, part) draws one part's arguments, and reference() takes and returns one part's arrays. A program takes and returns all parts, laid end to end along the dimension named above; an argument that names none is the same for every part. Nothing has to cross between parts.
Inputs may be any that keep to these rules, and one draw needn't show every extreme that they name: `owner_dev`: within the 64 tiles of one device no owner is named more than 8 times, a bound that some block reaches.
All inputs are finite; a program needn't handle non-finite values.
Results may differ from the reference program's by a relative error of at most 0.014.
Values may be sent and summed in bfloat16 or wider, within the bound.
No kernel may reach another device: no remote copies, remote signals or barrier semaphores. Data moves between devices by JAX's collectives and lax.ppermute only.
A program may use at most 128 MiB of HBM per device.

```python
import math
import jax
import jax.numpy as jnp
import numpy as np

D = 128
EDGES = 8
TILE_ROWS = 32
BLOCK_ROWS = 8
HALO = 256
TILES = 64
CAP = 8
NC1 = 512
NC2 = 16
NF_TOTAL = 32768
TILES_TOTAL = 1024
NC1_TOTAL = 8192
NC2_TOTAL = 256
N_NODES = 16


def with_ends(result, stream_key, low, largest):
    place = [jax.random.randint(jax.random.fold_in(stream_key, axis), (), 0, length) for axis, length in enumerate(result.shape)]
    widest = result.shape.index(max(result.shape))
    beside = place[:widest] + [(place[widest] + 1) % result.shape[widest]] + place[widest + 1:]
    return result.at[tuple(place)].set(low).at[tuple(beside)].set(largest)


def block_levels(stream_key, extent, split, smallest, top_value):
    def one(axis_at, parts):
        heights = jax.random.uniform(jax.random.fold_in(jax.random.fold_in(stream_key, 6), axis_at), (parts,), jnp.float32, smallest / len(split), top_value / len(split))
        return jnp.repeat(jnp.exp(heights), extent[axis_at] // parts).reshape((-1,) + (1,) * (len(extent) - axis_at - 1))

    factor_of = one(*split[0])
    for cut in split[1:]:
        factor_of = factor_of * one(*cut)
    return factor_of


def deal_out(own_key, own, number, rows, amount, top, most, lean):
    ranking = jax.random.permutation(own_key, amount)
    heavy_load, usual = portions_of(amount, rows * top, most, lean, True), portions_of(amount, rows * top, most, lean, False)
    places = jnp.arange(amount)

    def named(sizes, turn):
        used = int((sizes > 0).sum())
        fixed = max(1, used // 4)
        moved = fixed + (places - fixed + turn * (used - fixed)) % max(1, amount - fixed)
        return jnp.zeros((amount,), jnp.int32).at[ranking[jnp.where(places < fixed, places, moved)]].set(jnp.asarray(sizes, jnp.int32))

    sizes = jnp.where(number % 4 == 0, named(heavy_load, number // 4), named(usual, number - number // 4 - 1))
    mixed = jax.random.permutation(jax.random.fold_in(own, 3), amount)
    donor, taker = mixed[0:amount // 2 * 2:2], mixed[1:amount // 2 * 2:2]
    slack = jnp.minimum(sizes[donor] - 1, most - sizes[taker]) // 2
    slack = jnp.where((donor == ranking[0]) | (taker == ranking[0]) | (sizes[taker] == 0), 0, jnp.maximum(slack, 0))
    moved = jax.random.randint(jax.random.fold_in(own, 4), (amount // 2,), 0, 1 << 20) % (slack + 1)
    sizes = sizes.at[donor].add(-moved).at[taker].add(moved)
    items = jnp.searchsorted(jnp.cumsum(sizes), jnp.arange(rows * top), side="right").astype(jnp.int32)
    table = items.reshape(top, rows).T
    table = table[jax.random.permutation(jax.random.fold_in(own, 1), rows)]
    turn = jax.random.randint(jax.random.fold_in(own, 2), (rows, 1), 0, top)
    return jnp.take_along_axis(table, (jnp.arange(top)[None, :] + turn) % top, axis=1)


def portions_of(amount, total, limit, lean, full):
    loads = [(1 << 20) // math.isqrt(standing ** lean) + 1 for standing in range(1, amount + 1)]
    largest = limit if full else min(limit, max(-(-total // amount), total * loads[0] // sum(loads)))
    least = 1 if total - largest >= amount - 1 else 0
    counts, rest = [largest] + [least] * (amount - 1), total - largest - least * (amount - 1)
    while rest > 0:
        candidates = [i for i in range(1, amount) if counts[i] < largest] or [i for i in range(1, amount) if counts[i] < limit]
        mass, budget = sum([loads[i] for i in candidates]), rest
        for i in candidates:
            more = min(limit - counts[i], max(1, budget * loads[i] // mass), rest)
            counts[i] = counts[i] + more
            rest = rest - more
    return np.array(counts)


def gaussian(stream_key, extent, scale, bound, pieces=(), kind=jnp.bfloat16):
    entries = jax.random.normal(stream_key, extent, jnp.float32) * scale
    if len(pieces) > 0:
        entries = block_levels(stream_key, extent, pieces, -0.22, 0.18) * entries
    return jnp.clip(entries, min=-bound, max=bound).astype(kind)


def setup_inputs(seed: int = 0, part: int = 0) -> dict:
    splits = jax.random.split(jax.random.key(seed), 16)
    part_keys = jax.random.split(jax.random.fold_in(splits[15], part), 16)
    features = gaussian(part_keys[0], (NF_TOTAL, D), 1.0, 6.0, ((0, 16),))
    fine_cotangent = gaussian(part_keys[1], (NF_TOTAL, D), 1.0, 6.0, ((0, 16),))
    mid_cotangent = gaussian(part_keys[2], (NC1_TOTAL, D), 1.0, 6.0, ((0, 16),))
    coarse_cotangent = gaussian(part_keys[3], (NC2_TOTAL, D), 1.0, 6.0, ((0, 16),))
    weights = gaussian(splits[4], (3, 4, D, D), D ** -0.5, 0.5)
    fine_offsets = with_ends(jax.random.randint(part_keys[5], (EDGES, NF_TOTAL), -HALO, HALO + 1), jax.random.fold_in(part_keys[5], 1), -HALO, HALO).astype(jnp.int32)
    fine_edge_w = gaussian(part_keys[6], (EDGES, NF_TOTAL), EDGES ** -0.5, 2.0, ((1, 16),), jnp.float32)
    pool_fine = gaussian(part_keys[7], (BLOCK_ROWS, NF_TOTAL), TILE_ROWS ** -0.5, 1.0, ((1, 16),))
    owner_dev_keys = jax.random.split(jax.random.fold_in(part_keys[8], 1), TILES_TOTAL // TILES)
    owner_dev_turns = jax.random.permutation(jax.random.fold_in(part_keys[8], 3), TILES_TOTAL // TILES)
    owner_dev = jax.vmap(lambda own, number: deal_out(jax.random.fold_in(part_keys[8], 2), own, number, TILES, N_NODES, 1, CAP, 2))(owner_dev_keys, owner_dev_turns).reshape((TILES_TOTAL, 1))
    coarse_slot = with_ends(jax.random.randint(part_keys[9], (TILES_TOTAL,), 0, TILES), jax.random.fold_in(part_keys[9], 1), 0, TILES - 1).astype(jnp.int32)
    mid_nbrs = with_ends(jax.random.randint(part_keys[10], (EDGES, NC1_TOTAL), 0, NC1), jax.random.fold_in(part_keys[10], 1), 0, NC1 - 1).astype(jnp.int32)
    mid_edge_w = gaussian(part_keys[11], (EDGES, NC1_TOTAL), EDGES ** -0.5, 2.0, ((1, 16),), jnp.float32)
    pool_mid = gaussian(part_keys[12], (NC2_TOTAL, NC1), NC1 ** -0.5, 0.25, ((0, 16),))
    coarse_nbrs = with_ends(jax.random.randint(part_keys[13], (EDGES, NC2_TOTAL), 0, NC2_TOTAL), jax.random.fold_in(part_keys[13], 1), 0, NC2_TOTAL - 1).astype(jnp.int32)
    coarse_edge_w = gaussian(part_keys[14], (EDGES, NC2_TOTAL), EDGES ** -0.5, 2.0, ((1, 16),), jnp.float32)
    return {"features": features, "fine_cotangent": fine_cotangent, "mid_cotangent": mid_cotangent, "coarse_cotangent": coarse_cotangent, "weights": weights, "fine_offsets": fine_offsets, "fine_edge_w": fine_edge_w, "pool_fine": pool_fine, "owner_dev": owner_dev, "coarse_slot": coarse_slot, "mid_nbrs": mid_nbrs, "mid_edge_w": mid_edge_w, "pool_mid": pool_mid, "coarse_nbrs": coarse_nbrs, "coarse_edge_w": coarse_edge_w}


def silu_slope(values):
    logistic = jax.nn.sigmoid(values)
    return logistic * (1.0 + values * (1.0 - logistic))

def gather_rows(source, neighbour_index, edge_weight):
    summed = jnp.zeros((neighbour_index.shape[1], source.shape[1]), jnp.float32)
    for neighbour in range(neighbour_index.shape[0]):
        picked = source[neighbour_index[neighbour]].astype(jnp.float32)
        summed = summed + edge_weight[neighbour][:, None] * picked
    return summed.astype(jnp.bfloat16)

def spread_rows(gradient, neighbour_index, edge_weight, row_count):
    summed = jnp.zeros((row_count, gradient.shape[1]), jnp.float32)
    for neighbour in range(neighbour_index.shape[0]):
        summed = summed.at[neighbour_index[neighbour]].add(edge_weight[neighbour][:, None] * gradient)
    return summed

def node_forward(hidden, gathered, level_weights):
    first = jnp.dot(hidden, level_weights[0], preferred_element_type=jnp.float32)
    first = first + jnp.dot(gathered, level_weights[1], preferred_element_type=jnp.float32)
    middle = jax.nn.silu(first).astype(jnp.bfloat16)
    second = jnp.dot(middle, level_weights[2], preferred_element_type=jnp.float32)
    outer = jax.nn.silu(second).astype(jnp.bfloat16)
    return (first, middle, second, outer)

def node_output(hidden, saved, level_weights):
    added = hidden.astype(jnp.float32) + jnp.dot(saved[3], level_weights[3], preferred_element_type=jnp.float32)
    return added.astype(jnp.bfloat16)

def node_backward(out_grad, hidden, gathered, saved, level_weights):
    first, middle, second, outer = saved
    grad_outer = jnp.dot(outer.T, out_grad, preferred_element_type=jnp.float32)
    second_grad = jnp.dot(out_grad, level_weights[3].T, preferred_element_type=jnp.float32)
    second_grad = (second_grad * silu_slope(second)).astype(jnp.bfloat16)
    grad_middle = jnp.dot(middle.T, second_grad, preferred_element_type=jnp.float32)
    first_grad = jnp.dot(second_grad, level_weights[2].T, preferred_element_type=jnp.float32)
    first_grad = (first_grad * silu_slope(first)).astype(jnp.bfloat16)
    grad_hidden = jnp.dot(hidden.T, first_grad, preferred_element_type=jnp.float32)
    grad_gathered = jnp.dot(gathered.T, first_grad, preferred_element_type=jnp.float32)
    direct = out_grad.astype(jnp.float32) + jnp.dot(first_grad, level_weights[0].T, preferred_element_type=jnp.float32)
    spill = jnp.dot(first_grad, level_weights[1].T, preferred_element_type=jnp.float32)
    return (direct, spill, jnp.stack([grad_hidden, grad_gathered, grad_middle, grad_outer]))

def reference(features, fine_cotangent, mid_cotangent, coarse_cotangent, weights, fine_offsets, fine_edge_w, pool_fine, owner_dev, coarse_slot, mid_nbrs, mid_edge_w, pool_mid, coarse_nbrs, coarse_edge_w):
    padded = jnp.pad(features, ((HALO, HALO), (0, 0)))
    fine_index = fine_offsets + HALO + jnp.arange(NF_TOTAL, dtype=jnp.int32)[None, :]
    fine_agg = gather_rows(padded, fine_index, fine_edge_w)
    fine_saved = node_forward(features, fine_agg, weights[0])
    fine_out = node_output(features, fine_saved, weights[0])
    pool_tiles = pool_fine.astype(jnp.float32).reshape(BLOCK_ROWS, TILES_TOTAL, TILE_ROWS)
    blocks = jnp.einsum('rtj,tjd->trd', pool_tiles, fine_out.astype(jnp.float32).reshape(TILES_TOTAL, TILE_ROWS, D)).astype(jnp.bfloat16)
    target = owner_dev[:, 0] * TILES + coarse_slot
    mid_sum = jax.ops.segment_sum(blocks.reshape(TILES_TOTAL, BLOCK_ROWS * D).astype(jnp.float32), target, num_segments=NC1_TOTAL // BLOCK_ROWS)
    mid_in = mid_sum.reshape(NC1_TOTAL, D).astype(jnp.bfloat16)
    mid_base = jnp.arange(NC1_TOTAL, dtype=jnp.int32) // NC1 * NC1
    mid_index = mid_nbrs + mid_base[None, :]
    mid_agg = gather_rows(mid_in, mid_index, mid_edge_w)
    mid_saved = node_forward(mid_in, mid_agg, weights[1])
    mid_out = node_output(mid_in, mid_saved, weights[1])
    pool_blocks = pool_mid.astype(jnp.float32).reshape(N_NODES, NC2, NC1)
    coarse_in = jnp.einsum('dij,djk->dik', pool_blocks, mid_out.astype(jnp.float32).reshape(N_NODES, NC1, D))
    coarse_in = coarse_in.reshape(NC2_TOTAL, D).astype(jnp.bfloat16)
    coarse_agg = gather_rows(coarse_in, coarse_nbrs, coarse_edge_w)
    coarse_saved = node_forward(coarse_in, coarse_agg, weights[2])
    coarse_direct, coarse_spill, coarse_wgrad = node_backward(coarse_cotangent, coarse_in, coarse_agg, coarse_saved, weights[2])
    coarse_grad = (coarse_direct + spread_rows(coarse_spill, coarse_nbrs, coarse_edge_w, NC2_TOTAL)).astype(jnp.bfloat16)
    back_mid = jnp.einsum('dij,dik->djk', pool_blocks, coarse_grad.astype(jnp.float32).reshape(N_NODES, NC2, D))
    mid_out_grad = (mid_cotangent.astype(jnp.float32) + back_mid.reshape(NC1_TOTAL, D)).astype(jnp.bfloat16)
    mid_direct, mid_spill, mid_wgrad = node_backward(mid_out_grad, mid_in, mid_agg, mid_saved, weights[1])
    mid_grad = (mid_direct + spread_rows(mid_spill, mid_index, mid_edge_w, NC1_TOTAL)).astype(jnp.bfloat16)
    block_grads = mid_grad.reshape(NC1_TOTAL // BLOCK_ROWS, BLOCK_ROWS, D)[target]
    back_fine = jnp.einsum('rtj,trd->tjd', pool_tiles, block_grads.astype(jnp.float32)).reshape(NF_TOTAL, D)
    fine_out_grad = (fine_cotangent.astype(jnp.float32) + back_fine).astype(jnp.bfloat16)
    fine_direct, fine_spill, fine_wgrad = node_backward(fine_out_grad, features, fine_agg, fine_saved, weights[0])
    spread_fine = spread_rows(fine_spill, fine_index, fine_edge_w, NF_TOTAL + 2 * HALO)
    feature_grads = (fine_direct + spread_fine[HALO:HALO + NF_TOTAL]).astype(jnp.bfloat16)
    weight_grads = jnp.stack([fine_wgrad * (1.0 / jnp.sqrt(jnp.float32(NF_TOTAL))), mid_wgrad * (1.0 / jnp.sqrt(jnp.float32(NC1_TOTAL))), coarse_wgrad * (1.0 / jnp.sqrt(jnp.float32(NC2_TOTAL)))])
    return (feature_grads, weight_grads)
```

```python
import functools
import math

import jax
import jax.numpy as jnp
from jax import lax
from jax.experimental import pallas as pl
from jax.experimental.pallas import tpu as pltpu
from jax.sharding import PartitionSpec as P

HALO = 256
TILE = 256
BF = jnp.bfloat16
F32 = jnp.float32

VM = pl.BlockSpec(memory_space=pltpu.VMEM)
SM = pl.BlockSpec(memory_space=pltpu.SMEM)
ANY = pl.BlockSpec(memory_space=pl.ANY)


def dot(a, b):
    return jnp.dot(a, b, preferred_element_type=F32)


def dot_nt(a, b):
    return lax.dot_general(a, b, (((1,), (1,)), ((), ())), preferred_element_type=F32)


def dot_tn(a, b):
    return lax.dot_general(a, b, (((0,), (0,)), ((), ())), preferred_element_type=F32)


def silu(v):
    return v / (1.0 + jnp.exp(-v))


def silu_slope(v):
    s = 1.0 / (1.0 + jnp.exp(-v))
    return s * (1.0 + v * (1.0 - s))


def merged_weights(idx, ew):
    total = ew
    for r in range(1, idx.shape[0]):
        total = total + jnp.where(pltpu.roll(idx, r, 0) == idx, pltpu.roll(ew, r, 0), 0.0)
    return total.astype(BF)


def edge_columns(idx, ew, start, rows):
    count = idx.shape[0]
    lanes = idx.shape[1]
    position = lax.broadcasted_iota(jnp.int32, (rows, lanes), 0) + start
    position = position.astype(jnp.int16)
    picked = jnp.zeros((rows, lanes), BF)
    for k in range(count):
        picked = jnp.where(idx[k : k + 1, :] == position, ew[k : k + 1, :], picked)
    return picked


def fine_edges(off, ew, s_ref):
    for h in range(TILE // 128):
        lane = slice(128 * h, 128 * (h + 1))
        o = off[:, lane]
        weight = merged_weights(o, ew[:, lane])
        rel = o + lax.broadcasted_iota(jnp.int32, o.shape, 1) + HALO
        rel = rel.astype(jnp.int16)
        for c in range(2 * HALO // 128 + 1):
            s_ref[128 * (h + c) : 128 * (h + c + 1), lane] = edge_columns(
                rel, weight, 128 * c, 128
            )


def clear_corners(s_ref):
    for h in range(TILE // 128):
        lane = slice(128 * h, 128 * (h + 1))
        if h > 0:
            s_ref[: 128 * h, lane] = jnp.zeros((128 * h, 128), BF)
        last = 128 * h + 2 * HALO + 128
        if last < TILE + 2 * HALO:
            s_ref[last:, lane] = jnp.zeros((TILE + 2 * HALO - last, 128), BF)


def forward_weights(w):
    w01 = jnp.concatenate([jnp.transpose(w[0]), jnp.transpose(w[1])], axis=1)
    return w01, jnp.transpose(w[2]), jnp.transpose(w[3])


def pool_matrix(pool, tile_rows):
    lane = lax.broadcasted_iota(jnp.int32, pool.shape, 1) // tile_rows
    values = pool.astype(F32)
    parts = [jnp.where(lane == r, values, 0.0) for r in range(pool.shape[1] // tile_rows)]
    return jnp.concatenate(parts, axis=0).astype(BF)


def fine_tile(h_t, window_t, s, weights, pool, tile_rows):
    w01, w2t, w3t = weights
    agg = dot(window_t, s).astype(BF)
    first = dot(w01, jnp.concatenate([h_t, agg], axis=0))
    middle = silu(first).astype(BF)
    second = dot(w2t, middle)
    outer = silu(second).astype(BF)
    fine_out = (h_t.astype(F32) + dot(w3t, outer)).astype(BF)
    blocks = dot_nt(pool_matrix(pool, tile_rows), fine_out)
    return agg, blocks


def inner_kernel(
    tile_rows, feat_h, off_h, ew_h, w_h, pool_h, agg_ref, blocks_ref,
    feat, off, ew, w, pool, feat_t, s_ref, sems,
):
    copies = []
    for i, (src, dst) in enumerate(
        ((off_h, off), (ew_h, ew), (feat_h, feat), (w_h.at[0], w), (pool_h, pool))
    ):
        copy = pltpu.make_async_copy(src, dst, sems.at[i])
        copy.start()
        copies.append(copy)
    clear_corners(s_ref.at[0])
    clear_corners(s_ref.at[1])
    for copy in copies:
        copy.wait()
    feat_t[...] = jnp.transpose(feat[...])
    weights = forward_weights(w[...])
    tiles = feat.shape[0] // TILE
    per = TILE // tile_rows * pool.shape[0]
    for i in range(1, tiles - 1):
        cols = slice(i * TILE, (i + 1) * TILE)
        s = s_ref.at[i % 2]
        fine_edges(off[:, cols], ew[:, cols], s)
        agg, blocks = fine_tile(
            feat_t[:, cols],
            feat_t[:, i * TILE - HALO : (i + 1) * TILE + HALO],
            s[...],
            weights,
            pool[:, cols],
            tile_rows,
        )
        agg_ref[:, cols] = agg
        blocks_ref[i * per : (i + 1) * per, :] = blocks


def outer_kernel(
    tile_rows, peers, cap,
    left, right, feat, off, ew, w, pool, blocks_in, owner, slot, cot, nbrs, cew,
    agg_ref, send_ref, place_ref,
    s_ref, spread, ids, extra, counts,
):
    rows = feat.shape[0]
    block_rows = pool.shape[0]
    per_tile = TILE // tile_rows
    tile_count = rows // tile_rows
    n2 = cot.shape[0]
    clear_corners(s_ref.at[0])
    clear_corners(s_ref.at[1])
    weights = forward_weights(w[0])
    spread[...] = jnp.zeros(spread.shape, F32)
    ids[...] = jnp.full(ids.shape, -1.0, F32)
    for p in range(peers):
        counts[p] = 0
    lane_slot = lax.broadcasted_iota(jnp.int32, (1, 128), 1) // block_rows

    def place(t, values):
        o = owner[t]
        c = counts[o]
        counts[o] = c + 1
        q = o * cap + c
        place_ref[t] = q
        spread[pl.ds(pl.multiple_of(q * block_rows, 8), block_rows), :] = values
        row = ids[pl.ds(o, 1), :]
        ids[pl.ds(o, 1), :] = jnp.where(lane_slot == c, slot[t].astype(F32), row)

    results = {}
    for n, i in enumerate((0, rows // TILE - 1)):
        cols = slice(i * TILE, (i + 1) * TILE)
        s = s_ref.at[n]
        fine_edges(off[:, cols], ew[:, cols], s)
        if n == 0:
            window = jnp.concatenate([left[...], feat[: TILE + HALO, :]], axis=0)
            mine = slice(HALO, HALO + TILE)
        else:
            window = jnp.concatenate([feat[rows - TILE - HALO :, :], right[...]], axis=0)
            mine = slice(HALO, HALO + TILE)
        window_t = jnp.transpose(window)
        agg, blocks = fine_tile(
            window_t[:, mine], window_t, s[...], weights, pool[:, cols], tile_rows
        )
        agg_ref[:, n * TILE : (n + 1) * TILE] = agg
        results[i] = blocks
    for t in range(tile_count):
        i = t // per_tile
        if i in results:
            at = (t - i * per_tile) * block_rows
            values = results[i][at : at + block_rows, :]
        else:
            values = blocks_in[t * block_rows : (t + 1) * block_rows, :]
        place(t, values)
    nb = nbrs[...]
    extra[...] = jnp.zeros(extra.shape, F32)
    high = nb // 256
    extra[0:8, 0:n2] = high.astype(F32)
    extra[0:8, n2 : 2 * n2] = (nb - high * 256).astype(F32)
    ce = cew[...]
    ce_high = ce.astype(BF).astype(F32)
    extra[0:8, 2 * n2 : 3 * n2] = ce_high
    extra[0:8, 3 * n2 : 4 * n2] = ce - ce_high
    top = extra[0:8, :]
    last = lax.broadcasted_iota(jnp.int32, (8, 128), 0)
    chunk = cap * block_rows
    for p in range(peers):
        send_ref[p, 0:chunk, :] = spread[p * chunk : (p + 1) * chunk, :].astype(BF)
        send_ref[p, chunk : chunk + n2, :] = cot[...]
        below = jnp.where(last == 0, ids[p : p + 1, :], 0.0)
        send_ref[p, chunk + n2 : chunk + n2 + 16, :] = jnp.concatenate(
            [top, below], axis=0
        ).astype(BF)


def saved_kernel(
    feat, agg_in, agg_out, w, fine_cot, mid_nbrs, mid_ew, mid_cot,
    hid_ref, agg_ref, mid_ref, outer_ref, slope1_ref, slope2_ref, cot_ref,
    smid_ref, mcot_ref,
):
    rows = feat.shape[0]
    w01, w2t, _ = forward_weights(w[0])
    hid_ref[...] = jnp.transpose(feat[...])
    cot_ref[...] = jnp.transpose(fine_cot[...])
    mcot_ref[...] = jnp.transpose(mid_cot[...])
    tiles = rows // TILE
    for i in range(tiles):
        cols = slice(i * TILE, (i + 1) * TILE)
        if i == 0:
            agg = agg_out[:, :TILE]
        elif i == tiles - 1:
            agg = agg_out[:, TILE:]
        else:
            agg = agg_in[:, cols]
        agg_ref[:, cols] = agg
        first = dot(w01, jnp.concatenate([hid_ref[:, cols], agg], axis=0))
        s1 = 1.0 / (1.0 + jnp.exp(-first))
        middle = (first * s1).astype(BF)
        mid_ref[:, cols] = middle
        slope1_ref[:, cols] = s1 * (1.0 + first * (1.0 - s1))
        second = dot(w2t, middle)
        s2 = 1.0 / (1.0 + jnp.exp(-second))
        outer_ref[:, cols] = (second * s2).astype(BF)
        slope2_ref[:, cols] = s2 * (1.0 + second * (1.0 - s2))
    nodes = mid_nbrs.shape[1]
    for c in range(nodes // 128):
        lane = slice(128 * c, 128 * (c + 1))
        idx = mid_nbrs[:, lane]
        weight = merged_weights(idx, mid_ew[:, lane])
        idx = idx.astype(jnp.int16)
        for r in range(nodes // 128):
            smid_ref[128 * r : 128 * (r + 1), lane] = edge_columns(idx, weight, 128 * r, 128)


def mid_kernel(
    peers, cap, block_rows,
    got, smid, w, pool_mid,
    send_ref, hid_ref, agg_ref, mid_ref, outer_ref, slope1_ref, slope2_ref, sel_ref,
    blocks,
):
    chunk = cap * block_rows
    nodes = smid.shape[0]
    n2 = pool_mid.shape[0]
    rows = []
    for p in range(peers):
        rows.append(got[p, chunk + n2 : chunk + n2 + 16, :].astype(F32)[8:9, :])
    keys = jnp.transpose(jnp.concatenate(rows, axis=0))
    keys = keys * block_rows
    keys = keys + (lax.broadcasted_iota(jnp.int32, keys.shape, 0) % block_rows).astype(F32)
    keys = keys.astype(jnp.int32)
    lane = lax.broadcasted_iota(jnp.int32, (chunk, nodes), 1)
    for p in range(peers):
        sel_ref[p * chunk : (p + 1) * chunk, :] = jnp.where(
            keys[0:chunk, p : p + 1] == lane, 1.0, 0.0
        ).astype(BF)
        blocks[p * chunk : (p + 1) * chunk, :] = got[p, 0:chunk, :]
    w01, w2t, w3t = forward_weights(w[1])
    hidden = dot_tn(blocks[...], sel_ref[...]).astype(BF)
    hid_ref[...] = hidden
    agg = dot(hidden, smid[...]).astype(BF)
    agg_ref[...] = agg
    first = dot(w01, jnp.concatenate([hidden, agg], axis=0))
    s1 = 1.0 / (1.0 + jnp.exp(-first))
    middle = (first * s1).astype(BF)
    mid_ref[...] = middle
    second = dot(w2t, middle)
    s2 = 1.0 / (1.0 + jnp.exp(-second))
    outer = (second * s2).astype(BF)
    outer_ref[...] = outer
    mid_out = (hidden.astype(F32) + dot(w3t, outer)).astype(BF)
    coarse = dot_nt(pool_mid[...], mid_out).astype(BF)
    for p in range(peers):
        send_ref[p * n2 : (p + 1) * n2, :] = coarse
    slope1_ref[...] = s1 * (1.0 + first * (1.0 - s1))
    slope2_ref[...] = s2 * (1.0 + second * (1.0 - s2))


def coarse_edges_kernel(nbrs, ew, cot, s_ref, cot_ref):
    nodes = nbrs.shape[1]
    cot_ref[...] = jnp.transpose(cot[...])

    def column(c, _):
        lane = pl.ds(pl.multiple_of(c * 128, 128), 128)
        idx = nbrs[:, lane]
        weight = merged_weights(idx, ew[:, lane])
        idx = idx.astype(jnp.int16)
        for r in range(nodes // 128):
            s_ref[128 * r : 128 * (r + 1), lane] = edge_columns(idx, weight, 128 * r, 128)
        return 0

    lax.fori_loop(0, nodes // 128, column, 0)


def coarse_kernel(
    peers,
    got, sco, cot_all, w, cot_my, pool_mid, mcot, mhid, magg, mmid, mouter, msl1, msl2, smid, sel,
    send_ref, cwg_ref, gmid_ref, sg_ref, fg_ref,
):
    nodes = got.shape[0]
    n2 = cot_my.shape[0]
    me = lax.axis_index("nodes")
    width = min(TILE, nodes)
    hidden = jnp.transpose(got[...])
    w01, w2t, _ = forward_weights(w[2])
    mine = pl.ds(pl.multiple_of(me * n2, 16), n2)
    spread = jnp.zeros((n2, 128), F32)
    fg_mine = jnp.zeros((n2, 128), F32)
    grads = [jnp.zeros((128, 128), F32) for _ in range(4)]
    row = lax.broadcasted_iota(jnp.int32, (n2, width), 0) + me * n2
    lane = lax.broadcasted_iota(jnp.int32, (n2, width), 1)
    for i in range(nodes // width):
        cols = slice(i * width, (i + 1) * width)
        h = hidden[:, cols]
        agg = dot(hidden, sco[:, cols]).astype(BF)
        first = dot(w01, jnp.concatenate([h, agg], axis=0))
        s1 = 1.0 / (1.0 + jnp.exp(-first))
        middle = (first * s1).astype(BF)
        second = dot(w2t, middle)
        s2 = 1.0 / (1.0 + jnp.exp(-second))
        outer = (second * s2).astype(BF)
        g = cot_all[:, cols]
        sg = (dot(w[2, 3], g) * (s2 * (1.0 + second * (1.0 - s2)))).astype(BF)
        fg = (dot(w[2, 2], sg) * (s1 * (1.0 + first * (1.0 - s1)))).astype(BF)
        spill = dot(w[2, 1], fg).astype(BF)
        spread = spread + dot_nt(sco[mine, cols], spill)
        here = jnp.where(lane + i * width == row, 1.0, 0.0).astype(BF)
        fg_mine = fg_mine + dot_nt(here, fg)
        grads = [
            grads[0] + dot_nt(h, fg),
            grads[1] + dot_nt(agg, fg),
            grads[2] + dot_nt(middle, sg),
            grads[3] + dot_nt(outer, g),
        ]
    scale = 1.0 / math.sqrt(nodes)
    for m in range(4):
        cwg_ref[m] = grads[m] * scale
    direct = cot_my[...].astype(F32) + dot_nt(fg_mine.astype(BF), w[2, 0])
    coarse_grad = (direct + spread).astype(BF)
    back = dot_tn(coarse_grad, pool_mid[...])
    g = (mcot[...].astype(F32) + back).astype(BF)
    sg = (dot(w[1, 3], g) * msl2[...]).astype(BF)
    fg = (dot(w[1, 2], sg) * msl1[...]).astype(BF)
    spill = dot(w[1, 1], fg).astype(BF)
    mid_grad = (g.astype(F32) + dot(w[1, 0], fg) + dot_nt(spill, smid[...])).astype(BF)
    send_ref[...] = dot_nt(sel[...], mid_grad).astype(BF)
    gmid_ref[...] = g
    sg_ref[...] = sg
    fg_ref[...] = fg


def mid_wgrad_kernel(scale, hid, agg, mid, outer, g, sg, fg, out_ref):
    d = hid.shape[0]
    out_ref[0:d, :] = (dot_nt(hid[...], fg[...]) * scale).astype(BF)
    out_ref[d : 2 * d, :] = (dot_nt(agg[...], fg[...]) * scale).astype(BF)
    out_ref[2 * d : 3 * d, :] = (dot_nt(mid[...], sg[...]) * scale).astype(BF)
    out_ref[3 * d : 4 * d, :] = (dot_nt(outer[...], g[...]) * scale).astype(BF)


def fine_grad_kernel(
    tile_rows, scale,
    got, place, pool, w, hid, agg, mid, outer, slope1, slope2, cot, mid_wg,
    send_ref, g_ref, fg_ref,
    unpacked, blocks,
):
    rows = hid.shape[1]
    d = hid.shape[0]
    block_rows = pool.shape[0]
    unpacked[...] = got[...].astype(F32)
    for t in range(rows // tile_rows):
        at = pl.ds(pl.multiple_of(place[t] * block_rows, 8), block_rows)
        blocks[t * block_rows : (t + 1) * block_rows, :] = unpacked[at, :]
    per = TILE // tile_rows * block_rows
    grads = [jnp.zeros((d, d), F32) for _ in range(4)]
    for i in range(rows // TILE):
        cols = slice(i * TILE, (i + 1) * TILE)
        back = dot_tn(
            blocks[i * per : (i + 1) * per, :].astype(BF), pool_matrix(pool[:, cols], tile_rows)
        )
        g = (cot[:, cols].astype(F32) + back).astype(BF)
        sg = (dot(w[0, 3], g) * slope2[:, cols]).astype(BF)
        fg = (dot(w[0, 2], sg) * slope1[:, cols]).astype(BF)
        g_ref[:, cols] = g
        fg_ref[:, cols] = fg
        grads = [
            grads[0] + dot_nt(hid[:, cols], fg),
            grads[1] + dot_nt(agg[:, cols], fg),
            grads[2] + dot_nt(mid[:, cols], sg),
            grads[3] + dot_nt(outer[:, cols], g),
        ]
    for m in range(4):
        send_ref[m * d : (m + 1) * d, :] = (grads[m] * scale).astype(BF)
    send_ref[4 * d : 8 * d, :] = mid_wg[...]


def fine_spread_kernel(off, ew, w, g, fg, rim_l, rim_r, out_ref, s_ref, total):
    rows = g.shape[1]
    clear_corners(s_ref.at[0])
    clear_corners(s_ref.at[1])
    total[...] = jnp.zeros(total.shape, F32)
    for i in range(rows // TILE):
        cols = slice(i * TILE, (i + 1) * TILE)
        s = s_ref.at[i % 2]
        fine_edges(off[:, cols], ew[:, cols], s)
        fg_tile = fg[:, cols]
        direct = g[:, cols].astype(F32) + dot(w[0, 0], fg_tile)
        spill = dot(w[0, 1], fg_tile).astype(BF)
        window = slice(i * TILE, (i + 1) * TILE + 2 * HALO)
        total[window, :] = total[window, :] + dot_nt(s[...], spill)
        here = slice(HALO + i * TILE, HALO + (i + 1) * TILE)
        total[here, :] = total[here, :] + jnp.transpose(direct)
    rim_l[...] = total[:HALO, :].astype(BF)
    rim_r[...] = total[HALO + rows :, :].astype(BF)
    out_ref[...] = total[HALO : HALO + rows, :]


def join_kernel(total, from_left, from_right, out_ref):
    rows = total.shape[0]
    out_ref[:HALO, :] = (total[:HALO, :] + from_left[...].astype(F32)).astype(BF)
    out_ref[HALO : rows - HALO, :] = total[HALO : rows - HALO, :].astype(BF)
    out_ref[rows - HALO :, :] = (total[rows - HALO :, :] + from_right[...].astype(F32)).astype(BF)


def call(kernel, outs, args, in_specs=None, out_specs=None, scratch=(), us=3, mib=24):
    return pl.pallas_call(
        kernel,
        out_shape=outs,
        in_specs=in_specs or [VM] * len(args),
        out_specs=out_specs or jax.tree.map(lambda _: VM, outs),
        scratch_shapes=list(scratch),
        compiler_params=pltpu.CompilerParams(vmem_limit_bytes=mib << 20),
        cost_estimate=pl.CostEstimate(
            flops=0, bytes_accessed=int(us * 3_000_000), transcendentals=0
        ),
    )(*args)


def shape(dims, dtype=BF):
    return jax.ShapeDtypeStruct(dims, dtype)


def exchange(x):
    return lax.all_to_all(x, "nodes", split_axis=0, concat_axis=0, tiled=True)


def per_device(
    features,
    fine_cotangent,
    mid_cotangent,
    coarse_cotangent,
    weights,
    fine_offsets,
    fine_edge_w,
    pool_fine,
    owner_dev,
    coarse_slot,
    mid_nbrs,
    mid_edge_w,
    pool_mid,
    coarse_nbrs,
    coarse_edge_w,
):
    n, d = features.shape
    tile_count = owner_dev.shape[0]
    tile_rows = n // tile_count
    block_rows = pool_fine.shape[0]
    n1 = mid_cotangent.shape[0]
    n2 = coarse_cotangent.shape[0]
    edges = fine_offsets.shape[0]
    peers = lax.axis_size("nodes")
    cap = max(2, 2 * tile_count // peers)
    chunk = cap * block_rows
    window = TILE + 2 * HALO
    ends = peers - 1
    up = [(i, i + 1) for i in range(ends)]
    down = [(i + 1, i) for i in range(ends)]

    left = lax.ppermute(features[n - HALO :], "nodes", up)
    right = lax.ppermute(features[:HALO], "nodes", down)
    agg_in, blocks_in = call(
        functools.partial(inner_kernel, tile_rows),
        (shape((d, n)), shape((tile_count * block_rows, d), F32)),
        (features, fine_offsets, fine_edge_w, weights, pool_fine),
        in_specs=[ANY] * 5,
        scratch=(
            pltpu.VMEM((n, d), BF),
            pltpu.VMEM((edges, n), jnp.int32),
            pltpu.VMEM((edges, n), F32),
            pltpu.VMEM((4, d, d), BF),
            pltpu.VMEM((block_rows, n), BF),
            pltpu.VMEM((d, n), BF),
            pltpu.VMEM((2, window, TILE), BF),
            pltpu.SemaphoreType.DMA((5,)),
        ),
        us=6,
    )
    rows1 = chunk + n2 + 16
    agg_out, send1, place = call(
        functools.partial(outer_kernel, tile_rows, peers, cap),
        (shape((d, 2 * TILE)), shape((peers, rows1, d)), shape((tile_count,), jnp.int32)),
        (
            left, right, features, fine_offsets, fine_edge_w, weights, pool_fine, blocks_in,
            owner_dev.reshape(-1), coarse_slot, coarse_cotangent, coarse_nbrs, coarse_edge_w,
        ),
        in_specs=[VM] * 8 + [SM] * 2 + [VM] * 3,
        out_specs=(VM, VM, SM),
        scratch=(
            pltpu.VMEM((2, window, TILE), BF),
            pltpu.VMEM((peers * chunk, d), F32),
            pltpu.VMEM((peers, 128), F32),
            pltpu.VMEM((8, 128), F32),
            pltpu.SMEM((peers,), jnp.int32),
        ),
        us=3,
    )
    got1 = exchange(send1)
    hid, agg, mid, outer, slope1, slope2, cot, smid, mcot = call(
        saved_kernel,
        (
            shape((d, n)), shape((d, n)), shape((d, n)), shape((d, n)),
            shape((d, n), F32), shape((d, n), F32), shape((d, n)),
            shape((n1, n1)), shape((d, n1)),
        ),
        (
            features, agg_in, agg_out, weights, fine_cotangent, mid_nbrs, mid_edge_w,
            mid_cotangent,
        ),
        us=5,
    )
    send2, mhid, magg, mmid, mouter, mslope1, mslope2, sel = call(
        functools.partial(mid_kernel, peers, cap, block_rows),
        (
            shape((peers * n2, d)), shape((d, n1)), shape((d, n1)), shape((d, n1)),
            shape((d, n1)), shape((d, n1), F32), shape((d, n1), F32),
            shape((peers * chunk, n1)),
        ),
        (got1, smid, weights, pool_mid),
        scratch=(pltpu.VMEM((peers * chunk, d), BF),),
        us=3,
    )
    got2 = exchange(send2)
    extra = got1[:, chunk + n2 : chunk + n2 + edges, : 4 * n2].astype(F32)
    extra = extra.reshape(peers, edges, 4, n2).transpose(2, 1, 0, 3).reshape(4, edges, peers * n2)
    all_nbrs = (extra[0] * 256.0 + extra[1]).astype(jnp.int32)
    all_ew = extra[2] + extra[3]
    all_cot = got1[:, chunk : chunk + n2].reshape(peers * n2, d)
    total2 = peers * n2
    sco, cot_all = call(
        coarse_edges_kernel,
        (shape((total2, total2)), shape((d, total2))),
        (all_nbrs, all_ew, all_cot),
        us=2,
    )
    send3, coarse_wg, gmid, msg, mfg = call(
        functools.partial(coarse_kernel, peers),
        (
            shape((peers * chunk, d)), shape((4, d, d), F32), shape((d, n1)), shape((d, n1)),
            shape((d, n1)),
        ),
        (
            got2, sco, cot_all, weights, coarse_cotangent, pool_mid, mcot, mhid, magg, mmid,
            mouter, mslope1, mslope2, smid, sel,
        ),
        us=3,
    )
    got3 = exchange(send3)
    mid_wg = call(
        functools.partial(mid_wgrad_kernel, 1.0 / math.sqrt(n1 * peers)),
        shape((4 * d, d)),
        (mhid, magg, mmid, mouter, gmid, msg, mfg),
        us=2,
    )
    send4, g, fg = call(
        functools.partial(fine_grad_kernel, tile_rows, 1.0 / math.sqrt(n * peers)),
        (shape((8 * d, d)), shape((d, n)), shape((d, n))),
        (
            got3, place, pool_fine, weights, hid, agg, mid, outer, slope1, slope2, cot, mid_wg,
        ),
        in_specs=[VM, SM] + [VM] * 10,
        scratch=(
            pltpu.VMEM((peers * chunk, d), F32),
            pltpu.VMEM((tile_count * block_rows, d), F32),
        ),
        us=4,
    )
    got4 = exchange(send4)
    rim_l, rim_r, spread = call(
        fine_spread_kernel,
        (shape((HALO, d)), shape((HALO, d)), shape((n, d), F32)),
        (fine_offsets, fine_edge_w, weights, g, fg),
        scratch=(pltpu.VMEM((2, window, TILE), BF), pltpu.VMEM((n + 2 * HALO, d), F32)),
        us=6,
    )
    from_left = lax.ppermute(rim_r, "nodes", up)
    from_right = lax.ppermute(rim_l, "nodes", down)
    part = got4.astype(F32).reshape(peers, 8 * d // peers, d).sum(axis=0).astype(BF)
    got5 = exchange(jnp.tile(part, (peers, 1)))
    feature_grads = call(
        join_kernel, shape((n, d)), (spread, from_left, from_right), us=1
    )
    weight_grads = jnp.concatenate(
        [got5.reshape(2, 4, d, d).astype(F32), coarse_wg[None]], axis=0
    )
    return (feature_grads, weight_grads)


def solution(mesh):
    rows = P(("groups", "nodes"), None)
    cols = P("groups", "nodes")
    in_specs = (
        rows, rows, rows, rows, P(), cols, cols, cols, rows, P(("groups", "nodes")),
        cols, cols, rows, cols, cols,
    )
    out_specs = (rows, P("groups", None, None, None))
    return jax.shard_map(
        per_device, mesh=mesh, in_specs=in_specs, out_specs=out_specs, check_vma=False
    )
```

```python
import functools
import math

import jax
import jax.numpy as jnp
from jax import lax
from jax.experimental import pallas as pl
from jax.experimental.pallas import tpu as pltpu
from jax.sharding import PartitionSpec as P

HALO = 256
TILE = 256
BF = jnp.bfloat16
F32 = jnp.float32

VM = pl.BlockSpec(memory_space=pltpu.VMEM)
HB = pl.BlockSpec(memory_space=pltpu.HBM)
ANY = pl.BlockSpec(memory_space=pl.ANY)


def dot(a, b):
    return jnp.dot(a, b, preferred_element_type=F32)


def dot_nt(a, b):
    return lax.dot_general(a, b, (((1,), (1,)), ((), ())), preferred_element_type=F32)


def dot_tn(a, b):
    return lax.dot_general(a, b, (((0,), (0,)), ((), ())), preferred_element_type=F32)


def silu(v):
    return v / (1.0 + jnp.exp(-v))


def silu_slope(v):
    s = 1.0 / (1.0 + jnp.exp(-v))
    return s * (1.0 + v * (1.0 - s))


def merged_weights(idx, ew):
    total = ew
    for r in range(1, idx.shape[0]):
        total = total + jnp.where(pltpu.roll(idx, r, 0) == idx, pltpu.roll(ew, r, 0), 0.0)
    return total.astype(BF)


def edge_columns(idx, ew, start, rows):
    count = idx.shape[0]
    lanes = idx.shape[1]
    position = lax.broadcasted_iota(jnp.int32, (rows, lanes), 0) + start
    position = position.astype(jnp.int16)
    picked = jnp.zeros((rows, lanes), BF)
    for k in range(count):
        picked = jnp.where(idx[k : k + 1, :] == position, ew[k : k + 1, :], picked)
    return picked


def fine_edges(off, ew, s_ref):
    for h in range(TILE // 128):
        lane = slice(128 * h, 128 * (h + 1))
        o = off[:, lane]
        weight = merged_weights(o, ew[:, lane])
        rel = o + lax.broadcasted_iota(jnp.int32, o.shape, 1) + HALO
        rel = rel.astype(jnp.int16)
        for c in range(2 * HALO // 128 + 1):
            s_ref[128 * (h + c) : 128 * (h + c + 1), lane] = edge_columns(
                rel, weight, 128 * c, 128
            )


def clear_corners(s_ref):
    for h in range(TILE // 128):
        lane = slice(128 * h, 128 * (h + 1))
        if h > 0:
            s_ref[: 128 * h, lane] = jnp.zeros((128 * h, 128), BF)
        last = 128 * h + 2 * HALO + 128
        if last < TILE + 2 * HALO:
            s_ref[last:, lane] = jnp.zeros((TILE + 2 * HALO - last, 128), BF)


def forward_weights(w):
    w01 = jnp.concatenate([jnp.transpose(w[0]), jnp.transpose(w[1])], axis=1)
    return w01, jnp.transpose(w[2]), jnp.transpose(w[3])


def pool_matrix(pool, tile_rows):
    lane = lax.broadcasted_iota(jnp.int32, pool.shape, 1) // tile_rows
    values = pool.astype(F32)
    parts = [jnp.where(lane == r, values, 0.0) for r in range(pool.shape[1] // tile_rows)]
    return jnp.concatenate(parts, axis=0).astype(BF)


class Copies:
    def __init__(self, sems):
        self.sems = sems
        self.used = 0
        self.open = {}

    def start(self, source, target):
        copy = pltpu.make_async_copy(source, target, self.sems.at[self.used])
        self.used += 1
        copy.start()
        self.open[id(copy)] = copy
        return copy

    def wait(self, *copies):
        for copy in copies:
            if id(copy) in self.open:
                copy.wait()
                del self.open[id(copy)]

    def finish(self):
        self.wait(*list(self.open.values()))


def shape(dims, dtype=BF):
    return jax.ShapeDtypeStruct(dims, dtype)


def call(kernel, ins, outs, scratch=(), copies=0, us=3, mib=24):
    n_in, n_out = len(ins), len(outs)
    staged_in = [i for i, (_, kind) in enumerate(ins) if kind in "hs012"]
    staged_out = [i for i, (_, kind) in enumerate(outs) if kind in "hs"]
    spaces = {"h": pltpu.VMEM, "s": pltpu.SMEM}
    stage = []
    for i in staged_in:
        array, kind = ins[i]
        dims = array.shape[1:] if kind.isdigit() else array.shape
        stage.append(spaces.get(kind, pltpu.VMEM)(dims, array.dtype))
    stage += [spaces[outs[i][1]](outs[i][0].shape, outs[i][0].dtype) for i in staged_out]
    total = len(staged_in) + len(staged_out) + copies

    def body(*refs):
        in_refs, out_refs = list(refs[:n_in]), list(refs[n_in : n_in + n_out])
        rest = list(refs[n_in + n_out :])
        sems = rest.pop() if total else None
        stages, user = rest[: len(stage)], rest[len(stage) :]
        io = Copies(sems)
        pending = {}
        for i, ref in zip(staged_in, stages):
            kind = ins[i][1]
            source = in_refs[i].at[int(kind)] if kind.isdigit() else in_refs[i]
            pending[i] = io.start(source, ref)
            in_refs[i] = ref
        targets = {}
        for i, ref in zip(staged_out, stages[len(staged_in) :]):
            targets[i] = out_refs[i]
            out_refs[i] = ref

        def need(*which):
            io.wait(*[pending[i] for i in which or pending])

        def flush(*which):
            for i in which:
                io.start(out_refs[i], targets.pop(i))

        kernel(io, need, flush, in_refs, out_refs, *user)
        flush(*list(targets))
        io.finish()

    return pl.pallas_call(
        body,
        out_shape=[s for s, _ in outs],
        in_specs=[{"v": VM, "a": ANY}.get(kind, HB) for _, kind in ins],
        out_specs=[VM if kind == "v" else HB for _, kind in outs],
        scratch_shapes=stage
        + list(scratch)
        + ([pltpu.SemaphoreType.DMA((total,))] if total else []),
        compiler_params=pltpu.CompilerParams(vmem_limit_bytes=mib << 20),
        cost_estimate=pl.CostEstimate(
            flops=0, bytes_accessed=int(us * 3_000_000), transcendentals=0
        ),
    )(*[a for a, _ in ins])


def fine_tile(h_t, window_t, s, weights, pool):
    w01, w2t, w3t = weights
    agg = dot(window_t, s).astype(BF)
    first = dot(w01, jnp.concatenate([h_t, agg], axis=0))
    middle = silu(first).astype(BF)
    second = dot(w2t, middle)
    outer = silu(second).astype(BF)
    fine_out = (h_t.astype(F32) + dot(w3t, outer)).astype(BF)
    return agg, dot_nt(pool, fine_out)


def outer_tiles(tile_count, per):
    return list(range(per)) + list(range(tile_count - per, tile_count))


def inner_kernel(tile_rows, peers, cap, io, need, flush, ins, outs, feat_t, s_ref, ids, counts):
    off, ew, feat, w, pool, owner, slot, nbrs, cew, cot = ins
    so_ref, win_ref, w01_ref, w2t_ref, w3t_ref, po_ref, spread, ext_ref, agg_ref, place = outs
    rows, d = feat.shape
    block_rows = pool.shape[0]
    n2 = cot.shape[0]
    tiles = rows // TILE
    per = TILE // tile_rows
    tile_count = rows // tile_rows
    clear_corners(s_ref.at[0])
    clear_corners(s_ref.at[1])
    clear_corners(so_ref.at[0])
    clear_corners(so_ref.at[1])
    spread[...] = jnp.zeros(spread.shape, F32)
    ids[...] = jnp.full(ids.shape, -1.0, F32)
    for p in range(peers):
        counts[p] = 0
    need(5, 6)
    lane_slot = lax.broadcasted_iota(jnp.int32, (1, 128), 1) // block_rows
    first_tiles = outer_tiles(tile_count, per)
    for t in first_tiles + [t for t in range(tile_count) if t not in first_tiles]:
        o = owner[t]
        c = counts[o]
        counts[o] = c + 1
        place[t] = o * cap + c
        row = ids[pl.ds(o, 1), :]
        ids[pl.ds(o, 1), :] = jnp.where(lane_slot == c, slot[t].astype(F32), row)
    flush(9)
    need(0, 1)
    need(2)
    feat_t[...] = jnp.transpose(feat[...])
    need()
    weights = forward_weights(w)
    for i in range(1, tiles - 1):
        cols = slice(i * TILE, (i + 1) * TILE)
        s = s_ref.at[i % 2]
        fine_edges(off[:, cols], ew[:, cols], s)
        agg, blocks = fine_tile(
            feat_t[:, cols],
            feat_t[:, i * TILE - HALO : (i + 1) * TILE + HALO],
            s[...],
            weights,
            pool_matrix(pool[:, cols], tile_rows),
        )
        agg_ref[:, cols] = agg
        for j in range(per):
            at = pl.ds(pl.multiple_of(place[i * per + j] * block_rows, 8), block_rows)
            spread[at, :] = blocks[j * block_rows : (j + 1) * block_rows, :]
    for n, i in enumerate((0, tiles - 1)):
        cols = slice(i * TILE, (i + 1) * TILE)
        fine_edges(off[:, cols], ew[:, cols], so_ref.at[n])
        po_ref[n] = pool_matrix(pool[:, cols], tile_rows)
    win_ref[0] = feat_t[:, : TILE + HALO]
    win_ref[1] = feat_t[:, rows - TILE - HALO :]
    w01_ref[...], w2t_ref[...], w3t_ref[...] = weights
    nb = nbrs[...].astype(F32)
    high = jnp.floor(nb * (1.0 / 256.0))
    ce = cew[...]
    ce_high = ce.astype(BF).astype(F32)
    fields = [high, nb - high * 256.0, ce_high, ce - ce_high]
    fields.append(jnp.zeros((nb.shape[0], 128 - 4 * n2), F32))
    top = jnp.concatenate(fields, axis=1)
    sub = lax.broadcasted_iota(jnp.int32, (8, 128), 0)
    for p in range(peers):
        ext_ref[p, 0:n2, :] = cot[...]
        below = jnp.where(sub == 0, ids[p : p + 1, :], 0.0)
        ext_ref[p, n2 : n2 + 16, :] = jnp.concatenate([top, below], axis=0).astype(BF)


def outer_kernel(
    tile_rows, cap, block_rows, io, need, flush, ins, outs, agg_edge, spread, stage, counts
):
    left, right, s_in, win, w01, w2t, w3t, pool, spread_in, ext, agg_in, owner = ins
    send_ref, agg_ref = outs
    peers, chunk, d = stage.shape
    rows = agg_in.shape[1]
    per = TILE // tile_rows
    io.start(ext, send_ref.at[:, pl.ds(chunk, ext.shape[1]), :])
    inside = pl.ds(TILE, rows - 2 * TILE)
    io.start(agg_in.at[:, inside], agg_ref.at[:, inside])
    spread[...] = spread_in[...]
    for p in range(peers):
        counts[p] = 0
    weights = (w01[...], w2t[...], w3t[...])
    results = []
    for n in range(2):
        if n == 0:
            window_t = jnp.concatenate([jnp.transpose(left[...]), win[0]], axis=1)
        else:
            window_t = jnp.concatenate([win[1], jnp.transpose(right[...])], axis=1)
        agg, blocks = fine_tile(
            window_t[:, HALO : HALO + TILE], window_t, s_in[n], weights, pool[n]
        )
        agg_edge[:, n * TILE : (n + 1) * TILE] = agg
        results.append(blocks)
    io.start(agg_edge.at[:, pl.ds(0, TILE)], agg_ref.at[:, pl.ds(0, TILE)])
    io.start(agg_edge.at[:, pl.ds(TILE, TILE)], agg_ref.at[:, pl.ds(rows - TILE, TILE)])
    need()
    for j, t in enumerate(outer_tiles(rows // tile_rows, per)):
        o = owner[t]
        c = counts[o]
        counts[o] = c + 1
        at = pl.ds(pl.multiple_of((o * cap + c) * block_rows, 8), block_rows)
        blocks = results[j // per]
        spread[at, :] = blocks[j % per * block_rows : (j % per + 1) * block_rows, :]
    group = max(1, peers // 4)
    for p in range(peers):
        stage[p] = spread[p * chunk : (p + 1) * chunk, :].astype(BF)
        if p % group == group - 1:
            part = pl.ds(p + 1 - group, group)
            io.start(stage.at[part], send_ref.at[part, pl.ds(0, chunk), :])


def mid_edges(nbrs, ew, s_ref):
    nodes = nbrs.shape[1]
    for c in range(nodes // 128):
        lane = slice(128 * c, 128 * (c + 1))
        idx = nbrs[:, lane]
        weight = merged_weights(idx, ew[:, lane])
        idx = idx.astype(jnp.int16)
        for r in range(nodes // 128):
            s_ref[128 * r : 128 * (r + 1), lane] = edge_columns(idx, weight, 128 * r, 128)


def first_window_kernel(io, need, flush, ins, outs):
    nbrs, ew, w, pool_mid, _ = ins
    smid, w01_ref, w2t_ref, w3t_ref, pool_out = outs
    io.start(pool_mid, pool_out)
    need(0, 1)
    mid_edges(nbrs, ew, smid)
    need()
    w01_ref[...], w2t_ref[...], w3t_ref[...] = forward_weights(w)


def mid_kernel(block_rows, chunk, io, need, flush, ins, outs, blocks, coarse):
    got, smid, w01, w2t, w3t, pool_mid = ins
    send_ref, hid_ref, agg_ref, sel_ref, ext_ref = outs
    peers = got.shape[0]
    nodes = smid.shape[0]
    n2 = pool_mid.shape[0]
    io.start(got.at[:, pl.ds(chunk, n2 + 16), :], ext_ref)
    rows = [got[p, chunk + n2 : chunk + n2 + 16, :].astype(F32)[8:9, :] for p in range(peers)]
    keys = jnp.transpose(jnp.concatenate(rows, axis=0))
    keys = keys * block_rows
    keys = keys + (lax.broadcasted_iota(jnp.int32, keys.shape, 0) % block_rows).astype(F32)
    keys = keys.astype(jnp.int32)
    lane = lax.broadcasted_iota(jnp.int32, (chunk, nodes), 1)
    for p in range(peers):
        sel_ref[p * chunk : (p + 1) * chunk, :] = jnp.where(
            keys[0:chunk, p : p + 1] == lane, 1.0, 0.0
        ).astype(BF)
        blocks[p * chunk : (p + 1) * chunk, :] = got[p, 0:chunk, :]
    flush(3)
    hidden = dot_tn(blocks[...], sel_ref[...]).astype(BF)
    hid_ref[...] = hidden
    agg = dot(hidden, smid[...]).astype(BF)
    agg_ref[...] = agg
    flush(1, 2)
    middle = silu(dot(w01[...], jnp.concatenate([hidden, agg], axis=0))).astype(BF)
    outer = silu(dot(w2t[...], middle)).astype(BF)
    mid_out = (hidden.astype(F32) + dot(w3t[...], outer)).astype(BF)
    coarse[...] = dot_nt(pool_mid[...], mid_out).astype(BF)
    for p in range(peers):
        io.start(coarse, send_ref.at[p])


def second_window_kernel(io, need, flush, ins, outs, nb_ref, ew_ref):
    ext, hid, agg, mid_nbrs, mid_ew, mid_cot, sel_h, w_h, pool_h, cot_h, w1 = ins
    sco, cot_all, smid, mcot, sl1_ref, sl2_ref, sel, w12, pool_mid, cot_my = outs
    io.start(sel_h, sel)
    io.start(w_h.at[pl.ds(1, 2)], w12)
    io.start(pool_h, pool_mid)
    io.start(cot_h, cot_my)
    peers = ext.shape[0]
    n2 = cot_h.shape[0]
    nodes = peers * n2
    edges = mid_nbrs.shape[0]
    need()
    for p in range(peers):
        part = ext[p, n2 : n2 + 16, :].astype(F32)[0:edges, :]
        at = slice(p * n2, (p + 1) * n2)
        nb_ref[:, at] = (part[:, 0:n2] * 256.0 + part[:, n2 : 2 * n2]).astype(jnp.int32)
        ew_ref[:, at] = part[:, 2 * n2 : 3 * n2] + part[:, 3 * n2 : 4 * n2]
    cots = jnp.concatenate([ext[p, 0:n2, :] for p in range(peers)], axis=0)
    cot_all[...] = jnp.transpose(cots)
    mcot[...] = jnp.transpose(mid_cot[...])

    def column(c, _):
        lane = pl.ds(pl.multiple_of(c * 128, 128), 128)
        idx = nb_ref[:, lane]
        weight = merged_weights(idx, ew_ref[:, lane])
        idx = idx.astype(jnp.int16)
        for r in range(nodes // 128):
            sco[128 * r : 128 * (r + 1), lane] = edge_columns(idx, weight, 128 * r, 128)
        return 0

    lax.fori_loop(0, nodes // 128, column, 0)
    mid_edges(mid_nbrs, mid_ew, smid)
    w01, w2t, _ = forward_weights(w1)
    first = dot(w01, jnp.concatenate([hid[...], agg[...]], axis=0))
    s1 = 1.0 / (1.0 + jnp.exp(-first))
    second = dot(w2t, (first * s1).astype(BF))
    s2 = 1.0 / (1.0 + jnp.exp(-second))
    sl1_ref[...] = s1 * (1.0 + first * (1.0 - s1))
    sl2_ref[...] = s2 * (1.0 + second * (1.0 - s2))


def coarse_kernel(io, need, flush, ins, outs):
    got, sco, cot_all, smid, mcot, msl1, msl2, sel, w, pool_mid, cot_my = ins
    send_ref, gmid_ref, sg_ref, fg_ref, cwg_ref = outs
    nodes = got.shape[0]
    n2 = cot_my.shape[0]
    me = lax.axis_index("nodes")
    width = min(TILE, nodes)
    hidden = jnp.transpose(got[...])
    w01, w2t, _ = forward_weights(w.at[1])
    mine = pl.ds(pl.multiple_of(me * n2, 16), n2)
    spread = jnp.zeros((n2, 128), F32)
    fg_mine = jnp.zeros((n2, 128), F32)
    grads = [jnp.zeros((128, 128), F32) for _ in range(4)]
    row = lax.broadcasted_iota(jnp.int32, (n2, width), 0) + me * n2
    lane = lax.broadcasted_iota(jnp.int32, (n2, width), 1)
    for i in range(nodes // width):
        cols = slice(i * width, (i + 1) * width)
        h = hidden[:, cols]
        agg = dot(hidden, sco[:, cols]).astype(BF)
        first = dot(w01, jnp.concatenate([h, agg], axis=0))
        s1 = 1.0 / (1.0 + jnp.exp(-first))
        middle = (first * s1).astype(BF)
        second = dot(w2t, middle)
        s2 = 1.0 / (1.0 + jnp.exp(-second))
        outer = (second * s2).astype(BF)
        g = cot_all[:, cols]
        sg = (dot(w[1, 3], g) * (s2 * (1.0 + second * (1.0 - s2)))).astype(BF)
        fg = (dot(w[1, 2], sg) * (s1 * (1.0 + first * (1.0 - s1)))).astype(BF)
        spill = dot(w[1, 1], fg).astype(BF)
        spread = spread + dot_nt(sco[mine, cols], spill)
        here = jnp.where(lane + i * width == row, 1.0, 0.0).astype(BF)
        fg_mine = fg_mine + dot_nt(here, fg)
        grads = [
            grads[0] + dot_nt(h, fg),
            grads[1] + dot_nt(agg, fg),
            grads[2] + dot_nt(middle, sg),
            grads[3] + dot_nt(outer, g),
        ]
    scale = 1.0 / math.sqrt(nodes)
    for m in range(4):
        cwg_ref[m] = grads[m] * scale
    flush(4)
    direct = cot_my[...].astype(F32) + dot_nt(fg_mine.astype(BF), w[1, 0])
    coarse_grad = (direct + spread).astype(BF)
    back = dot_tn(coarse_grad, pool_mid[...])
    g = (mcot[...].astype(F32) + back).astype(BF)
    gmid_ref[...] = g
    sg = (dot(w[0, 3], g) * msl2[...]).astype(BF)
    sg_ref[...] = sg
    fg = (dot(w[0, 2], sg) * msl1[...]).astype(BF)
    fg_ref[...] = fg
    flush(1, 2, 3)
    spill = dot(w[0, 1], fg).astype(BF)
    mid_grad = (g.astype(F32) + dot(w[0, 0], fg) + dot_nt(spill, smid[...])).astype(BF)
    send_ref[...] = dot_nt(sel[...], mid_grad).astype(BF)


def third_window_kernel(tile_rows, mid_scale, io, need, flush, ins, outs):
    mhid, magg, gmid, msg, mfg, feat, fine_cot, w, pool, place, agg_h, w1 = ins
    wg_ref, hid_ref, agg, mid_ref, outer_ref, sl1_ref, sl2_ref, cot_ref, pick_ref, po_ref, w0 = outs
    d, rows = hid_ref.shape
    block_rows = pool.shape[0]
    per = TILE // tile_rows
    agg_copy = io.start(agg_h, agg)
    w_copy = io.start(w.at[0], w0)
    need()
    w01, w2t, _ = forward_weights(w1)
    middle = silu(dot(w01, jnp.concatenate([mhid[...], magg[...]], axis=0))).astype(BF)
    outer = silu(dot(w2t, middle)).astype(BF)
    wg_ref[0:d, :] = (dot_nt(mhid[...], mfg[...]) * mid_scale).astype(BF)
    wg_ref[d : 2 * d, :] = (dot_nt(magg[...], mfg[...]) * mid_scale).astype(BF)
    wg_ref[2 * d : 3 * d, :] = (dot_nt(middle, msg[...]) * mid_scale).astype(BF)
    wg_ref[3 * d : 4 * d, :] = (dot_nt(outer, gmid[...]) * mid_scale).astype(BF)
    hid_ref[...] = jnp.transpose(feat[...])
    cot_ref[...] = jnp.transpose(fine_cot[...])
    slots = pick_ref.shape[1]
    lane = lax.broadcasted_iota(jnp.int32, (block_rows, slots), 1)
    lane = lane - lax.broadcasted_iota(jnp.int32, (block_rows, slots), 0)
    for t in range(0, rows // tile_rows, 2):
        both = [jnp.where(lane == place[t + j] * block_rows, 1.0, 0.0) for j in range(2)]
        pick_ref[t * block_rows : (t + 2) * block_rows, :] = jnp.concatenate(
            both, axis=0
        ).astype(BF)
    io.wait(agg_copy, w_copy)
    w01, w2t, _ = forward_weights(w0)
    for i in range(rows // TILE):
        cols = slice(i * TILE, (i + 1) * TILE)
        first = dot(w01, jnp.concatenate([hid_ref[:, cols], agg[:, cols]], axis=0))
        s1 = 1.0 / (1.0 + jnp.exp(-first))
        middle = (first * s1).astype(BF)
        mid_ref[:, cols] = middle
        sl1_ref[:, cols] = s1 * (1.0 + first * (1.0 - s1))
        second = dot(w2t, middle)
        s2 = 1.0 / (1.0 + jnp.exp(-second))
        outer_ref[:, cols] = (second * s2).astype(BF)
        sl2_ref[:, cols] = s2 * (1.0 + second * (1.0 - s2))
        po_ref[i] = pool_matrix(pool[:, cols], tile_rows)


def fine_grad_kernel(scale, io, need, flush, ins, outs, g_ref, fg_ref):
    got, mid_wg, hid, agg, mid, outer, slope1, slope2, cot, pick, pool, w = ins
    send_ref, g_out, fg_out = outs
    d, rows = hid.shape
    send_ref[4 * d : 8 * d, :] = mid_wg[...]
    blocks = dot(pick[...], got[...]).astype(BF)
    per = pool.shape[1]
    grads = [jnp.zeros((d, d), F32) for _ in range(4)]
    for i in range(rows // TILE):
        cols = slice(i * TILE, (i + 1) * TILE)
        back = dot_tn(blocks[i * per : (i + 1) * per, :], pool[i])
        g = (cot[:, cols].astype(F32) + back).astype(BF)
        sg = (dot(w[3], g) * slope2[:, cols]).astype(BF)
        fg = (dot(w[2], sg) * slope1[:, cols]).astype(BF)
        g_ref[:, cols] = g
        fg_ref[:, cols] = fg
        grads = [
            grads[0] + dot_nt(hid[:, cols], fg),
            grads[1] + dot_nt(agg[:, cols], fg),
            grads[2] + dot_nt(mid[:, cols], sg),
            grads[3] + dot_nt(outer[:, cols], g),
        ]
    io.start(g_ref, g_out)
    io.start(fg_ref, fg_out)
    for m in range(4):
        send_ref[m * d : (m + 1) * d, :] = (grads[m] * scale).astype(BF)


def fine_spread_kernel(io, need, flush, ins, outs, s_ref, total):
    off, ew, w, g, fg = ins
    rim_l, rim_r, out_ref = outs
    rows = g.shape[1]
    clear_corners(s_ref.at[0])
    clear_corners(s_ref.at[1])
    total[...] = jnp.zeros(total.shape, F32)
    need()
    for i in range(rows // TILE):
        cols = slice(i * TILE, (i + 1) * TILE)
        s = s_ref.at[i % 2]
        fine_edges(off[:, cols], ew[:, cols], s)
        fg_tile = fg[:, cols]
        direct = g[:, cols].astype(F32) + dot(w[0], fg_tile)
        spill = dot(w[1], fg_tile).astype(BF)
        window = slice(i * TILE, (i + 1) * TILE + 2 * HALO)
        total[window, :] = total[window, :] + dot_nt(s[...], spill)
        here = slice(HALO + i * TILE, HALO + (i + 1) * TILE)
        total[here, :] = total[here, :] + jnp.transpose(direct)
    rim_l[...] = total[:HALO, :].astype(BF)
    rim_r[...] = total[HALO + rows :, :].astype(BF)
    out_ref[...] = total[HALO : HALO + rows, :]


def sum_kernel(io, need, flush, ins, outs, part):
    got, _ = ins
    send_ref = outs[0]
    peers = got.shape[0]
    part[...] = sum(got[p].astype(F32) for p in range(peers)).astype(BF)
    for p in range(peers):
        io.start(part, send_ref.at[p])


def join_kernel(io, need, flush, ins, outs):
    total, from_left, from_right = ins
    out_ref = outs[0]
    rows = total.shape[0]
    out_ref[:HALO, :] = (total[:HALO, :] + from_left[...].astype(F32)).astype(BF)
    out_ref[HALO : rows - HALO, :] = total[HALO : rows - HALO, :].astype(BF)
    out_ref[rows - HALO :, :] = (total[rows - HALO :, :] + from_right[...].astype(F32)).astype(BF)


def exchange(x):
    return lax.all_to_all(x, "nodes", split_axis=0, concat_axis=0, tiled=True)


def per_device(
    features,
    fine_cotangent,
    mid_cotangent,
    coarse_cotangent,
    weights,
    fine_offsets,
    fine_edge_w,
    pool_fine,
    owner_dev,
    coarse_slot,
    mid_nbrs,
    mid_edge_w,
    pool_mid,
    coarse_nbrs,
    coarse_edge_w,
):
    n, d = features.shape
    tile_count = owner_dev.shape[0]
    tile_rows = n // tile_count
    block_rows = pool_fine.shape[0]
    n1 = mid_cotangent.shape[0]
    n2 = coarse_cotangent.shape[0]
    edges = fine_offsets.shape[0]
    peers = lax.axis_size("nodes")
    cap = max(2, 2 * tile_count // peers)
    chunk = cap * block_rows
    window = TILE + 2 * HALO
    per = TILE // tile_rows * block_rows
    ends = peers - 1
    up = [(i, i + 1) for i in range(ends)]
    down = [(i + 1, i) for i in range(ends)]
    total2 = peers * n2

    left = lax.ppermute(features[n - HALO :], "nodes", up)
    right = lax.ppermute(features[:HALO], "nodes", down)
    owners = owner_dev.reshape(-1)
    s_out, win, w01, w2t, w3t, pool_out, spread, ext, agg_in, place = call(
        functools.partial(inner_kernel, tile_rows, peers, cap),
        [
            (fine_offsets, "h"), (fine_edge_w, "h"), (features, "h"), (weights, "0"),
            (pool_fine, "h"), (owners, "s"), (coarse_slot, "s"), (coarse_nbrs, "h"),
            (coarse_edge_w, "h"), (coarse_cotangent, "h"),
        ],
        [
            (shape((2, window, TILE)), "v"), (shape((2, d, TILE + HALO)), "v"),
            (shape((d, 2 * d)), "v"), (shape((d, d)), "v"), (shape((d, d)), "v"),
            (shape((2, per, TILE)), "v"), (shape((peers * chunk, d), F32), "v"),
            (shape((peers, n2 + 16, d)), "v"), (shape((d, n)), "v"),
            (shape((tile_count,), jnp.int32), "s"),
        ],
        scratch=(
            pltpu.VMEM((d, n), BF),
            pltpu.VMEM((2, window, TILE), BF),
            pltpu.VMEM((peers, 128), F32),
            pltpu.SMEM((peers,), jnp.int32),
        ),
        us=6,
    )
    send1, agg = call(
        functools.partial(outer_kernel, tile_rows, cap, block_rows),
        [
            (left, "v"), (right, "v"), (s_out, "v"), (win, "v"), (w01, "v"), (w2t, "v"),
            (w3t, "v"), (pool_out, "v"), (spread, "v"), (ext, "v"), (agg_in, "v"), (owners, "s"),
        ],
        [(shape((peers, chunk + n2 + 16, d)), "r"), (shape((d, n)), "r")],
        scratch=(
            pltpu.VMEM((d, 2 * TILE), BF),
            pltpu.VMEM((peers * chunk, d), F32),
            pltpu.VMEM((peers, chunk, d), BF),
            pltpu.SMEM((peers,), jnp.int32),
        ),
        copies=8,
        us=3,
    )
    got1 = exchange(send1)
    smid, m01, m2t, m3t, pool_v = call(
        first_window_kernel,
        [
            (mid_nbrs, "h"), (mid_edge_w, "h"), (weights, "1"), (pool_mid, "r"), (agg, "r"),
        ],
        [
            (shape((n1, n1)), "v"), (shape((d, 2 * d)), "v"), (shape((d, d)), "v"),
            (shape((d, d)), "v"), (shape((n2, n1)), "v"),
        ],
        copies=1,
        us=6,
    )
    send2, mhid, magg, sel, ext = call(
        functools.partial(mid_kernel, block_rows, chunk),
        [(got1, "v"), (smid, "v"), (m01, "v"), (m2t, "v"), (m3t, "v"), (pool_v, "v")],
        [
            (shape((peers, n2, d)), "r"), (shape((d, n1)), "h"), (shape((d, n1)), "h"),
            (shape((peers * chunk, n1)), "h"), (shape((peers, n2 + 16, d)), "r"),
        ],
        scratch=(pltpu.VMEM((peers * chunk, d), BF), pltpu.VMEM((n2, d), BF)),
        copies=peers + 1,
        us=3,
    )
    got2 = exchange(send2)
    second = call(
        second_window_kernel,
        [
            (ext, "h"), (mhid, "h"), (magg, "h"), (mid_nbrs, "h"), (mid_edge_w, "h"),
            (mid_cotangent, "h"), (sel, "r"), (weights, "r"), (pool_mid, "r"),
            (coarse_cotangent, "r"), (weights, "1"),
        ],
        [
            (shape((total2, total2)), "v"), (shape((d, total2)), "v"), (shape((n1, n1)), "v"),
            (shape((d, n1)), "v"), (shape((d, n1), F32), "v"), (shape((d, n1), F32), "v"),
            (shape((peers * chunk, n1)), "v"), (shape((2, 4, d, d)), "v"),
            (shape((n2, n1)), "v"), (shape((n2, d)), "v"),
        ],
        scratch=(pltpu.VMEM((edges, total2), jnp.int32), pltpu.VMEM((edges, total2), F32)),
        copies=4,
        us=6,
    )
    send3, gmid, msg, mfg, coarse_wg = call(
        coarse_kernel,
        [(got2.reshape(total2, d), "v")] + [(x, "v") for x in second],
        [
            (shape((peers * chunk, d)), "h"), (shape((d, n1)), "h"), (shape((d, n1)), "h"),
            (shape((d, n1)), "h"), (shape((4, d, d), F32), "h"),
        ],
        us=3,
    )
    got3 = exchange(send3.reshape(peers, chunk, d))
    third = call(
        functools.partial(third_window_kernel, tile_rows, 1.0 / math.sqrt(n1 * peers)),
        [
            (mhid, "h"), (magg, "h"), (gmid, "h"), (msg, "h"), (mfg, "h"), (features, "h"),
            (fine_cotangent, "h"), (weights, "r"), (pool_fine, "h"), (place, "s"), (agg, "r"),
            (weights, "1"),
        ],
        [
            (shape((4 * d, d)), "v"), (shape((d, n)), "v"), (shape((d, n)), "v"),
            (shape((d, n)), "v"), (shape((d, n)), "v"), (shape((d, n), F32), "v"),
            (shape((d, n), F32), "v"), (shape((d, n)), "v"),
            (shape((tile_count * block_rows, peers * chunk)), "v"),
            (shape((n // TILE, per, TILE)), "v"), (shape((4, d, d)), "v"),
        ],
        copies=2,
        us=6,
    )
    send4, g, fg = call(
        functools.partial(fine_grad_kernel, 1.0 / math.sqrt(n * peers)),
        [(got3.reshape(peers * chunk, d), "v")] + [(x, "v") for x in third],
        [(shape((8 * d, d)), "h"), (shape((d, n)), "r"), (shape((d, n)), "r")],
        scratch=(pltpu.VMEM((d, n), BF), pltpu.VMEM((d, n), BF)),
        copies=2,
        us=4,
    )
    got4 = exchange(send4.reshape(peers, 8 * d // peers, d))
    rim_l, rim_r, spread = call(
        fine_spread_kernel,
        [(fine_offsets, "h"), (fine_edge_w, "h"), (weights, "0"), (g, "h"), (fg, "h")],
        [(shape((HALO, d)), "v"), (shape((HALO, d)), "v"), (shape((n, d), F32), "v")],
        scratch=(pltpu.VMEM((2, window, TILE), BF), pltpu.VMEM((n + 2 * HALO, d), F32)),
        us=6,
    )
    (send5,) = call(
        sum_kernel,
        [(got4, "v"), (rim_l, "a")],
        [(shape((peers, 8 * d // peers, d)), "r")],
        scratch=(pltpu.VMEM((8 * d // peers, d), BF),),
        copies=peers,
        us=1,
    )
    got5 = exchange(send5)
    from_left = lax.ppermute(rim_r, "nodes", up)
    from_right = lax.ppermute(rim_l, "nodes", down)
    (feature_grads,) = call(
        join_kernel,
        [(spread, "v"), (from_left, "v"), (from_right, "v")],
        [(shape((n, d)), "v")],
        us=1,
    )
    weight_grads = jnp.concatenate(
        [got5.reshape(2, 4, d, d).astype(F32), coarse_wg[None]], axis=0
    )
    return (feature_grads, weight_grads)


def solution(mesh):
    rows = P(("groups", "nodes"), None)
    cols = P("groups", "nodes")
    in_specs = (
        rows, rows, rows, rows, P(), cols, cols, cols, rows, P(("groups", "nodes")),
        cols, cols, rows, cols, cols,
    )
    out_specs = (rows, P("groups", None, None, None))
    return jax.shard_map(
        per_device, mesh=mesh, in_specs=in_specs, out_specs=out_specs, check_vma=False
    )
```

```python
import functools
import math

import jax
import jax.numpy as jnp
from jax import lax
from jax.experimental import pallas as pl
from jax.experimental.pallas import tpu as pltpu
from jax.sharding import PartitionSpec as P

HALO = 256
TILE = 256
BIG = 56
BF = jnp.bfloat16
F32 = jnp.float32

VM = pl.BlockSpec(memory_space=pltpu.VMEM)
HB = pl.BlockSpec(memory_space=pltpu.HBM)
ANY = pl.BlockSpec(memory_space=pl.ANY)


def dot(a, b):
    return jnp.dot(a, b, preferred_element_type=F32)


def dot_nt(a, b):
    return lax.dot_general(a, b, (((1,), (1,)), ((), ())), preferred_element_type=F32)


def dot_tn(a, b):
    return lax.dot_general(a, b, (((0,), (0,)), ((), ())), preferred_element_type=F32)


def silu(v):
    return v / (1.0 + jnp.exp(-v))


def silu_slope(v):
    s = 1.0 / (1.0 + jnp.exp(-v))
    return s * (1.0 + v * (1.0 - s))


def merged_weights(idx, ew):
    total = ew
    for r in range(1, idx.shape[0]):
        total = total + jnp.where(pltpu.roll(idx, r, 0) == idx, pltpu.roll(ew, r, 0), 0.0)
    return total.astype(BF)


def edge_columns(idx, ew, start, rows):
    count = idx.shape[0]
    lanes = idx.shape[1]
    position = lax.broadcasted_iota(jnp.int32, (rows, lanes), 0) + start
    position = position.astype(jnp.int16)
    picked = jnp.zeros((rows, lanes), BF)
    for k in range(count):
        picked = jnp.where(idx[k : k + 1, :] == position, ew[k : k + 1, :], picked)
    return picked


def fine_edges(off, ew, s_ref):
    for h in range(TILE // 128):
        lane = slice(128 * h, 128 * (h + 1))
        o = off[:, lane]
        weight = merged_weights(o, ew[:, lane])
        rel = o + lax.broadcasted_iota(jnp.int32, o.shape, 1) + HALO
        rel = rel.astype(jnp.int16)
        for c in range(2 * HALO // 128 + 1):
            s_ref[128 * (h + c) : 128 * (h + c + 1), lane] = edge_columns(
                rel, weight, 128 * c, 128
            )


def clear_corners(s_ref):
    for h in range(TILE // 128):
        lane = slice(128 * h, 128 * (h + 1))
        if h > 0:
            s_ref[: 128 * h, lane] = jnp.zeros((128 * h, 128), BF)
        last = 128 * h + 2 * HALO + 128
        if last < TILE + 2 * HALO:
            s_ref[last:, lane] = jnp.zeros((TILE + 2 * HALO - last, 128), BF)


def forward_weights(w):
    w01 = jnp.concatenate([jnp.transpose(w[0]), jnp.transpose(w[1])], axis=1)
    return w01, jnp.transpose(w[2]), jnp.transpose(w[3])


def pool_matrix(pool, tile_rows):
    lane = lax.broadcasted_iota(jnp.int32, pool.shape, 1) // tile_rows
    values = pool.astype(F32)
    parts = [jnp.where(lane == r, values, 0.0) for r in range(pool.shape[1] // tile_rows)]
    return jnp.concatenate(parts, axis=0).astype(BF)


class Copies:
    def __init__(self, sems):
        self.sems = sems
        self.used = 0
        self.open = {}

    def start(self, source, target):
        copy = pltpu.make_async_copy(source, target, self.sems.at[self.used])
        self.used += 1
        copy.start()
        self.open[id(copy)] = copy
        return copy

    def wait(self, *copies):
        for copy in copies:
            if id(copy) in self.open:
                copy.wait()
                del self.open[id(copy)]

    def finish(self):
        self.wait(*list(self.open.values()))


def shape(dims, dtype=BF):
    return jax.ShapeDtypeStruct(dims, dtype)


def call(kernel, ins, outs, scratch=(), copies=0, us=3, mib=24):
    n_in, n_out = len(ins), len(outs)
    staged_in = [i for i, (_, kind) in enumerate(ins) if kind in "hs012"]
    staged_out = [i for i, (_, kind) in enumerate(outs) if kind in "hs"]
    spaces = {"h": pltpu.VMEM, "s": pltpu.SMEM}
    stage = []
    for i in staged_in:
        array, kind = ins[i]
        dims = array.shape[1:] if kind.isdigit() else array.shape
        stage.append(spaces.get(kind, pltpu.VMEM)(dims, array.dtype))
    stage += [spaces[outs[i][1]](outs[i][0].shape, outs[i][0].dtype) for i in staged_out]
    total = len(staged_in) + len(staged_out) + copies

    def body(*refs):
        in_refs, out_refs = list(refs[:n_in]), list(refs[n_in : n_in + n_out])
        rest = list(refs[n_in + n_out :])
        sems = rest.pop() if total else None
        stages, user = rest[: len(stage)], rest[len(stage) :]
        io = Copies(sems)
        pending = {}
        for i, ref in zip(staged_in, stages):
            kind = ins[i][1]
            source = in_refs[i].at[int(kind)] if kind.isdigit() else in_refs[i]
            pending[i] = io.start(source, ref)
            in_refs[i] = ref
        targets = {}
        for i, ref in zip(staged_out, stages[len(staged_in) :]):
            targets[i] = out_refs[i]
            out_refs[i] = ref

        def need(*which):
            io.wait(*[pending[i] for i in which or pending])

        def flush(*which):
            for i in which:
                io.start(out_refs[i], targets.pop(i))

        kernel(io, need, flush, in_refs, out_refs, *user)
        flush(*list(targets))
        io.finish()

    return pl.pallas_call(
        body,
        out_shape=[s for s, _ in outs],
        in_specs=[{"v": VM, "a": ANY}.get(kind, HB) for _, kind in ins],
        out_specs=[VM if kind == "v" else HB for _, kind in outs],
        scratch_shapes=stage
        + list(scratch)
        + ([pltpu.SemaphoreType.DMA((total,))] if total else []),
        compiler_params=pltpu.CompilerParams(vmem_limit_bytes=mib << 20),
        cost_estimate=pl.CostEstimate(
            flops=0, bytes_accessed=int(us * 3_000_000), transcendentals=0
        ),
    )(*[a for a, _ in ins])


def fine_tile(h_t, window_t, s, weights, pool):
    w01, w2t, w3t = weights
    agg = dot(window_t, s).astype(BF)
    first = dot(w01, jnp.concatenate([h_t, agg], axis=0))
    middle = silu(first).astype(BF)
    second = dot(w2t, middle)
    outer = silu(second).astype(BF)
    fine_out = (h_t.astype(F32) + dot(w3t, outer)).astype(BF)
    return agg, dot_nt(pool, fine_out)


def outer_tiles(tile_count, per):
    return list(range(per)) + list(range(tile_count - per, tile_count))


def inner_kernel(tile_rows, peers, cap, io, need, flush, ins, outs, feat_t, s_ref, ids, counts):
    off, ew, feat, w, pool, owner, slot, nbrs, cew, cot = ins
    so_ref, win_ref, w01_ref, w2t_ref, w3t_ref, po_ref, spread, ext_ref, agg_ref, place = outs
    rows, d = feat.shape
    block_rows = pool.shape[0]
    n2 = cot.shape[0]
    tiles = rows // TILE
    per = TILE // tile_rows
    tile_count = rows // tile_rows
    clear_corners(s_ref.at[0])
    clear_corners(s_ref.at[1])
    clear_corners(so_ref.at[0])
    clear_corners(so_ref.at[1])
    spread[...] = jnp.zeros(spread.shape, F32)
    ids[...] = jnp.full(ids.shape, -1.0, F32)
    for p in range(peers):
        counts[p] = 0
    need(5, 6)
    lane_slot = lax.broadcasted_iota(jnp.int32, (1, 128), 1) // block_rows
    first_tiles = outer_tiles(tile_count, per)
    for t in first_tiles + [t for t in range(tile_count) if t not in first_tiles]:
        o = owner[t]
        c = counts[o]
        counts[o] = c + 1
        place[t] = o * cap + c
        row = ids[pl.ds(o, 1), :]
        ids[pl.ds(o, 1), :] = jnp.where(lane_slot == c, slot[t].astype(F32), row)
    flush(9)
    need(0, 1)
    need(2)
    feat_t[...] = jnp.transpose(feat[...])
    need()
    weights = forward_weights(w)
    for i in range(1, tiles - 1):
        cols = slice(i * TILE, (i + 1) * TILE)
        s = s_ref.at[i % 2]
        fine_edges(off[:, cols], ew[:, cols], s)
        agg, blocks = fine_tile(
            feat_t[:, cols],
            feat_t[:, i * TILE - HALO : (i + 1) * TILE + HALO],
            s[...],
            weights,
            pool_matrix(pool[:, cols], tile_rows),
        )
        agg_ref[:, cols] = agg
        for j in range(per):
            at = pl.ds(pl.multiple_of(place[i * per + j] * block_rows, 8), block_rows)
            spread[at, :] = blocks[j * block_rows : (j + 1) * block_rows, :]
    for n, i in enumerate((0, tiles - 1)):
        cols = slice(i * TILE, (i + 1) * TILE)
        fine_edges(off[:, cols], ew[:, cols], so_ref.at[n])
        po_ref[n] = pool_matrix(pool[:, cols], tile_rows)
    win_ref[0] = feat_t[:, : TILE + HALO]
    win_ref[1] = feat_t[:, rows - TILE - HALO :]
    w01_ref[...], w2t_ref[...], w3t_ref[...] = weights
    nb = nbrs[...].astype(F32)
    high = jnp.floor(nb * (1.0 / 256.0))
    ce = cew[...]
    ce_high = ce.astype(BF).astype(F32)
    fields = [high, nb - high * 256.0, ce_high, ce - ce_high]
    fields.append(jnp.zeros((nb.shape[0], 128 - 4 * n2), F32))
    top = jnp.concatenate(fields, axis=1)
    sub = lax.broadcasted_iota(jnp.int32, (8, 128), 0)
    for p in range(peers):
        ext_ref[p, 0:n2, :] = cot[...]
        below = jnp.where(sub == 0, ids[p : p + 1, :], 0.0)
        ext_ref[p, n2 : n2 + 16, :] = jnp.concatenate([top, below], axis=0).astype(BF)


def outer_kernel(
    tile_rows, cap, block_rows, io, need, flush, ins, outs, agg_edge, spread, stage, counts
):
    left, right, s_in, win, w01, w2t, w3t, pool, spread_in, ext, agg_in, owner = ins
    send_ref, agg_ref = outs
    peers, chunk, d = stage.shape
    rows = agg_in.shape[1]
    per = TILE // tile_rows
    io.start(ext, send_ref.at[:, pl.ds(chunk, ext.shape[1]), :])
    inside = pl.ds(TILE, rows - 2 * TILE)
    io.start(agg_in.at[:, inside], agg_ref.at[:, inside])
    spread[...] = spread_in[...]
    for p in range(peers):
        counts[p] = 0
    weights = (w01[...], w2t[...], w3t[...])
    results = []
    for n in range(2):
        if n == 0:
            window_t = jnp.concatenate([jnp.transpose(left[...]), win[0]], axis=1)
        else:
            window_t = jnp.concatenate([win[1], jnp.transpose(right[...])], axis=1)
        agg, blocks = fine_tile(
            window_t[:, HALO : HALO + TILE], window_t, s_in[n], weights, pool[n]
        )
        agg_edge[:, n * TILE : (n + 1) * TILE] = agg
        results.append(blocks)
    io.start(agg_edge.at[:, pl.ds(0, TILE)], agg_ref.at[:, pl.ds(0, TILE)])
    io.start(agg_edge.at[:, pl.ds(TILE, TILE)], agg_ref.at[:, pl.ds(rows - TILE, TILE)])
    need()
    for j, t in enumerate(outer_tiles(rows // tile_rows, per)):
        o = owner[t]
        c = counts[o]
        counts[o] = c + 1
        at = pl.ds(pl.multiple_of((o * cap + c) * block_rows, 8), block_rows)
        blocks = results[j // per]
        spread[at, :] = blocks[j % per * block_rows : (j % per + 1) * block_rows, :]
    group = max(1, peers // 4)
    for p in range(peers):
        stage[p] = spread[p * chunk : (p + 1) * chunk, :].astype(BF)
        if p % group == group - 1:
            part = pl.ds(p + 1 - group, group)
            io.start(stage.at[part], send_ref.at[part, pl.ds(0, chunk), :])


def mid_edges(nbrs, ew, s_ref):
    nodes = nbrs.shape[1]
    for c in range(nodes // 128):
        lane = slice(128 * c, 128 * (c + 1))
        idx = nbrs[:, lane]
        weight = merged_weights(idx, ew[:, lane])
        idx = idx.astype(jnp.int16)
        for r in range(nodes // 128):
            s_ref[128 * r : 128 * (r + 1), lane] = edge_columns(idx, weight, 128 * r, 128)


def first_window_kernel(io, need, flush, ins, outs):
    nbrs, ew, w, _ = ins
    smid, w01_ref, w2t_ref, w3t_ref = outs
    need(0, 1)
    mid_edges(nbrs, ew, smid)
    flush(0)
    need()
    w01_ref[...], w2t_ref[...], w3t_ref[...] = forward_weights(w)


def mid_kernel(block_rows, chunk, io, need, flush, ins, outs, blocks, coarse):
    got, smid, w01, w2t, w3t, pool_mid = ins
    send_ref, hid_ref, agg_ref, sel_ref, ext_ref = outs
    peers = got.shape[0]
    nodes = smid.shape[0]
    n2 = pool_mid.shape[0]
    need(0)
    io.start(got.at[:, pl.ds(chunk, n2 + 16), :], ext_ref)
    rows = [got[p, chunk + n2 : chunk + n2 + 16, :].astype(F32)[8:9, :] for p in range(peers)]
    keys = jnp.transpose(jnp.concatenate(rows, axis=0))
    keys = keys * block_rows
    keys = keys + (lax.broadcasted_iota(jnp.int32, keys.shape, 0) % block_rows).astype(F32)
    keys = keys.astype(jnp.int32)
    lane = lax.broadcasted_iota(jnp.int32, (chunk, nodes), 1)
    for p in range(peers):
        sel_ref[p * chunk : (p + 1) * chunk, :] = jnp.where(
            keys[0:chunk, p : p + 1] == lane, 1.0, 0.0
        ).astype(BF)
        blocks[p * chunk : (p + 1) * chunk, :] = got[p, 0:chunk, :]
    flush(3)
    hidden = dot_tn(blocks[...], sel_ref[...]).astype(BF)
    hid_ref[...] = hidden
    need()
    agg = dot(hidden, smid[...]).astype(BF)
    agg_ref[...] = agg
    flush(1, 2)
    middle = silu(dot(w01[...], jnp.concatenate([hidden, agg], axis=0))).astype(BF)
    outer = silu(dot(w2t[...], middle)).astype(BF)
    mid_out = (hidden.astype(F32) + dot(w3t[...], outer)).astype(BF)
    coarse[...] = dot_nt(pool_mid[...], mid_out).astype(BF)
    for p in range(peers):
        io.start(coarse, send_ref.at[p])


def second_window_kernel(io, need, flush, ins, outs, nb_ref, ew_ref):
    ext, hid, agg, mid_cot, w1 = ins
    sco, cot_all, mcot, sl1_ref, sl2_ref = outs
    peers = ext.shape[0]
    n2 = ext.shape[1] - 16
    nodes = peers * n2
    edges = nb_ref.shape[0]
    need()
    for p in range(peers):
        part = ext[p, n2 : n2 + 16, :].astype(F32)[0:edges, :]
        at = slice(p * n2, (p + 1) * n2)
        nb_ref[:, at] = (part[:, 0:n2] * 256.0 + part[:, n2 : 2 * n2]).astype(jnp.int32)
        ew_ref[:, at] = part[:, 2 * n2 : 3 * n2] + part[:, 3 * n2 : 4 * n2]
    cots = jnp.concatenate([ext[p, 0:n2, :] for p in range(peers)], axis=0)
    cot_all[...] = jnp.transpose(cots)
    mcot[...] = jnp.transpose(mid_cot[...])

    def column(c, _):
        lane = pl.ds(pl.multiple_of(c * 128, 128), 128)
        idx = nb_ref[:, lane]
        weight = merged_weights(idx, ew_ref[:, lane])
        idx = idx.astype(jnp.int16)
        for r in range(nodes // 128):
            sco[128 * r : 128 * (r + 1), lane] = edge_columns(idx, weight, 128 * r, 128)
        return 0

    lax.fori_loop(0, nodes // 128, column, 0)
    flush(0, 1, 2)
    w01, w2t, _ = forward_weights(w1)
    first = dot(w01, jnp.concatenate([hid[...], agg[...]], axis=0))
    s1 = 1.0 / (1.0 + jnp.exp(-first))
    second = dot(w2t, (first * s1).astype(BF))
    s2 = 1.0 / (1.0 + jnp.exp(-second))
    sl1_ref[...] = s1 * (1.0 + first * (1.0 - s1))
    sl2_ref[...] = s2 * (1.0 + second * (1.0 - s2))


def coarse_kernel(io, need, flush, ins, outs):
    got, sco, w2, cot_all, cot_my, pool_mid, mcot, w1, msl2, msl1, smid, sel = ins
    send_ref, gmid_ref, sg_ref, fg_ref, cwg_ref = outs
    nodes = got.shape[0]
    n2 = cot_my.shape[0]
    me = lax.axis_index("nodes")
    width = min(TILE, nodes)
    need(0)
    hidden = jnp.transpose(got[...])
    need(1, 2, 3)
    w01, w2t, _ = forward_weights(w2)
    mine = pl.ds(pl.multiple_of(me * n2, 16), n2)
    spread = jnp.zeros((n2, 128), F32)
    fg_mine = jnp.zeros((n2, 128), F32)
    grads = [jnp.zeros((128, 128), F32) for _ in range(4)]
    row = lax.broadcasted_iota(jnp.int32, (n2, width), 0) + me * n2
    lane = lax.broadcasted_iota(jnp.int32, (n2, width), 1)
    for i in range(nodes // width):
        cols = slice(i * width, (i + 1) * width)
        h = hidden[:, cols]
        agg = dot(hidden, sco[:, cols]).astype(BF)
        first = dot(w01, jnp.concatenate([h, agg], axis=0))
        s1 = 1.0 / (1.0 + jnp.exp(-first))
        middle = (first * s1).astype(BF)
        second = dot(w2t, middle)
        s2 = 1.0 / (1.0 + jnp.exp(-second))
        outer = (second * s2).astype(BF)
        g = cot_all[:, cols]
        sg = (dot(w2[3], g) * (s2 * (1.0 + second * (1.0 - s2)))).astype(BF)
        fg = (dot(w2[2], sg) * (s1 * (1.0 + first * (1.0 - s1)))).astype(BF)
        spill = dot(w2[1], fg).astype(BF)
        spread = spread + dot_nt(sco[mine, cols], spill)
        here = jnp.where(lane + i * width == row, 1.0, 0.0).astype(BF)
        fg_mine = fg_mine + dot_nt(here, fg)
        grads = [
            grads[0] + dot_nt(h, fg),
            grads[1] + dot_nt(agg, fg),
            grads[2] + dot_nt(middle, sg),
            grads[3] + dot_nt(outer, g),
        ]
    scale = 1.0 / math.sqrt(nodes)
    for m in range(4):
        cwg_ref[m] = grads[m] * scale
    flush(4)
    need(4, 5, 6, 7, 8, 9)
    direct = cot_my[...].astype(F32) + dot_nt(fg_mine.astype(BF), w2[0])
    coarse_grad = (direct + spread).astype(BF)
    back = dot_tn(coarse_grad, pool_mid[...])
    g = (mcot[...].astype(F32) + back).astype(BF)
    gmid_ref[...] = g
    sg = (dot(w1[3], g) * msl2[...]).astype(BF)
    sg_ref[...] = sg
    fg = (dot(w1[2], sg) * msl1[...]).astype(BF)
    fg_ref[...] = fg
    flush(1, 2, 3)
    spill = dot(w1[1], fg).astype(BF)
    need()
    mid_grad = (g.astype(F32) + dot(w1[0], fg) + dot_nt(spill, smid[...])).astype(BF)
    send_ref[...] = dot_nt(sel[...], mid_grad).astype(BF)


def third_window_kernel(tile_rows, mid_scale, io, need, flush, ins, outs):
    mhid, magg, gmid, msg, mfg, feat, fine_cot, w0, pool, place, agg, w1 = ins
    wg_ref, hid_ref, mid_ref, outer_ref, sl1_ref, sl2_ref, cot_ref, pick_ref, po_ref = outs
    d, rows = hid_ref.shape
    block_rows = pool.shape[0]
    per = TILE // tile_rows
    need()
    w01, w2t, _ = forward_weights(w1)
    middle = silu(dot(w01, jnp.concatenate([mhid[...], magg[...]], axis=0))).astype(BF)
    outer = silu(dot(w2t, middle)).astype(BF)
    wg_ref[0:d, :] = (dot_nt(mhid[...], mfg[...]) * mid_scale).astype(BF)
    wg_ref[d : 2 * d, :] = (dot_nt(magg[...], mfg[...]) * mid_scale).astype(BF)
    wg_ref[2 * d : 3 * d, :] = (dot_nt(middle, msg[...]) * mid_scale).astype(BF)
    wg_ref[3 * d : 4 * d, :] = (dot_nt(outer, gmid[...]) * mid_scale).astype(BF)
    hid_ref[...] = jnp.transpose(feat[...])
    cot_ref[...] = jnp.transpose(fine_cot[...])
    slots = pick_ref.shape[1]
    lane = lax.broadcasted_iota(jnp.int32, (block_rows, slots), 1)
    lane = lane - lax.broadcasted_iota(jnp.int32, (block_rows, slots), 0)
    for t in range(0, rows // tile_rows, 2):
        both = [jnp.where(lane == place[t + j] * block_rows, 1.0, 0.0) for j in range(2)]
        pick_ref[t * block_rows : (t + 2) * block_rows, :] = jnp.concatenate(
            both, axis=0
        ).astype(BF)
    flush(0, 1, 6, 7)
    w01, w2t, _ = forward_weights(w0)
    for i in range(rows // TILE):
        cols = slice(i * TILE, (i + 1) * TILE)
        first = dot(w01, jnp.concatenate([hid_ref[:, cols], agg[:, cols]], axis=0))
        s1 = 1.0 / (1.0 + jnp.exp(-first))
        middle = (first * s1).astype(BF)
        mid_ref[:, cols] = middle
        sl1_ref[:, cols] = s1 * (1.0 + first * (1.0 - s1))
        second = dot(w2t, middle)
        s2 = 1.0 / (1.0 + jnp.exp(-second))
        outer_ref[:, cols] = (second * s2).astype(BF)
        sl2_ref[:, cols] = s2 * (1.0 + second * (1.0 - s2))
        po_ref[i] = pool_matrix(pool[:, cols], tile_rows)


def fine_grad_kernel(scale, io, need, flush, ins, outs, g_ref, fg_ref):
    got, pick, cot, pool, w, slope2, slope1, hid, agg, mid, outer, mid_wg = ins
    send_ref, g_out, fg_out = outs
    d, rows = hid.shape
    need(0, 1)
    blocks = dot(pick[...], got[...]).astype(BF)
    need()
    send_ref[4 * d : 8 * d, :] = mid_wg[...]
    per = pool.shape[1]
    grads = [jnp.zeros((d, d), F32) for _ in range(4)]
    for i in range(rows // TILE):
        cols = slice(i * TILE, (i + 1) * TILE)
        back = dot_tn(blocks[i * per : (i + 1) * per, :], pool[i])
        g = (cot[:, cols].astype(F32) + back).astype(BF)
        sg = (dot(w[3], g) * slope2[:, cols]).astype(BF)
        fg = (dot(w[2], sg) * slope1[:, cols]).astype(BF)
        g_ref[:, cols] = g
        fg_ref[:, cols] = fg
        grads = [
            grads[0] + dot_nt(hid[:, cols], fg),
            grads[1] + dot_nt(agg[:, cols], fg),
            grads[2] + dot_nt(mid[:, cols], sg),
            grads[3] + dot_nt(outer[:, cols], g),
        ]
    io.start(g_ref, g_out)
    io.start(fg_ref, fg_out)
    for m in range(4):
        send_ref[m * d : (m + 1) * d, :] = (grads[m] * scale).astype(BF)


def fine_spread_kernel(io, need, flush, ins, outs, s_ref, total):
    off, ew, w, g, fg = ins
    rim_l, rim_r, out_ref = outs
    rows = g.shape[1]
    clear_corners(s_ref.at[0])
    clear_corners(s_ref.at[1])
    total[...] = jnp.zeros(total.shape, F32)
    need()
    for i in range(rows // TILE):
        cols = slice(i * TILE, (i + 1) * TILE)
        s = s_ref.at[i % 2]
        fine_edges(off[:, cols], ew[:, cols], s)
        fg_tile = fg[:, cols]
        direct = g[:, cols].astype(F32) + dot(w[0], fg_tile)
        spill = dot(w[1], fg_tile).astype(BF)
        window = slice(i * TILE, (i + 1) * TILE + 2 * HALO)
        total[window, :] = total[window, :] + dot_nt(s[...], spill)
        here = slice(HALO + i * TILE, HALO + (i + 1) * TILE)
        total[here, :] = total[here, :] + jnp.transpose(direct)
    rim_l[...] = total[:HALO, :].astype(BF)
    rim_r[...] = total[HALO + rows :, :].astype(BF)
    out_ref[...] = total[HALO : HALO + rows, :]


def sum_kernel(io, need, flush, ins, outs, part):
    got, _ = ins
    send_ref = outs[0]
    peers = got.shape[0]
    need()
    part[...] = sum(got[p].astype(F32) for p in range(peers)).astype(BF)
    for p in range(peers):
        io.start(part, send_ref.at[p])


def join_kernel(io, need, flush, ins, outs):
    total, from_left, from_right = ins
    out_ref = outs[0]
    rows = total.shape[0]
    need()
    out_ref[:HALO, :] = (total[:HALO, :] + from_left[...].astype(F32)).astype(BF)
    out_ref[HALO : rows - HALO, :] = total[HALO : rows - HALO, :].astype(BF)
    out_ref[rows - HALO :, :] = (total[rows - HALO :, :] + from_right[...].astype(F32)).astype(BF)


def exchange(x):
    return lax.all_to_all(x, "nodes", split_axis=0, concat_axis=0, tiled=True)


def per_device(
    features,
    fine_cotangent,
    mid_cotangent,
    coarse_cotangent,
    weights,
    fine_offsets,
    fine_edge_w,
    pool_fine,
    owner_dev,
    coarse_slot,
    mid_nbrs,
    mid_edge_w,
    pool_mid,
    coarse_nbrs,
    coarse_edge_w,
):
    n, d = features.shape
    tile_count = owner_dev.shape[0]
    tile_rows = n // tile_count
    block_rows = pool_fine.shape[0]
    n1 = mid_cotangent.shape[0]
    n2 = coarse_cotangent.shape[0]
    edges = fine_offsets.shape[0]
    peers = lax.axis_size("nodes")
    cap = max(2, 2 * tile_count // peers)
    chunk = cap * block_rows
    window = TILE + 2 * HALO
    per = TILE // tile_rows * block_rows
    ends = peers - 1
    up = [(i, i + 1) for i in range(ends)]
    down = [(i + 1, i) for i in range(ends)]
    total2 = peers * n2

    left = lax.ppermute(features[n - HALO :], "nodes", up)
    right = lax.ppermute(features[:HALO], "nodes", down)
    owners = owner_dev.reshape(-1)
    s_out, win, w01, w2t, w3t, pool_out, spread, ext, agg_in, place = call(
        functools.partial(inner_kernel, tile_rows, peers, cap),
        [
            (fine_offsets, "h"), (fine_edge_w, "h"), (features, "h"), (weights, "0"),
            (pool_fine, "h"), (owners, "s"), (coarse_slot, "s"), (coarse_nbrs, "h"),
            (coarse_edge_w, "h"), (coarse_cotangent, "h"),
        ],
        [
            (shape((2, window, TILE)), "v"), (shape((2, d, TILE + HALO)), "v"),
            (shape((d, 2 * d)), "v"), (shape((d, d)), "v"), (shape((d, d)), "v"),
            (shape((2, per, TILE)), "v"), (shape((peers * chunk, d), F32), "v"),
            (shape((peers, n2 + 16, d)), "v"), (shape((d, n)), "v"),
            (shape((tile_count,), jnp.int32), "s"),
        ],
        scratch=(
            pltpu.VMEM((d, n), BF),
            pltpu.VMEM((2, window, TILE), BF),
            pltpu.VMEM((peers, 128), F32),
            pltpu.SMEM((peers,), jnp.int32),
        ),
        us=6,
    )
    send1, agg = call(
        functools.partial(outer_kernel, tile_rows, cap, block_rows),
        [
            (left, "v"), (right, "v"), (s_out, "v"), (win, "v"), (w01, "v"), (w2t, "v"),
            (w3t, "v"), (pool_out, "v"), (spread, "v"), (ext, "v"), (agg_in, "v"), (owners, "s"),
        ],
        [(shape((peers, chunk + n2 + 16, d)), "r"), (shape((d, n)), "r")],
        scratch=(
            pltpu.VMEM((d, 2 * TILE), BF),
            pltpu.VMEM((peers * chunk, d), F32),
            pltpu.VMEM((peers, chunk, d), BF),
            pltpu.SMEM((peers,), jnp.int32),
        ),
        copies=8,
        us=3,
    )
    got1 = exchange(send1)
    smid, m01, m2t, m3t = call(
        first_window_kernel,
        [(mid_nbrs, "h"), (mid_edge_w, "h"), (weights, "1"), (agg, "a")],
        [
            (shape((n1, n1)), "h"), (shape((d, 2 * d)), "h"), (shape((d, d)), "h"),
            (shape((d, d)), "h"),
        ],
        us=6,
        mib=BIG,
    )
    send2, mhid, magg, sel, ext = call(
        functools.partial(mid_kernel, block_rows, chunk),
        [(got1, "h"), (smid, "h"), (m01, "h"), (m2t, "h"), (m3t, "h"), (pool_mid, "h")],
        [
            (shape((peers, n2, d)), "r"), (shape((d, n1)), "h"), (shape((d, n1)), "h"),
            (shape((peers * chunk, n1)), "h"), (shape((peers, n2 + 16, d)), "r"),
        ],
        scratch=(pltpu.VMEM((peers * chunk, d), BF), pltpu.VMEM((n2, d), BF)),
        copies=peers + 1,
        us=3,
        mib=BIG,
    )
    got2 = exchange(send2)
    sco, cot_all, mcot, mslope1, mslope2 = call(
        second_window_kernel,
        [
            (ext, "h"), (mhid, "h"), (magg, "h"), (mid_cotangent, "h"), (weights, "1"),
        ],
        [
            (shape((total2, total2)), "h"), (shape((d, total2)), "h"), (shape((d, n1)), "h"),
            (shape((d, n1), F32), "h"), (shape((d, n1), F32), "h"),
        ],
        scratch=(pltpu.VMEM((edges, total2), jnp.int32), pltpu.VMEM((edges, total2), F32)),
        us=6,
        mib=BIG,
    )
    send3, gmid, msg, mfg, coarse_wg = call(
        coarse_kernel,
        [
            (got2.reshape(total2, d), "h"), (sco, "h"), (weights, "2"), (cot_all, "h"),
            (coarse_cotangent, "h"), (pool_mid, "h"), (mcot, "h"), (weights, "1"),
            (mslope2, "h"), (mslope1, "h"), (smid, "h"), (sel, "h"),
        ],
        [
            (shape((peers * chunk, d)), "h"), (shape((d, n1)), "h"), (shape((d, n1)), "h"),
            (shape((d, n1)), "h"), (shape((4, d, d), F32), "h"),
        ],
        us=3,
        mib=BIG,
    )
    got3 = exchange(send3.reshape(peers, chunk, d))
    mid_wg, hid, mid, outer, slope1, slope2, cot, pick, pool_b = call(
        functools.partial(third_window_kernel, tile_rows, 1.0 / math.sqrt(n1 * peers)),
        [
            (mhid, "h"), (magg, "h"), (gmid, "h"), (msg, "h"), (mfg, "h"), (features, "h"),
            (fine_cotangent, "h"), (weights, "0"), (pool_fine, "h"), (place, "s"), (agg, "h"),
            (weights, "1"),
        ],
        [
            (shape((4 * d, d)), "h"), (shape((d, n)), "h"), (shape((d, n)), "h"),
            (shape((d, n)), "h"), (shape((d, n), F32), "h"), (shape((d, n), F32), "h"),
            (shape((d, n)), "h"), (shape((tile_count * block_rows, peers * chunk)), "h"),
            (shape((n // TILE, per, TILE)), "h"),
        ],
        us=6,
        mib=BIG,
    )
    send4, g, fg = call(
        functools.partial(fine_grad_kernel, 1.0 / math.sqrt(n * peers)),
        [
            (got3.reshape(peers * chunk, d), "h"), (pick, "h"), (cot, "h"), (pool_b, "h"),
            (weights, "0"), (slope2, "h"), (slope1, "h"), (hid, "h"), (agg, "h"), (mid, "h"),
            (outer, "h"), (mid_wg, "h"),
        ],
        [(shape((8 * d, d)), "h"), (shape((d, n)), "r"), (shape((d, n)), "r")],
        scratch=(pltpu.VMEM((d, n), BF), pltpu.VMEM((d, n), BF)),
        copies=2,
        us=4,
        mib=BIG,
    )
    got4 = exchange(send4.reshape(peers, 8 * d // peers, d))
    rim_l, rim_r, spread = call(
        fine_spread_kernel,
        [(fine_offsets, "h"), (fine_edge_w, "h"), (weights, "0"), (g, "h"), (fg, "h")],
        [(shape((HALO, d)), "h"), (shape((HALO, d)), "h"), (shape((n, d), F32), "h")],
        scratch=(pltpu.VMEM((2, window, TILE), BF), pltpu.VMEM((n + 2 * HALO, d), F32)),
        us=6,
        mib=BIG,
    )
    (send5,) = call(
        sum_kernel,
        [(got4, "v"), (rim_l, "a")],
        [(shape((peers, 8 * d // peers, d)), "r")],
        scratch=(pltpu.VMEM((8 * d // peers, d), BF),),
        copies=peers,
        us=1,
        mib=24,
    )
    got5 = exchange(send5)
    from_left = lax.ppermute(rim_r, "nodes", up)
    from_right = lax.ppermute(rim_l, "nodes", down)
    (feature_grads,) = call(
        join_kernel,
        [(spread, "h"), (from_left, "h"), (from_right, "h")],
        [(shape((n, d)), "h")],
        us=1,
        mib=BIG,
    )
    weight_grads = jnp.concatenate(
        [got5.reshape(2, 4, d, d).astype(F32), coarse_wg[None]], axis=0
    )
    return (feature_grads, weight_grads)


def solution(mesh):
    rows = P(("groups", "nodes"), None)
    cols = P("groups", "nodes")
    in_specs = (
        rows, rows, rows, rows, P(), cols, cols, cols, rows, P(("groups", "nodes")),
        cols, cols, rows, cols, cols,
    )
    out_specs = (rows, P("groups", None, None, None))
    return jax.shard_map(
        per_device, mesh=mesh, in_specs=in_specs, out_specs=out_specs, check_vma=False
    )
```

```python
import functools
import math

import jax
import jax.numpy as jnp
from jax import lax
from jax.experimental import pallas as pl
from jax.experimental.pallas import tpu as pltpu
from jax.sharding import PartitionSpec as P

HALO = 256
TILE = 256
BF = jnp.bfloat16
F32 = jnp.float32

VM = pl.BlockSpec(memory_space=pltpu.VMEM)
HB = pl.BlockSpec(memory_space=pltpu.HBM)


def dot(a, b):
    return jnp.dot(a, b, preferred_element_type=F32)


def dot_nt(a, b):
    return lax.dot_general(a, b, (((1,), (1,)), ((), ())), preferred_element_type=F32)


def dot_tn(a, b):
    return lax.dot_general(a, b, (((0,), (0,)), ((), ())), preferred_element_type=F32)


def silu(v):
    return v / (1.0 + jnp.exp(-v))


def silu_slope(v):
    s = 1.0 / (1.0 + jnp.exp(-v))
    return s * (1.0 + v * (1.0 - s))


def merged_weights(idx, ew):
    total = ew
    for r in range(1, idx.shape[0]):
        total = total + jnp.where(pltpu.roll(idx, r, 0) == idx, pltpu.roll(ew, r, 0), 0.0)
    return total.astype(BF)


def edge_columns(idx, ew, start, rows):
    count = idx.shape[0]
    lanes = idx.shape[1]
    position = lax.broadcasted_iota(jnp.int32, (rows, lanes), 0) + start
    position = position.astype(jnp.int16)
    picked = jnp.zeros((rows, lanes), BF)
    for k in range(count):
        picked = jnp.where(idx[k : k + 1, :] == position, ew[k : k + 1, :], picked)
    return picked


def fine_edges(off, ew, s_ref):
    for h in range(TILE // 128):
        lane = slice(128 * h, 128 * (h + 1))
        o = off[:, lane]
        weight = merged_weights(o, ew[:, lane])
        rel = o + lax.broadcasted_iota(jnp.int32, o.shape, 1) + HALO
        rel = rel.astype(jnp.int16)
        for c in range(2 * HALO // 128 + 1):
            s_ref[128 * (h + c) : 128 * (h + c + 1), lane] = edge_columns(
                rel, weight, 128 * c, 128
            )


def clear_corners(s_ref):
    for h in range(TILE // 128):
        lane = slice(128 * h, 128 * (h + 1))
        if h > 0:
            s_ref[: 128 * h, lane] = jnp.zeros((128 * h, 128), BF)
        last = 128 * h + 2 * HALO + 128
        if last < TILE + 2 * HALO:
            s_ref[last:, lane] = jnp.zeros((TILE + 2 * HALO - last, 128), BF)


def forward_weights(w):
    w01 = jnp.concatenate([jnp.transpose(w[0]), jnp.transpose(w[1])], axis=1)
    return w01, jnp.transpose(w[2]), jnp.transpose(w[3])


def pool_matrix(pool, tile_rows):
    lane = lax.broadcasted_iota(jnp.int32, pool.shape, 1) // tile_rows
    values = pool.astype(F32)
    parts = [jnp.where(lane == r, values, 0.0) for r in range(pool.shape[1] // tile_rows)]
    return jnp.concatenate(parts, axis=0).astype(BF)


class Copies:
    def __init__(self, sems):
        self.sems = sems
        self.used = 0
        self.open = {}

    def start(self, source, target):
        copy = pltpu.make_async_copy(source, target, self.sems.at[self.used])
        self.used += 1
        copy.start()
        self.open[id(copy)] = copy
        return copy

    def wait(self, *copies):
        for copy in copies:
            if id(copy) in self.open:
                copy.wait()
                del self.open[id(copy)]

    def finish(self):
        self.wait(*list(self.open.values()))


def shape(dims, dtype=BF):
    return jax.ShapeDtypeStruct(dims, dtype)


def call(kernel, ins, outs, scratch=(), copies=0, us=3, mib=24):
    n_in, n_out = len(ins), len(outs)
    staged_in = [i for i, (_, kind) in enumerate(ins) if kind in "hs012"]
    staged_out = [i for i, (_, kind) in enumerate(outs) if kind in "hs"]
    spaces = {"h": pltpu.VMEM, "s": pltpu.SMEM}
    stage = []
    for i in staged_in:
        array, kind = ins[i]
        dims = array.shape[1:] if kind.isdigit() else array.shape
        stage.append(spaces.get(kind, pltpu.VMEM)(dims, array.dtype))
    stage += [spaces[outs[i][1]](outs[i][0].shape, outs[i][0].dtype) for i in staged_out]
    total = len(staged_in) + len(staged_out) + copies

    def body(*refs):
        in_refs, out_refs = list(refs[:n_in]), list(refs[n_in : n_in + n_out])
        rest = list(refs[n_in + n_out :])
        sems = rest.pop() if total else None
        stages, user = rest[: len(stage)], rest[len(stage) :]
        io = Copies(sems)
        pending = {}
        for i, ref in zip(staged_in, stages):
            kind = ins[i][1]
            source = in_refs[i].at[int(kind)] if kind.isdigit() else in_refs[i]
            pending[i] = io.start(source, ref)
            in_refs[i] = ref
        targets = {}
        for i, ref in zip(staged_out, stages[len(staged_in) :]):
            targets[i] = out_refs[i]
            out_refs[i] = ref

        def need(*which):
            io.wait(*[pending[i] for i in which or pending])

        def flush(*which):
            for i in which:
                io.start(out_refs[i], targets.pop(i))

        kernel(io, need, flush, in_refs, out_refs, *user)
        flush(*list(targets))
        io.finish()

    return pl.pallas_call(
        body,
        out_shape=[
            s if kind == "v" else pltpu.HBM(s.shape, s.dtype) for s, kind in outs
        ],
        in_specs=[VM if kind == "v" else HB for _, kind in ins],
        out_specs=[VM if kind == "v" else HB for _, kind in outs],
        scratch_shapes=stage
        + list(scratch)
        + ([pltpu.SemaphoreType.DMA((total,))] if total else []),
        compiler_params=pltpu.CompilerParams(vmem_limit_bytes=mib << 20),
        cost_estimate=pl.CostEstimate(
            flops=0, bytes_accessed=int(us * 3_000_000), transcendentals=0
        ),
    )(*[
        a if kind == "v" else pltpu.with_memory_space_constraint(a, pltpu.HBM)
        for a, kind in ins
    ])


def fine_tile(h_t, window_t, s, weights, pool):
    w01, w2t, w3t = weights
    agg = dot(window_t, s).astype(BF)
    first = dot(w01, jnp.concatenate([h_t, agg], axis=0))
    middle = silu(first).astype(BF)
    second = dot(w2t, middle)
    outer = silu(second).astype(BF)
    fine_out = (h_t.astype(F32) + dot(w3t, outer)).astype(BF)
    return agg, dot_nt(pool, fine_out)


def outer_tiles(tile_count, per):
    return list(range(per)) + list(range(tile_count - per, tile_count))


def inner_kernel(tile_rows, peers, cap, io, need, flush, ins, outs, feat_t, s_ref, ids, counts):
    off, ew, feat, w, pool, owner, slot, nbrs, cew, cot = ins
    so_ref, win_ref, w01_ref, w2t_ref, w3t_ref, po_ref, spread, ext_ref, agg_ref, place = outs
    rows, d = feat.shape
    block_rows = pool.shape[0]
    n2 = cot.shape[0]
    tiles = rows // TILE
    per = TILE // tile_rows
    tile_count = rows // tile_rows
    clear_corners(s_ref.at[0])
    clear_corners(s_ref.at[1])
    clear_corners(so_ref.at[0])
    clear_corners(so_ref.at[1])
    spread[...] = jnp.zeros(spread.shape, F32)
    ids[...] = jnp.full(ids.shape, -1.0, F32)
    for p in range(peers):
        counts[p] = 0
    need(5, 6)
    lane_slot = lax.broadcasted_iota(jnp.int32, (1, 128), 1) // block_rows
    first_tiles = outer_tiles(tile_count, per)
    for t in first_tiles + [t for t in range(tile_count) if t not in first_tiles]:
        o = owner[t]
        c = counts[o]
        counts[o] = c + 1
        place[t] = o * cap + c
        row = ids[pl.ds(o, 1), :]
        ids[pl.ds(o, 1), :] = jnp.where(lane_slot == c, slot[t].astype(F32), row)
    flush(9)
    need(0, 1)
    need(2)
    feat_t[...] = jnp.transpose(feat[...])
    need()
    weights = forward_weights(w)
    for i in range(1, tiles - 1):
        cols = slice(i * TILE, (i + 1) * TILE)
        s = s_ref.at[i % 2]
        fine_edges(off[:, cols], ew[:, cols], s)
        agg, blocks = fine_tile(
            feat_t[:, cols],
            feat_t[:, i * TILE - HALO : (i + 1) * TILE + HALO],
            s[...],
            weights,
            pool_matrix(pool[:, cols], tile_rows),
        )
        agg_ref[:, cols] = agg
        for j in range(per):
            at = pl.ds(pl.multiple_of(place[i * per + j] * block_rows, 8), block_rows)
            spread[at, :] = blocks[j * block_rows : (j + 1) * block_rows, :]
    for n, i in enumerate((0, tiles - 1)):
        cols = slice(i * TILE, (i + 1) * TILE)
        fine_edges(off[:, cols], ew[:, cols], so_ref.at[n])
        po_ref[n] = pool_matrix(pool[:, cols], tile_rows)
    win_ref[0] = feat_t[:, : TILE + HALO]
    win_ref[1] = feat_t[:, rows - TILE - HALO :]
    w01_ref[...], w2t_ref[...], w3t_ref[...] = weights
    nb = nbrs[...].astype(F32)
    high = jnp.floor(nb * (1.0 / 256.0))
    ce = cew[...]
    ce_high = ce.astype(BF).astype(F32)
    fields = [high, nb - high * 256.0, ce_high, ce - ce_high]
    fields.append(jnp.zeros((nb.shape[0], 128 - 4 * n2), F32))
    top = jnp.concatenate(fields, axis=1)
    sub = lax.broadcasted_iota(jnp.int32, (8, 128), 0)
    for p in range(peers):
        ext_ref[p, 0:n2, :] = cot[...]
        below = jnp.where(sub == 0, ids[p : p + 1, :], 0.0)
        ext_ref[p, n2 : n2 + 16, :] = jnp.concatenate([top, below], axis=0).astype(BF)


def outer_kernel(
    tile_rows, cap, block_rows, io, need, flush, ins, outs, agg_edge, spread, stage, counts
):
    left, right, s_in, win, w01, w2t, w3t, pool, spread_in, ext, agg_in, owner = ins
    send_ref, agg_ref = outs
    peers, chunk, d = stage.shape
    rows = agg_in.shape[1]
    per = TILE // tile_rows
    io.start(ext, send_ref.at[:, pl.ds(chunk, ext.shape[1]), :])
    inside = pl.ds(TILE, rows - 2 * TILE)
    io.start(agg_in.at[:, inside], agg_ref.at[:, inside])
    spread[...] = spread_in[...]
    for p in range(peers):
        counts[p] = 0
    weights = (w01[...], w2t[...], w3t[...])
    results = []
    for n in range(2):
        if n == 0:
            window_t = jnp.concatenate([jnp.transpose(left[...]), win[0]], axis=1)
        else:
            window_t = jnp.concatenate([win[1], jnp.transpose(right[...])], axis=1)
        agg, blocks = fine_tile(
            window_t[:, HALO : HALO + TILE], window_t, s_in[n], weights, pool[n]
        )
        agg_edge[:, n * TILE : (n + 1) * TILE] = agg
        results.append(blocks)
    io.start(agg_edge.at[:, pl.ds(0, TILE)], agg_ref.at[:, pl.ds(0, TILE)])
    io.start(agg_edge.at[:, pl.ds(TILE, TILE)], agg_ref.at[:, pl.ds(rows - TILE, TILE)])
    need()
    for j, t in enumerate(outer_tiles(rows // tile_rows, per)):
        o = owner[t]
        c = counts[o]
        counts[o] = c + 1
        at = pl.ds(pl.multiple_of((o * cap + c) * block_rows, 8), block_rows)
        blocks = results[j // per]
        spread[at, :] = blocks[j % per * block_rows : (j % per + 1) * block_rows, :]
    group = max(1, peers // 4)
    for p in range(peers):
        stage[p] = spread[p * chunk : (p + 1) * chunk, :].astype(BF)
        if p % group == group - 1:
            part = pl.ds(p + 1 - group, group)
            io.start(stage.at[part], send_ref.at[part, pl.ds(0, chunk), :])


def mid_edges(nbrs, ew, s_ref):
    nodes = nbrs.shape[1]
    for c in range(nodes // 128):
        lane = slice(128 * c, 128 * (c + 1))
        idx = nbrs[:, lane]
        weight = merged_weights(idx, ew[:, lane])
        idx = idx.astype(jnp.int16)
        for r in range(nodes // 128):
            s_ref[128 * r : 128 * (r + 1), lane] = edge_columns(idx, weight, 128 * r, 128)


def first_window_kernel(io, need, flush, ins, outs):
    nbrs, ew, w, _ = ins
    smid, w01_ref, w2t_ref, w3t_ref = outs
    need(0, 1)
    mid_edges(nbrs, ew, smid)
    flush(0)
    need()
    w01_ref[...], w2t_ref[...], w3t_ref[...] = forward_weights(w)


def mid_kernel(block_rows, chunk, io, need, flush, ins, outs, blocks, coarse):
    got, smid, w01, w2t, w3t, pool_mid = ins
    send_ref, hid_ref, agg_ref, sel_ref, ext_ref = outs
    peers = got.shape[0]
    nodes = smid.shape[0]
    n2 = pool_mid.shape[0]
    io.start(got.at[:, pl.ds(chunk, n2 + 16), :], ext_ref)
    rows = [got[p, chunk + n2 : chunk + n2 + 16, :].astype(F32)[8:9, :] for p in range(peers)]
    keys = jnp.transpose(jnp.concatenate(rows, axis=0))
    keys = keys * block_rows
    keys = keys + (lax.broadcasted_iota(jnp.int32, keys.shape, 0) % block_rows).astype(F32)
    keys = keys.astype(jnp.int32)
    lane = lax.broadcasted_iota(jnp.int32, (chunk, nodes), 1)
    for p in range(peers):
        sel_ref[p * chunk : (p + 1) * chunk, :] = jnp.where(
            keys[0:chunk, p : p + 1] == lane, 1.0, 0.0
        ).astype(BF)
        blocks[p * chunk : (p + 1) * chunk, :] = got[p, 0:chunk, :]
    flush(3)
    hidden = dot_tn(blocks[...], sel_ref[...]).astype(BF)
    hid_ref[...] = hidden
    need()
    agg = dot(hidden, smid[...]).astype(BF)
    agg_ref[...] = agg
    flush(1, 2)
    middle = silu(dot(w01[...], jnp.concatenate([hidden, agg], axis=0))).astype(BF)
    outer = silu(dot(w2t[...], middle)).astype(BF)
    mid_out = (hidden.astype(F32) + dot(w3t[...], outer)).astype(BF)
    coarse[...] = dot_nt(pool_mid[...], mid_out).astype(BF)
    for p in range(peers):
        io.start(coarse, send_ref.at[p])


def second_window_kernel(io, need, flush, ins, outs, nb_ref, ew_ref):
    ext, hid, agg, mid_cot, w1 = ins
    sco, cot_all, mcot, sl1_ref, sl2_ref = outs
    peers = ext.shape[0]
    n2 = ext.shape[1] - 16
    nodes = peers * n2
    edges = nb_ref.shape[0]
    need()
    for p in range(peers):
        part = ext[p, n2 : n2 + 16, :].astype(F32)[0:edges, :]
        at = slice(p * n2, (p + 1) * n2)
        nb_ref[:, at] = (part[:, 0:n2] * 256.0 + part[:, n2 : 2 * n2]).astype(jnp.int32)
        ew_ref[:, at] = part[:, 2 * n2 : 3 * n2] + part[:, 3 * n2 : 4 * n2]
    cots = jnp.concatenate([ext[p, 0:n2, :] for p in range(peers)], axis=0)
    cot_all[...] = jnp.transpose(cots)
    mcot[...] = jnp.transpose(mid_cot[...])

    def column(c, _):
        lane = pl.ds(pl.multiple_of(c * 128, 128), 128)
        idx = nb_ref[:, lane]
        weight = merged_weights(idx, ew_ref[:, lane])
        idx = idx.astype(jnp.int16)
        for r in range(nodes // 128):
            sco[128 * r : 128 * (r + 1), lane] = edge_columns(idx, weight, 128 * r, 128)
        return 0

    lax.fori_loop(0, nodes // 128, column, 0)
    flush(0, 1, 2)
    w01, w2t, _ = forward_weights(w1)
    first = dot(w01, jnp.concatenate([hid[...], agg[...]], axis=0))
    s1 = 1.0 / (1.0 + jnp.exp(-first))
    second = dot(w2t, (first * s1).astype(BF))
    s2 = 1.0 / (1.0 + jnp.exp(-second))
    sl1_ref[...] = s1 * (1.0 + first * (1.0 - s1))
    sl2_ref[...] = s2 * (1.0 + second * (1.0 - s2))


def coarse_kernel(io, need, flush, ins, outs):
    got, sco, w2, cot_all, cot_my, pool_mid, mcot, w1, msl2, msl1, smid, sel = ins
    send_ref, gmid_ref, sg_ref, fg_ref, cwg_ref = outs
    nodes = got.shape[0]
    n2 = cot_my.shape[0]
    me = lax.axis_index("nodes")
    width = min(TILE, nodes)
    hidden = jnp.transpose(got[...])
    need(1, 2, 3)
    w01, w2t, _ = forward_weights(w2)
    mine = pl.ds(pl.multiple_of(me * n2, 16), n2)
    spread = jnp.zeros((n2, 128), F32)
    fg_mine = jnp.zeros((n2, 128), F32)
    grads = [jnp.zeros((128, 128), F32) for _ in range(4)]
    row = lax.broadcasted_iota(jnp.int32, (n2, width), 0) + me * n2
    lane = lax.broadcasted_iota(jnp.int32, (n2, width), 1)
    for i in range(nodes // width):
        cols = slice(i * width, (i + 1) * width)
        h = hidden[:, cols]
        agg = dot(hidden, sco[:, cols]).astype(BF)
        first = dot(w01, jnp.concatenate([h, agg], axis=0))
        s1 = 1.0 / (1.0 + jnp.exp(-first))
        middle = (first * s1).astype(BF)
        second = dot(w2t, middle)
        s2 = 1.0 / (1.0 + jnp.exp(-second))
        outer = (second * s2).astype(BF)
        g = cot_all[:, cols]
        sg = (dot(w2[3], g) * (s2 * (1.0 + second * (1.0 - s2)))).astype(BF)
        fg = (dot(w2[2], sg) * (s1 * (1.0 + first * (1.0 - s1)))).astype(BF)
        spill = dot(w2[1], fg).astype(BF)
        spread = spread + dot_nt(sco[mine, cols], spill)
        here = jnp.where(lane + i * width == row, 1.0, 0.0).astype(BF)
        fg_mine = fg_mine + dot_nt(here, fg)
        grads = [
            grads[0] + dot_nt(h, fg),
            grads[1] + dot_nt(agg, fg),
            grads[2] + dot_nt(middle, sg),
            grads[3] + dot_nt(outer, g),
        ]
    scale = 1.0 / math.sqrt(nodes)
    for m in range(4):
        cwg_ref[m] = grads[m] * scale
    flush(4)
    need(4, 5, 6, 7, 8, 9)
    direct = cot_my[...].astype(F32) + dot_nt(fg_mine.astype(BF), w2[0])
    coarse_grad = (direct + spread).astype(BF)
    back = dot_tn(coarse_grad, pool_mid[...])
    g = (mcot[...].astype(F32) + back).astype(BF)
    gmid_ref[...] = g
    sg = (dot(w1[3], g) * msl2[...]).astype(BF)
    sg_ref[...] = sg
    fg = (dot(w1[2], sg) * msl1[...]).astype(BF)
    fg_ref[...] = fg
    flush(1, 2, 3)
    spill = dot(w1[1], fg).astype(BF)
    need()
    mid_grad = (g.astype(F32) + dot(w1[0], fg) + dot_nt(spill, smid[...])).astype(BF)
    send_ref[...] = dot_nt(sel[...], mid_grad).astype(BF)


def third_window_kernel(tile_rows, mid_scale, io, need, flush, ins, outs):
    mhid, magg, gmid, msg, mfg, feat, fine_cot, w0, pool, place, agg, w1 = ins
    wg_ref, hid_ref, mid_ref, outer_ref, sl1_ref, sl2_ref, cot_ref, pick_ref, po_ref = outs
    d, rows = hid_ref.shape
    block_rows = pool.shape[0]
    per = TILE // tile_rows
    need()
    w01, w2t, _ = forward_weights(w1)
    middle = silu(dot(w01, jnp.concatenate([mhid[...], magg[...]], axis=0))).astype(BF)
    outer = silu(dot(w2t, middle)).astype(BF)
    wg_ref[0:d, :] = (dot_nt(mhid[...], mfg[...]) * mid_scale).astype(BF)
    wg_ref[d : 2 * d, :] = (dot_nt(magg[...], mfg[...]) * mid_scale).astype(BF)
    wg_ref[2 * d : 3 * d, :] = (dot_nt(middle, msg[...]) * mid_scale).astype(BF)
    wg_ref[3 * d : 4 * d, :] = (dot_nt(outer, gmid[...]) * mid_scale).astype(BF)
    hid_ref[...] = jnp.transpose(feat[...])
    cot_ref[...] = jnp.transpose(fine_cot[...])
    slots = pick_ref.shape[1]
    lane = lax.broadcasted_iota(jnp.int32, (block_rows, slots), 1)
    lane = lane - lax.broadcasted_iota(jnp.int32, (block_rows, slots), 0)
    for t in range(0, rows // tile_rows, 2):
        both = [jnp.where(lane == place[t + j] * block_rows, 1.0, 0.0) for j in range(2)]
        pick_ref[t * block_rows : (t + 2) * block_rows, :] = jnp.concatenate(
            both, axis=0
        ).astype(BF)
    flush(0, 1, 6, 7)
    w01, w2t, _ = forward_weights(w0)
    for i in range(rows // TILE):
        cols = slice(i * TILE, (i + 1) * TILE)
        first = dot(w01, jnp.concatenate([hid_ref[:, cols], agg[:, cols]], axis=0))
        s1 = 1.0 / (1.0 + jnp.exp(-first))
        middle = (first * s1).astype(BF)
        mid_ref[:, cols] = middle
        sl1_ref[:, cols] = s1 * (1.0 + first * (1.0 - s1))
        second = dot(w2t, middle)
        s2 = 1.0 / (1.0 + jnp.exp(-second))
        outer_ref[:, cols] = (second * s2).astype(BF)
        sl2_ref[:, cols] = s2 * (1.0 + second * (1.0 - s2))
        po_ref[i] = pool_matrix(pool[:, cols], tile_rows)


def fine_grad_kernel(scale, io, need, flush, ins, outs, g_ref, fg_ref):
    got, pick, cot, pool, w, slope2, slope1, hid, agg, mid, outer, mid_wg = ins
    send_ref, g_out, fg_out = outs
    d, rows = hid.shape
    need(1)
    blocks = dot(pick[...], got[...]).astype(BF)
    need()
    send_ref[4 * d : 8 * d, :] = mid_wg[...]
    per = pool.shape[1]
    grads = [jnp.zeros((d, d), F32) for _ in range(4)]
    for i in range(rows // TILE):
        cols = slice(i * TILE, (i + 1) * TILE)
        back = dot_tn(blocks[i * per : (i + 1) * per, :], pool[i])
        g = (cot[:, cols].astype(F32) + back).astype(BF)
        sg = (dot(w[3], g) * slope2[:, cols]).astype(BF)
        fg = (dot(w[2], sg) * slope1[:, cols]).astype(BF)
        g_ref[:, cols] = g
        fg_ref[:, cols] = fg
        grads = [
            grads[0] + dot_nt(hid[:, cols], fg),
            grads[1] + dot_nt(agg[:, cols], fg),
            grads[2] + dot_nt(mid[:, cols], sg),
            grads[3] + dot_nt(outer[:, cols], g),
        ]
    io.start(g_ref, g_out)
    io.start(fg_ref, fg_out)
    for m in range(4):
        send_ref[m * d : (m + 1) * d, :] = (grads[m] * scale).astype(BF)


def fine_spread_kernel(io, need, flush, ins, outs, s_ref, total):
    off, ew, w, g, fg = ins
    rim_l, rim_r, out_ref = outs
    rows = g.shape[1]
    clear_corners(s_ref.at[0])
    clear_corners(s_ref.at[1])
    total[...] = jnp.zeros(total.shape, F32)
    need()
    for i in range(rows // TILE):
        cols = slice(i * TILE, (i + 1) * TILE)
        s = s_ref.at[i % 2]
        fine_edges(off[:, cols], ew[:, cols], s)
        fg_tile = fg[:, cols]
        direct = g[:, cols].astype(F32) + dot(w[0], fg_tile)
        spill = dot(w[1], fg_tile).astype(BF)
        window = slice(i * TILE, (i + 1) * TILE + 2 * HALO)
        total[window, :] = total[window, :] + dot_nt(s[...], spill)
        here = slice(HALO + i * TILE, HALO + (i + 1) * TILE)
        total[here, :] = total[here, :] + jnp.transpose(direct)
    rim_l[...] = total[:HALO, :].astype(BF)
    rim_r[...] = total[HALO + rows :, :].astype(BF)
    out_ref[...] = total[HALO : HALO + rows, :]


def sum_kernel(io, need, flush, ins, outs, part):
    got, _ = ins
    send_ref = outs[0]
    peers = got.shape[0]
    need()
    part[...] = sum(got[p].astype(F32) for p in range(peers)).astype(BF)
    for p in range(peers):
        io.start(part, send_ref.at[p])


def join_kernel(io, need, flush, ins, outs):
    total, from_left, from_right = ins
    out_ref = outs[0]
    rows = total.shape[0]
    need()
    out_ref[:HALO, :] = (total[:HALO, :] + from_left[...].astype(F32)).astype(BF)
    out_ref[HALO : rows - HALO, :] = total[HALO : rows - HALO, :].astype(BF)
    out_ref[rows - HALO :, :] = (total[rows - HALO :, :] + from_right[...].astype(F32)).astype(BF)


def gather_kernel(io, need, flush, ins, outs, wide):
    summed, coarse = ins
    out_ref = outs[0]
    io.start(coarse, out_ref.at[pl.ds(8, 4)])
    for half in range(2):
        wide[4 * half : 4 * half + 4] = summed[4 * half : 4 * half + 4].astype(F32)
        part = pl.ds(4 * half, 4)
        io.start(wide.at[part], out_ref.at[part])


def exchange(x):
    return lax.all_to_all(x, "nodes", split_axis=0, concat_axis=0, tiled=True)


def per_device(
    features,
    fine_cotangent,
    mid_cotangent,
    coarse_cotangent,
    weights,
    fine_offsets,
    fine_edge_w,
    pool_fine,
    owner_dev,
    coarse_slot,
    mid_nbrs,
    mid_edge_w,
    pool_mid,
    coarse_nbrs,
    coarse_edge_w,
):
    n, d = features.shape
    tile_count = owner_dev.shape[0]
    tile_rows = n // tile_count
    block_rows = pool_fine.shape[0]
    n1 = mid_cotangent.shape[0]
    n2 = coarse_cotangent.shape[0]
    edges = fine_offsets.shape[0]
    peers = lax.axis_size("nodes")
    cap = max(2, 2 * tile_count // peers)
    chunk = cap * block_rows
    window = TILE + 2 * HALO
    per = TILE // tile_rows * block_rows
    ends = peers - 1
    up = [(i, i + 1) for i in range(ends)]
    down = [(i + 1, i) for i in range(ends)]
    total2 = peers * n2

    left = lax.ppermute(features[n - HALO :], "nodes", up)
    right = lax.ppermute(features[:HALO], "nodes", down)
    owners = owner_dev.reshape(-1)
    s_out, win, w01, w2t, w3t, pool_out, spread, ext, agg_in, place = call(
        functools.partial(inner_kernel, tile_rows, peers, cap),
        [
            (fine_offsets, "h"), (fine_edge_w, "h"), (features, "h"), (weights, "0"),
            (pool_fine, "h"), (owners, "s"), (coarse_slot, "s"), (coarse_nbrs, "h"),
            (coarse_edge_w, "h"), (coarse_cotangent, "h"),
        ],
        [
            (shape((2, window, TILE)), "v"), (shape((2, d, TILE + HALO)), "v"),
            (shape((d, 2 * d)), "v"), (shape((d, d)), "v"), (shape((d, d)), "v"),
            (shape((2, per, TILE)), "v"), (shape((peers * chunk, d), F32), "v"),
            (shape((peers, n2 + 16, d)), "v"), (shape((d, n)), "v"),
            (shape((tile_count,), jnp.int32), "s"),
        ],
        scratch=(
            pltpu.VMEM((d, n), BF),
            pltpu.VMEM((2, window, TILE), BF),
            pltpu.VMEM((peers, 128), F32),
            pltpu.SMEM((peers,), jnp.int32),
        ),
        us=6,
    )
    send1, agg = call(
        functools.partial(outer_kernel, tile_rows, cap, block_rows),
        [
            (left, "v"), (right, "v"), (s_out, "v"), (win, "v"), (w01, "v"), (w2t, "v"),
            (w3t, "v"), (pool_out, "v"), (spread, "v"), (ext, "v"), (agg_in, "v"), (owners, "s"),
        ],
        [(shape((peers, chunk + n2 + 16, d)), "r"), (shape((d, n)), "r")],
        scratch=(
            pltpu.VMEM((d, 2 * TILE), BF),
            pltpu.VMEM((peers * chunk, d), F32),
            pltpu.VMEM((peers, chunk, d), BF),
            pltpu.SMEM((peers,), jnp.int32),
        ),
        copies=8,
        us=3,
    )
    got1 = exchange(send1)
    smid, m01, m2t, m3t = call(
        first_window_kernel,
        [(mid_nbrs, "h"), (mid_edge_w, "h"), (weights, "1"), (agg, "r")],
        [
            (shape((n1, n1)), "h"), (shape((d, 2 * d)), "h"), (shape((d, d)), "h"),
            (shape((d, d)), "h"),
        ],
        us=6,
    )
    send2, mhid, magg, sel, ext = call(
        functools.partial(mid_kernel, block_rows, chunk),
        [(got1, "v"), (smid, "h"), (m01, "h"), (m2t, "h"), (m3t, "h"), (pool_mid, "h")],
        [
            (shape((peers, n2, d)), "r"), (shape((d, n1)), "h"), (shape((d, n1)), "h"),
            (shape((peers * chunk, n1)), "h"), (shape((peers, n2 + 16, d)), "r"),
        ],
        scratch=(pltpu.VMEM((peers * chunk, d), BF), pltpu.VMEM((n2, d), BF)),
        copies=peers + 1,
        us=3,
    )
    got2 = exchange(send2)
    sco, cot_all, mcot, mslope1, mslope2 = call(
        second_window_kernel,
        [
            (ext, "h"), (mhid, "h"), (magg, "h"), (mid_cotangent, "h"), (weights, "1"),
        ],
        [
            (shape((total2, total2)), "h"), (shape((d, total2)), "h"), (shape((d, n1)), "h"),
            (shape((d, n1), F32), "h"), (shape((d, n1), F32), "h"),
        ],
        scratch=(pltpu.VMEM((edges, total2), jnp.int32), pltpu.VMEM((edges, total2), F32)),
        us=6,
    )
    send3, gmid, msg, mfg, coarse_wg = call(
        coarse_kernel,
        [
            (got2.reshape(total2, d), "v"), (sco, "h"), (weights, "2"), (cot_all, "h"),
            (coarse_cotangent, "h"), (pool_mid, "h"), (mcot, "h"), (weights, "1"),
            (mslope2, "h"), (mslope1, "h"), (smid, "h"), (sel, "h"),
        ],
        [
            (shape((peers * chunk, d)), "h"), (shape((d, n1)), "h"), (shape((d, n1)), "h"),
            (shape((d, n1)), "h"), (shape((4, d, d), F32), "h"),
        ],
        us=3,
    )
    got3 = exchange(send3.reshape(peers, chunk, d))
    mid_wg, hid, mid, outer, slope1, slope2, cot, pick, pool_b = call(
        functools.partial(third_window_kernel, tile_rows, 1.0 / math.sqrt(n1 * peers)),
        [
            (mhid, "h"), (magg, "h"), (gmid, "h"), (msg, "h"), (mfg, "h"), (features, "h"),
            (fine_cotangent, "h"), (weights, "0"), (pool_fine, "h"), (place, "s"), (agg, "h"),
            (weights, "1"),
        ],
        [
            (shape((4 * d, d)), "h"), (shape((d, n)), "h"), (shape((d, n)), "h"),
            (shape((d, n)), "h"), (shape((d, n), F32), "h"), (shape((d, n), F32), "h"),
            (shape((d, n)), "h"), (shape((tile_count * block_rows, peers * chunk)), "h"),
            (shape((n // TILE, per, TILE)), "h"),
        ],
        us=6,
    )
    send4, g, fg = call(
        functools.partial(fine_grad_kernel, 1.0 / math.sqrt(n * peers)),
        [
            (got3.reshape(peers * chunk, d), "v"), (pick, "h"), (cot, "h"), (pool_b, "h"),
            (weights, "0"), (slope2, "h"), (slope1, "h"), (hid, "h"), (agg, "h"), (mid, "h"),
            (outer, "h"), (mid_wg, "h"),
        ],
        [(shape((8 * d, d)), "h"), (shape((d, n)), "r"), (shape((d, n)), "r")],
        scratch=(pltpu.VMEM((d, n), BF), pltpu.VMEM((d, n), BF)),
        copies=2,
        us=4,
    )
    got4 = exchange(send4.reshape(peers, 8 * d // peers, d))
    rim_l, rim_r, spread = call(
        fine_spread_kernel,
        [(fine_offsets, "h"), (fine_edge_w, "h"), (weights, "0"), (g, "h"), (fg, "h")],
        [(shape((HALO, d)), "h"), (shape((HALO, d)), "h"), (shape((n, d), F32), "h")],
        scratch=(pltpu.VMEM((2, window, TILE), BF), pltpu.VMEM((n + 2 * HALO, d), F32)),
        us=6,
    )
    (send5,) = call(
        sum_kernel,
        [(got4, "v"), (rim_l, "r")],
        [(shape((peers, 8 * d // peers, d)), "r")],
        scratch=(pltpu.VMEM((8 * d // peers, d), BF),),
        copies=peers,
        us=1,
    )
    got5 = exchange(send5)
    from_left = lax.ppermute(rim_r, "nodes", up)
    from_right = lax.ppermute(rim_l, "nodes", down)
    (feature_grads,) = call(
        join_kernel,
        [(spread, "h"), (from_left, "v"), (from_right, "v")],
        [(shape((n, d)), "h")],
        us=1,
    )
    (weight_grads,) = call(
        gather_kernel,
        [(got5.reshape(8, d, d), "v"), (coarse_wg, "r")],
        [(shape((12, d, d), F32), "r")],
        scratch=(pltpu.VMEM((8, d, d), F32),),
        copies=3,
        us=1,
    )
    weight_grads = weight_grads.reshape(3, 4, d, d)
    return (feature_grads, weight_grads)


def solution(mesh):
    rows = P(("groups", "nodes"), None)
    cols = P("groups", "nodes")
    in_specs = (
        rows, rows, rows, rows, P(), cols, cols, cols, rows, P(("groups", "nodes")),
        cols, cols, rows, cols, cols,
    )
    out_specs = (rows, P("groups", None, None, None))
    return jax.shard_map(
        per_device, mesh=mesh, in_specs=in_specs, out_specs=out_specs, check_vma=False
    )
```

```python
import functools
import math

import jax
import jax.numpy as jnp
from jax import lax
from jax.experimental import pallas as pl
from jax.experimental.pallas import tpu as pltpu
from jax.sharding import PartitionSpec as P

HALO = 256
TILE = 256
WIDE = 2048
BF = jnp.bfloat16
F32 = jnp.float32

VM = pl.BlockSpec(memory_space=pltpu.VMEM)
HB = pl.BlockSpec(memory_space=pltpu.HBM)


def dot(a, b):
    return jnp.dot(a, b, preferred_element_type=F32)


def dot_nt(a, b):
    return lax.dot_general(a, b, (((1,), (1,)), ((), ())), preferred_element_type=F32)


def dot_tn(a, b):
    return lax.dot_general(a, b, (((0,), (0,)), ((), ())), preferred_element_type=F32)


def silu(v):
    return v / (1.0 + jnp.exp(-v))


def silu_slope(v):
    s = 1.0 / (1.0 + jnp.exp(-v))
    return s * (1.0 + v * (1.0 - s))


def merged_weights(idx, ew):
    total = ew
    for r in range(1, idx.shape[0]):
        total = total + jnp.where(pltpu.roll(idx, r, 0) == idx, pltpu.roll(ew, r, 0), 0.0)
    return total.astype(BF)


def edge_columns(idx, ew, start, rows):
    count = idx.shape[0]
    lanes = idx.shape[1]
    position = lax.broadcasted_iota(jnp.int32, (rows, lanes), 0) + start
    position = position.astype(jnp.int16)
    picked = jnp.zeros((rows, lanes), BF)
    for k in range(count):
        picked = jnp.where(idx[k : k + 1, :] == position, ew[k : k + 1, :], picked)
    return picked


def fine_edges(off, ew, s_ref):
    for h in range(TILE // 128):
        lane = slice(128 * h, 128 * (h + 1))
        o = off[:, lane]
        weight = merged_weights(o, ew[:, lane])
        rel = o + lax.broadcasted_iota(jnp.int32, o.shape, 1) + HALO
        rel = rel.astype(jnp.int16)
        for c in range(2 * HALO // 128 + 1):
            s_ref[128 * (h + c) : 128 * (h + c + 1), lane] = edge_columns(
                rel, weight, 128 * c, 128
            )


def clear_corners(s_ref):
    for h in range(TILE // 128):
        lane = slice(128 * h, 128 * (h + 1))
        if h > 0:
            s_ref[: 128 * h, lane] = jnp.zeros((128 * h, 128), BF)
        last = 128 * h + 2 * HALO + 128
        if last < TILE + 2 * HALO:
            s_ref[last:, lane] = jnp.zeros((TILE + 2 * HALO - last, 128), BF)


def forward_weights(w):
    w01 = jnp.concatenate([jnp.transpose(w[0]), jnp.transpose(w[1])], axis=1)
    return w01, jnp.transpose(w[2]), jnp.transpose(w[3])


def pool_matrix(pool, tile_rows):
    lane = lax.broadcasted_iota(jnp.int32, pool.shape, 1) // tile_rows
    values = pool.astype(F32)
    parts = [jnp.where(lane == r, values, 0.0) for r in range(pool.shape[1] // tile_rows)]
    return jnp.concatenate(parts, axis=0).astype(BF)


class Copies:
    def __init__(self, sems):
        self.sems = sems
        self.used = 0
        self.open = {}

    def start(self, source, target):
        copy = pltpu.make_async_copy(source, target, self.sems.at[self.used])
        self.used += 1
        copy.start()
        self.open[id(copy)] = copy
        return copy

    def wait(self, *copies):
        for copy in copies:
            if id(copy) in self.open:
                copy.wait()
                del self.open[id(copy)]

    def finish(self):
        self.wait(*list(self.open.values()))


def shape(dims, dtype=BF):
    return jax.ShapeDtypeStruct(dims, dtype)


def call(kernel, ins, outs, scratch=(), copies=0, us=3, mib=24):
    n_in, n_out = len(ins), len(outs)
    staged_in = [i for i, (_, kind) in enumerate(ins) if kind in "hs012"]
    staged_out = [i for i, (_, kind) in enumerate(outs) if kind in "hs"]
    spaces = {"h": pltpu.VMEM, "s": pltpu.SMEM}
    stage = []
    for i in staged_in:
        array, kind = ins[i]
        dims = array.shape[1:] if kind.isdigit() else array.shape
        stage.append(spaces.get(kind, pltpu.VMEM)(dims, array.dtype))
    stage += [spaces[outs[i][1]](outs[i][0].shape, outs[i][0].dtype) for i in staged_out]
    total = len(staged_in) + len(staged_out) + copies

    def body(*refs):
        in_refs, out_refs = list(refs[:n_in]), list(refs[n_in : n_in + n_out])
        rest = list(refs[n_in + n_out :])
        sems = rest.pop() if total else None
        stages, user = rest[: len(stage)], rest[len(stage) :]
        io = Copies(sems)
        pending = {}
        for i, ref in zip(staged_in, stages):
            kind = ins[i][1]
            source = in_refs[i].at[int(kind)] if kind.isdigit() else in_refs[i]
            pending[i] = io.start(source, ref)
            in_refs[i] = ref
        targets = {}
        for i, ref in zip(staged_out, stages[len(staged_in) :]):
            targets[i] = out_refs[i]
            out_refs[i] = ref

        def need(*which):
            io.wait(*[pending[i] for i in which or pending])

        def flush(*which):
            for i in which:
                io.start(out_refs[i], targets.pop(i))

        kernel(io, need, flush, in_refs, out_refs, *user)
        flush(*list(targets))
        io.finish()

    return pl.pallas_call(
        body,
        out_shape=[
            s if kind == "v" else pltpu.HBM(s.shape, s.dtype) for s, kind in outs
        ],
        in_specs=[VM if kind == "v" else HB for _, kind in ins],
        out_specs=[VM if kind == "v" else HB for _, kind in outs],
        scratch_shapes=stage
        + list(scratch)
        + ([pltpu.SemaphoreType.DMA((total,))] if total else []),
        compiler_params=pltpu.CompilerParams(vmem_limit_bytes=mib << 20),
        cost_estimate=pl.CostEstimate(
            flops=0, bytes_accessed=int(us * 3_000_000), transcendentals=0
        ),
    )(*[
        a if kind == "v" else pltpu.with_memory_space_constraint(a, pltpu.HBM)
        for a, kind in ins
    ])


def fine_forward(h_t, agg, weights):
    w01, w2t, w3t = weights
    first = dot(w01, jnp.concatenate([h_t, agg], axis=0))
    middle = silu(first).astype(BF)
    second = dot(w2t, middle)
    outer = silu(second).astype(BF)
    return (h_t.astype(F32) + dot(w3t, outer)).astype(BF)


def outer_tiles(tile_count, per):
    return list(range(per)) + list(range(tile_count - per, tile_count))


def inner_kernel(tile_rows, peers, cap, io, need, flush, ins, outs, feat_t, s_ref, ids, counts):
    off, ew, feat, w, pool, owner, slot, nbrs, cew, cot = ins
    so_ref, win_ref, w01_ref, w2t_ref, w3t_ref, po_ref, spread, ext_ref, agg_ref, place = outs
    rows, d = feat.shape
    block_rows = pool.shape[0]
    n2 = cot.shape[0]
    tiles = rows // TILE
    per = TILE // tile_rows
    tile_count = rows // tile_rows
    for i in range(tiles - 2):
        clear_corners(s_ref.at[i])
    clear_corners(so_ref.at[0])
    clear_corners(so_ref.at[1])
    spread[...] = jnp.zeros(spread.shape, F32)
    ids[...] = jnp.full(ids.shape, -1.0, F32)
    for p in range(peers):
        counts[p] = 0
    need(5, 6)
    lane_slot = lax.broadcasted_iota(jnp.int32, (1, 128), 1) // block_rows
    first_tiles = outer_tiles(tile_count, per)
    for t in first_tiles + [t for t in range(tile_count) if t not in first_tiles]:
        o = owner[t]
        c = counts[o]
        counts[o] = c + 1
        place[t] = o * cap + c
        row = ids[pl.ds(o, 1), :]
        ids[pl.ds(o, 1), :] = jnp.where(lane_slot == c, slot[t].astype(F32), row)
    flush(9)
    need(0, 1)
    need(2)
    feat_t[...] = jnp.transpose(feat[...])
    need()
    weights = forward_weights(w)
    for i in range(1, tiles - 1):
        cols = slice(i * TILE, (i + 1) * TILE)
        fine_edges(off[:, cols], ew[:, cols], s_ref.at[i - 1])
        around = feat_t[:, i * TILE - HALO : (i + 1) * TILE + HALO]
        agg_ref[:, cols] = dot(around, s_ref[i - 1]).astype(BF)
    for start in range(TILE, rows - TILE, WIDE):
        stop = min(start + WIDE, rows - TILE)
        cols = slice(start, stop)
        fine_out = fine_forward(feat_t[:, cols], agg_ref[:, cols], weights)
        for i in range(start // TILE, stop // TILE):
            at = slice(i * TILE - start, (i + 1) * TILE - start)
            matrix = pool_matrix(pool[:, i * TILE : (i + 1) * TILE], tile_rows)
            blocks = dot_nt(matrix, fine_out[:, at])
            for j in range(per):
                at = pl.ds(pl.multiple_of(place[i * per + j] * block_rows, 8), block_rows)
                spread[at, :] = blocks[j * block_rows : (j + 1) * block_rows, :]
    for n, i in enumerate((0, tiles - 1)):
        cols = slice(i * TILE, (i + 1) * TILE)
        fine_edges(off[:, cols], ew[:, cols], so_ref.at[n])
        po_ref[n] = pool_matrix(pool[:, cols], tile_rows)
    win_ref[0] = feat_t[:, : TILE + HALO]
    win_ref[1] = feat_t[:, rows - TILE - HALO :]
    w01_ref[...], w2t_ref[...], w3t_ref[...] = weights
    nb = nbrs[...].astype(F32)
    high = jnp.floor(nb * (1.0 / 256.0))
    ce = cew[...]
    ce_high = ce.astype(BF).astype(F32)
    fields = [high, nb - high * 256.0, ce_high, ce - ce_high]
    fields.append(jnp.zeros((nb.shape[0], 128 - 4 * n2), F32))
    top = jnp.concatenate(fields, axis=1)
    sub = lax.broadcasted_iota(jnp.int32, (8, 128), 0)
    for p in range(peers):
        ext_ref[p, 0:n2, :] = cot[...]
        below = jnp.where(sub == 0, ids[p : p + 1, :], 0.0)
        ext_ref[p, n2 : n2 + 16, :] = jnp.concatenate([top, below], axis=0).astype(BF)


def outer_kernel(
    tile_rows, cap, block_rows, io, need, flush, ins, outs, agg_edge, spread, stage, counts
):
    across, beside, s_in, win, w01, w2t, w3t, pool, spread_in, ext, agg_in, owner = ins
    even = lax.rem(lax.axis_index("nodes"), 2) == 0
    left = jnp.where(even, beside[...], across[...])
    right = jnp.where(even, across[...], beside[...])
    send_ref, agg_ref = outs
    peers, chunk, d = stage.shape
    rows = agg_in.shape[1]
    per = TILE // tile_rows
    io.start(ext, send_ref.at[:, pl.ds(chunk, ext.shape[1]), :])
    inside = pl.ds(TILE, rows - 2 * TILE)
    io.start(agg_in.at[:, inside], agg_ref.at[:, inside])
    spread[...] = spread_in[...]
    for p in range(peers):
        counts[p] = 0
    weights = (w01[...], w2t[...], w3t[...])
    for n in range(2):
        if n == 0:
            window_t = jnp.concatenate([jnp.transpose(left), win[0]], axis=1)
        else:
            window_t = jnp.concatenate([win[1], jnp.transpose(right)], axis=1)
        agg_edge[:, n * TILE : (n + 1) * TILE] = dot(window_t, s_in[n]).astype(BF)
    h_t = jnp.concatenate([win[0, :, :TILE], win[1, :, HALO:]], axis=1)
    fine_out = fine_forward(h_t, agg_edge[...], weights)
    results = [dot_nt(pool[n], fine_out[:, n * TILE : (n + 1) * TILE]) for n in range(2)]
    io.start(agg_edge.at[:, pl.ds(0, TILE)], agg_ref.at[:, pl.ds(0, TILE)])
    io.start(agg_edge.at[:, pl.ds(TILE, TILE)], agg_ref.at[:, pl.ds(rows - TILE, TILE)])
    need()
    for j, t in enumerate(outer_tiles(rows // tile_rows, per)):
        o = owner[t]
        c = counts[o]
        counts[o] = c + 1
        at = pl.ds(pl.multiple_of((o * cap + c) * block_rows, 8), block_rows)
        blocks = results[j // per]
        spread[at, :] = blocks[j % per * block_rows : (j % per + 1) * block_rows, :]
    group = max(1, peers // 4)
    for p in range(peers):
        stage[p] = spread[p * chunk : (p + 1) * chunk, :].astype(BF)
        if p % group == group - 1:
            part = pl.ds(p + 1 - group, group)
            io.start(stage.at[part], send_ref.at[part, pl.ds(0, chunk), :])


def mid_edges(nbrs, ew, s_ref):
    nodes = nbrs.shape[1]
    for c in range(nodes // 128):
        lane = slice(128 * c, 128 * (c + 1))
        idx = nbrs[:, lane]
        weight = merged_weights(idx, ew[:, lane])
        idx = idx.astype(jnp.int16)
        for r in range(nodes // 128):
            s_ref[128 * r : 128 * (r + 1), lane] = edge_columns(idx, weight, 128 * r, 128)


def first_window_kernel(io, need, flush, ins, outs):
    nbrs, ew, w, _ = ins
    smid, w01_ref, w2t_ref, w3t_ref = outs
    need(0, 1)
    mid_edges(nbrs, ew, smid)
    flush(0)
    need()
    w01_ref[...], w2t_ref[...], w3t_ref[...] = forward_weights(w)


def mid_kernel(block_rows, chunk, io, need, flush, ins, outs, blocks, coarse):
    got, smid, w01, w2t, w3t, pool_mid = ins
    send_ref, hid_ref, agg_ref, sel_ref, ext_ref = outs
    peers = got.shape[0]
    nodes = smid.shape[0]
    n2 = pool_mid.shape[0]
    io.start(got.at[:, pl.ds(chunk, n2 + 16), :], ext_ref)
    rows = [got[p, chunk + n2 : chunk + n2 + 16, :].astype(F32)[8:9, :] for p in range(peers)]
    keys = jnp.transpose(jnp.concatenate(rows, axis=0))
    keys = keys * block_rows
    keys = keys + (lax.broadcasted_iota(jnp.int32, keys.shape, 0) % block_rows).astype(F32)
    keys = keys.astype(jnp.int32)
    lane = lax.broadcasted_iota(jnp.int32, (chunk, nodes), 1)
    for p in range(peers):
        sel_ref[p * chunk : (p + 1) * chunk, :] = jnp.where(
            keys[0:chunk, p : p + 1] == lane, 1.0, 0.0
        ).astype(BF)
        blocks[p * chunk : (p + 1) * chunk, :] = got[p, 0:chunk, :]
    flush(3)
    hidden = dot_tn(blocks[...], sel_ref[...]).astype(BF)
    hid_ref[...] = hidden
    need()
    agg = dot(hidden, smid[...]).astype(BF)
    agg_ref[...] = agg
    flush(1, 2)
    middle = silu(dot(w01[...], jnp.concatenate([hidden, agg], axis=0))).astype(BF)
    outer = silu(dot(w2t[...], middle)).astype(BF)
    mid_out = (hidden.astype(F32) + dot(w3t[...], outer)).astype(BF)
    coarse[...] = dot_nt(pool_mid[...], mid_out).astype(BF)
    for p in range(peers):
        io.start(coarse, send_ref.at[p])


def second_window_kernel(io, need, flush, ins, outs, nb_ref, ew_ref):
    ext, hid, agg, mid_cot, w1 = ins
    sco, cot_all, mcot, sl1_ref, sl2_ref = outs
    peers = ext.shape[0]
    n2 = ext.shape[1] - 16
    nodes = peers * n2
    edges = nb_ref.shape[0]
    need()
    for p in range(peers):
        part = ext[p, n2 : n2 + 16, :].astype(F32)[0:edges, :]
        at = slice(p * n2, (p + 1) * n2)
        nb_ref[:, at] = (part[:, 0:n2] * 256.0 + part[:, n2 : 2 * n2]).astype(jnp.int32)
        ew_ref[:, at] = part[:, 2 * n2 : 3 * n2] + part[:, 3 * n2 : 4 * n2]
    cots = jnp.concatenate([ext[p, 0:n2, :] for p in range(peers)], axis=0)
    cot_all[...] = jnp.transpose(cots)
    mcot[...] = jnp.transpose(mid_cot[...])

    def column(c, _):
        lane = pl.ds(pl.multiple_of(c * 128, 128), 128)
        idx = nb_ref[:, lane]
        weight = merged_weights(idx, ew_ref[:, lane])
        idx = idx.astype(jnp.int16)
        for r in range(nodes // 128):
            sco[128 * r : 128 * (r + 1), lane] = edge_columns(idx, weight, 128 * r, 128)
        return 0

    lax.fori_loop(0, nodes // 128, column, 0)
    flush(0, 1, 2)
    w01, w2t, _ = forward_weights(w1)
    first = dot(w01, jnp.concatenate([hid[...], agg[...]], axis=0))
    s1 = 1.0 / (1.0 + jnp.exp(-first))
    second = dot(w2t, (first * s1).astype(BF))
    s2 = 1.0 / (1.0 + jnp.exp(-second))
    sl1_ref[...] = s1 * (1.0 + first * (1.0 - s1))
    sl2_ref[...] = s2 * (1.0 + second * (1.0 - s2))


def coarse_kernel(io, need, flush, ins, outs):
    got, sco, w2, cot_all, cot_my, pool_mid, mcot, w1, msl2, msl1, smid, sel = ins
    send_ref, gmid_ref, sg_ref, fg_ref, cwg_ref = outs
    nodes = got.shape[0]
    n2 = cot_my.shape[0]
    me = lax.axis_index("nodes")
    width = min(TILE, nodes)
    hidden = jnp.transpose(got[...])
    need(1, 2, 3)
    w01, w2t, _ = forward_weights(w2)
    mine = pl.ds(pl.multiple_of(me * n2, 16), n2)
    spread = jnp.zeros((n2, 128), F32)
    fg_mine = jnp.zeros((n2, 128), F32)
    grads = [jnp.zeros((128, 128), F32) for _ in range(4)]
    row = lax.broadcasted_iota(jnp.int32, (n2, width), 0) + me * n2
    lane = lax.broadcasted_iota(jnp.int32, (n2, width), 1)
    for i in range(nodes // width):
        cols = slice(i * width, (i + 1) * width)
        h = hidden[:, cols]
        agg = dot(hidden, sco[:, cols]).astype(BF)
        first = dot(w01, jnp.concatenate([h, agg], axis=0))
        s1 = 1.0 / (1.0 + jnp.exp(-first))
        middle = (first * s1).astype(BF)
        second = dot(w2t, middle)
        s2 = 1.0 / (1.0 + jnp.exp(-second))
        outer = (second * s2).astype(BF)
        g = cot_all[:, cols]
        sg = (dot(w2[3], g) * (s2 * (1.0 + second * (1.0 - s2)))).astype(BF)
        fg = (dot(w2[2], sg) * (s1 * (1.0 + first * (1.0 - s1)))).astype(BF)
        spill = dot(w2[1], fg).astype(BF)
        spread = spread + dot_nt(sco[mine, cols], spill)
        here = jnp.where(lane + i * width == row, 1.0, 0.0).astype(BF)
        fg_mine = fg_mine + dot_nt(here, fg)
        grads = [
            grads[0] + dot_nt(h, fg),
            grads[1] + dot_nt(agg, fg),
            grads[2] + dot_nt(middle, sg),
            grads[3] + dot_nt(outer, g),
        ]
    scale = 1.0 / math.sqrt(nodes)
    for m in range(4):
        cwg_ref[m] = grads[m] * scale
    flush(4)
    need(4, 5, 6, 7, 8, 9)
    direct = cot_my[...].astype(F32) + dot_nt(fg_mine.astype(BF), w2[0])
    coarse_grad = (direct + spread).astype(BF)
    back = dot_tn(coarse_grad, pool_mid[...])
    g = (mcot[...].astype(F32) + back).astype(BF)
    gmid_ref[...] = g
    sg = (dot(w1[3], g) * msl2[...]).astype(BF)
    sg_ref[...] = sg
    fg = (dot(w1[2], sg) * msl1[...]).astype(BF)
    fg_ref[...] = fg
    flush(1, 2, 3)
    spill = dot(w1[1], fg).astype(BF)
    need()
    mid_grad = (g.astype(F32) + dot(w1[0], fg) + dot_nt(spill, smid[...])).astype(BF)
    send_ref[...] = dot_nt(sel[...], mid_grad).astype(BF)


def third_window_kernel(tile_rows, mid_scale, io, need, flush, ins, outs):
    mhid, magg, gmid, msg, mfg, feat, fine_cot, w0, pool, place, agg, w1 = ins
    wg_ref, hid_ref, mid_ref, outer_ref, sl1_ref, sl2_ref, cot_ref, pick_ref, po_ref = outs
    d, rows = hid_ref.shape
    block_rows = pool.shape[0]
    per = TILE // tile_rows
    need()
    w01, w2t, _ = forward_weights(w1)
    middle = silu(dot(w01, jnp.concatenate([mhid[...], magg[...]], axis=0))).astype(BF)
    outer = silu(dot(w2t, middle)).astype(BF)
    wg_ref[0:d, :] = (dot_nt(mhid[...], mfg[...]) * mid_scale).astype(BF)
    wg_ref[d : 2 * d, :] = (dot_nt(magg[...], mfg[...]) * mid_scale).astype(BF)
    wg_ref[2 * d : 3 * d, :] = (dot_nt(middle, msg[...]) * mid_scale).astype(BF)
    wg_ref[3 * d : 4 * d, :] = (dot_nt(outer, gmid[...]) * mid_scale).astype(BF)
    hid_ref[...] = jnp.transpose(feat[...])
    cot_ref[...] = jnp.transpose(fine_cot[...])
    slots = pick_ref.shape[1]
    lane = lax.broadcasted_iota(jnp.int32, (block_rows, slots), 1)
    lane = lane - lax.broadcasted_iota(jnp.int32, (block_rows, slots), 0)
    for t in range(0, rows // tile_rows, 2):
        both = [jnp.where(lane == place[t + j] * block_rows, 1.0, 0.0) for j in range(2)]
        pick_ref[t * block_rows : (t + 2) * block_rows, :] = jnp.concatenate(
            both, axis=0
        ).astype(BF)
    flush(0, 1, 6, 7)
    w01, w2t, _ = forward_weights(w0)
    for i in range(rows // TILE):
        cols = slice(i * TILE, (i + 1) * TILE)
        first = dot(w01, jnp.concatenate([hid_ref[:, cols], agg[:, cols]], axis=0))
        s1 = 1.0 / (1.0 + jnp.exp(-first))
        middle = (first * s1).astype(BF)
        mid_ref[:, cols] = middle
        sl1_ref[:, cols] = s1 * (1.0 + first * (1.0 - s1))
        second = dot(w2t, middle)
        s2 = 1.0 / (1.0 + jnp.exp(-second))
        outer_ref[:, cols] = (second * s2).astype(BF)
        sl2_ref[:, cols] = s2 * (1.0 + second * (1.0 - s2))
        po_ref[i] = pool_matrix(pool[:, cols], tile_rows)


def fine_grad_kernel(scale, io, need, flush, ins, outs, g_ref, fg_ref):
    got, pick, cot, pool, w, slope2, slope1, hid, agg, mid, outer, mid_wg = ins
    send_ref, g_out, fg_out = outs
    d, rows = hid.shape
    need(1)
    blocks = dot(pick[...], got[...]).astype(BF)
    need(2, 3)
    per = pool.shape[1]
    for i in range(rows // TILE):
        cols = slice(i * TILE, (i + 1) * TILE)
        back = dot_tn(blocks[i * per : (i + 1) * per, :], pool[i])
        g_ref[:, cols] = (cot[:, cols].astype(F32) + back).astype(BF)
    io.start(g_ref, g_out)
    g = g_ref[...]
    need(4, 5, 6)
    sg = (dot(w[3], g) * slope2[...]).astype(BF)
    fg = (dot(w[2], sg) * slope1[...]).astype(BF)
    fg_ref[...] = fg
    io.start(fg_ref, fg_out)
    need()
    send_ref[4 * d : 8 * d, :] = mid_wg[...]
    for m, (a, b) in enumerate(
        ((hid[...], fg), (agg[...], fg), (mid[...], sg), (outer[...], g))
    ):
        send_ref[m * d : (m + 1) * d, :] = (dot_nt(a, b) * scale).astype(BF)


def fine_spread_kernel(io, need, flush, ins, outs, s_ref, total):
    off, ew, w, g, fg = ins
    rim_near, rim_far, out_ref = outs
    rows = g.shape[1]
    clear_corners(s_ref.at[0])
    clear_corners(s_ref.at[1])
    total[...] = jnp.zeros(total.shape, F32)
    need()
    for i in range(rows // TILE):
        cols = slice(i * TILE, (i + 1) * TILE)
        s = s_ref.at[i % 2]
        fine_edges(off[:, cols], ew[:, cols], s)
        fg_tile = fg[:, cols]
        direct = g[:, cols].astype(F32) + dot(w[0], fg_tile)
        spill = dot(w[1], fg_tile).astype(BF)
        window = slice(i * TILE, (i + 1) * TILE + 2 * HALO)
        total[window, :] = total[window, :] + dot_nt(s[...], spill)
        here = slice(HALO + i * TILE, HALO + (i + 1) * TILE)
        total[here, :] = total[here, :] + jnp.transpose(direct)
    even = lax.rem(lax.axis_index("nodes"), 2) == 0
    low, high = total[:HALO, :].astype(BF), total[HALO + rows :, :].astype(BF)
    rim_near[...] = jnp.where(even, high, low)
    rim_far[...] = jnp.where(even, low, high)
    out_ref[...] = total[HALO : HALO + rows, :]


def sum_kernel(io, need, flush, ins, outs, part):
    got, _ = ins
    send_ref = outs[0]
    peers = got.shape[0]
    need()
    part[...] = sum(got[p].astype(F32) for p in range(peers)).astype(BF)
    for p in range(peers):
        io.start(part, send_ref.at[p])


def join_kernel(io, need, flush, ins, outs):
    total, across, beside = ins
    out_ref = outs[0]
    even = lax.rem(lax.axis_index("nodes"), 2) == 0
    from_left = jnp.where(even, beside[...], across[...])
    from_right = jnp.where(even, across[...], beside[...])
    rows = total.shape[0]
    need()
    out_ref[:HALO, :] = (total[:HALO, :] + from_left.astype(F32)).astype(BF)
    out_ref[HALO : rows - HALO, :] = total[HALO : rows - HALO, :].astype(BF)
    out_ref[rows - HALO :, :] = (total[rows - HALO :, :] + from_right.astype(F32)).astype(BF)


def gather_kernel(io, need, flush, ins, outs, wide):
    summed, coarse = ins
    out_ref = outs[0]
    for half in range(2):
        wide[4 * half : 4 * half + 4] = summed[4 * half : 4 * half + 4].astype(F32)
        part = pl.ds(4 * half, 4)
        io.start(wide.at[part], out_ref.at[part])
    need()
    io.start(coarse, out_ref.at[pl.ds(8, 4)])


def exchange(x):
    return lax.all_to_all(x, "nodes", split_axis=0, concat_axis=0, tiled=True)


def per_device(
    features,
    fine_cotangent,
    mid_cotangent,
    coarse_cotangent,
    weights,
    fine_offsets,
    fine_edge_w,
    pool_fine,
    owner_dev,
    coarse_slot,
    mid_nbrs,
    mid_edge_w,
    pool_mid,
    coarse_nbrs,
    coarse_edge_w,
):
    n, d = features.shape
    tile_count = owner_dev.shape[0]
    tile_rows = n // tile_count
    block_rows = pool_fine.shape[0]
    n1 = mid_cotangent.shape[0]
    n2 = coarse_cotangent.shape[0]
    edges = fine_offsets.shape[0]
    peers = lax.axis_size("nodes")
    cap = max(2, 2 * tile_count // peers)
    chunk = cap * block_rows
    window = TILE + 2 * HALO
    per = TILE // tile_rows * block_rows
    ends = peers - 1
    inside_pairs = [(i, i ^ 1) for i in range(peers)]
    between_pairs = [(i, ((i + 1) ^ 1) - 1) for i in range(1, ends)]
    total2 = peers * n2

    odd = lax.rem(lax.axis_index("nodes"), 2)
    near = lax.dynamic_slice_in_dim(features, (1 - odd) * (n - HALO), HALO, 0)
    far = lax.dynamic_slice_in_dim(features, odd * (n - HALO), HALO, 0)
    across = lax.ppermute(near, "nodes", inside_pairs)
    beside = lax.ppermute(far, "nodes", between_pairs)
    owners = owner_dev.reshape(-1)
    s_out, win, w01, w2t, w3t, pool_out, spread, ext, agg_in, place = call(
        functools.partial(inner_kernel, tile_rows, peers, cap),
        [
            (fine_offsets, "h"), (fine_edge_w, "h"), (features, "h"), (weights, "0"),
            (pool_fine, "h"), (owners, "s"), (coarse_slot, "s"), (coarse_nbrs, "h"),
            (coarse_edge_w, "h"), (coarse_cotangent, "h"),
        ],
        [
            (shape((2, window, TILE)), "v"), (shape((2, d, TILE + HALO)), "v"),
            (shape((d, 2 * d)), "v"), (shape((d, d)), "v"), (shape((d, d)), "v"),
            (shape((2, per, TILE)), "v"), (shape((peers * chunk, d), F32), "v"),
            (shape((peers, n2 + 16, d)), "v"), (shape((d, n)), "v"),
            (shape((tile_count,), jnp.int32), "s"),
        ],
        scratch=(
            pltpu.VMEM((d, n), BF),
            pltpu.VMEM((n // TILE - 2, window, TILE), BF),
            pltpu.VMEM((peers, 128), F32),
            pltpu.SMEM((peers,), jnp.int32),
        ),
        us=6,
    )
    send1, agg = call(
        functools.partial(outer_kernel, tile_rows, cap, block_rows),
        [
            (across, "v"), (beside, "v"), (s_out, "v"), (win, "v"), (w01, "v"), (w2t, "v"),
            (w3t, "v"), (pool_out, "v"), (spread, "v"), (ext, "v"), (agg_in, "v"), (owners, "s"),
        ],
        [(shape((peers, chunk + n2 + 16, d)), "r"), (shape((d, n)), "r")],
        scratch=(
            pltpu.VMEM((d, 2 * TILE), BF),
            pltpu.VMEM((peers * chunk, d), F32),
            pltpu.VMEM((peers, chunk, d), BF),
            pltpu.SMEM((peers,), jnp.int32),
        ),
        copies=8,
        us=3,
    )
    got1 = exchange(send1)
    smid, m01, m2t, m3t = call(
        first_window_kernel,
        [(mid_nbrs, "h"), (mid_edge_w, "h"), (weights, "1"), (agg, "r")],
        [
            (shape((n1, n1)), "h"), (shape((d, 2 * d)), "h"), (shape((d, d)), "h"),
            (shape((d, d)), "h"),
        ],
        us=6,
    )
    send2, mhid, magg, sel, ext = call(
        functools.partial(mid_kernel, block_rows, chunk),
        [(got1, "v"), (smid, "h"), (m01, "h"), (m2t, "h"), (m3t, "h"), (pool_mid, "h")],
        [
            (shape((peers, n2, d)), "r"), (shape((d, n1)), "h"), (shape((d, n1)), "h"),
            (shape((peers * chunk, n1)), "h"), (shape((peers, n2 + 16, d)), "r"),
        ],
        scratch=(pltpu.VMEM((peers * chunk, d), BF), pltpu.VMEM((n2, d), BF)),
        copies=peers + 1,
        us=3,
    )
    got2 = exchange(send2)
    sco, cot_all, mcot, mslope1, mslope2 = call(
        second_window_kernel,
        [
            (ext, "h"), (mhid, "h"), (magg, "h"), (mid_cotangent, "h"), (weights, "1"),
        ],
        [
            (shape((total2, total2)), "h"), (shape((d, total2)), "h"), (shape((d, n1)), "h"),
            (shape((d, n1), F32), "h"), (shape((d, n1), F32), "h"),
        ],
        scratch=(pltpu.VMEM((edges, total2), jnp.int32), pltpu.VMEM((edges, total2), F32)),
        us=6,
    )
    send3, gmid, msg, mfg, coarse_wg = call(
        coarse_kernel,
        [
            (got2.reshape(total2, d), "v"), (sco, "h"), (weights, "2"), (cot_all, "h"),
            (coarse_cotangent, "h"), (pool_mid, "h"), (mcot, "h"), (weights, "1"),
            (mslope2, "h"), (mslope1, "h"), (smid, "h"), (sel, "h"),
        ],
        [
            (shape((peers * chunk, d)), "h"), (shape((d, n1)), "h"), (shape((d, n1)), "h"),
            (shape((d, n1)), "h"), (shape((4, d, d), F32), "h"),
        ],
        us=3,
    )
    got3 = exchange(send3.reshape(peers, chunk, d))
    mid_wg, hid, mid, outer, slope1, slope2, cot, pick, pool_b = call(
        functools.partial(third_window_kernel, tile_rows, 1.0 / math.sqrt(n1 * peers)),
        [
            (mhid, "h"), (magg, "h"), (gmid, "h"), (msg, "h"), (mfg, "h"), (features, "h"),
            (fine_cotangent, "h"), (weights, "0"), (pool_fine, "h"), (place, "s"), (agg, "h"),
            (weights, "1"),
        ],
        [
            (shape((4 * d, d)), "h"), (shape((d, n)), "h"), (shape((d, n)), "h"),
            (shape((d, n)), "h"), (shape((d, n), F32), "h"), (shape((d, n), F32), "h"),
            (shape((d, n)), "h"), (shape((tile_count * block_rows, peers * chunk)), "h"),
            (shape((n // TILE, per, TILE)), "h"),
        ],
        us=6,
    )
    send4, g, fg = call(
        functools.partial(fine_grad_kernel, 1.0 / math.sqrt(n * peers)),
        [
            (got3.reshape(peers * chunk, d), "v"), (pick, "h"), (cot, "h"), (pool_b, "h"),
            (weights, "0"), (slope2, "h"), (slope1, "h"), (hid, "h"), (agg, "h"), (mid, "h"),
            (outer, "h"), (mid_wg, "h"),
        ],
        [(shape((8 * d, d)), "h"), (shape((d, n)), "r"), (shape((d, n)), "r")],
        scratch=(pltpu.VMEM((d, n), BF), pltpu.VMEM((d, n), BF)),
        copies=2,
        us=4,
    )
    got4 = exchange(send4.reshape(peers, 8 * d // peers, d))
    rim_near, rim_far, spread = call(
        fine_spread_kernel,
        [(fine_offsets, "h"), (fine_edge_w, "h"), (weights, "0"), (g, "h"), (fg, "h")],
        [(shape((HALO, d)), "h"), (shape((HALO, d)), "h"), (shape((n, d), F32), "h")],
        scratch=(pltpu.VMEM((2, window, TILE), BF), pltpu.VMEM((n + 2 * HALO, d), F32)),
        us=6,
    )
    (send5,) = call(
        sum_kernel,
        [(got4, "v"), (rim_near, "r")],
        [(shape((peers, 8 * d // peers, d)), "r")],
        scratch=(pltpu.VMEM((8 * d // peers, d), BF),),
        copies=peers,
        us=1,
    )
    got5 = exchange(send5)
    from_across = lax.ppermute(rim_near, "nodes", inside_pairs)
    from_beside = lax.ppermute(rim_far, "nodes", between_pairs)
    (feature_grads,) = call(
        join_kernel,
        [(spread, "h"), (from_across, "v"), (from_beside, "v")],
        [(shape((n, d)), "h")],
        us=1,
    )
    (weight_grads,) = call(
        gather_kernel,
        [(got5.reshape(8, d, d), "v"), (coarse_wg, "h")],
        [(shape((12, d, d), F32), "r")],
        scratch=(pltpu.VMEM((8, d, d), F32),),
        copies=3,
        us=1,
    )
    weight_grads = weight_grads.reshape(3, 4, d, d)
    return (feature_grads, weight_grads)


def solution(mesh):
    rows = P(("groups", "nodes"), None)
    cols = P("groups", "nodes")
    in_specs = (
        rows, rows, rows, rows, P(), cols, cols, cols, rows, P(("groups", "nodes")),
        cols, cols, rows, cols, cols,
    )
    out_specs = (rows, P("groups", None, None, None))
    return jax.shard_map(
        per_device, mesh=mesh, in_specs=in_specs, out_specs=out_specs, check_vma=False
    )
```

```python
import functools
import math

import jax
import jax.numpy as jnp
from jax import lax
from jax.experimental import pallas as pl
from jax.experimental.pallas import tpu as pltpu
from jax.sharding import PartitionSpec as P

HALO = 256
TILE = 256
WIDE = 2048
BF = jnp.bfloat16
F32 = jnp.float32

VM = pl.BlockSpec(memory_space=pltpu.VMEM)
HB = pl.BlockSpec(memory_space=pltpu.HBM)


def dot(a, b):
    return jnp.dot(a, b, preferred_element_type=F32)


def dot_nt(a, b):
    return lax.dot_general(a, b, (((1,), (1,)), ((), ())), preferred_element_type=F32)


def dot_tn(a, b):
    return lax.dot_general(a, b, (((0,), (0,)), ((), ())), preferred_element_type=F32)


def silu(v):
    return v / (1.0 + jnp.exp(-v))


def silu_slope(v):
    s = 1.0 / (1.0 + jnp.exp(-v))
    return s * (1.0 + v * (1.0 - s))


def merged_weights(idx, ew):
    total = ew
    for r in range(1, idx.shape[0]):
        total = total + jnp.where(pltpu.roll(idx, r, 0) == idx, pltpu.roll(ew, r, 0), 0.0)
    return total.astype(BF)


def edge_columns(idx, ew, start, rows):
    count = idx.shape[0]
    lanes = idx.shape[1]
    position = lax.broadcasted_iota(jnp.int32, (rows, lanes), 0) + start
    position = position.astype(jnp.int16)
    picked = jnp.zeros((rows, lanes), BF)
    for k in range(count):
        picked = jnp.where(idx[k : k + 1, :] == position, ew[k : k + 1, :], picked)
    return picked


def fine_edges(off, ew, s_ref):
    for h in range(TILE // 128):
        lane = slice(128 * h, 128 * (h + 1))
        o = off[:, lane]
        weight = merged_weights(o, ew[:, lane])
        rel = o + lax.broadcasted_iota(jnp.int32, o.shape, 1) + HALO
        rel = rel.astype(jnp.int16)
        for c in range(2 * HALO // 128 + 1):
            s_ref[128 * (h + c) : 128 * (h + c + 1), lane] = edge_columns(
                rel, weight, 128 * c, 128
            )


def clear_corners(s_ref):
    for h in range(TILE // 128):
        lane = slice(128 * h, 128 * (h + 1))
        if h > 0:
            s_ref[: 128 * h, lane] = jnp.zeros((128 * h, 128), BF)
        last = 128 * h + 2 * HALO + 128
        if last < TILE + 2 * HALO:
            s_ref[last:, lane] = jnp.zeros((TILE + 2 * HALO - last, 128), BF)


def forward_weights(w):
    w01 = jnp.concatenate([jnp.transpose(w[0]), jnp.transpose(w[1])], axis=1)
    return w01, jnp.transpose(w[2]), jnp.transpose(w[3])


def pool_matrix(pool, tile_rows):
    lane = lax.broadcasted_iota(jnp.int32, pool.shape, 1) // tile_rows
    values = pool.astype(F32)
    parts = [jnp.where(lane == r, values, 0.0) for r in range(pool.shape[1] // tile_rows)]
    return jnp.concatenate(parts, axis=0).astype(BF)


class Copies:
    def __init__(self, sems):
        self.sems = sems
        self.used = 0
        self.open = {}

    def start(self, source, target):
        copy = pltpu.make_async_copy(source, target, self.sems.at[self.used])
        self.used += 1
        copy.start()
        self.open[id(copy)] = copy
        return copy

    def wait(self, *copies):
        for copy in copies:
            if id(copy) in self.open:
                copy.wait()
                del self.open[id(copy)]

    def finish(self):
        self.wait(*list(self.open.values()))


def shape(dims, dtype=BF):
    return jax.ShapeDtypeStruct(dims, dtype)


def call(kernel, ins, outs, scratch=(), copies=0, us=3, mib=24, aliases={}):
    n_in, n_out = len(ins), len(outs)
    staged_in = [i for i, (_, kind) in enumerate(ins) if kind in "hs012"]
    staged_out = [i for i, (_, kind) in enumerate(outs) if kind in "hs"]
    spaces = {"h": pltpu.VMEM, "s": pltpu.SMEM}
    stage = []
    for i in staged_in:
        array, kind = ins[i]
        dims = array.shape[1:] if kind.isdigit() else array.shape
        stage.append(spaces.get(kind, pltpu.VMEM)(dims, array.dtype))
    stage += [spaces[outs[i][1]](outs[i][0].shape, outs[i][0].dtype) for i in staged_out]
    total = len(staged_in) + len(staged_out) + copies

    def body(*refs):
        in_refs, out_refs = list(refs[:n_in]), list(refs[n_in : n_in + n_out])
        rest = list(refs[n_in + n_out :])
        sems = rest.pop() if total else None
        stages, user = rest[: len(stage)], rest[len(stage) :]
        io = Copies(sems)
        pending = {}
        for i, ref in zip(staged_in, stages):
            kind = ins[i][1]
            source = in_refs[i].at[int(kind)] if kind.isdigit() else in_refs[i]
            pending[i] = io.start(source, ref)
            in_refs[i] = ref
        targets = {}
        for i, ref in zip(staged_out, stages[len(staged_in) :]):
            targets[i] = out_refs[i]
            out_refs[i] = ref

        def need(*which):
            io.wait(*[pending[i] for i in which or pending])

        def flush(*which):
            for i in which:
                io.start(out_refs[i], targets.pop(i))

        kernel(io, need, flush, in_refs, out_refs, *user)
        flush(*list(targets))
        io.finish()

    return pl.pallas_call(
        body,
        out_shape=[
            s if kind == "v" else pltpu.HBM(s.shape, s.dtype) for s, kind in outs
        ],
        in_specs=[VM if kind == "v" else HB for _, kind in ins],
        out_specs=[VM if kind == "v" else HB for _, kind in outs],
        scratch_shapes=stage
        + list(scratch)
        + ([pltpu.SemaphoreType.DMA((total,))] if total else []),
        input_output_aliases=aliases,
        compiler_params=pltpu.CompilerParams(vmem_limit_bytes=mib << 20),
        cost_estimate=pl.CostEstimate(
            flops=0, bytes_accessed=int(us * 3_000_000), transcendentals=0
        ),
    )(*[
        a if kind == "v" else pltpu.with_memory_space_constraint(a, pltpu.HBM)
        for a, kind in ins
    ])


def fine_forward(h_t, agg, weights):
    w01, w2t, w3t = weights
    first = dot(w01, jnp.concatenate([h_t, agg], axis=0))
    middle = silu(first).astype(BF)
    second = dot(w2t, middle)
    outer = silu(second).astype(BF)
    return (h_t.astype(F32) + dot(w3t, outer)).astype(BF)


def outer_tiles(tile_count, per):
    return list(range(per)) + list(range(tile_count - per, tile_count))


def inner_kernel(tile_rows, peers, cap, io, need, flush, ins, outs, feat_t, s_ref, ids, counts):
    off, ew, feat, w, pool, owner, slot, nbrs, cew, cot = ins
    so_ref, win_ref, w01_ref, w2t_ref, w3t_ref, po_ref, spread, ext_ref, agg_ref, place = outs
    rows, d = feat.shape
    block_rows = pool.shape[0]
    n2 = cot.shape[0]
    tiles = rows // TILE
    per = TILE // tile_rows
    tile_count = rows // tile_rows
    for i in range(tiles - 2):
        clear_corners(s_ref.at[i])
    clear_corners(so_ref.at[0])
    clear_corners(so_ref.at[1])
    spread[...] = jnp.zeros(spread.shape, F32)
    ids[...] = jnp.full(ids.shape, -1.0, F32)
    for p in range(peers):
        counts[p] = 0
    need(5, 6)
    lane_slot = lax.broadcasted_iota(jnp.int32, (1, 128), 1) // block_rows
    first_tiles = outer_tiles(tile_count, per)
    for t in first_tiles + [t for t in range(tile_count) if t not in first_tiles]:
        o = owner[t]
        c = counts[o]
        counts[o] = c + 1
        place[t] = o * cap + c
        row = ids[pl.ds(o, 1), :]
        ids[pl.ds(o, 1), :] = jnp.where(lane_slot == c, slot[t].astype(F32), row)
    flush(9)
    need(0, 1)
    for n, i in enumerate((0, tiles - 1)):
        cols = slice(i * TILE, (i + 1) * TILE)
        fine_edges(off[:, cols], ew[:, cols], so_ref.at[n])
    need()
    feat_t[...] = jnp.transpose(feat[...])
    weights = forward_weights(w)
    for i in range(1, tiles - 1):
        cols = slice(i * TILE, (i + 1) * TILE)
        fine_edges(off[:, cols], ew[:, cols], s_ref.at[i - 1])
        around = feat_t[:, i * TILE - HALO : (i + 1) * TILE + HALO]
        agg_ref[:, cols] = dot(around, s_ref[i - 1]).astype(BF)
    for start in range(TILE, rows - TILE, WIDE):
        stop = min(start + WIDE, rows - TILE)
        cols = slice(start, stop)
        fine_out = fine_forward(feat_t[:, cols], agg_ref[:, cols], weights)
        for i in range(start // TILE, stop // TILE):
            at = slice(i * TILE - start, (i + 1) * TILE - start)
            matrix = pool_matrix(pool[:, i * TILE : (i + 1) * TILE], tile_rows)
            blocks = dot_nt(matrix, fine_out[:, at])
            for j in range(per):
                at = pl.ds(pl.multiple_of(place[i * per + j] * block_rows, 8), block_rows)
                spread[at, :] = blocks[j * block_rows : (j + 1) * block_rows, :]
    for n, i in enumerate((0, tiles - 1)):
        po_ref[n] = pool_matrix(pool[:, i * TILE : (i + 1) * TILE], tile_rows)
    win_ref[0] = feat_t[:, : TILE + HALO]
    win_ref[1] = feat_t[:, rows - TILE - HALO :]
    w01_ref[...], w2t_ref[...], w3t_ref[...] = weights
    nb = nbrs[...].astype(F32)
    high = jnp.floor(nb * (1.0 / 256.0))
    ce = cew[...]
    ce_high = ce.astype(BF).astype(F32)
    fields = [high, nb - high * 256.0, ce_high, ce - ce_high]
    fields.append(jnp.zeros((nb.shape[0], 128 - 4 * n2), F32))
    top = jnp.concatenate(fields, axis=1)
    sub = lax.broadcasted_iota(jnp.int32, (8, 128), 0)
    for p in range(peers):
        ext_ref[p, 0:n2, :] = cot[...]
        below = jnp.where(sub == 0, ids[p : p + 1, :], 0.0)
        ext_ref[p, n2 : n2 + 16, :] = jnp.concatenate([top, below], axis=0).astype(BF)


def outer_kernel(
    tile_rows, cap, block_rows, io, need, flush, ins, outs, agg_edge, spread, stage, counts
):
    across, beside, s_in, win, w01, w2t, w3t, pool, spread_in, ext, agg_in, owner = ins
    even = lax.rem(lax.axis_index("nodes"), 2) == 0
    left = jnp.where(even, beside[...], across[...])
    right = jnp.where(even, across[...], beside[...])
    send_ref, agg_ref = outs
    peers, chunk, d = stage.shape
    rows = agg_in.shape[1]
    per = TILE // tile_rows
    io.start(ext, send_ref.at[:, pl.ds(chunk, ext.shape[1]), :])
    inside = pl.ds(TILE, rows - 2 * TILE)
    io.start(agg_in.at[:, inside], agg_ref.at[:, inside])
    spread[...] = spread_in[...]
    for p in range(peers):
        counts[p] = 0
    weights = (w01[...], w2t[...], w3t[...])
    for n in range(2):
        if n == 0:
            window_t = jnp.concatenate([jnp.transpose(left), win[0]], axis=1)
        else:
            window_t = jnp.concatenate([win[1], jnp.transpose(right)], axis=1)
        agg_edge[:, n * TILE : (n + 1) * TILE] = dot(window_t, s_in[n]).astype(BF)
    h_t = jnp.concatenate([win[0, :, :TILE], win[1, :, HALO:]], axis=1)
    fine_out = fine_forward(h_t, agg_edge[...], weights)
    results = [dot_nt(pool[n], fine_out[:, n * TILE : (n + 1) * TILE]) for n in range(2)]
    io.start(agg_edge.at[:, pl.ds(0, TILE)], agg_ref.at[:, pl.ds(0, TILE)])
    io.start(agg_edge.at[:, pl.ds(TILE, TILE)], agg_ref.at[:, pl.ds(rows - TILE, TILE)])
    need()
    for j, t in enumerate(outer_tiles(rows // tile_rows, per)):
        o = owner[t]
        c = counts[o]
        counts[o] = c + 1
        at = pl.ds(pl.multiple_of((o * cap + c) * block_rows, 8), block_rows)
        blocks = results[j // per]
        spread[at, :] = blocks[j % per * block_rows : (j % per + 1) * block_rows, :]
    group = max(1, peers // 4)
    for p in range(peers):
        stage[p] = spread[p * chunk : (p + 1) * chunk, :].astype(BF)
        if p % group == group - 1:
            part = pl.ds(p + 1 - group, group)
            io.start(stage.at[part], send_ref.at[part, pl.ds(0, chunk), :])


def mid_edges(nbrs, ew, s_ref):
    nodes = nbrs.shape[1]
    for c in range(nodes // 128):
        lane = slice(128 * c, 128 * (c + 1))
        idx = nbrs[:, lane]
        weight = merged_weights(idx, ew[:, lane])
        idx = idx.astype(jnp.int16)
        for r in range(nodes // 128):
            s_ref[128 * r : 128 * (r + 1), lane] = edge_columns(idx, weight, 128 * r, 128)


def first_window_kernel(io, need, flush, ins, outs):
    nbrs, ew, w, _ = ins
    smid, w01_ref, w2t_ref, w3t_ref = outs
    need(0, 1)
    mid_edges(nbrs, ew, smid)
    flush(0)
    need()
    w01_ref[...], w2t_ref[...], w3t_ref[...] = forward_weights(w)


def mid_kernel(block_rows, chunk, io, need, flush, ins, outs, blocks, coarse):
    got, smid, w01, w2t, w3t, pool_mid = ins
    send_ref, hid_ref, agg_ref, sel_ref, ext_ref = outs
    peers = got.shape[0]
    nodes = smid.shape[0]
    n2 = pool_mid.shape[0]
    io.start(got.at[:, pl.ds(chunk, n2 + 16), :], ext_ref)
    rows = [got[p, chunk + n2 : chunk + n2 + 16, :].astype(F32)[8:9, :] for p in range(peers)]
    keys = jnp.transpose(jnp.concatenate(rows, axis=0))
    keys = keys * block_rows
    keys = keys + (lax.broadcasted_iota(jnp.int32, keys.shape, 0) % block_rows).astype(F32)
    keys = keys.astype(jnp.int32)
    lane = lax.broadcasted_iota(jnp.int32, (chunk, nodes), 1)
    for p in range(peers):
        sel_ref[p * chunk : (p + 1) * chunk, :] = jnp.where(
            keys[0:chunk, p : p + 1] == lane, 1.0, 0.0
        ).astype(BF)
        blocks[p * chunk : (p + 1) * chunk, :] = got[p, 0:chunk, :]
    flush(3)
    hidden = dot_tn(blocks[...], sel_ref[...]).astype(BF)
    hid_ref[...] = hidden
    need()
    agg = dot(hidden, smid[...]).astype(BF)
    agg_ref[...] = agg
    flush(1, 2)
    middle = silu(dot(w01[...], jnp.concatenate([hidden, agg], axis=0))).astype(BF)
    outer = silu(dot(w2t[...], middle)).astype(BF)
    mid_out = (hidden.astype(F32) + dot(w3t[...], outer)).astype(BF)
    coarse[...] = dot_nt(pool_mid[...], mid_out).astype(BF)
    for p in range(peers):
        io.start(coarse, send_ref.at[p])


def second_window_kernel(io, need, flush, ins, outs, nb_ref, ew_ref):
    ext, hid, agg, mid_cot, w1, w2 = ins
    sco, cot_all, back_ref, w01_ref, w2t_ref, mcot, sl1_ref, sl2_ref = outs
    peers = ext.shape[0]
    n2 = ext.shape[1] - 16
    nodes = peers * n2
    edges = nb_ref.shape[0]
    need()
    for p in range(peers):
        part = ext[p, n2 : n2 + 16, :].astype(F32)[0:edges, :]
        at = slice(p * n2, (p + 1) * n2)
        nb_ref[:, at] = (part[:, 0:n2] * 256.0 + part[:, n2 : 2 * n2]).astype(jnp.int32)
        ew_ref[:, at] = part[:, 2 * n2 : 3 * n2] + part[:, 3 * n2 : 4 * n2]
    cots = jnp.concatenate([ext[p, 0:n2, :] for p in range(peers)], axis=0)
    cot_all[...] = jnp.transpose(cots)
    mcot[...] = jnp.transpose(mid_cot[...])

    def column(c, _):
        lane = pl.ds(pl.multiple_of(c * 128, 128), 128)
        idx = nb_ref[:, lane]
        weight = merged_weights(idx, ew_ref[:, lane])
        idx = idx.astype(jnp.int16)
        for r in range(nodes // 128):
            sco[128 * r : 128 * (r + 1), lane] = edge_columns(idx, weight, 128 * r, 128)
        return 0

    lax.fori_loop(0, nodes // 128, column, 0)
    w01_ref[...], w2t_ref[...], _ = forward_weights(w2)
    back_ref[...] = dot(w2[3], cot_all[...])
    w01, w2t, _ = forward_weights(w1)
    first = dot(w01, jnp.concatenate([hid[...], agg[...]], axis=0))
    s1 = 1.0 / (1.0 + jnp.exp(-first))
    second = dot(w2t, (first * s1).astype(BF))
    s2 = 1.0 / (1.0 + jnp.exp(-second))
    sl1_ref[...] = s1 * (1.0 + first * (1.0 - s1))
    sl2_ref[...] = s2 * (1.0 + second * (1.0 - s2))


def coarse_kernel(io, need, flush, ins, outs):
    got, sco, c01, c2t, cot_all, cot_back, w2, *rest = ins
    cot_my, pool_mid, mcot, w1, msl2, msl1, smid, sel = rest
    send_ref, gmid_ref, sg_ref, fg_ref, cwg_ref = outs
    nodes = got.shape[0]
    n2 = cot_my.shape[0]
    me = lax.axis_index("nodes")
    width = min(TILE, nodes)
    hidden = jnp.transpose(got[...])
    if sco.shape[0] > 512:
        need(1, 2, 3, 4, 5)
    w01, w2t = c01[...], c2t[...]
    mine = pl.ds(pl.multiple_of(me * n2, 16), n2)
    mixed = jnp.zeros((2 * n2, 128), F32)
    grads = [jnp.zeros((128, 128), F32) for _ in range(4)]
    row = lax.broadcasted_iota(jnp.int32, (n2, width), 0) + me * n2
    lane = lax.broadcasted_iota(jnp.int32, (n2, width), 1)
    for i in range(nodes // width):
        cols = slice(i * width, (i + 1) * width)
        h = hidden[:, cols]
        agg = dot(hidden, sco[:, cols]).astype(BF)
        first = dot(w01, jnp.concatenate([h, agg], axis=0))
        s1 = 1.0 / (1.0 + jnp.exp(-first))
        middle = (first * s1).astype(BF)
        second = dot(w2t, middle)
        s2 = 1.0 / (1.0 + jnp.exp(-second))
        outer = (second * s2).astype(BF)
        g = cot_all[:, cols]
        if i == 0:
            need(6)
        sg = (cot_back[:, cols] * (s2 * (1.0 + second * (1.0 - s2)))).astype(BF)
        fg = (dot(w2[2], sg) * (s1 * (1.0 + first * (1.0 - s1)))).astype(BF)
        here = jnp.where(lane + i * width == row, 1.0, 0.0).astype(BF)
        mixed = mixed + dot_nt(jnp.concatenate([here, sco[mine, cols]], axis=0), fg)
        grads = [
            grads[0] + dot_nt(h, fg),
            grads[1] + dot_nt(agg, fg),
            grads[2] + dot_nt(middle, sg),
            grads[3] + dot_nt(outer, g),
        ]
    scale = 1.0 / math.sqrt(nodes)
    for m in range(4):
        cwg_ref[m] = grads[m] * scale
    flush(4)
    need(7, 8, 9, 10, 11, 12)
    mixed = mixed.astype(BF)
    into = jnp.concatenate([mixed[:n2], mixed[n2:]], axis=1)
    back_weights = jnp.concatenate([w2[0], w2[1]], axis=1)
    coarse_grad = (cot_my[...].astype(F32) + dot_nt(into, back_weights)).astype(BF)
    back = dot_tn(coarse_grad, pool_mid[...])
    g = (mcot[...].astype(F32) + back).astype(BF)
    gmid_ref[...] = g
    sg = (dot(w1[3], g) * msl2[...]).astype(BF)
    sg_ref[...] = sg
    fg = (dot(w1[2], sg) * msl1[...]).astype(BF)
    fg_ref[...] = fg
    flush(1, 2, 3)
    spill = dot(w1[1], fg).astype(BF)
    need()
    mid_grad = (g.astype(F32) + dot(w1[0], fg) + dot_nt(spill, smid[...])).astype(BF)
    send_ref[...] = dot_nt(sel[...], mid_grad).astype(BF)


def third_window_kernel(tile_rows, mid_scale, io, need, flush, ins, outs):
    mhid, magg, gmid, msg, mfg, feat, fine_cot, w0, pool, place, agg, w1 = ins
    wg_ref, hid_ref, mid_ref, outer_ref, sl1_ref, sl2_ref, cot_ref, pick_ref, po_ref = outs
    d, rows = hid_ref.shape
    block_rows = pool.shape[0]
    per = TILE // tile_rows
    need()
    w01, w2t, _ = forward_weights(w1)
    middle = silu(dot(w01, jnp.concatenate([mhid[...], magg[...]], axis=0))).astype(BF)
    outer = silu(dot(w2t, middle)).astype(BF)
    wg_ref[0:d, :] = (dot_nt(mhid[...], mfg[...]) * mid_scale).astype(BF)
    wg_ref[d : 2 * d, :] = (dot_nt(magg[...], mfg[...]) * mid_scale).astype(BF)
    wg_ref[2 * d : 3 * d, :] = (dot_nt(middle, msg[...]) * mid_scale).astype(BF)
    wg_ref[3 * d : 4 * d, :] = (dot_nt(outer, gmid[...]) * mid_scale).astype(BF)
    hid_ref[...] = jnp.transpose(feat[...])
    cot_ref[...] = jnp.transpose(fine_cot[...])
    slots = pick_ref.shape[1]
    lane = lax.broadcasted_iota(jnp.int32, (block_rows, slots), 1)
    lane = lane - lax.broadcasted_iota(jnp.int32, (block_rows, slots), 0)
    for t in range(0, rows // tile_rows, 2):
        both = [jnp.where(lane == place[t + j] * block_rows, 1.0, 0.0) for j in range(2)]
        pick_ref[t * block_rows : (t + 2) * block_rows, :] = jnp.concatenate(
            both, axis=0
        ).astype(BF)
    flush(0, 1, 6)
    w01, w2t, _ = forward_weights(w0)
    for i in range(rows // TILE):
        cols = slice(i * TILE, (i + 1) * TILE)
        first = dot(w01, jnp.concatenate([hid_ref[:, cols], agg[:, cols]], axis=0))
        s1 = 1.0 / (1.0 + jnp.exp(-first))
        middle = (first * s1).astype(BF)
        mid_ref[:, cols] = middle
        sl1_ref[:, cols] = s1 * (1.0 + first * (1.0 - s1))
        second = dot(w2t, middle)
        s2 = 1.0 / (1.0 + jnp.exp(-second))
        outer_ref[:, cols] = (second * s2).astype(BF)
        sl2_ref[:, cols] = s2 * (1.0 + second * (1.0 - s2))
        po_ref[i] = pool_matrix(pool[:, cols], tile_rows)


def fine_grad_kernel(scale, io, need, flush, ins, outs, g_ref, fg_ref):
    got, pick, cot, pool, w, slope2, slope1, hid, agg, mid, outer, mid_wg = ins
    send_ref, g_out, fg_out = outs
    d, rows = hid.shape
    if pick.shape[1] > 1024:
        need(1)
    blocks = dot(pick[...], got[...]).astype(BF)
    need(2, 3)
    per = pool.shape[1]
    for i in range(rows // TILE):
        cols = slice(i * TILE, (i + 1) * TILE)
        back = dot_tn(blocks[i * per : (i + 1) * per, :], pool[i])
        g_ref[:, cols] = (cot[:, cols].astype(F32) + back).astype(BF)
    io.start(g_ref, g_out)
    g = g_ref[...]
    need(4, 5, 6)
    sg = (dot(w[3], g) * slope2[...]).astype(BF)
    fg = (dot(w[2], sg) * slope1[...]).astype(BF)
    fg_ref[...] = fg
    io.start(fg_ref, fg_out)
    need()
    send_ref[4 * d : 8 * d, :] = mid_wg[...]
    for m, (a, b) in enumerate(
        ((hid[...], fg), (agg[...], fg), (mid[...], sg), (outer[...], g))
    ):
        send_ref[m * d : (m + 1) * d, :] = (dot_nt(a, b) * scale).astype(BF)


def fine_spread_kernel(io, need, flush, ins, outs, s_ref, total):
    off, ew, w, g, fg = ins
    rim_near, rim_far, out_ref = outs
    rows = g.shape[1]
    clear_corners(s_ref.at[0])
    clear_corners(s_ref.at[1])
    total[...] = jnp.zeros(total.shape, F32)
    need()
    for i in range(rows // TILE):
        cols = slice(i * TILE, (i + 1) * TILE)
        s = s_ref.at[i % 2]
        fine_edges(off[:, cols], ew[:, cols], s)
        fg_tile = fg[:, cols]
        direct = g[:, cols].astype(F32) + dot(w[0], fg_tile)
        spill = dot(w[1], fg_tile).astype(BF)
        window = slice(i * TILE, (i + 1) * TILE + 2 * HALO)
        total[window, :] = total[window, :] + dot_nt(s[...], spill)
        here = slice(HALO + i * TILE, HALO + (i + 1) * TILE)
        total[here, :] = total[here, :] + jnp.transpose(direct)
    even = lax.rem(lax.axis_index("nodes"), 2) == 0
    low, high = total[:HALO, :].astype(BF), total[HALO + rows :, :].astype(BF)
    rim_near[...] = jnp.where(even, high, low)
    rim_far[...] = jnp.where(even, low, high)
    out_ref[...] = total[HALO : HALO + rows, :]


def sum_kernel(io, need, flush, ins, outs, part):
    got, _ = ins
    send_ref = outs[0]
    peers = got.shape[0]
    need()
    part[...] = sum(got[p].astype(F32) for p in range(peers)).astype(BF)
    for p in range(peers):
        io.start(part, send_ref.at[p])


def join_kernel(io, need, flush, ins, outs):
    total, across, beside, coarse = ins
    out_ref, wg_ref = outs
    even = lax.rem(lax.axis_index("nodes"), 2) == 0
    from_left = jnp.where(even, beside[...], across[...])
    from_right = jnp.where(even, across[...], beside[...])
    rows = total.shape[0]
    need()
    io.start(coarse, wg_ref.at[pl.ds(8, 4)])
    out_ref[:HALO, :] = (total[:HALO, :] + from_left.astype(F32)).astype(BF)
    out_ref[HALO : rows - HALO, :] = total[HALO : rows - HALO, :].astype(BF)
    out_ref[rows - HALO :, :] = (total[rows - HALO :, :] + from_right.astype(F32)).astype(BF)


def gather_kernel(io, need, flush, ins, outs, wide):
    summed, _ = ins
    out_ref = outs[0]
    for half in range(2):
        wide[4 * half : 4 * half + 4] = summed[4 * half : 4 * half + 4].astype(F32)
        part = pl.ds(4 * half, 4)
        io.start(wide.at[part], out_ref.at[part])


def exchange(x):
    return lax.all_to_all(x, "nodes", split_axis=0, concat_axis=0, tiled=True)


def per_device(
    features,
    fine_cotangent,
    mid_cotangent,
    coarse_cotangent,
    weights,
    fine_offsets,
    fine_edge_w,
    pool_fine,
    owner_dev,
    coarse_slot,
    mid_nbrs,
    mid_edge_w,
    pool_mid,
    coarse_nbrs,
    coarse_edge_w,
):
    n, d = features.shape
    tile_count = owner_dev.shape[0]
    tile_rows = n // tile_count
    block_rows = pool_fine.shape[0]
    n1 = mid_cotangent.shape[0]
    n2 = coarse_cotangent.shape[0]
    edges = fine_offsets.shape[0]
    peers = lax.axis_size("nodes")
    cap = max(2, 2 * tile_count // peers)
    chunk = cap * block_rows
    window = TILE + 2 * HALO
    per = TILE // tile_rows * block_rows
    ends = peers - 1
    inside_pairs = [(i, i ^ 1) for i in range(peers)]
    between_pairs = [(i, ((i + 1) ^ 1) - 1) for i in range(1, ends)]
    total2 = peers * n2

    odd = lax.rem(lax.axis_index("nodes"), 2)
    near = lax.dynamic_slice_in_dim(features, (1 - odd) * (n - HALO), HALO, 0)
    far = lax.dynamic_slice_in_dim(features, odd * (n - HALO), HALO, 0)
    across = lax.ppermute(near, "nodes", inside_pairs)
    beside = lax.ppermute(far, "nodes", between_pairs)
    owners = owner_dev.reshape(-1)
    s_out, win, w01, w2t, w3t, pool_out, spread, ext, agg_in, place = call(
        functools.partial(inner_kernel, tile_rows, peers, cap),
        [
            (fine_offsets, "h"), (fine_edge_w, "h"), (features, "h"), (weights, "0"),
            (pool_fine, "h"), (owners, "s"), (coarse_slot, "s"), (coarse_nbrs, "h"),
            (coarse_edge_w, "h"), (coarse_cotangent, "h"),
        ],
        [
            (shape((2, window, TILE)), "v"), (shape((2, d, TILE + HALO)), "v"),
            (shape((d, 2 * d)), "v"), (shape((d, d)), "v"), (shape((d, d)), "v"),
            (shape((2, per, TILE)), "v"), (shape((peers * chunk, d), F32), "v"),
            (shape((peers, n2 + 16, d)), "v"), (shape((d, n)), "v"),
            (shape((tile_count,), jnp.int32), "s"),
        ],
        scratch=(
            pltpu.VMEM((d, n), BF),
            pltpu.VMEM((n // TILE - 2, window, TILE), BF),
            pltpu.VMEM((peers, 128), F32),
            pltpu.SMEM((peers,), jnp.int32),
        ),
        us=6,
    )
    send1, agg = call(
        functools.partial(outer_kernel, tile_rows, cap, block_rows),
        [
            (across, "v"), (beside, "v"), (s_out, "v"), (win, "v"), (w01, "v"), (w2t, "v"),
            (w3t, "v"), (pool_out, "v"), (spread, "v"), (ext, "v"), (agg_in, "v"), (owners, "s"),
        ],
        [(shape((peers, chunk + n2 + 16, d)), "r"), (shape((d, n)), "r")],
        scratch=(
            pltpu.VMEM((d, 2 * TILE), BF),
            pltpu.VMEM((peers * chunk, d), F32),
            pltpu.VMEM((peers, chunk, d), BF),
            pltpu.SMEM((peers,), jnp.int32),
        ),
        copies=8,
        us=3,
    )
    got1 = exchange(send1)
    smid, m01, m2t, m3t = call(
        first_window_kernel,
        [(mid_nbrs, "h"), (mid_edge_w, "h"), (weights, "1"), (agg, "r")],
        [
            (shape((n1, n1)), "h"), (shape((d, 2 * d)), "h"), (shape((d, d)), "h"),
            (shape((d, d)), "h"),
        ],
        us=6,
    )
    send2, mhid, magg, sel, ext = call(
        functools.partial(mid_kernel, block_rows, chunk),
        [(got1, "v"), (smid, "h"), (m01, "h"), (m2t, "h"), (m3t, "h"), (pool_mid, "h")],
        [
            (shape((peers, n2, d)), "r"), (shape((d, n1)), "h"), (shape((d, n1)), "h"),
            (shape((peers * chunk, n1)), "h"), (shape((peers, n2 + 16, d)), "r"),
        ],
        scratch=(pltpu.VMEM((peers * chunk, d), BF), pltpu.VMEM((n2, d), BF)),
        copies=peers + 1,
        us=3,
    )
    got2 = exchange(send2)
    near = "v" if total2 <= 512 else "h"
    sco, cot_all, cot_back, c01, c2t, mcot, mslope1, mslope2 = call(
        second_window_kernel,
        [
            (ext, "h"), (mhid, "h"), (magg, "h"), (mid_cotangent, "h"), (weights, "1"),
            (weights, "2"),
        ],
        [
            (shape((total2, total2)), near), (shape((d, total2)), near),
            (shape((d, total2), F32), near), (shape((d, 2 * d)), near), (shape((d, d)), near),
            (shape((d, n1)), "h"),
            (shape((d, n1), F32), "h"), (shape((d, n1), F32), "h"),
        ],
        scratch=(pltpu.VMEM((edges, total2), jnp.int32), pltpu.VMEM((edges, total2), F32)),
        us=6,
    )
    send3, gmid, msg, mfg, coarse_wg = call(
        coarse_kernel,
        [
            (got2.reshape(total2, d), "v"), (sco, near), (c01, near), (c2t, near),
            (cot_all, near), (cot_back, near), (weights, "2"),
            (coarse_cotangent, "h"), (pool_mid, "h"), (mcot, "h"), (weights, "1"),
            (mslope2, "h"), (mslope1, "h"), (smid, "h"), (sel, "h"),
        ],
        [
            (shape((peers * chunk, d)), "h"), (shape((d, n1)), "h"), (shape((d, n1)), "h"),
            (shape((d, n1)), "h"), (shape((4, d, d), F32), "h"),
        ],
        us=3,
    )
    got3 = exchange(send3.reshape(peers, chunk, d))
    pick_kind = "v" if peers * chunk <= 1024 else "h"
    mid_wg, hid, mid, outer, slope1, slope2, cot, pick, pool_b = call(
        functools.partial(third_window_kernel, tile_rows, 1.0 / math.sqrt(n1 * peers)),
        [
            (mhid, "h"), (magg, "h"), (gmid, "h"), (msg, "h"), (mfg, "h"), (features, "h"),
            (fine_cotangent, "h"), (weights, "0"), (pool_fine, "h"), (place, "s"), (agg, "h"),
            (weights, "1"),
        ],
        [
            (shape((4 * d, d)), "h"), (shape((d, n)), "h"), (shape((d, n)), "h"),
            (shape((d, n)), "h"), (shape((d, n), F32), "h"), (shape((d, n), F32), "h"),
            (shape((d, n)), "h"), (shape((tile_count * block_rows, peers * chunk)), pick_kind),
            (shape((n // TILE, per, TILE)), "h"),
        ],
        us=6,
    )
    send4, g, fg = call(
        functools.partial(fine_grad_kernel, 1.0 / math.sqrt(n * peers)),
        [
            (got3.reshape(peers * chunk, d), "v"), (pick, pick_kind), (cot, "h"), (pool_b, "h"),
            (weights, "0"), (slope2, "h"), (slope1, "h"), (hid, "h"), (agg, "h"), (mid, "h"),
            (outer, "h"), (mid_wg, "h"),
        ],
        [(shape((8 * d, d)), "h"), (shape((d, n)), "r"), (shape((d, n)), "r")],
        scratch=(pltpu.VMEM((d, n), BF), pltpu.VMEM((d, n), BF)),
        copies=2,
        us=4,
    )
    got4 = exchange(send4.reshape(peers, 8 * d // peers, d))
    rim_near, rim_far, spread = call(
        fine_spread_kernel,
        [(fine_offsets, "h"), (fine_edge_w, "h"), (weights, "0"), (g, "h"), (fg, "h")],
        [(shape((HALO, d)), "h"), (shape((HALO, d)), "h"), (shape((n, d), F32), "h")],
        scratch=(pltpu.VMEM((2, window, TILE), BF), pltpu.VMEM((n + 2 * HALO, d), F32)),
        us=6,
    )
    (send5,) = call(
        sum_kernel,
        [(got4, "v"), (rim_near, "r")],
        [(shape((peers, 8 * d // peers, d)), "r")],
        scratch=(pltpu.VMEM((8 * d // peers, d), BF),),
        copies=peers,
        us=1,
    )
    got5 = exchange(send5)
    from_across = lax.ppermute(rim_near, "nodes", inside_pairs)
    from_beside = lax.ppermute(rim_far, "nodes", between_pairs)
    feature_grads, weight_grads = call(
        join_kernel,
        [(spread, "h"), (from_across, "v"), (from_beside, "v"), (coarse_wg, "h")],
        [(shape((n, d)), "h"), (shape((12, d, d), F32), "r")],
        copies=1,
        us=1,
    )
    (weight_grads,) = call(
        gather_kernel,
        [(got5.reshape(8, d, d), "v"), (weight_grads, "r")],
        [(shape((12, d, d), F32), "r")],
        scratch=(pltpu.VMEM((8, d, d), F32),),
        copies=2,
        aliases={1: 0},
        us=1,
    )
    weight_grads = weight_grads.reshape(3, 4, d, d)
    return (feature_grads, weight_grads)


def solution(mesh):
    rows = P(("groups", "nodes"), None)
    cols = P("groups", "nodes")
    in_specs = (
        rows, rows, rows, rows, P(), cols, cols, cols, rows, P(("groups", "nodes")),
        cols, cols, rows, cols, cols,
    )
    out_specs = (rows, P("groups", None, None, None))
    return jax.shard_map(
        per_device, mesh=mesh, in_specs=in_specs, out_specs=out_specs, check_vma=False
    )
```

```python
import functools
import math

import jax
import jax.numpy as jnp
from jax import lax
from jax.experimental import pallas as pl
from jax.experimental.pallas import tpu as pltpu
from jax.sharding import PartitionSpec as P

HALO = 256
TILE = 256
WIDE = 2048
BF = jnp.bfloat16
F32 = jnp.float32

VM = pl.BlockSpec(memory_space=pltpu.VMEM)
HB = pl.BlockSpec(memory_space=pltpu.HBM)


def dot(a, b):
    return jnp.dot(a, b, preferred_element_type=F32)


def dot_nt(a, b):
    return lax.dot_general(a, b, (((1,), (1,)), ((), ())), preferred_element_type=F32)


def dot_tn(a, b):
    return lax.dot_general(a, b, (((0,), (0,)), ((), ())), preferred_element_type=F32)


def silu(v):
    return v / (1.0 + jnp.exp(-v))


def silu_slope(v):
    s = 1.0 / (1.0 + jnp.exp(-v))
    return s * (1.0 + v * (1.0 - s))


def merged_weights(idx, ew):
    total = ew
    for r in range(1, idx.shape[0]):
        total = total + jnp.where(pltpu.roll(idx, r, 0) == idx, pltpu.roll(ew, r, 0), 0.0)
    return total.astype(BF)


def edge_columns(idx, ew, start, rows):
    count = idx.shape[0]
    lanes = idx.shape[1]
    position = lax.broadcasted_iota(jnp.int32, (rows, lanes), 0) + start
    position = position.astype(jnp.int16)
    picked = jnp.zeros((rows, lanes), BF)
    for k in range(count):
        picked = jnp.where(idx[k : k + 1, :] == position, ew[k : k + 1, :], picked)
    return picked


def fine_edges(off, ew, s_ref):
    for h in range(TILE // 128):
        lane = slice(128 * h, 128 * (h + 1))
        o = off[:, lane]
        weight = merged_weights(o, ew[:, lane])
        rel = o + lax.broadcasted_iota(jnp.int32, o.shape, 1) + HALO
        rel = rel.astype(jnp.int16)
        for c in range(2 * HALO // 128 + 1):
            s_ref[128 * (h + c) : 128 * (h + c + 1), lane] = edge_columns(
                rel, weight, 128 * c, 128
            )


def clear_corners(s_ref):
    for h in range(TILE // 128):
        lane = slice(128 * h, 128 * (h + 1))
        if h > 0:
            s_ref[: 128 * h, lane] = jnp.zeros((128 * h, 128), BF)
        last = 128 * h + 2 * HALO + 128
        if last < TILE + 2 * HALO:
            s_ref[last:, lane] = jnp.zeros((TILE + 2 * HALO - last, 128), BF)


def forward_weights(w):
    w01 = jnp.concatenate([jnp.transpose(w[0]), jnp.transpose(w[1])], axis=1)
    return w01, jnp.transpose(w[2]), jnp.transpose(w[3])


def pool_matrix(pool, tile_rows):
    lane = lax.broadcasted_iota(jnp.int32, pool.shape, 1) // tile_rows
    values = pool.astype(F32)
    parts = [jnp.where(lane == r, values, 0.0) for r in range(pool.shape[1] // tile_rows)]
    return jnp.concatenate(parts, axis=0).astype(BF)


class Copies:
    def __init__(self, sems):
        self.sems = sems
        self.used = 0
        self.open = {}

    def start(self, source, target):
        copy = pltpu.make_async_copy(source, target, self.sems.at[self.used])
        self.used += 1
        copy.start()
        self.open[id(copy)] = copy
        return copy

    def wait(self, *copies):
        for copy in copies:
            if id(copy) in self.open:
                copy.wait()
                del self.open[id(copy)]

    def finish(self):
        self.wait(*list(self.open.values()))


def shape(dims, dtype=BF):
    return jax.ShapeDtypeStruct(dims, dtype)


def call(kernel, ins, outs, scratch=(), copies=0, us=3, mib=24, aliases={}):
    n_in, n_out = len(ins), len(outs)
    staged_in = [i for i, (_, kind) in enumerate(ins) if kind in "hs012"]
    staged_out = [i for i, (_, kind) in enumerate(outs) if kind in "hs"]
    spaces = {"h": pltpu.VMEM, "s": pltpu.SMEM}
    stage = []
    for i in staged_in:
        array, kind = ins[i]
        dims = array.shape[1:] if kind.isdigit() else array.shape
        stage.append(spaces.get(kind, pltpu.VMEM)(dims, array.dtype))
    stage += [spaces[outs[i][1]](outs[i][0].shape, outs[i][0].dtype) for i in staged_out]
    total = len(staged_in) + len(staged_out) + copies

    def body(*refs):
        in_refs, out_refs = list(refs[:n_in]), list(refs[n_in : n_in + n_out])
        rest = list(refs[n_in + n_out :])
        sems = rest.pop() if total else None
        stages, user = rest[: len(stage)], rest[len(stage) :]
        io = Copies(sems)
        pending = {}
        for i, ref in zip(staged_in, stages):
            kind = ins[i][1]
            source = in_refs[i].at[int(kind)] if kind.isdigit() else in_refs[i]
            pending[i] = io.start(source, ref)
            in_refs[i] = ref
        targets = {}
        for i, ref in zip(staged_out, stages[len(staged_in) :]):
            targets[i] = out_refs[i]
            out_refs[i] = ref

        def need(*which):
            io.wait(*[pending[i] for i in which or pending])

        def flush(*which):
            for i in which:
                io.start(out_refs[i], targets.pop(i))

        kernel(io, need, flush, in_refs, out_refs, *user)
        flush(*list(targets))
        io.finish()

    return pl.pallas_call(
        body,
        out_shape=[
            s if kind == "v" else pltpu.HBM(s.shape, s.dtype) for s, kind in outs
        ],
        in_specs=[VM if kind == "v" else HB for _, kind in ins],
        out_specs=[VM if kind == "v" else HB for _, kind in outs],
        scratch_shapes=stage
        + list(scratch)
        + ([pltpu.SemaphoreType.DMA((total,))] if total else []),
        input_output_aliases=aliases,
        compiler_params=pltpu.CompilerParams(vmem_limit_bytes=mib << 20),
        cost_estimate=pl.CostEstimate(
            flops=0, bytes_accessed=int(us * 3_000_000), transcendentals=0
        ),
    )(*[
        a if kind == "v" else pltpu.with_memory_space_constraint(a, pltpu.HBM)
        for a, kind in ins
    ])


def fine_forward(h_t, agg, weights):
    w01, w2t, w3t = weights
    first = dot(w01, jnp.concatenate([h_t, agg], axis=0))
    middle = silu(first).astype(BF)
    second = dot(w2t, middle)
    outer = silu(second).astype(BF)
    return (h_t.astype(F32) + dot(w3t, outer)).astype(BF)


def outer_tiles(tile_count, per):
    return list(range(per)) + list(range(tile_count - per, tile_count))


def inner_kernel(tile_rows, peers, cap, io, need, flush, ins, outs, feat_t, s_ref, ids, counts):
    off, ew, feat, w, pool, owner, slot, nbrs, cew, cot = ins
    so_ref, win_ref, w01_ref, w2t_ref, w3t_ref, po_ref, spread, ext_ref, agg_ref, place = outs
    rows, d = feat.shape
    block_rows = pool.shape[0]
    n2 = cot.shape[0]
    tiles = rows // TILE
    per = TILE // tile_rows
    tile_count = rows // tile_rows
    for i in range(tiles - 2):
        clear_corners(s_ref.at[i])
    clear_corners(so_ref.at[0])
    clear_corners(so_ref.at[1])
    spread[...] = jnp.zeros(spread.shape, F32)
    ids[...] = jnp.full(ids.shape, -1.0, F32)
    for p in range(peers):
        counts[p] = 0
    need(5, 6)
    lane_slot = lax.broadcasted_iota(jnp.int32, (1, 128), 1) // block_rows
    first_tiles = outer_tiles(tile_count, per)
    for t in first_tiles + [t for t in range(tile_count) if t not in first_tiles]:
        o = owner[t]
        c = counts[o]
        counts[o] = c + 1
        place[t] = o * cap + c
        row = ids[pl.ds(o, 1), :]
        ids[pl.ds(o, 1), :] = jnp.where(lane_slot == c, slot[t].astype(F32), row)
    flush(9)
    need(0, 1)
    for n, i in enumerate((0, tiles - 1)):
        cols = slice(i * TILE, (i + 1) * TILE)
        fine_edges(off[:, cols], ew[:, cols], so_ref.at[n])
    need()
    feat_t[...] = jnp.transpose(feat[...])
    weights = forward_weights(w)
    for i in range(1, tiles - 1):
        cols = slice(i * TILE, (i + 1) * TILE)
        fine_edges(off[:, cols], ew[:, cols], s_ref.at[i - 1])
        around = feat_t[:, i * TILE - HALO : (i + 1) * TILE + HALO]
        agg_ref[:, cols] = dot(around, s_ref[i - 1]).astype(BF)
    for start in range(TILE, rows - TILE, WIDE):
        stop = min(start + WIDE, rows - TILE)
        cols = slice(start, stop)
        fine_out = fine_forward(feat_t[:, cols], agg_ref[:, cols], weights)
        for i in range(start // TILE, stop // TILE):
            at = slice(i * TILE - start, (i + 1) * TILE - start)
            matrix = pool_matrix(pool[:, i * TILE : (i + 1) * TILE], tile_rows)
            blocks = dot_nt(matrix, fine_out[:, at])
            for j in range(per):
                at = pl.ds(pl.multiple_of(place[i * per + j] * block_rows, 8), block_rows)
                spread[at, :] = blocks[j * block_rows : (j + 1) * block_rows, :]
    for n, i in enumerate((0, tiles - 1)):
        po_ref[n] = pool_matrix(pool[:, i * TILE : (i + 1) * TILE], tile_rows)
    win_ref[0] = feat_t[:, : TILE + HALO]
    win_ref[1] = feat_t[:, rows - TILE - HALO :]
    w01_ref[...], w2t_ref[...], w3t_ref[...] = weights
    nb = nbrs[...].astype(F32)
    high = jnp.floor(nb * (1.0 / 256.0))
    ce = cew[...]
    ce_high = ce.astype(BF).astype(F32)
    fields = [high, nb - high * 256.0, ce_high, ce - ce_high]
    fields.append(jnp.zeros((nb.shape[0], 128 - 4 * n2), F32))
    top = jnp.concatenate(fields, axis=1)
    sub = lax.broadcasted_iota(jnp.int32, (8, 128), 0)
    for p in range(peers):
        ext_ref[p, 0:n2, :] = cot[...]
        below = jnp.where(sub == 0, ids[p : p + 1, :], 0.0)
        ext_ref[p, n2 : n2 + 16, :] = jnp.concatenate([top, below], axis=0).astype(BF)


def outer_kernel(
    tile_rows, cap, block_rows, io, need, flush, ins, outs, agg_edge, spread, stage, counts
):
    across, beside, s_in, win, w01, w2t, w3t, pool, spread_in, ext, agg_in, owner = ins
    even = lax.rem(lax.axis_index("nodes"), 2) == 0
    left = jnp.where(even, beside[...], across[...])
    right = jnp.where(even, across[...], beside[...])
    send_ref, agg_ref = outs
    peers, chunk, d = stage.shape
    rows = agg_in.shape[1]
    per = TILE // tile_rows
    io.start(ext, send_ref.at[:, pl.ds(chunk, ext.shape[1]), :])
    inside = pl.ds(TILE, rows - 2 * TILE)
    io.start(agg_in.at[:, inside], agg_ref.at[:, inside])
    spread[...] = spread_in[...]
    for p in range(peers):
        counts[p] = 0
    weights = (w01[...], w2t[...], w3t[...])
    for n in range(2):
        if n == 0:
            window_t = jnp.concatenate([jnp.transpose(left), win[0]], axis=1)
        else:
            window_t = jnp.concatenate([win[1], jnp.transpose(right)], axis=1)
        agg_edge[:, n * TILE : (n + 1) * TILE] = dot(window_t, s_in[n]).astype(BF)
    h_t = jnp.concatenate([win[0, :, :TILE], win[1, :, HALO:]], axis=1)
    fine_out = fine_forward(h_t, agg_edge[...], weights)
    results = [dot_nt(pool[n], fine_out[:, n * TILE : (n + 1) * TILE]) for n in range(2)]
    io.start(agg_edge.at[:, pl.ds(0, TILE)], agg_ref.at[:, pl.ds(0, TILE)])
    io.start(agg_edge.at[:, pl.ds(TILE, TILE)], agg_ref.at[:, pl.ds(rows - TILE, TILE)])
    need()
    for j, t in enumerate(outer_tiles(rows // tile_rows, per)):
        o = owner[t]
        c = counts[o]
        counts[o] = c + 1
        at = pl.ds(pl.multiple_of((o * cap + c) * block_rows, 8), block_rows)
        blocks = results[j // per]
        spread[at, :] = blocks[j % per * block_rows : (j % per + 1) * block_rows, :]
    group = max(1, peers // 4)
    for p in range(peers):
        stage[p] = spread[p * chunk : (p + 1) * chunk, :].astype(BF)
        if p % group == group - 1:
            part = pl.ds(p + 1 - group, group)
            io.start(stage.at[part], send_ref.at[part, pl.ds(0, chunk), :])


def mid_edges(nbrs, ew, s_ref):
    nodes = nbrs.shape[1]
    for c in range(nodes // 128):
        lane = slice(128 * c, 128 * (c + 1))
        idx = nbrs[:, lane]
        weight = merged_weights(idx, ew[:, lane])
        idx = idx.astype(jnp.int16)
        for r in range(nodes // 128):
            s_ref[128 * r : 128 * (r + 1), lane] = edge_columns(idx, weight, 128 * r, 128)


def first_window_kernel(io, need, flush, ins, outs):
    nbrs, ew, w, _ = ins
    smid, w01_ref, w2t_ref, w3t_ref = outs
    need(0, 1)
    mid_edges(nbrs, ew, smid)
    flush(0)
    need()
    w01_ref[...], w2t_ref[...], w3t_ref[...] = forward_weights(w)


def mid_kernel(block_rows, chunk, io, need, flush, ins, outs, blocks, coarse):
    got, smid, w01, w2t, w3t, pool_mid, _ = ins
    send_ref, hid_ref, agg_ref, sel_ref, ext_ref = outs
    peers = got.shape[0]
    nodes = smid.shape[0]
    n2 = pool_mid.shape[0]
    io.start(got.at[:, pl.ds(chunk, n2 + 16), :], ext_ref)
    rows = [got[p, chunk + n2 : chunk + n2 + 16, :].astype(F32)[8:9, :] for p in range(peers)]
    keys = jnp.transpose(jnp.concatenate(rows, axis=0))
    keys = keys * block_rows
    keys = keys + (lax.broadcasted_iota(jnp.int32, keys.shape, 0) % block_rows).astype(F32)
    keys = keys.astype(jnp.int32)
    lane = lax.broadcasted_iota(jnp.int32, (chunk, nodes), 1)
    for p in range(peers):
        sel_ref[p * chunk : (p + 1) * chunk, :] = jnp.where(
            keys[0:chunk, p : p + 1] == lane, 1.0, 0.0
        ).astype(BF)
        blocks[p * chunk : (p + 1) * chunk, :] = got[p, 0:chunk, :]
    flush(3)
    hidden = dot_tn(blocks[...], sel_ref[...]).astype(BF)
    hid_ref[...] = hidden
    need()
    agg = dot(hidden, smid[...]).astype(BF)
    agg_ref[...] = agg
    flush(1, 2)
    middle = silu(dot(w01[...], jnp.concatenate([hidden, agg], axis=0))).astype(BF)
    outer = silu(dot(w2t[...], middle)).astype(BF)
    mid_out = (hidden.astype(F32) + dot(w3t[...], outer)).astype(BF)
    coarse[...] = dot_nt(pool_mid[...], mid_out).astype(BF)
    for p in range(peers):
        io.start(coarse, send_ref.at[p])


def second_window_kernel(io, need, flush, ins, outs, nb_ref, ew_ref):
    ext, hid, agg, mid_cot, w1, w2 = ins
    sco, cot_all, back_ref, w01_ref, w2t_ref, mcot, sl1_ref, sl2_ref = outs
    peers = ext.shape[0]
    n2 = ext.shape[1] - 16
    nodes = peers * n2
    edges = nb_ref.shape[0]
    need()
    for p in range(peers):
        part = ext[p, n2 : n2 + 16, :].astype(F32)[0:edges, :]
        at = slice(p * n2, (p + 1) * n2)
        nb_ref[:, at] = (part[:, 0:n2] * 256.0 + part[:, n2 : 2 * n2]).astype(jnp.int32)
        ew_ref[:, at] = part[:, 2 * n2 : 3 * n2] + part[:, 3 * n2 : 4 * n2]
    cots = jnp.concatenate([ext[p, 0:n2, :] for p in range(peers)], axis=0)
    cot_all[...] = jnp.transpose(cots)
    mcot[...] = jnp.transpose(mid_cot[...])

    def column(c, _):
        lane = pl.ds(pl.multiple_of(c * 128, 128), 128)
        idx = nb_ref[:, lane]
        weight = merged_weights(idx, ew_ref[:, lane])
        idx = idx.astype(jnp.int16)
        for r in range(nodes // 128):
            sco[128 * r : 128 * (r + 1), lane] = edge_columns(idx, weight, 128 * r, 128)
        return 0

    lax.fori_loop(0, nodes // 128, column, 0)
    w01_ref[...], w2t_ref[...], _ = forward_weights(w2)
    back_ref[...] = dot(w2[3], cot_all[...])
    w01, w2t, _ = forward_weights(w1)
    first = dot(w01, jnp.concatenate([hid[...], agg[...]], axis=0))
    s1 = 1.0 / (1.0 + jnp.exp(-first))
    second = dot(w2t, (first * s1).astype(BF))
    s2 = 1.0 / (1.0 + jnp.exp(-second))
    sl1_ref[...] = s1 * (1.0 + first * (1.0 - s1))
    sl2_ref[...] = s2 * (1.0 + second * (1.0 - s2))


def coarse_kernel(io, need, flush, ins, outs):
    got, sco, c01, c2t, cot_all, cot_back, w2, *rest = ins
    cot_my, pool_mid, mcot, w1, msl2, msl1, smid, sel = rest
    send_ref, gmid_ref, sg_ref, fg_ref, cwg_ref = outs
    nodes = got.shape[0]
    n2 = cot_my.shape[0]
    me = lax.axis_index("nodes")
    width = min(TILE, nodes)
    hidden = jnp.transpose(got[...])
    if sco.shape[0] > 512:
        need(1, 2, 3, 4, 5)
    w01, w2t = c01[...], c2t[...]
    mine = pl.ds(pl.multiple_of(me * n2, 16), n2)
    mixed = jnp.zeros((2 * n2, 128), F32)
    grads = [jnp.zeros((128, 128), F32) for _ in range(4)]
    row = lax.broadcasted_iota(jnp.int32, (n2, width), 0) + me * n2
    lane = lax.broadcasted_iota(jnp.int32, (n2, width), 1)
    for i in range(nodes // width):
        cols = slice(i * width, (i + 1) * width)
        h = hidden[:, cols]
        agg = dot(hidden, sco[:, cols]).astype(BF)
        first = dot(w01, jnp.concatenate([h, agg], axis=0))
        s1 = 1.0 / (1.0 + jnp.exp(-first))
        middle = (first * s1).astype(BF)
        second = dot(w2t, middle)
        s2 = 1.0 / (1.0 + jnp.exp(-second))
        outer = (second * s2).astype(BF)
        g = cot_all[:, cols]
        if i == 0:
            need(6)
        sg = (cot_back[:, cols] * (s2 * (1.0 + second * (1.0 - s2)))).astype(BF)
        fg = (dot(w2[2], sg) * (s1 * (1.0 + first * (1.0 - s1)))).astype(BF)
        here = jnp.where(lane + i * width == row, 1.0, 0.0).astype(BF)
        mixed = mixed + dot_nt(jnp.concatenate([here, sco[mine, cols]], axis=0), fg)
        grads = [
            grads[0] + dot_nt(h, fg),
            grads[1] + dot_nt(agg, fg),
            grads[2] + dot_nt(middle, sg),
            grads[3] + dot_nt(outer, g),
        ]
    scale = 1.0 / math.sqrt(nodes)
    for m in range(4):
        cwg_ref[m] = grads[m] * scale
    flush(4)
    need(7, 8, 9, 10, 11, 12)
    mixed = mixed.astype(BF)
    into = jnp.concatenate([mixed[:n2], mixed[n2:]], axis=1)
    back_weights = jnp.concatenate([w2[0], w2[1]], axis=1)
    coarse_grad = (cot_my[...].astype(F32) + dot_nt(into, back_weights)).astype(BF)
    back = dot_tn(coarse_grad, pool_mid[...])
    g = (mcot[...].astype(F32) + back).astype(BF)
    gmid_ref[...] = g
    sg = (dot(w1[3], g) * msl2[...]).astype(BF)
    sg_ref[...] = sg
    fg = (dot(w1[2], sg) * msl1[...]).astype(BF)
    fg_ref[...] = fg
    flush(1, 2, 3)
    spill = dot(w1[1], fg).astype(BF)
    need()
    mid_grad = (g.astype(F32) + dot(w1[0], fg) + dot_nt(spill, smid[...])).astype(BF)
    send_ref[...] = dot_nt(sel[...], mid_grad).astype(BF)


def saved_kernel(tile_rows, io, need, flush, ins, outs):
    feat, agg, w, fine_cot, pool, _ = ins
    hid_ref, mid_ref, outer_ref, sl1_ref, sl2_ref, cot_ref, po_ref = outs
    rows = feat.shape[0]
    need(0, 1, 2)
    hid_ref[...] = jnp.transpose(feat[...])
    flush(0)
    w01, w2t, _ = forward_weights(w)
    for start in range(0, rows, 512):
        cols = slice(start, min(start + 512, rows))
        first = dot(w01, jnp.concatenate([hid_ref[:, cols], agg[:, cols]], axis=0))
        s1 = 1.0 / (1.0 + jnp.exp(-first))
        middle = (first * s1).astype(BF)
        mid_ref[:, cols] = middle
        sl1_ref[:, cols] = s1 * (1.0 + first * (1.0 - s1))
        second = dot(w2t, middle)
        s2 = 1.0 / (1.0 + jnp.exp(-second))
        outer_ref[:, cols] = (second * s2).astype(BF)
        sl2_ref[:, cols] = s2 * (1.0 + second * (1.0 - s2))
    need()
    cot_ref[...] = jnp.transpose(fine_cot[...])
    for i in range(rows // TILE):
        po_ref[i] = pool_matrix(pool[:, i * TILE : (i + 1) * TILE], tile_rows)


def third_window_kernel(mid_scale, io, need, flush, ins, outs):
    mhid, magg, gmid, msg, mfg, w1, place = ins
    wg_ref, pick_ref = outs
    d = mhid.shape[0]
    block_rows = pick_ref.shape[0] // place.shape[0]
    need()
    w01, w2t, _ = forward_weights(w1)
    middle = silu(dot(w01, jnp.concatenate([mhid[...], magg[...]], axis=0))).astype(BF)
    outer = silu(dot(w2t, middle)).astype(BF)
    wg_ref[0:d, :] = (dot_nt(mhid[...], mfg[...]) * mid_scale).astype(BF)
    wg_ref[d : 2 * d, :] = (dot_nt(magg[...], mfg[...]) * mid_scale).astype(BF)
    wg_ref[2 * d : 3 * d, :] = (dot_nt(middle, msg[...]) * mid_scale).astype(BF)
    wg_ref[3 * d : 4 * d, :] = (dot_nt(outer, gmid[...]) * mid_scale).astype(BF)
    slots = pick_ref.shape[1]
    lane = lax.broadcasted_iota(jnp.int32, (block_rows, slots), 1)
    lane = lane - lax.broadcasted_iota(jnp.int32, (block_rows, slots), 0)
    for t in range(0, place.shape[0], 2):
        both = [jnp.where(lane == place[t + j] * block_rows, 1.0, 0.0) for j in range(2)]
        pick_ref[t * block_rows : (t + 2) * block_rows, :] = jnp.concatenate(
            both, axis=0
        ).astype(BF)


def add_kernel(io, need, flush, ins, outs):
    mine, other = ins[:2]
    outs[0][...] = (mine[...].astype(F32) + other[...].astype(F32)).astype(BF)


def fine_grad_kernel(scale, io, need, flush, ins, outs, g_ref, fg_ref):
    got, pick, cot, pool, w, slope2, slope1, hid, agg, mid, outer, _ = ins
    send_ref, g_out, fg_out = outs
    d, rows = hid.shape
    if pick.shape[1] > 1024:
        need(1)
    blocks = dot(pick[...], got[...]).astype(BF)
    need(2, 3)
    per = pool.shape[1]
    for i in range(rows // TILE):
        cols = slice(i * TILE, (i + 1) * TILE)
        back = dot_tn(blocks[i * per : (i + 1) * per, :], pool[i])
        g_ref[:, cols] = (cot[:, cols].astype(F32) + back).astype(BF)
    io.start(g_ref, g_out)
    g = g_ref[...]
    need(4, 5, 6)
    sg = (dot(w[3], g) * slope2[...]).astype(BF)
    fg = (dot(w[2], sg) * slope1[...]).astype(BF)
    fg_ref[...] = fg
    io.start(fg_ref, fg_out)
    need()
    for m, (a, b) in enumerate(
        ((hid[...], fg), (agg[...], fg), (mid[...], sg), (outer[...], g))
    ):
        send_ref[m * d : (m + 1) * d, :] = (dot_nt(a, b) * scale).astype(BF)


def fine_spread_kernel(io, need, flush, ins, outs, s_ref, total):
    off, ew, w, g, fg, _ = ins
    rim_near, rim_far, out_ref = outs
    rows = g.shape[1]
    clear_corners(s_ref.at[0])
    clear_corners(s_ref.at[1])
    total[...] = jnp.zeros(total.shape, F32)
    need()
    for i in range(rows // TILE):
        cols = slice(i * TILE, (i + 1) * TILE)
        s = s_ref.at[i % 2]
        fine_edges(off[:, cols], ew[:, cols], s)
        fg_tile = fg[:, cols]
        direct = g[:, cols].astype(F32) + dot(w[0], fg_tile)
        spill = dot(w[1], fg_tile).astype(BF)
        window = slice(i * TILE, (i + 1) * TILE + 2 * HALO)
        total[window, :] = total[window, :] + dot_nt(s[...], spill)
        here = slice(HALO + i * TILE, HALO + (i + 1) * TILE)
        total[here, :] = total[here, :] + jnp.transpose(direct)
    even = lax.rem(lax.axis_index("nodes"), 2) == 0
    low, high = total[:HALO, :].astype(BF), total[HALO + rows :, :].astype(BF)
    rim_near[...] = jnp.where(even, high, low)
    rim_far[...] = jnp.where(even, low, high)
    out_ref[...] = total[HALO : HALO + rows, :]


def sum_kernel(io, need, flush, ins, outs, part):
    got = ins[0]
    send_ref = outs[0]
    peers = got.shape[0]
    need()
    part[...] = sum(got[p].astype(F32) for p in range(peers)).astype(BF)
    for p in range(peers):
        io.start(part, send_ref.at[p])


def join_kernel(io, need, flush, ins, outs):
    total, across, beside, coarse = ins
    out_ref, wg_ref = outs
    even = lax.rem(lax.axis_index("nodes"), 2) == 0
    from_left = jnp.where(even, beside[...], across[...])
    from_right = jnp.where(even, across[...], beside[...])
    rows = total.shape[0]
    need()
    io.start(coarse, wg_ref.at[pl.ds(8, 4)])
    out_ref[:HALO, :] = (total[:HALO, :] + from_left.astype(F32)).astype(BF)
    out_ref[HALO : rows - HALO, :] = total[HALO : rows - HALO, :].astype(BF)
    out_ref[rows - HALO :, :] = (total[rows - HALO :, :] + from_right.astype(F32)).astype(BF)


def gather_kernel(io, need, flush, ins, outs, wide):
    out_ref = outs[0]
    for half in range(2):
        wide[4 * half : 4 * half + 4] = ins[half][...].astype(F32)
        part = pl.ds(4 * half, 4)
        io.start(wide.at[part], out_ref.at[part])


def exchange(x):
    return lax.all_to_all(x, "nodes", split_axis=0, concat_axis=0, tiled=True)


def per_device(
    features,
    fine_cotangent,
    mid_cotangent,
    coarse_cotangent,
    weights,
    fine_offsets,
    fine_edge_w,
    pool_fine,
    owner_dev,
    coarse_slot,
    mid_nbrs,
    mid_edge_w,
    pool_mid,
    coarse_nbrs,
    coarse_edge_w,
):
    n, d = features.shape
    tile_count = owner_dev.shape[0]
    tile_rows = n // tile_count
    block_rows = pool_fine.shape[0]
    n1 = mid_cotangent.shape[0]
    n2 = coarse_cotangent.shape[0]
    edges = fine_offsets.shape[0]
    peers = lax.axis_size("nodes")
    cap = max(2, 2 * tile_count // peers)
    chunk = cap * block_rows
    window = TILE + 2 * HALO
    per = TILE // tile_rows * block_rows
    ends = peers - 1
    inside_pairs = [(i, i ^ 1) for i in range(peers)]
    between_pairs = [(i, ((i + 1) ^ 1) - 1) for i in range(1, ends)]
    total2 = peers * n2

    odd = lax.rem(lax.axis_index("nodes"), 2)
    near = lax.dynamic_slice_in_dim(features, (1 - odd) * (n - HALO), HALO, 0)
    far = lax.dynamic_slice_in_dim(features, odd * (n - HALO), HALO, 0)
    across = lax.ppermute(near, "nodes", inside_pairs)
    beside = lax.ppermute(far, "nodes", between_pairs)
    owners = owner_dev.reshape(-1)
    s_out, win, w01, w2t, w3t, pool_out, spread, ext, agg_in, place = call(
        functools.partial(inner_kernel, tile_rows, peers, cap),
        [
            (fine_offsets, "h"), (fine_edge_w, "h"), (features, "h"), (weights, "0"),
            (pool_fine, "h"), (owners, "s"), (coarse_slot, "s"), (coarse_nbrs, "h"),
            (coarse_edge_w, "h"), (coarse_cotangent, "h"),
        ],
        [
            (shape((2, window, TILE)), "v"), (shape((2, d, TILE + HALO)), "v"),
            (shape((d, 2 * d)), "v"), (shape((d, d)), "v"), (shape((d, d)), "v"),
            (shape((2, per, TILE)), "v"), (shape((peers * chunk, d), F32), "v"),
            (shape((peers, n2 + 16, d)), "v"), (shape((d, n)), "v"),
            (shape((tile_count,), jnp.int32), "s"),
        ],
        scratch=(
            pltpu.VMEM((d, n), BF),
            pltpu.VMEM((n // TILE - 2, window, TILE), BF),
            pltpu.VMEM((peers, 128), F32),
            pltpu.SMEM((peers,), jnp.int32),
        ),
        us=6,
    )
    send1, agg = call(
        functools.partial(outer_kernel, tile_rows, cap, block_rows),
        [
            (across, "v"), (beside, "v"), (s_out, "v"), (win, "v"), (w01, "v"), (w2t, "v"),
            (w3t, "v"), (pool_out, "v"), (spread, "v"), (ext, "v"), (agg_in, "v"), (owners, "s"),
        ],
        [(shape((peers, chunk + n2 + 16, d)), "r"), (shape((d, n)), "r")],
        scratch=(
            pltpu.VMEM((d, 2 * TILE), BF),
            pltpu.VMEM((peers * chunk, d), F32),
            pltpu.VMEM((peers, chunk, d), BF),
            pltpu.SMEM((peers,), jnp.int32),
        ),
        copies=8,
        us=3,
    )
    got1 = exchange(send1)
    smid, m01, m2t, m3t = call(
        first_window_kernel,
        [(mid_nbrs, "h"), (mid_edge_w, "h"), (weights, "1"), (agg, "r")],
        [
            (shape((n1, n1)), "h"), (shape((d, 2 * d)), "h"), (shape((d, d)), "h"),
            (shape((d, d)), "h"),
        ],
        us=6,
    )
    hid, mid, outer, slope1, slope2, cot, pool_b = call(
        functools.partial(saved_kernel, tile_rows),
        [
            (features, "h"), (agg, "h"), (weights, "0"), (fine_cotangent, "h"),
            (pool_fine, "h"), (m3t, "r"),
        ],
        [
            (shape((d, n)), "h"), (shape((d, n)), "h"), (shape((d, n)), "h"),
            (shape((d, n), F32), "h"), (shape((d, n), F32), "h"), (shape((d, n)), "h"),
            (shape((n // TILE, per, TILE)), "h"),
        ],
        us=4,
    )
    send2, mhid, magg, sel, ext = call(
        functools.partial(mid_kernel, block_rows, chunk),
        [
            (got1, "v"), (smid, "h"), (m01, "h"), (m2t, "h"), (m3t, "h"), (pool_mid, "h"),
            (pool_b, "r"),
        ],
        [
            (shape((peers, n2, d)), "r"), (shape((d, n1)), "h"), (shape((d, n1)), "h"),
            (shape((peers * chunk, n1)), "h"), (shape((peers, n2 + 16, d)), "r"),
        ],
        scratch=(pltpu.VMEM((peers * chunk, d), BF), pltpu.VMEM((n2, d), BF)),
        copies=peers + 1,
        us=3,
    )
    got2 = exchange(send2)
    near = "v" if total2 <= 512 else "h"
    sco, cot_all, cot_back, c01, c2t, mcot, mslope1, mslope2 = call(
        second_window_kernel,
        [
            (ext, "h"), (mhid, "h"), (magg, "h"), (mid_cotangent, "h"), (weights, "1"),
            (weights, "2"),
        ],
        [
            (shape((total2, total2)), near), (shape((d, total2)), near),
            (shape((d, total2), F32), near), (shape((d, 2 * d)), near), (shape((d, d)), near),
            (shape((d, n1)), "h"),
            (shape((d, n1), F32), "h"), (shape((d, n1), F32), "h"),
        ],
        scratch=(pltpu.VMEM((edges, total2), jnp.int32), pltpu.VMEM((edges, total2), F32)),
        us=6,
    )
    send3, gmid, msg, mfg, coarse_wg = call(
        coarse_kernel,
        [
            (got2.reshape(total2, d), "v"), (sco, near), (c01, near), (c2t, near),
            (cot_all, near), (cot_back, near), (weights, "2"),
            (coarse_cotangent, "h"), (pool_mid, "h"), (mcot, "h"), (weights, "1"),
            (mslope2, "h"), (mslope1, "h"), (smid, "h"), (sel, "h"),
        ],
        [
            (shape((peers * chunk, d)), "h"), (shape((d, n1)), "h"), (shape((d, n1)), "h"),
            (shape((d, n1)), "h"), (shape((4, d, d), F32), "h"),
        ],
        us=3,
    )
    got3 = exchange(send3.reshape(peers, chunk, d))
    pick_kind = "v" if peers * chunk <= 1024 else "h"
    mid_wg, pick = call(
        functools.partial(third_window_kernel, 1.0 / math.sqrt(n1 * peers)),
        [
            (mhid, "h"), (magg, "h"), (gmid, "h"), (msg, "h"), (mfg, "h"), (weights, "1"),
            (place, "s"),
        ],
        [
            (shape((4 * d, d)), "v"),
            (shape((tile_count * block_rows, peers * chunk)), pick_kind),
        ],
        us=3,
    )
    reaches = [1 << i for i in range((peers - 1).bit_length())]
    reaches = reaches[:1] + reaches[-1:] + reaches[1:-1]

    def double(total, reach, *after):
        other = lax.ppermute(total, "nodes", [(i, i ^ reach) for i in range(peers)])
        ins = [(total, "v"), (other, "v")] + [(x, "r") for x in after]
        return call(add_kernel, ins, [(shape((4 * d, d)), "v")], us=1)[0]

    sums = [mid_wg]
    for reach in reaches[:2]:
        sums.append(double(sums[-1], reach))
    send4, g, fg = call(
        functools.partial(fine_grad_kernel, 1.0 / math.sqrt(n * peers)),
        [
            (got3.reshape(peers * chunk, d), "v"), (pick, pick_kind), (cot, "h"), (pool_b, "h"),
            (weights, "0"), (slope2, "h"), (slope1, "h"), (hid, "h"), (agg, "h"), (mid, "h"),
            (outer, "h"), (sums[1], "v"),
        ],
        [(shape((4 * d, d)), "h"), (shape((d, n)), "r"), (shape((d, n)), "r")],
        scratch=(pltpu.VMEM((d, n), BF), pltpu.VMEM((d, n), BF)),
        copies=2,
        us=4,
    )
    got4 = exchange(send4.reshape(peers, 4 * d // peers, d))
    rim_near, rim_far, spread = call(
        fine_spread_kernel,
        [(fine_offsets, "h"), (fine_edge_w, "h"), (weights, "0"), (g, "h"), (fg, "h"), (sums[2], "v")],
        [(shape((HALO, d)), "h"), (shape((HALO, d)), "h"), (shape((n, d), F32), "h")],
        scratch=(pltpu.VMEM((2, window, TILE), BF), pltpu.VMEM((n + 2 * HALO, d), F32)),
        us=6,
    )
    sums.append(double(sums[2], reaches[2], rim_near))
    (send5,) = call(
        sum_kernel,
        [(got4, "v"), (rim_near, "r"), (sums[3], "v")],
        [(shape((peers, 4 * d // peers, d)), "r")],
        scratch=(pltpu.VMEM((4 * d // peers, d), BF),),
        copies=peers,
        us=1,
    )
    got5 = exchange(send5)
    for reach in reaches[3:]:
        sums.append(double(sums[-1], reach))
    from_across = lax.ppermute(rim_near, "nodes", inside_pairs)
    from_beside = lax.ppermute(rim_far, "nodes", between_pairs)
    feature_grads, weight_grads = call(
        join_kernel,
        [(spread, "h"), (from_across, "v"), (from_beside, "v"), (coarse_wg, "h")],
        [(shape((n, d)), "h"), (shape((12, d, d), F32), "r")],
        copies=1,
        us=1,
    )
    (weight_grads,) = call(
        gather_kernel,
        [
            (got5.reshape(4, d, d), "v"), (sums[-1].reshape(4, d, d), "v"), (weight_grads, "r"),
        ],
        [(shape((12, d, d), F32), "r")],
        scratch=(pltpu.VMEM((8, d, d), F32),),
        copies=2,
        aliases={2: 0},
        us=1,
    )
    weight_grads = weight_grads.reshape(3, 4, d, d)
    return (feature_grads, weight_grads)


def solution(mesh):
    rows = P(("groups", "nodes"), None)
    cols = P("groups", "nodes")
    in_specs = (
        rows, rows, rows, rows, P(), cols, cols, cols, rows, P(("groups", "nodes")),
        cols, cols, rows, cols, cols,
    )
    out_specs = (rows, P("groups", None, None, None))
    return jax.shard_map(
        per_device, mesh=mesh, in_specs=in_specs, out_specs=out_specs, check_vma=False
    )
```

```python
import functools
import math

import jax
import jax.numpy as jnp
from jax import lax
from jax.experimental import pallas as pl
from jax.experimental.pallas import tpu as pltpu
from jax.sharding import PartitionSpec as P

HALO = 256
TILE = 256
WIDE = 2048
BF = jnp.bfloat16
F32 = jnp.float32

VM = pl.BlockSpec(memory_space=pltpu.VMEM)
HB = pl.BlockSpec(memory_space=pltpu.HBM)


def dot(a, b):
    return jnp.dot(a, b, preferred_element_type=F32)


def dot_nt(a, b):
    return lax.dot_general(a, b, (((1,), (1,)), ((), ())), preferred_element_type=F32)


def dot_tn(a, b):
    return lax.dot_general(a, b, (((0,), (0,)), ((), ())), preferred_element_type=F32)


def silu(v):
    return v / (1.0 + jnp.exp(-v))


def silu_slope(v):
    s = 1.0 / (1.0 + jnp.exp(-v))
    return s * (1.0 + v * (1.0 - s))


def merged_weights(idx, ew):
    total = ew
    for r in range(1, idx.shape[0]):
        total = total + jnp.where(pltpu.roll(idx, r, 0) == idx, pltpu.roll(ew, r, 0), 0.0)
    return total.astype(BF)


def edge_columns(idx, ew, start, rows):
    count = idx.shape[0]
    lanes = idx.shape[1]
    position = lax.broadcasted_iota(jnp.int32, (rows, lanes), 0) + start
    position = position.astype(jnp.int16)
    picked = jnp.zeros((rows, lanes), BF)
    for k in range(count):
        picked = jnp.where(idx[k : k + 1, :] == position, ew[k : k + 1, :], picked)
    return picked


def fine_edges(off, ew, s_ref):
    for h in range(TILE // 128):
        lane = slice(128 * h, 128 * (h + 1))
        o = off[:, lane]
        weight = merged_weights(o, ew[:, lane])
        rel = o + lax.broadcasted_iota(jnp.int32, o.shape, 1) + HALO
        rel = rel.astype(jnp.int16)
        for c in range(2 * HALO // 128 + 1):
            s_ref[128 * (h + c) : 128 * (h + c + 1), lane] = edge_columns(
                rel, weight, 128 * c, 128
            )


def clear_corners(s_ref):
    for h in range(TILE // 128):
        lane = slice(128 * h, 128 * (h + 1))
        if h > 0:
            s_ref[: 128 * h, lane] = jnp.zeros((128 * h, 128), BF)
        last = 128 * h + 2 * HALO + 128
        if last < TILE + 2 * HALO:
            s_ref[last:, lane] = jnp.zeros((TILE + 2 * HALO - last, 128), BF)


def forward_weights(w):
    w01 = jnp.concatenate([jnp.transpose(w[0]), jnp.transpose(w[1])], axis=1)
    return w01, jnp.transpose(w[2]), jnp.transpose(w[3])


def pool_matrix(pool, tile_rows):
    lane = lax.broadcasted_iota(jnp.int32, pool.shape, 1) // tile_rows
    values = pool.astype(F32)
    parts = [jnp.where(lane == r, values, 0.0) for r in range(pool.shape[1] // tile_rows)]
    return jnp.concatenate(parts, axis=0).astype(BF)


class Copies:
    def __init__(self, sems):
        self.sems = sems
        self.used = 0
        self.open = {}

    def start(self, source, target):
        copy = pltpu.make_async_copy(source, target, self.sems.at[self.used])
        self.used += 1
        copy.start()
        self.open[id(copy)] = copy
        return copy

    def wait(self, *copies):
        for copy in copies:
            if id(copy) in self.open:
                copy.wait()
                del self.open[id(copy)]

    def finish(self):
        self.wait(*list(self.open.values()))


def shape(dims, dtype=BF):
    return jax.ShapeDtypeStruct(dims, dtype)


def call(kernel, ins, outs, scratch=(), copies=0, us=3, mib=24, aliases={}):
    n_in, n_out = len(ins), len(outs)
    staged_in = [i for i, (_, kind) in enumerate(ins) if kind in "hs012"]
    staged_out = [i for i, (_, kind) in enumerate(outs) if kind in "hs"]
    spaces = {"h": pltpu.VMEM, "s": pltpu.SMEM}
    stage = []
    for i in staged_in:
        array, kind = ins[i]
        dims = array.shape[1:] if kind.isdigit() else array.shape
        stage.append(spaces.get(kind, pltpu.VMEM)(dims, array.dtype))
    stage += [spaces[outs[i][1]](outs[i][0].shape, outs[i][0].dtype) for i in staged_out]
    total = len(staged_in) + len(staged_out) + copies

    def body(*refs):
        in_refs, out_refs = list(refs[:n_in]), list(refs[n_in : n_in + n_out])
        rest = list(refs[n_in + n_out :])
        sems = rest.pop() if total else None
        stages, user = rest[: len(stage)], rest[len(stage) :]
        io = Copies(sems)
        pending = {}
        for i, ref in zip(staged_in, stages):
            kind = ins[i][1]
            source = in_refs[i].at[int(kind)] if kind.isdigit() else in_refs[i]
            pending[i] = io.start(source, ref)
            in_refs[i] = ref
        targets = {}
        for i, ref in zip(staged_out, stages[len(staged_in) :]):
            targets[i] = out_refs[i]
            out_refs[i] = ref

        def need(*which):
            io.wait(*[pending[i] for i in which or pending])

        def flush(*which):
            for i in which:
                io.start(out_refs[i], targets.pop(i))

        kernel(io, need, flush, in_refs, out_refs, *user)
        flush(*list(targets))
        io.finish()

    return pl.pallas_call(
        body,
        out_shape=[
            s if kind == "v" else pltpu.HBM(s.shape, s.dtype) for s, kind in outs
        ],
        in_specs=[VM if kind == "v" else HB for _, kind in ins],
        out_specs=[VM if kind == "v" else HB for _, kind in outs],
        scratch_shapes=stage
        + list(scratch)
        + ([pltpu.SemaphoreType.DMA((total,))] if total else []),
        input_output_aliases=aliases,
        compiler_params=pltpu.CompilerParams(vmem_limit_bytes=mib << 20),
        cost_estimate=pl.CostEstimate(
            flops=0, bytes_accessed=int(us * 3_000_000), transcendentals=0
        ),
    )(*[
        a if kind == "v" else pltpu.with_memory_space_constraint(a, pltpu.HBM)
        for a, kind in ins
    ])


def fine_forward(h_t, agg, weights):
    w01, w2t, w3t = weights
    first = dot(w01, jnp.concatenate([h_t, agg], axis=0))
    middle = silu(first).astype(BF)
    second = dot(w2t, middle)
    outer = silu(second).astype(BF)
    return (h_t.astype(F32) + dot(w3t, outer)).astype(BF)


def outer_tiles(tile_count, per):
    return list(range(per)) + list(range(tile_count - per, tile_count))


def inner_kernel(tile_rows, peers, cap, io, need, flush, ins, outs, feat_t, s_ref, ids, counts):
    off, ew, feat, w, pool, owner, slot, nbrs, cew, cot = ins
    so_ref, win_ref, w01_ref, w2t_ref, w3t_ref, po_ref, spread, ext_ref, agg_ref, place = outs
    rows, d = feat.shape
    block_rows = pool.shape[0]
    n2 = cot.shape[0]
    tiles = rows // TILE
    per = TILE // tile_rows
    tile_count = rows // tile_rows
    for i in range(tiles - 2):
        clear_corners(s_ref.at[i])
    clear_corners(so_ref.at[0])
    clear_corners(so_ref.at[1])
    spread[...] = jnp.zeros(spread.shape, F32)
    ids[...] = jnp.full(ids.shape, -1.0, F32)
    for p in range(peers):
        counts[p] = 0
    need(5, 6)
    lane_slot = lax.broadcasted_iota(jnp.int32, (1, 128), 1) // block_rows
    first_tiles = outer_tiles(tile_count, per)
    for t in first_tiles + [t for t in range(tile_count) if t not in first_tiles]:
        o = owner[t]
        c = counts[o]
        counts[o] = c + 1
        place[t] = o * cap + c
        row = ids[pl.ds(o, 1), :]
        ids[pl.ds(o, 1), :] = jnp.where(lane_slot == c, slot[t].astype(F32), row)
    flush(9)
    need(0, 1)
    for n, i in enumerate((0, tiles - 1)):
        cols = slice(i * TILE, (i + 1) * TILE)
        fine_edges(off[:, cols], ew[:, cols], so_ref.at[n])
    need()
    feat_t[...] = jnp.transpose(feat[...])
    weights = forward_weights(w)
    for i in range(1, tiles - 1):
        cols = slice(i * TILE, (i + 1) * TILE)
        fine_edges(off[:, cols], ew[:, cols], s_ref.at[i - 1])
        around = feat_t[:, i * TILE - HALO : (i + 1) * TILE + HALO]
        agg_ref[:, cols] = dot(around, s_ref[i - 1]).astype(BF)
    for start in range(TILE, rows - TILE, WIDE):
        stop = min(start + WIDE, rows - TILE)
        cols = slice(start, stop)
        fine_out = fine_forward(feat_t[:, cols], agg_ref[:, cols], weights)
        for i in range(start // TILE, stop // TILE):
            at = slice(i * TILE - start, (i + 1) * TILE - start)
            matrix = pool_matrix(pool[:, i * TILE : (i + 1) * TILE], tile_rows)
            blocks = dot_nt(matrix, fine_out[:, at])
            for j in range(per):
                at = pl.ds(pl.multiple_of(place[i * per + j] * block_rows, 8), block_rows)
                spread[at, :] = blocks[j * block_rows : (j + 1) * block_rows, :]
    for n, i in enumerate((0, tiles - 1)):
        po_ref[n] = pool_matrix(pool[:, i * TILE : (i + 1) * TILE], tile_rows)
    win_ref[0] = feat_t[:, : TILE + HALO]
    win_ref[1] = feat_t[:, rows - TILE - HALO :]
    w01_ref[...], w2t_ref[...], w3t_ref[...] = weights
    nb = nbrs[...].astype(F32)
    high = jnp.floor(nb * (1.0 / 256.0))
    ce = cew[...]
    ce_high = ce.astype(BF).astype(F32)
    fields = [high, nb - high * 256.0, ce_high, ce - ce_high]
    fields.append(jnp.zeros((nb.shape[0], 128 - 4 * n2), F32))
    top = jnp.concatenate(fields, axis=1)
    sub = lax.broadcasted_iota(jnp.int32, (8, 128), 0)
    for p in range(peers):
        ext_ref[p, 0:n2, :] = cot[...]
        below = jnp.where(sub == 0, ids[p : p + 1, :], 0.0)
        ext_ref[p, n2 : n2 + 16, :] = jnp.concatenate([top, below], axis=0).astype(BF)


def outer_kernel(
    tile_rows, cap, block_rows, io, need, flush, ins, outs, agg_edge, spread, stage, counts
):
    across, beside, s_in, win, w01, w2t, w3t, pool, spread_in, ext, agg_in, owner = ins
    even = lax.rem(lax.axis_index("nodes"), 2) == 0
    left = jnp.where(even, beside[...], across[...])
    right = jnp.where(even, across[...], beside[...])
    send_ref, agg_ref = outs
    peers, chunk, d = stage.shape
    rows = agg_in.shape[1]
    per = TILE // tile_rows
    io.start(ext, send_ref.at[:, pl.ds(chunk, ext.shape[1]), :])
    inside = pl.ds(TILE, rows - 2 * TILE)
    io.start(agg_in.at[:, inside], agg_ref.at[:, inside])
    spread[...] = spread_in[...]
    for p in range(peers):
        counts[p] = 0
    weights = (w01[...], w2t[...], w3t[...])
    for n in range(2):
        if n == 0:
            window_t = jnp.concatenate([jnp.transpose(left), win[0]], axis=1)
        else:
            window_t = jnp.concatenate([win[1], jnp.transpose(right)], axis=1)
        agg_edge[:, n * TILE : (n + 1) * TILE] = dot(window_t, s_in[n]).astype(BF)
    h_t = jnp.concatenate([win[0, :, :TILE], win[1, :, HALO:]], axis=1)
    fine_out = fine_forward(h_t, agg_edge[...], weights)
    results = [dot_nt(pool[n], fine_out[:, n * TILE : (n + 1) * TILE]) for n in range(2)]
    io.start(agg_edge.at[:, pl.ds(0, TILE)], agg_ref.at[:, pl.ds(0, TILE)])
    io.start(agg_edge.at[:, pl.ds(TILE, TILE)], agg_ref.at[:, pl.ds(rows - TILE, TILE)])
    need()
    for j, t in enumerate(outer_tiles(rows // tile_rows, per)):
        o = owner[t]
        c = counts[o]
        counts[o] = c + 1
        at = pl.ds(pl.multiple_of((o * cap + c) * block_rows, 8), block_rows)
        blocks = results[j // per]
        spread[at, :] = blocks[j % per * block_rows : (j % per + 1) * block_rows, :]
    group = max(1, peers // 4)
    for p in range(peers):
        stage[p] = spread[p * chunk : (p + 1) * chunk, :].astype(BF)
        if p % group == group - 1:
            part = pl.ds(p + 1 - group, group)
            io.start(stage.at[part], send_ref.at[part, pl.ds(0, chunk), :])


def mid_edges(nbrs, ew, s_ref):
    nodes = nbrs.shape[1]
    for c in range(nodes // 128):
        lane = slice(128 * c, 128 * (c + 1))
        idx = nbrs[:, lane]
        weight = merged_weights(idx, ew[:, lane])
        idx = idx.astype(jnp.int16)
        for r in range(nodes // 128):
            s_ref[128 * r : 128 * (r + 1), lane] = edge_columns(idx, weight, 128 * r, 128)


def first_window_kernel(io, need, flush, ins, outs):
    nbrs, ew, w, _ = ins
    smid, w01_ref, w2t_ref, w3t_ref = outs
    need(0, 1)
    mid_edges(nbrs, ew, smid)
    flush(0)
    need()
    w01_ref[...], w2t_ref[...], w3t_ref[...] = forward_weights(w)


def mid_kernel(block_rows, chunk, io, need, flush, ins, outs, blocks, coarse):
    got, smid, w01, w2t, w3t, pool_mid, _ = ins
    send_ref, hid_ref, agg_ref, sel_ref, ext_ref = outs
    peers = got.shape[0]
    nodes = smid.shape[0]
    n2 = pool_mid.shape[0]
    io.start(got.at[:, pl.ds(chunk, n2 + 16), :], ext_ref)
    rows = [got[p, chunk + n2 : chunk + n2 + 16, :].astype(F32)[8:9, :] for p in range(peers)]
    keys = jnp.transpose(jnp.concatenate(rows, axis=0))
    keys = keys * block_rows
    keys = keys + (lax.broadcasted_iota(jnp.int32, keys.shape, 0) % block_rows).astype(F32)
    keys = keys.astype(jnp.int32)
    lane = lax.broadcasted_iota(jnp.int32, (chunk, nodes), 1)
    for p in range(peers):
        sel_ref[p * chunk : (p + 1) * chunk, :] = jnp.where(
            keys[0:chunk, p : p + 1] == lane, 1.0, 0.0
        ).astype(BF)
        blocks[p * chunk : (p + 1) * chunk, :] = got[p, 0:chunk, :]
    flush(3)
    hidden = dot_tn(blocks[...], sel_ref[...]).astype(BF)
    hid_ref[...] = hidden
    need()
    agg = dot(hidden, smid[...]).astype(BF)
    agg_ref[...] = agg
    flush(1, 2)
    middle = silu(dot(w01[...], jnp.concatenate([hidden, agg], axis=0))).astype(BF)
    outer = silu(dot(w2t[...], middle)).astype(BF)
    mid_out = (hidden.astype(F32) + dot(w3t[...], outer)).astype(BF)
    coarse[...] = dot_nt(pool_mid[...], mid_out).astype(BF)
    for p in range(peers):
        io.start(coarse, send_ref.at[p])


def second_window_kernel(io, need, flush, ins, outs, nb_ref, ew_ref):
    ext, hid, agg, mid_cot, w1, w2 = ins
    sco, cot_all, back_ref, w01_ref, w2t_ref, mcot, sl1_ref, sl2_ref = outs
    peers = ext.shape[0]
    n2 = ext.shape[1] - 16
    nodes = peers * n2
    edges = nb_ref.shape[0]
    need()
    for p in range(peers):
        part = ext[p, n2 : n2 + 16, :].astype(F32)[0:edges, :]
        at = slice(p * n2, (p + 1) * n2)
        nb_ref[:, at] = (part[:, 0:n2] * 256.0 + part[:, n2 : 2 * n2]).astype(jnp.int32)
        ew_ref[:, at] = part[:, 2 * n2 : 3 * n2] + part[:, 3 * n2 : 4 * n2]
    cots = jnp.concatenate([ext[p, 0:n2, :] for p in range(peers)], axis=0)
    cot_all[...] = jnp.transpose(cots)
    mcot[...] = jnp.transpose(mid_cot[...])

    def column(c, _):
        lane = pl.ds(pl.multiple_of(c * 128, 128), 128)
        idx = nb_ref[:, lane]
        weight = merged_weights(idx, ew_ref[:, lane])
        idx = idx.astype(jnp.int16)
        for r in range(nodes // 128):
            sco[128 * r : 128 * (r + 1), lane] = edge_columns(idx, weight, 128 * r, 128)
        return 0

    lax.fori_loop(0, nodes // 128, column, 0)
    w01_ref[...], w2t_ref[...], _ = forward_weights(w2)
    back_ref[...] = dot(w2[3], cot_all[...])
    w01, w2t, _ = forward_weights(w1)
    first = dot(w01, jnp.concatenate([hid[...], agg[...]], axis=0))
    s1 = 1.0 / (1.0 + jnp.exp(-first))
    second = dot(w2t, (first * s1).astype(BF))
    s2 = 1.0 / (1.0 + jnp.exp(-second))
    sl1_ref[...] = s1 * (1.0 + first * (1.0 - s1))
    sl2_ref[...] = s2 * (1.0 + second * (1.0 - s2))


def coarse_kernel(io, need, flush, ins, outs):
    got, sco, c01, c2t, cot_all, cot_back, w2, *rest = ins
    cot_my, pool_mid, mcot, w1, msl2, msl1, smid, sel, _ = rest
    send_ref, gmid_ref, sg_ref, fg_ref, cwg_ref = outs
    nodes = got.shape[0]
    n2 = cot_my.shape[0]
    me = lax.axis_index("nodes")
    width = min(TILE, nodes)
    hidden = jnp.transpose(got[...])
    if sco.shape[0] > 512:
        need(1, 2, 3, 4, 5)
    w01, w2t = c01[...], c2t[...]
    mine = pl.ds(pl.multiple_of(me * n2, 16), n2)
    mixed = jnp.zeros((2 * n2, 128), F32)
    grads = [jnp.zeros((128, 128), F32) for _ in range(4)]
    row = lax.broadcasted_iota(jnp.int32, (n2, width), 0) + me * n2
    lane = lax.broadcasted_iota(jnp.int32, (n2, width), 1)
    for i in range(nodes // width):
        cols = slice(i * width, (i + 1) * width)
        h = hidden[:, cols]
        agg = dot(hidden, sco[:, cols]).astype(BF)
        first = dot(w01, jnp.concatenate([h, agg], axis=0))
        s1 = 1.0 / (1.0 + jnp.exp(-first))
        middle = (first * s1).astype(BF)
        second = dot(w2t, middle)
        s2 = 1.0 / (1.0 + jnp.exp(-second))
        outer = (second * s2).astype(BF)
        g = cot_all[:, cols]
        if i == 0:
            need(6)
        sg = (cot_back[:, cols] * (s2 * (1.0 + second * (1.0 - s2)))).astype(BF)
        fg = (dot(w2[2], sg) * (s1 * (1.0 + first * (1.0 - s1)))).astype(BF)
        here = jnp.where(lane + i * width == row, 1.0, 0.0).astype(BF)
        mixed = mixed + dot_nt(jnp.concatenate([here, sco[mine, cols]], axis=0), fg)
        grads = [
            grads[0] + dot_nt(h, fg),
            grads[1] + dot_nt(agg, fg),
            grads[2] + dot_nt(middle, sg),
            grads[3] + dot_nt(outer, g),
        ]
    scale = 1.0 / math.sqrt(nodes)
    for m in range(4):
        cwg_ref[m] = grads[m] * scale
    flush(4)
    need(7, 8, 9, 10, 11, 12)
    mixed = mixed.astype(BF)
    into = jnp.concatenate([mixed[:n2], mixed[n2:]], axis=1)
    back_weights = jnp.concatenate([w2[0], w2[1]], axis=1)
    coarse_grad = (cot_my[...].astype(F32) + dot_nt(into, back_weights)).astype(BF)
    back = dot_tn(coarse_grad, pool_mid[...])
    g = (mcot[...].astype(F32) + back).astype(BF)
    gmid_ref[...] = g
    sg = (dot(w1[3], g) * msl2[...]).astype(BF)
    sg_ref[...] = sg
    fg = (dot(w1[2], sg) * msl1[...]).astype(BF)
    fg_ref[...] = fg
    flush(1, 2, 3)
    spill = dot(w1[1], fg).astype(BF)
    need()
    mid_grad = (g.astype(F32) + dot(w1[0], fg) + dot_nt(spill, smid[...])).astype(BF)
    send_ref[...] = dot_nt(sel[...], mid_grad).astype(BF)


def saved_kernel(tile_rows, io, need, flush, ins, outs):
    feat, agg, w, fine_cot, pool, _ = ins
    hid_ref, mid_ref, outer_ref, sl1_ref, sl2_ref, cot_ref, po_ref = outs
    rows = feat.shape[0]
    need(0, 1, 2)
    hid_ref[...] = jnp.transpose(feat[...])
    flush(0)
    w01, w2t, _ = forward_weights(w)
    for start in range(0, rows, 512):
        cols = slice(start, min(start + 512, rows))
        first = dot(w01, jnp.concatenate([hid_ref[:, cols], agg[:, cols]], axis=0))
        s1 = 1.0 / (1.0 + jnp.exp(-first))
        middle = (first * s1).astype(BF)
        mid_ref[:, cols] = middle
        sl1_ref[:, cols] = s1 * (1.0 + first * (1.0 - s1))
        second = dot(w2t, middle)
        s2 = 1.0 / (1.0 + jnp.exp(-second))
        outer_ref[:, cols] = (second * s2).astype(BF)
        sl2_ref[:, cols] = s2 * (1.0 + second * (1.0 - s2))
    need()
    cot_ref[...] = jnp.transpose(fine_cot[...])
    for i in range(rows // TILE):
        po_ref[i] = pool_matrix(pool[:, i * TILE : (i + 1) * TILE], tile_rows)


def third_window_kernel(mid_scale, io, need, flush, ins, outs):
    mhid, magg, gmid, msg, mfg, w1, place = ins
    wg_ref, pick_ref = outs
    d = mhid.shape[0]
    block_rows = pick_ref.shape[0] // place.shape[0]
    need()
    w01, w2t, _ = forward_weights(w1)
    middle = silu(dot(w01, jnp.concatenate([mhid[...], magg[...]], axis=0))).astype(BF)
    outer = silu(dot(w2t, middle)).astype(BF)
    wg_ref[0:d, :] = (dot_nt(mhid[...], mfg[...]) * mid_scale).astype(BF)
    wg_ref[d : 2 * d, :] = (dot_nt(magg[...], mfg[...]) * mid_scale).astype(BF)
    wg_ref[2 * d : 3 * d, :] = (dot_nt(middle, msg[...]) * mid_scale).astype(BF)
    wg_ref[3 * d : 4 * d, :] = (dot_nt(outer, gmid[...]) * mid_scale).astype(BF)
    slots = pick_ref.shape[1]
    lane = lax.broadcasted_iota(jnp.int32, (block_rows, slots), 1)
    lane = lane - lax.broadcasted_iota(jnp.int32, (block_rows, slots), 0)
    for t in range(0, place.shape[0], 2):
        both = [jnp.where(lane == place[t + j] * block_rows, 1.0, 0.0) for j in range(2)]
        pick_ref[t * block_rows : (t + 2) * block_rows, :] = jnp.concatenate(
            both, axis=0
        ).astype(BF)


def add_kernel(io, need, flush, ins, outs):
    mine, other = ins[:2]
    outs[0][...] = (mine[...].astype(F32) + other[...].astype(F32)).astype(BF)


def fine_grad_kernel(scale, io, need, flush, ins, outs, g_ref, fg_ref):
    got, pick, cot, pool, w, slope2, slope1, hid, agg, mid, outer, _ = ins
    send_ref, g_out, fg_out = outs
    d, rows = hid.shape
    if pick.shape[1] > 1024:
        need(1)
    blocks = dot(pick[...], got[...]).astype(BF)
    need(2, 3)
    per = pool.shape[1]
    for i in range(rows // TILE):
        cols = slice(i * TILE, (i + 1) * TILE)
        back = dot_tn(blocks[i * per : (i + 1) * per, :], pool[i])
        g_ref[:, cols] = (cot[:, cols].astype(F32) + back).astype(BF)
    io.start(g_ref, g_out)
    g = g_ref[...]
    need(4, 5, 6)
    sg = (dot(w[3], g) * slope2[...]).astype(BF)
    fg = (dot(w[2], sg) * slope1[...]).astype(BF)
    fg_ref[...] = fg
    io.start(fg_ref, fg_out)
    need()
    for m, (a, b) in enumerate(
        ((hid[...], fg), (agg[...], fg), (mid[...], sg), (outer[...], g))
    ):
        send_ref[m * d : (m + 1) * d, :] = (dot_nt(a, b) * scale).astype(BF)


def edge_kernel(io, need, flush, ins, outs, s_ref):
    off, ew, _ = ins
    tiles = s_ref.shape[0]
    for i in range(tiles):
        clear_corners(s_ref.at[i])
    need()
    for i in range(tiles):
        cols = slice(i * TILE, (i + 1) * TILE)
        fine_edges(off[:, cols], ew[:, cols], s_ref.at[i])
        io.start(s_ref.at[i], outs[0].at[i])


def fine_spread_kernel(io, need, flush, ins, outs, s_ref, total, inner):
    w, g, fg, s_all, _ = ins
    rim_near, rim_far, edge_ref, out_ref = outs
    rows = g.shape[1]
    arrive = [io.start(s_all.at[i], s_ref.at[i]) for i in range(rows // TILE)]
    total[:HALO, :] = jnp.zeros((HALO, total.shape[1]), F32)
    total[HALO + rows :, :] = jnp.zeros((HALO, total.shape[1]), F32)
    need()
    spill = dot(w[1], fg[...]).astype(BF)
    direct = g[...].astype(F32) + dot(w[0], fg[...])
    total[HALO : HALO + rows, :] = jnp.transpose(direct)
    for i in range(rows // TILE):
        io.wait(arrive[i])
        window = slice(i * TILE, (i + 1) * TILE + 2 * HALO)
        part = dot_nt(s_ref[i], spill[:, i * TILE : (i + 1) * TILE])
        total[window, :] = total[window, :] + part
    even = lax.rem(lax.axis_index("nodes"), 2) == 0
    low, high = total[:HALO, :].astype(BF), total[HALO + rows :, :].astype(BF)
    rim_near[...] = jnp.where(even, high, low)
    rim_far[...] = jnp.where(even, low, high)
    edge_ref[:HALO, :] = total[HALO : 2 * HALO, :]
    edge_ref[HALO:, :] = total[rows : rows + HALO, :]
    flush(0, 1, 2)
    inner[...] = total[2 * HALO : rows, :].astype(BF)
    io.start(inner, out_ref.at[pl.ds(HALO, rows - 2 * HALO)])


def sum_kernel(io, need, flush, ins, outs, part):
    got = ins[0]
    send_ref = outs[0]
    peers = got.shape[0]
    need()
    part[...] = sum(got[p].astype(F32) for p in range(peers)).astype(BF)
    for p in range(peers):
        io.start(part, send_ref.at[p])


def join_kernel(io, need, flush, ins, outs, joined):
    edge, across, beside, coarse, _ = ins
    out_ref, wg_ref = outs
    rows = out_ref.shape[0]
    even = lax.rem(lax.axis_index("nodes"), 2) == 0
    from_left = jnp.where(even, beside[...], across[...])
    from_right = jnp.where(even, across[...], beside[...])
    need(0)
    joined[:HALO, :] = (edge[:HALO, :] + from_left.astype(F32)).astype(BF)
    joined[HALO:, :] = (edge[HALO:, :] + from_right.astype(F32)).astype(BF)
    io.start(joined.at[pl.ds(0, HALO)], out_ref.at[pl.ds(0, HALO)])
    io.start(joined.at[pl.ds(HALO, HALO)], out_ref.at[pl.ds(rows - HALO, HALO)])
    need()
    io.start(coarse, wg_ref.at[pl.ds(8, 4)])


def gather_kernel(io, need, flush, ins, outs, wide):
    out_ref = outs[0]
    for half in range(2):
        wide[4 * half : 4 * half + 4] = ins[half][...].astype(F32)
        part = pl.ds(4 * half, 4)
        io.start(wide.at[part], out_ref.at[part])


def exchange(x):
    return lax.all_to_all(x, "nodes", split_axis=0, concat_axis=0, tiled=True)


def per_device(
    features,
    fine_cotangent,
    mid_cotangent,
    coarse_cotangent,
    weights,
    fine_offsets,
    fine_edge_w,
    pool_fine,
    owner_dev,
    coarse_slot,
    mid_nbrs,
    mid_edge_w,
    pool_mid,
    coarse_nbrs,
    coarse_edge_w,
):
    n, d = features.shape
    tile_count = owner_dev.shape[0]
    tile_rows = n // tile_count
    block_rows = pool_fine.shape[0]
    n1 = mid_cotangent.shape[0]
    n2 = coarse_cotangent.shape[0]
    edges = fine_offsets.shape[0]
    peers = lax.axis_size("nodes")
    cap = max(2, 2 * tile_count // peers)
    chunk = cap * block_rows
    window = TILE + 2 * HALO
    per = TILE // tile_rows * block_rows
    ends = peers - 1
    inside_pairs = [(i, i ^ 1) for i in range(peers)]
    between_pairs = [(i, ((i + 1) ^ 1) - 1) for i in range(1, ends)]
    total2 = peers * n2

    odd = lax.rem(lax.axis_index("nodes"), 2)
    near = lax.dynamic_slice_in_dim(features, (1 - odd) * (n - HALO), HALO, 0)
    far = lax.dynamic_slice_in_dim(features, odd * (n - HALO), HALO, 0)
    across = lax.ppermute(near, "nodes", inside_pairs)
    beside = lax.ppermute(far, "nodes", between_pairs)
    owners = owner_dev.reshape(-1)
    s_out, win, w01, w2t, w3t, pool_out, spread, ext, agg_in, place = call(
        functools.partial(inner_kernel, tile_rows, peers, cap),
        [
            (fine_offsets, "h"), (fine_edge_w, "h"), (features, "h"), (weights, "0"),
            (pool_fine, "h"), (owners, "s"), (coarse_slot, "s"), (coarse_nbrs, "h"),
            (coarse_edge_w, "h"), (coarse_cotangent, "h"),
        ],
        [
            (shape((2, window, TILE)), "v"), (shape((2, d, TILE + HALO)), "v"),
            (shape((d, 2 * d)), "v"), (shape((d, d)), "v"), (shape((d, d)), "v"),
            (shape((2, per, TILE)), "v"), (shape((peers * chunk, d), F32), "v"),
            (shape((peers, n2 + 16, d)), "v"), (shape((d, n)), "v"),
            (shape((tile_count,), jnp.int32), "s"),
        ],
        scratch=(
            pltpu.VMEM((d, n), BF),
            pltpu.VMEM((n // TILE - 2, window, TILE), BF),
            pltpu.VMEM((peers, 128), F32),
            pltpu.SMEM((peers,), jnp.int32),
        ),
        us=6,
    )
    send1, agg = call(
        functools.partial(outer_kernel, tile_rows, cap, block_rows),
        [
            (across, "v"), (beside, "v"), (s_out, "v"), (win, "v"), (w01, "v"), (w2t, "v"),
            (w3t, "v"), (pool_out, "v"), (spread, "v"), (ext, "v"), (agg_in, "v"), (owners, "s"),
        ],
        [(shape((peers, chunk + n2 + 16, d)), "r"), (shape((d, n)), "r")],
        scratch=(
            pltpu.VMEM((d, 2 * TILE), BF),
            pltpu.VMEM((peers * chunk, d), F32),
            pltpu.VMEM((peers, chunk, d), BF),
            pltpu.SMEM((peers,), jnp.int32),
        ),
        copies=8,
        us=3,
    )
    got1 = exchange(send1)
    smid, m01, m2t, m3t = call(
        first_window_kernel,
        [(mid_nbrs, "h"), (mid_edge_w, "h"), (weights, "1"), (agg, "r")],
        [
            (shape((n1, n1)), "h"), (shape((d, 2 * d)), "h"), (shape((d, d)), "h"),
            (shape((d, d)), "h"),
        ],
        us=6,
    )
    hid, mid, outer, slope1, slope2, cot, pool_b = call(
        functools.partial(saved_kernel, tile_rows),
        [
            (features, "h"), (agg, "h"), (weights, "0"), (fine_cotangent, "h"),
            (pool_fine, "h"), (m3t, "r"),
        ],
        [
            (shape((d, n)), "h"), (shape((d, n)), "h"), (shape((d, n)), "h"),
            (shape((d, n), F32), "h"), (shape((d, n), F32), "h"), (shape((d, n)), "h"),
            (shape((n // TILE, per, TILE)), "h"),
        ],
        us=4,
    )
    send2, mhid, magg, sel, ext = call(
        functools.partial(mid_kernel, block_rows, chunk),
        [
            (got1, "v"), (smid, "h"), (m01, "h"), (m2t, "h"), (m3t, "h"), (pool_mid, "h"),
            (pool_b, "r"),
        ],
        [
            (shape((peers, n2, d)), "r"), (shape((d, n1)), "h"), (shape((d, n1)), "h"),
            (shape((peers * chunk, n1)), "h"), (shape((peers, n2 + 16, d)), "r"),
        ],
        scratch=(pltpu.VMEM((peers * chunk, d), BF), pltpu.VMEM((n2, d), BF)),
        copies=peers + 1,
        us=3,
    )
    got2 = exchange(send2)
    (s_all,) = call(
        edge_kernel,
        [(fine_offsets, "h"), (fine_edge_w, "h"), (mhid, "r")],
        [(shape((n // TILE, window, TILE)), "r")],
        scratch=(pltpu.VMEM((n // TILE, window, TILE), BF),),
        copies=n // TILE,
        us=3,
    )
    near = "v" if total2 <= 512 else "h"
    sco, cot_all, cot_back, c01, c2t, mcot, mslope1, mslope2 = call(
        second_window_kernel,
        [
            (ext, "h"), (mhid, "h"), (magg, "h"), (mid_cotangent, "h"), (weights, "1"),
            (weights, "2"),
        ],
        [
            (shape((total2, total2)), near), (shape((d, total2)), near),
            (shape((d, total2), F32), near), (shape((d, 2 * d)), near), (shape((d, d)), near),
            (shape((d, n1)), "h"),
            (shape((d, n1), F32), "h"), (shape((d, n1), F32), "h"),
        ],
        scratch=(pltpu.VMEM((edges, total2), jnp.int32), pltpu.VMEM((edges, total2), F32)),
        us=6,
    )
    send3, gmid, msg, mfg, coarse_wg = call(
        coarse_kernel,
        [
            (got2.reshape(total2, d), "v"), (sco, near), (c01, near), (c2t, near),
            (cot_all, near), (cot_back, near), (weights, "2"),
            (coarse_cotangent, "h"), (pool_mid, "h"), (mcot, "h"), (weights, "1"),
            (mslope2, "h"), (mslope1, "h"), (smid, "h"), (sel, "h"),
            (s_all, "r"),
        ],
        [
            (shape((peers * chunk, d)), "h"), (shape((d, n1)), "h"), (shape((d, n1)), "h"),
            (shape((d, n1)), "h"), (shape((4, d, d), F32), "h"),
        ],
        us=3,
    )
    got3 = exchange(send3.reshape(peers, chunk, d))
    pick_kind = "v" if peers * chunk <= 1024 else "h"
    mid_wg, pick = call(
        functools.partial(third_window_kernel, 1.0 / math.sqrt(n1 * peers)),
        [
            (mhid, "h"), (magg, "h"), (gmid, "h"), (msg, "h"), (mfg, "h"), (weights, "1"),
            (place, "s"),
        ],
        [
            (shape((4 * d, d)), "v"),
            (shape((tile_count * block_rows, peers * chunk)), pick_kind),
        ],
        us=3,
    )
    reaches = [1 << i for i in range((peers - 1).bit_length())]
    reaches = reaches[:1] + reaches[-1:] + reaches[1:-1]

    def double(total, reach, *after):
        other = lax.ppermute(total, "nodes", [(i, i ^ reach) for i in range(peers)])
        ins = [(total, "v"), (other, "v")] + [(x, "r") for x in after]
        return call(add_kernel, ins, [(shape((4 * d, d)), "v")], us=1)[0]

    sums = [mid_wg]
    for reach in reaches[:2]:
        sums.append(double(sums[-1], reach))
    send4, g, fg = call(
        functools.partial(fine_grad_kernel, 1.0 / math.sqrt(n * peers)),
        [
            (got3.reshape(peers * chunk, d), "v"), (pick, pick_kind), (cot, "h"), (pool_b, "h"),
            (weights, "0"), (slope2, "h"), (slope1, "h"), (hid, "h"), (agg, "h"), (mid, "h"),
            (outer, "h"), (sums[1], "v"),
        ],
        [(shape((4 * d, d)), "h"), (shape((d, n)), "r"), (shape((d, n)), "r")],
        scratch=(pltpu.VMEM((d, n), BF), pltpu.VMEM((d, n), BF)),
        copies=2,
        us=4,
    )
    got4 = exchange(send4.reshape(peers, 4 * d // peers, d))
    rim_near, rim_far, edge_sums, inner_grads = call(
        fine_spread_kernel,
        [(weights, "0"), (g, "h"), (fg, "h"), (s_all, "r"), (sums[2], "v")],
        [
            (shape((HALO, d)), "h"), (shape((HALO, d)), "h"), (shape((2 * HALO, d), F32), "h"),
            (shape((n, d)), "r"),
        ],
        scratch=(
            pltpu.VMEM((n // TILE, window, TILE), BF),
            pltpu.VMEM((n + 2 * HALO, d), F32),
            pltpu.VMEM((n - 2 * HALO, d), BF),
        ),
        copies=n // TILE + 1,
        us=4,
    )
    sums.append(double(sums[2], reaches[2], rim_near))
    (send5,) = call(
        sum_kernel,
        [(got4, "v"), (rim_near, "r"), (sums[3], "v")],
        [(shape((peers, 4 * d // peers, d)), "r")],
        scratch=(pltpu.VMEM((4 * d // peers, d), BF),),
        copies=peers,
        us=1,
    )
    got5 = exchange(send5)
    for reach in reaches[3:]:
        sums.append(double(sums[-1], reach))
    from_across = lax.ppermute(rim_near, "nodes", inside_pairs)
    from_beside = lax.ppermute(rim_far, "nodes", between_pairs)
    feature_grads, weight_grads = call(
        join_kernel,
        [
            (edge_sums, "h"), (from_across, "v"), (from_beside, "v"), (coarse_wg, "h"),
            (inner_grads, "r"),
        ],
        [(shape((n, d)), "r"), (shape((12, d, d), F32), "r")],
        scratch=(pltpu.VMEM((2 * HALO, d), BF),),
        copies=3,
        aliases={4: 0},
        us=1,
    )
    (weight_grads,) = call(
        gather_kernel,
        [
            (got5.reshape(4, d, d), "v"), (sums[-1].reshape(4, d, d), "v"), (weight_grads, "r"),
        ],
        [(shape((12, d, d), F32), "r")],
        scratch=(pltpu.VMEM((8, d, d), F32),),
        copies=2,
        aliases={2: 0},
        us=1,
    )
    weight_grads = weight_grads.reshape(3, 4, d, d)
    return (feature_grads, weight_grads)


def solution(mesh):
    rows = P(("groups", "nodes"), None)
    cols = P("groups", "nodes")
    in_specs = (
        rows, rows, rows, rows, P(), cols, cols, cols, rows, P(("groups", "nodes")),
        cols, cols, rows, cols, cols,
    )
    out_specs = (rows, P("groups", None, None, None))
    return jax.shard_map(
        per_device, mesh=mesh, in_specs=in_specs, out_specs=out_specs, check_vma=False
    )
```

```python
import functools
import math

import jax
import jax.numpy as jnp
from jax import lax
from jax.experimental import pallas as pl
from jax.experimental.pallas import tpu as pltpu
from jax.sharding import PartitionSpec as P

HALO = 256
TILE = 256
WIDE = 2048
BF = jnp.bfloat16
F32 = jnp.float32

VM = pl.BlockSpec(memory_space=pltpu.VMEM)
HB = pl.BlockSpec(memory_space=pltpu.HBM)


def dot(a, b):
    return jnp.dot(a, b, preferred_element_type=F32)


def dot_nt(a, b):
    return lax.dot_general(a, b, (((1,), (1,)), ((), ())), preferred_element_type=F32)


def dot_tn(a, b):
    return lax.dot_general(a, b, (((0,), (0,)), ((), ())), preferred_element_type=F32)


def silu(v):
    return v / (1.0 + jnp.exp(-v))


def silu_slope(v):
    s = 1.0 / (1.0 + jnp.exp(-v))
    return s * (1.0 + v * (1.0 - s))


def merged_weights(idx, ew):
    total = ew
    for r in range(1, idx.shape[0]):
        total = total + jnp.where(pltpu.roll(idx, r, 0) == idx, pltpu.roll(ew, r, 0), 0.0)
    return total.astype(BF)


def edge_columns(idx, ew, start, rows):
    count = idx.shape[0]
    lanes = idx.shape[1]
    position = lax.broadcasted_iota(jnp.int32, (rows, lanes), 0) + start
    position = position.astype(jnp.int16)
    picked = jnp.zeros((rows, lanes), BF)
    for k in range(count):
        picked = jnp.where(idx[k : k + 1, :] == position, ew[k : k + 1, :], picked)
    return picked


def fine_edges(off, ew, s_ref):
    for h in range(TILE // 128):
        lane = slice(128 * h, 128 * (h + 1))
        o = off[:, lane]
        weight = merged_weights(o, ew[:, lane])
        rel = o + lax.broadcasted_iota(jnp.int32, o.shape, 1) + HALO
        rel = rel.astype(jnp.int16)
        for c in range(2 * HALO // 128 + 1):
            s_ref[128 * (h + c) : 128 * (h + c + 1), lane] = edge_columns(
                rel, weight, 128 * c, 128
            )


def clear_corners(s_ref):
    for h in range(TILE // 128):
        lane = slice(128 * h, 128 * (h + 1))
        if h > 0:
            s_ref[: 128 * h, lane] = jnp.zeros((128 * h, 128), BF)
        last = 128 * h + 2 * HALO + 128
        if last < TILE + 2 * HALO:
            s_ref[last:, lane] = jnp.zeros((TILE + 2 * HALO - last, 128), BF)


def forward_weights(w):
    w01 = jnp.concatenate([jnp.transpose(w[0]), jnp.transpose(w[1])], axis=1)
    return w01, jnp.transpose(w[2]), jnp.transpose(w[3])


def pool_matrix(pool, tile_rows):
    lane = lax.broadcasted_iota(jnp.int32, pool.shape, 1) // tile_rows
    values = pool.astype(F32)
    parts = [jnp.where(lane == r, values, 0.0) for r in range(pool.shape[1] // tile_rows)]
    return jnp.concatenate(parts, axis=0).astype(BF)


class Copies:
    def __init__(self, sems):
        self.sems = sems
        self.used = 0
        self.open = {}

    def start(self, source, target):
        copy = pltpu.make_async_copy(source, target, self.sems.at[self.used])
        self.used += 1
        copy.start()
        self.open[id(copy)] = copy
        return copy

    def wait(self, *copies):
        for copy in copies:
            if id(copy) in self.open:
                copy.wait()
                del self.open[id(copy)]

    def finish(self):
        self.wait(*list(self.open.values()))


def shape(dims, dtype=BF):
    return jax.ShapeDtypeStruct(dims, dtype)


def call(kernel, ins, outs, scratch=(), copies=0, us=3, mib=24, aliases={}):
    n_in, n_out = len(ins), len(outs)
    staged_in = [i for i, (_, kind) in enumerate(ins) if kind in "hs012"]
    staged_out = [i for i, (_, kind) in enumerate(outs) if kind in "hs"]
    spaces = {"h": pltpu.VMEM, "s": pltpu.SMEM}
    stage = []
    for i in staged_in:
        array, kind = ins[i]
        dims = array.shape[1:] if kind.isdigit() else array.shape
        stage.append(spaces.get(kind, pltpu.VMEM)(dims, array.dtype))
    stage += [spaces[outs[i][1]](outs[i][0].shape, outs[i][0].dtype) for i in staged_out]
    total = len(staged_in) + len(staged_out) + copies

    def body(*refs):
        in_refs, out_refs = list(refs[:n_in]), list(refs[n_in : n_in + n_out])
        rest = list(refs[n_in + n_out :])
        sems = rest.pop() if total else None
        stages, user = rest[: len(stage)], rest[len(stage) :]
        io = Copies(sems)
        pending = {}
        for i, ref in zip(staged_in, stages):
            kind = ins[i][1]
            source = in_refs[i].at[int(kind)] if kind.isdigit() else in_refs[i]
            pending[i] = io.start(source, ref)
            in_refs[i] = ref
        targets = {}
        for i, ref in zip(staged_out, stages[len(staged_in) :]):
            targets[i] = out_refs[i]
            out_refs[i] = ref

        def need(*which):
            io.wait(*[pending[i] for i in which or pending])

        def flush(*which):
            for i in which:
                io.start(out_refs[i], targets.pop(i))

        kernel(io, need, flush, in_refs, out_refs, *user)
        flush(*list(targets))
        io.finish()

    return pl.pallas_call(
        body,
        out_shape=[
            s if kind == "v" else pltpu.HBM(s.shape, s.dtype) for s, kind in outs
        ],
        in_specs=[VM if kind == "v" else HB for _, kind in ins],
        out_specs=[VM if kind == "v" else HB for _, kind in outs],
        scratch_shapes=stage
        + list(scratch)
        + ([pltpu.SemaphoreType.DMA((total,))] if total else []),
        input_output_aliases=aliases,
        compiler_params=pltpu.CompilerParams(vmem_limit_bytes=mib << 20),
        cost_estimate=pl.CostEstimate(
            flops=0, bytes_accessed=int(us * 3_000_000), transcendentals=0
        ),
    )(*[
        a if kind == "v" else pltpu.with_memory_space_constraint(a, pltpu.HBM)
        for a, kind in ins
    ])


def fine_forward(h_t, agg, weights):
    w01, w2t, w3t = weights
    first = dot(w01, jnp.concatenate([h_t, agg], axis=0))
    middle = silu(first).astype(BF)
    second = dot(w2t, middle)
    outer = silu(second).astype(BF)
    return (h_t.astype(F32) + dot(w3t, outer)).astype(BF)


def outer_tiles(tile_count, per):
    return list(range(per)) + list(range(tile_count - per, tile_count))


def inner_kernel(tile_rows, peers, cap, io, need, flush, ins, outs, feat_t, s_ref, ids, counts):
    off, ew, feat, w, pool, owner, slot, nbrs, cew, cot = ins
    so_ref, win_ref, w01_ref, w2t_ref, w3t_ref, po_ref, spread, ext_ref, agg_ref, place, s_all = outs
    rows, d = feat.shape
    block_rows = pool.shape[0]
    n2 = cot.shape[0]
    tiles = rows // TILE
    per = TILE // tile_rows
    tile_count = rows // tile_rows
    for i in range(tiles - 2):
        clear_corners(s_ref.at[i])
    clear_corners(so_ref.at[0])
    clear_corners(so_ref.at[1])
    spread[...] = jnp.zeros(spread.shape, F32)
    ids[...] = jnp.full(ids.shape, -1.0, F32)
    for p in range(peers):
        counts[p] = 0
    need(5, 6)
    lane_slot = lax.broadcasted_iota(jnp.int32, (1, 128), 1) // block_rows
    first_tiles = outer_tiles(tile_count, per)
    for t in first_tiles + [t for t in range(tile_count) if t not in first_tiles]:
        o = owner[t]
        c = counts[o]
        counts[o] = c + 1
        place[t] = o * cap + c
        row = ids[pl.ds(o, 1), :]
        ids[pl.ds(o, 1), :] = jnp.where(lane_slot == c, slot[t].astype(F32), row)
    flush(9)
    need(0, 1)
    for n, i in enumerate((0, tiles - 1)):
        cols = slice(i * TILE, (i + 1) * TILE)
        fine_edges(off[:, cols], ew[:, cols], so_ref.at[n])
        io.start(so_ref.at[n], s_all.at[i])
    need()
    feat_t[...] = jnp.transpose(feat[...])
    weights = forward_weights(w)
    for i in range(1, tiles - 1):
        cols = slice(i * TILE, (i + 1) * TILE)
        fine_edges(off[:, cols], ew[:, cols], s_ref.at[i - 1])
        io.start(s_ref.at[i - 1], s_all.at[i])
        around = feat_t[:, i * TILE - HALO : (i + 1) * TILE + HALO]
        agg_ref[:, cols] = dot(around, s_ref[i - 1]).astype(BF)
    for start in range(TILE, rows - TILE, WIDE):
        stop = min(start + WIDE, rows - TILE)
        cols = slice(start, stop)
        fine_out = fine_forward(feat_t[:, cols], agg_ref[:, cols], weights)
        for i in range(start // TILE, stop // TILE):
            at = slice(i * TILE - start, (i + 1) * TILE - start)
            matrix = pool_matrix(pool[:, i * TILE : (i + 1) * TILE], tile_rows)
            blocks = dot_nt(matrix, fine_out[:, at])
            for j in range(per):
                at = pl.ds(pl.multiple_of(place[i * per + j] * block_rows, 8), block_rows)
                spread[at, :] = blocks[j * block_rows : (j + 1) * block_rows, :]
    for n, i in enumerate((0, tiles - 1)):
        po_ref[n] = pool_matrix(pool[:, i * TILE : (i + 1) * TILE], tile_rows)
    win_ref[0] = feat_t[:, : TILE + HALO]
    win_ref[1] = feat_t[:, rows - TILE - HALO :]
    w01_ref[...], w2t_ref[...], w3t_ref[...] = weights
    nb = nbrs[...].astype(F32)
    high = jnp.floor(nb * (1.0 / 256.0))
    ce = cew[...]
    ce_high = ce.astype(BF).astype(F32)
    fields = [high, nb - high * 256.0, ce_high, ce - ce_high]
    fields.append(jnp.zeros((nb.shape[0], 128 - 4 * n2), F32))
    top = jnp.concatenate(fields, axis=1)
    sub = lax.broadcasted_iota(jnp.int32, (8, 128), 0)
    for p in range(peers):
        ext_ref[p, 0:n2, :] = cot[...]
        below = jnp.where(sub == 0, ids[p : p + 1, :], 0.0)
        ext_ref[p, n2 : n2 + 16, :] = jnp.concatenate([top, below], axis=0).astype(BF)


def outer_kernel(
    tile_rows, cap, block_rows, io, need, flush, ins, outs, agg_edge, spread, stage, counts
):
    across, beside, s_in, win, w01, w2t, w3t, pool, spread_in, ext, agg_in, owner = ins
    even = lax.rem(lax.axis_index("nodes"), 2) == 0
    left = jnp.where(even, beside[...], across[...])
    right = jnp.where(even, across[...], beside[...])
    send_ref, agg_ref = outs
    peers, chunk, d = stage.shape
    rows = agg_in.shape[1]
    per = TILE // tile_rows
    io.start(ext, send_ref.at[:, pl.ds(chunk, ext.shape[1]), :])
    inside = pl.ds(TILE, rows - 2 * TILE)
    io.start(agg_in.at[:, inside], agg_ref.at[:, inside])
    spread[...] = spread_in[...]
    for p in range(peers):
        counts[p] = 0
    weights = (w01[...], w2t[...], w3t[...])
    for n in range(2):
        if n == 0:
            window_t = jnp.concatenate([jnp.transpose(left), win[0]], axis=1)
        else:
            window_t = jnp.concatenate([win[1], jnp.transpose(right)], axis=1)
        agg_edge[:, n * TILE : (n + 1) * TILE] = dot(window_t, s_in[n]).astype(BF)
    h_t = jnp.concatenate([win[0, :, :TILE], win[1, :, HALO:]], axis=1)
    fine_out = fine_forward(h_t, agg_edge[...], weights)
    results = [dot_nt(pool[n], fine_out[:, n * TILE : (n + 1) * TILE]) for n in range(2)]
    io.start(agg_edge.at[:, pl.ds(0, TILE)], agg_ref.at[:, pl.ds(0, TILE)])
    io.start(agg_edge.at[:, pl.ds(TILE, TILE)], agg_ref.at[:, pl.ds(rows - TILE, TILE)])
    need()
    for j, t in enumerate(outer_tiles(rows // tile_rows, per)):
        o = owner[t]
        c = counts[o]
        counts[o] = c + 1
        at = pl.ds(pl.multiple_of((o * cap + c) * block_rows, 8), block_rows)
        blocks = results[j // per]
        spread[at, :] = blocks[j % per * block_rows : (j % per + 1) * block_rows, :]
    group = max(1, peers // 4)
    for p in range(peers):
        stage[p] = spread[p * chunk : (p + 1) * chunk, :].astype(BF)
        if p % group == group - 1:
            part = pl.ds(p + 1 - group, group)
            io.start(stage.at[part], send_ref.at[part, pl.ds(0, chunk), :])


def mid_edges(nbrs, ew, s_ref):
    nodes = nbrs.shape[1]
    for c in range(nodes // 128):
        lane = slice(128 * c, 128 * (c + 1))
        idx = nbrs[:, lane]
        weight = merged_weights(idx, ew[:, lane])
        idx = idx.astype(jnp.int16)
        for r in range(nodes // 128):
            s_ref[128 * r : 128 * (r + 1), lane] = edge_columns(idx, weight, 128 * r, 128)


def first_window_kernel(io, need, flush, ins, outs):
    nbrs, ew, w, _ = ins
    smid, w01_ref, w2t_ref, w3t_ref = outs
    need(0, 1)
    mid_edges(nbrs, ew, smid)
    flush(0)
    need()
    w01_ref[...], w2t_ref[...], w3t_ref[...] = forward_weights(w)


def mid_kernel(block_rows, chunk, io, need, flush, ins, outs, blocks, coarse):
    got, smid, w01, w2t, w3t, pool_mid, _ = ins
    send_ref, hid_ref, agg_ref, sel_ref, ext_ref = outs
    peers = got.shape[0]
    nodes = smid.shape[0]
    n2 = pool_mid.shape[0]
    io.start(got.at[:, pl.ds(chunk, n2 + 16), :], ext_ref)
    rows = [got[p, chunk + n2 : chunk + n2 + 16, :].astype(F32)[8:9, :] for p in range(peers)]
    keys = jnp.transpose(jnp.concatenate(rows, axis=0))
    keys = keys * block_rows
    keys = keys + (lax.broadcasted_iota(jnp.int32, keys.shape, 0) % block_rows).astype(F32)
    keys = keys.astype(jnp.int32)
    lane = lax.broadcasted_iota(jnp.int32, (chunk, nodes), 1)
    for p in range(peers):
        sel_ref[p * chunk : (p + 1) * chunk, :] = jnp.where(
            keys[0:chunk, p : p + 1] == lane, 1.0, 0.0
        ).astype(BF)
        blocks[p * chunk : (p + 1) * chunk, :] = got[p, 0:chunk, :]
    flush(3)
    hidden = dot_tn(blocks[...], sel_ref[...]).astype(BF)
    hid_ref[...] = hidden
    need()
    agg = dot(hidden, smid[...]).astype(BF)
    agg_ref[...] = agg
    flush(1, 2)
    middle = silu(dot(w01[...], jnp.concatenate([hidden, agg], axis=0))).astype(BF)
    outer = silu(dot(w2t[...], middle)).astype(BF)
    mid_out = (hidden.astype(F32) + dot(w3t[...], outer)).astype(BF)
    coarse[...] = dot_nt(pool_mid[...], mid_out).astype(BF)
    for p in range(peers):
        io.start(coarse, send_ref.at[p])


def second_window_kernel(io, need, flush, ins, outs, nb_ref, ew_ref):
    ext, hid, agg, mid_cot, w1, w2 = ins
    sco, cot_all, back_ref, w01_ref, w2t_ref, mcot, sl1_ref, sl2_ref = outs
    peers = ext.shape[0]
    n2 = ext.shape[1] - 16
    nodes = peers * n2
    edges = nb_ref.shape[0]
    need()
    for p in range(peers):
        part = ext[p, n2 : n2 + 16, :].astype(F32)[0:edges, :]
        at = slice(p * n2, (p + 1) * n2)
        nb_ref[:, at] = (part[:, 0:n2] * 256.0 + part[:, n2 : 2 * n2]).astype(jnp.int32)
        ew_ref[:, at] = part[:, 2 * n2 : 3 * n2] + part[:, 3 * n2 : 4 * n2]
    cots = jnp.concatenate([ext[p, 0:n2, :] for p in range(peers)], axis=0)
    cot_all[...] = jnp.transpose(cots)
    mcot[...] = jnp.transpose(mid_cot[...])

    def column(c, _):
        lane = pl.ds(pl.multiple_of(c * 128, 128), 128)
        idx = nb_ref[:, lane]
        weight = merged_weights(idx, ew_ref[:, lane])
        idx = idx.astype(jnp.int16)
        for r in range(nodes // 128):
            sco[128 * r : 128 * (r + 1), lane] = edge_columns(idx, weight, 128 * r, 128)
        return 0

    lax.fori_loop(0, nodes // 128, column, 0)
    w01_ref[...], w2t_ref[...], _ = forward_weights(w2)
    back_ref[...] = dot(w2[3], cot_all[...])
    w01, w2t, _ = forward_weights(w1)
    first = dot(w01, jnp.concatenate([hid[...], agg[...]], axis=0))
    s1 = 1.0 / (1.0 + jnp.exp(-first))
    second = dot(w2t, (first * s1).astype(BF))
    s2 = 1.0 / (1.0 + jnp.exp(-second))
    sl1_ref[...] = s1 * (1.0 + first * (1.0 - s1))
    sl2_ref[...] = s2 * (1.0 + second * (1.0 - s2))


def coarse_kernel(io, need, flush, ins, outs):
    got, sco, c01, c2t, cot_all, cot_back, w2, *rest = ins
    cot_my, pool_mid, mcot, w1, msl2, msl1, smid, sel = rest
    send_ref, gmid_ref, sg_ref, fg_ref, cwg_ref = outs
    nodes = got.shape[0]
    n2 = cot_my.shape[0]
    me = lax.axis_index("nodes")
    width = min(TILE, nodes)
    hidden = jnp.transpose(got[...])
    if sco.shape[0] > 512:
        need(1, 2, 3, 4, 5)
    w01, w2t = c01[...], c2t[...]
    mine = pl.ds(pl.multiple_of(me * n2, 16), n2)
    mixed = jnp.zeros((2 * n2, 128), F32)
    grads = [jnp.zeros((128, 128), F32) for _ in range(4)]
    row = lax.broadcasted_iota(jnp.int32, (n2, width), 0) + me * n2
    lane = lax.broadcasted_iota(jnp.int32, (n2, width), 1)
    for i in range(nodes // width):
        cols = slice(i * width, (i + 1) * width)
        h = hidden[:, cols]
        agg = dot(hidden, sco[:, cols]).astype(BF)
        first = dot(w01, jnp.concatenate([h, agg], axis=0))
        s1 = 1.0 / (1.0 + jnp.exp(-first))
        middle = (first * s1).astype(BF)
        second = dot(w2t, middle)
        s2 = 1.0 / (1.0 + jnp.exp(-second))
        outer = (second * s2).astype(BF)
        g = cot_all[:, cols]
        if i == 0:
            need(6)
        sg = (cot_back[:, cols] * (s2 * (1.0 + second * (1.0 - s2)))).astype(BF)
        fg = (dot(w2[2], sg) * (s1 * (1.0 + first * (1.0 - s1)))).astype(BF)
        here = jnp.where(lane + i * width == row, 1.0, 0.0).astype(BF)
        mixed = mixed + dot_nt(jnp.concatenate([here, sco[mine, cols]], axis=0), fg)
        grads = [
            grads[0] + dot_nt(h, fg),
            grads[1] + dot_nt(agg, fg),
            grads[2] + dot_nt(middle, sg),
            grads[3] + dot_nt(outer, g),
        ]
    scale = 1.0 / math.sqrt(nodes)
    for m in range(4):
        cwg_ref[m] = grads[m] * scale
    flush(4)
    need(7, 8, 9, 10, 11, 12)
    mixed = mixed.astype(BF)
    into = jnp.concatenate([mixed[:n2], mixed[n2:]], axis=1)
    back_weights = jnp.concatenate([w2[0], w2[1]], axis=1)
    coarse_grad = (cot_my[...].astype(F32) + dot_nt(into, back_weights)).astype(BF)
    back = dot_tn(coarse_grad, pool_mid[...])
    g = (mcot[...].astype(F32) + back).astype(BF)
    gmid_ref[...] = g
    sg = (dot(w1[3], g) * msl2[...]).astype(BF)
    sg_ref[...] = sg
    fg = (dot(w1[2], sg) * msl1[...]).astype(BF)
    fg_ref[...] = fg
    flush(1, 2, 3)
    spill = dot(w1[1], fg).astype(BF)
    need()
    mid_grad = (g.astype(F32) + dot(w1[0], fg) + dot_nt(spill, smid[...])).astype(BF)
    send_ref[...] = dot_nt(sel[...], mid_grad).astype(BF)


def saved_kernel(tile_rows, io, need, flush, ins, outs):
    feat, agg, w, fine_cot, pool, _ = ins
    hid_ref, mid_ref, outer_ref, sl1_ref, sl2_ref, cot_ref, po_ref = outs
    rows = feat.shape[0]
    need(0, 1, 2)
    hid_ref[...] = jnp.transpose(feat[...])
    flush(0)
    w01, w2t, _ = forward_weights(w)
    for start in range(0, rows, 512):
        cols = slice(start, min(start + 512, rows))
        first = dot(w01, jnp.concatenate([hid_ref[:, cols], agg[:, cols]], axis=0))
        s1 = 1.0 / (1.0 + jnp.exp(-first))
        middle = (first * s1).astype(BF)
        mid_ref[:, cols] = middle
        sl1_ref[:, cols] = s1 * (1.0 + first * (1.0 - s1))
        second = dot(w2t, middle)
        s2 = 1.0 / (1.0 + jnp.exp(-second))
        outer_ref[:, cols] = (second * s2).astype(BF)
        sl2_ref[:, cols] = s2 * (1.0 + second * (1.0 - s2))
    need()
    cot_ref[...] = jnp.transpose(fine_cot[...])
    for i in range(rows // TILE):
        po_ref[i] = pool_matrix(pool[:, i * TILE : (i + 1) * TILE], tile_rows)


def third_window_kernel(mid_scale, io, need, flush, ins, outs):
    mhid, magg, gmid, msg, mfg, w1, place = ins
    wg_ref, pick_ref = outs
    d = mhid.shape[0]
    block_rows = pick_ref.shape[0] // place.shape[0]
    need()
    w01, w2t, _ = forward_weights(w1)
    middle = silu(dot(w01, jnp.concatenate([mhid[...], magg[...]], axis=0))).astype(BF)
    outer = silu(dot(w2t, middle)).astype(BF)
    wg_ref[0:d, :] = (dot_nt(mhid[...], mfg[...]) * mid_scale).astype(BF)
    wg_ref[d : 2 * d, :] = (dot_nt(magg[...], mfg[...]) * mid_scale).astype(BF)
    wg_ref[2 * d : 3 * d, :] = (dot_nt(middle, msg[...]) * mid_scale).astype(BF)
    wg_ref[3 * d : 4 * d, :] = (dot_nt(outer, gmid[...]) * mid_scale).astype(BF)
    slots = pick_ref.shape[1]
    lane = lax.broadcasted_iota(jnp.int32, (block_rows, slots), 1)
    lane = lane - lax.broadcasted_iota(jnp.int32, (block_rows, slots), 0)
    for t in range(0, place.shape[0], 2):
        both = [jnp.where(lane == place[t + j] * block_rows, 1.0, 0.0) for j in range(2)]
        pick_ref[t * block_rows : (t + 2) * block_rows, :] = jnp.concatenate(
            both, axis=0
        ).astype(BF)


def add_kernel(io, need, flush, ins, outs):
    mine, other = ins[:2]
    outs[0][...] = (mine[...].astype(F32) + other[...].astype(F32)).astype(BF)


def fine_grad_kernel(scale, io, need, flush, ins, outs, g_ref, fg_ref):
    got, pick, cot, pool, w, slope2, slope1, hid, agg, mid, outer, _ = ins
    send_ref, g_out, fg_out = outs
    d, rows = hid.shape
    if pick.shape[1] > 1024:
        need(1)
    blocks = dot(pick[...], got[...]).astype(BF)
    need(2, 3)
    per = pool.shape[1]
    for i in range(rows // TILE):
        cols = slice(i * TILE, (i + 1) * TILE)
        back = dot_tn(blocks[i * per : (i + 1) * per, :], pool[i])
        g_ref[:, cols] = (cot[:, cols].astype(F32) + back).astype(BF)
    io.start(g_ref, g_out)
    g = g_ref[...]
    need(4, 5, 6)
    sg = (dot(w[3], g) * slope2[...]).astype(BF)
    fg = (dot(w[2], sg) * slope1[...]).astype(BF)
    fg_ref[...] = fg
    io.start(fg_ref, fg_out)
    need()
    for m, (a, b) in enumerate(
        ((hid[...], fg), (agg[...], fg), (mid[...], sg), (outer[...], g))
    ):
        send_ref[m * d : (m + 1) * d, :] = (dot_nt(a, b) * scale).astype(BF)


def fine_spread_kernel(io, need, flush, ins, outs, band, spill, inner):
    w, g, fg, s_all, _ = ins
    rim_near, rim_far, edge_ref, out_ref = outs
    d, rows = g.shape
    tiles = rows // TILE
    arrive = []
    for b in range(tiles + 2):
        arrive.append([])
        for j in range(3):
            lanes = pl.ds(j * TILE, TILE)
            if 0 <= b - 2 + j < tiles:
                source = s_all.at[b - 2 + j, pl.ds((2 - j) * TILE, TILE), :]
                arrive[b].append(io.start(source, band.at[b, :, lanes]))
            else:
                band[b, :, j * TILE : (j + 1) * TILE] = jnp.zeros((TILE, TILE), BF)
    spill[:, : 2 * TILE] = jnp.zeros((d, 2 * TILE), BF)
    spill[:, 2 * TILE + rows :] = jnp.zeros((d, 2 * TILE), BF)
    even = lax.rem(lax.axis_index("nodes"), 2) == 0
    need()
    spill[:, 2 * TILE : 2 * TILE + rows] = dot(w[1], fg[...]).astype(BF)
    rims = []
    for b in [0, tiles + 1] + list(range(1, tiles + 1)):
        io.wait(*arrive[b])
        part = dot_nt(band[b], spill[:, b * TILE : (b + 3) * TILE])
        if b in (0, tiles + 1):
            rims.append(part.astype(BF))
            continue
        if b == 1:
            rim_near[...] = jnp.where(even, rims[1], rims[0])
            rim_far[...] = jnp.where(even, rims[0], rims[1])
            flush(0, 1)
        cols = slice((b - 1) * TILE, b * TILE)
        part = part + jnp.transpose(g[:, cols].astype(F32) + dot(w[0], fg[:, cols]))
        if b == 1:
            edge_ref[:TILE, :] = part
        elif b == tiles:
            edge_ref[TILE:, :] = part
        else:
            inner[(b - 2) * TILE : (b - 1) * TILE, :] = part.astype(BF)
    io.start(inner, out_ref.at[pl.ds(TILE, rows - 2 * TILE)])


def sum_kernel(io, need, flush, ins, outs, part):
    got = ins[0]
    send_ref = outs[0]
    peers = got.shape[0]
    need()
    part[...] = sum(got[p].astype(F32) for p in range(peers)).astype(BF)
    for p in range(peers):
        io.start(part, send_ref.at[p])


def join_kernel(io, need, flush, ins, outs, joined):
    edge, across, beside, coarse, _ = ins
    out_ref, wg_ref = outs
    rows = out_ref.shape[0]
    even = lax.rem(lax.axis_index("nodes"), 2) == 0
    from_left = jnp.where(even, beside[...], across[...])
    from_right = jnp.where(even, across[...], beside[...])
    need(0)
    joined[:HALO, :] = (edge[:HALO, :] + from_left.astype(F32)).astype(BF)
    joined[HALO:, :] = (edge[HALO:, :] + from_right.astype(F32)).astype(BF)
    io.start(joined.at[pl.ds(0, HALO)], out_ref.at[pl.ds(0, HALO)])
    io.start(joined.at[pl.ds(HALO, HALO)], out_ref.at[pl.ds(rows - HALO, HALO)])
    need()
    io.start(coarse, wg_ref.at[pl.ds(8, 4)])


def gather_kernel(io, need, flush, ins, outs, wide):
    out_ref = outs[0]
    for half in range(2):
        wide[4 * half : 4 * half + 4] = ins[half][...].astype(F32)
        part = pl.ds(4 * half, 4)
        io.start(wide.at[part], out_ref.at[part])


def exchange(x):
    return lax.all_to_all(x, "nodes", split_axis=0, concat_axis=0, tiled=True)


def per_device(
    features,
    fine_cotangent,
    mid_cotangent,
    coarse_cotangent,
    weights,
    fine_offsets,
    fine_edge_w,
    pool_fine,
    owner_dev,
    coarse_slot,
    mid_nbrs,
    mid_edge_w,
    pool_mid,
    coarse_nbrs,
    coarse_edge_w,
):
    n, d = features.shape
    tile_count = owner_dev.shape[0]
    tile_rows = n // tile_count
    block_rows = pool_fine.shape[0]
    n1 = mid_cotangent.shape[0]
    n2 = coarse_cotangent.shape[0]
    edges = fine_offsets.shape[0]
    peers = lax.axis_size("nodes")
    cap = max(2, 2 * tile_count // peers)
    chunk = cap * block_rows
    window = TILE + 2 * HALO
    per = TILE // tile_rows * block_rows
    ends = peers - 1
    inside_pairs = [(i, i ^ 1) for i in range(peers)]
    between_pairs = [(i, ((i + 1) ^ 1) - 1) for i in range(1, ends)]
    total2 = peers * n2

    odd = lax.rem(lax.axis_index("nodes"), 2)
    near = lax.dynamic_slice_in_dim(features, (1 - odd) * (n - HALO), HALO, 0)
    far = lax.dynamic_slice_in_dim(features, odd * (n - HALO), HALO, 0)
    across = lax.ppermute(near, "nodes", inside_pairs)
    beside = lax.ppermute(far, "nodes", between_pairs)
    owners = owner_dev.reshape(-1)
    s_out, win, w01, w2t, w3t, pool_out, spread, ext, agg_in, place, s_all = call(
        functools.partial(inner_kernel, tile_rows, peers, cap),
        [
            (fine_offsets, "h"), (fine_edge_w, "h"), (features, "h"), (weights, "0"),
            (pool_fine, "h"), (owners, "s"), (coarse_slot, "s"), (coarse_nbrs, "h"),
            (coarse_edge_w, "h"), (coarse_cotangent, "h"),
        ],
        [
            (shape((2, window, TILE)), "v"), (shape((2, d, TILE + HALO)), "v"),
            (shape((d, 2 * d)), "v"), (shape((d, d)), "v"), (shape((d, d)), "v"),
            (shape((2, per, TILE)), "v"), (shape((peers * chunk, d), F32), "v"),
            (shape((peers, n2 + 16, d)), "v"), (shape((d, n)), "v"),
            (shape((tile_count,), jnp.int32), "s"), (shape((n // TILE, window, TILE)), "r"),
        ],
        scratch=(
            pltpu.VMEM((d, n), BF),
            pltpu.VMEM((n // TILE - 2, window, TILE), BF),
            pltpu.VMEM((peers, 128), F32),
            pltpu.SMEM((peers,), jnp.int32),
        ),
        copies=n // TILE,
        us=6,
    )
    send1, agg = call(
        functools.partial(outer_kernel, tile_rows, cap, block_rows),
        [
            (across, "v"), (beside, "v"), (s_out, "v"), (win, "v"), (w01, "v"), (w2t, "v"),
            (w3t, "v"), (pool_out, "v"), (spread, "v"), (ext, "v"), (agg_in, "v"), (owners, "s"),
        ],
        [(shape((peers, chunk + n2 + 16, d)), "r"), (shape((d, n)), "r")],
        scratch=(
            pltpu.VMEM((d, 2 * TILE), BF),
            pltpu.VMEM((peers * chunk, d), F32),
            pltpu.VMEM((peers, chunk, d), BF),
            pltpu.SMEM((peers,), jnp.int32),
        ),
        copies=8,
        us=3,
    )
    got1 = exchange(send1)
    smid, m01, m2t, m3t = call(
        first_window_kernel,
        [(mid_nbrs, "h"), (mid_edge_w, "h"), (weights, "1"), (agg, "r")],
        [
            (shape((n1, n1)), "h"), (shape((d, 2 * d)), "h"), (shape((d, d)), "h"),
            (shape((d, d)), "h"),
        ],
        us=6,
    )
    hid, mid, outer, slope1, slope2, cot, pool_b = call(
        functools.partial(saved_kernel, tile_rows),
        [
            (features, "h"), (agg, "h"), (weights, "0"), (fine_cotangent, "h"),
            (pool_fine, "h"), (m3t, "r"),
        ],
        [
            (shape((d, n)), "h"), (shape((d, n)), "h"), (shape((d, n)), "h"),
            (shape((d, n), F32), "h"), (shape((d, n), F32), "h"), (shape((d, n)), "h"),
            (shape((n // TILE, per, TILE)), "h"),
        ],
        us=4,
    )
    send2, mhid, magg, sel, ext = call(
        functools.partial(mid_kernel, block_rows, chunk),
        [
            (got1, "v"), (smid, "h"), (m01, "h"), (m2t, "h"), (m3t, "h"), (pool_mid, "h"),
            (pool_b, "r"),
        ],
        [
            (shape((peers, n2, d)), "r"), (shape((d, n1)), "h"), (shape((d, n1)), "h"),
            (shape((peers * chunk, n1)), "h"), (shape((peers, n2 + 16, d)), "r"),
        ],
        scratch=(pltpu.VMEM((peers * chunk, d), BF), pltpu.VMEM((n2, d), BF)),
        copies=peers + 1,
        us=3,
    )
    got2 = exchange(send2)
    near = "v" if total2 <= 512 else "h"
    sco, cot_all, cot_back, c01, c2t, mcot, mslope1, mslope2 = call(
        second_window_kernel,
        [
            (ext, "h"), (mhid, "h"), (magg, "h"), (mid_cotangent, "h"), (weights, "1"),
            (weights, "2"),
        ],
        [
            (shape((total2, total2)), near), (shape((d, total2)), near),
            (shape((d, total2), F32), near), (shape((d, 2 * d)), near), (shape((d, d)), near),
            (shape((d, n1)), "h"),
            (shape((d, n1), F32), "h"), (shape((d, n1), F32), "h"),
        ],
        scratch=(pltpu.VMEM((edges, total2), jnp.int32), pltpu.VMEM((edges, total2), F32)),
        us=6,
    )
    send3, gmid, msg, mfg, coarse_wg = call(
        coarse_kernel,
        [
            (got2.reshape(total2, d), "v"), (sco, near), (c01, near), (c2t, near),
            (cot_all, near), (cot_back, near), (weights, "2"),
            (coarse_cotangent, "h"), (pool_mid, "h"), (mcot, "h"), (weights, "1"),
            (mslope2, "h"), (mslope1, "h"), (smid, "h"), (sel, "h"),
        ],
        [
            (shape((peers * chunk, d)), "h"), (shape((d, n1)), "h"), (shape((d, n1)), "h"),
            (shape((d, n1)), "h"), (shape((4, d, d), F32), "h"),
        ],
        us=3,
    )
    got3 = exchange(send3.reshape(peers, chunk, d))
    pick_kind = "v" if peers * chunk <= 1024 else "h"
    mid_wg, pick = call(
        functools.partial(third_window_kernel, 1.0 / math.sqrt(n1 * peers)),
        [
            (mhid, "h"), (magg, "h"), (gmid, "h"), (msg, "h"), (mfg, "h"), (weights, "1"),
            (place, "s"),
        ],
        [
            (shape((4 * d, d)), "v"),
            (shape((tile_count * block_rows, peers * chunk)), pick_kind),
        ],
        us=3,
    )
    reaches = [1 << i for i in range((peers - 1).bit_length())]
    reaches = reaches[:1] + reaches[-1:] + reaches[1:-1]

    def double(total, reach, *after):
        other = lax.ppermute(total, "nodes", [(i, i ^ reach) for i in range(peers)])
        ins = [(total, "v"), (other, "v")] + [(x, "r") for x in after]
        return call(add_kernel, ins, [(shape((4 * d, d)), "v")], us=1)[0]

    sums = [mid_wg]
    for reach in reaches[:2]:
        sums.append(double(sums[-1], reach))
    send4, g, fg = call(
        functools.partial(fine_grad_kernel, 1.0 / math.sqrt(n * peers)),
        [
            (got3.reshape(peers * chunk, d), "v"), (pick, pick_kind), (cot, "h"), (pool_b, "h"),
            (weights, "0"), (slope2, "h"), (slope1, "h"), (hid, "h"), (agg, "h"), (mid, "h"),
            (outer, "h"), (sums[1], "v"),
        ],
        [(shape((4 * d, d)), "h"), (shape((d, n)), "r"), (shape((d, n)), "r")],
        scratch=(pltpu.VMEM((d, n), BF), pltpu.VMEM((d, n), BF)),
        copies=2,
        us=4,
    )
    got4 = exchange(send4.reshape(peers, 4 * d // peers, d))
    rim_near, rim_far, edge_sums, inner_grads = call(
        fine_spread_kernel,
        [(weights, "0"), (g, "h"), (fg, "h"), (s_all, "r"), (sums[2], "v")],
        [
            (shape((HALO, d)), "h"), (shape((HALO, d)), "h"), (shape((2 * HALO, d), F32), "h"),
            (shape((n, d)), "r"),
        ],
        scratch=(
            pltpu.VMEM((n // TILE + 2, TILE, window), BF),
            pltpu.VMEM((d, n + 4 * TILE), BF),
            pltpu.VMEM((n - 2 * HALO, d), BF),
        ),
        copies=3 * (n // TILE) + 1,
        us=4,
    )
    sums.append(double(sums[2], reaches[2], rim_near))
    (send5,) = call(
        sum_kernel,
        [(got4, "v"), (rim_near, "r"), (sums[3], "v")],
        [(shape((peers, 4 * d // peers, d)), "r")],
        scratch=(pltpu.VMEM((4 * d // peers, d), BF),),
        copies=peers,
        us=1,
    )
    got5 = exchange(send5)
    for reach in reaches[3:]:
        sums.append(double(sums[-1], reach))
    from_across = lax.ppermute(rim_near, "nodes", inside_pairs)
    from_beside = lax.ppermute(rim_far, "nodes", between_pairs)
    feature_grads, weight_grads = call(
        join_kernel,
        [
            (edge_sums, "h"), (from_across, "v"), (from_beside, "v"), (coarse_wg, "h"),
            (inner_grads, "r"),
        ],
        [(shape((n, d)), "r"), (shape((12, d, d), F32), "r")],
        scratch=(pltpu.VMEM((2 * HALO, d), BF),),
        copies=3,
        aliases={4: 0},
        us=1,
    )
    (weight_grads,) = call(
        gather_kernel,
        [
            (got5.reshape(4, d, d), "v"), (sums[-1].reshape(4, d, d), "v"), (weight_grads, "r"),
        ],
        [(shape((12, d, d), F32), "r")],
        scratch=(pltpu.VMEM((8, d, d), F32),),
        copies=2,
        aliases={2: 0},
        us=1,
    )
    weight_grads = weight_grads.reshape(3, 4, d, d)
    return (feature_grads, weight_grads)


def solution(mesh):
    rows = P(("groups", "nodes"), None)
    cols = P("groups", "nodes")
    in_specs = (
        rows, rows, rows, rows, P(), cols, cols, cols, rows, P(("groups", "nodes")),
        cols, cols, rows, cols, cols,
    )
    out_specs = (rows, P("groups", None, None, None))
    return jax.shard_map(
        per_device, mesh=mesh, in_specs=in_specs, out_specs=out_specs, check_vma=False
    )
```

```python
import functools
import math

import jax
import jax.numpy as jnp
from jax import lax
from jax.experimental import pallas as pl
from jax.experimental.pallas import tpu as pltpu
from jax.sharding import PartitionSpec as P

HALO = 256
TILE = 256
WIDE = 2048
BF = jnp.bfloat16
F32 = jnp.float32

VM = pl.BlockSpec(memory_space=pltpu.VMEM)
HB = pl.BlockSpec(memory_space=pltpu.HBM)


def dot(a, b):
    return jnp.dot(a, b, preferred_element_type=F32)


def dot_nt(a, b):
    return lax.dot_general(a, b, (((1,), (1,)), ((), ())), preferred_element_type=F32)


def dot_tn(a, b):
    return lax.dot_general(a, b, (((0,), (0,)), ((), ())), preferred_element_type=F32)


def silu(v):
    return v / (1.0 + jnp.exp(-v))


def silu_slope(v):
    s = 1.0 / (1.0 + jnp.exp(-v))
    return s * (1.0 + v * (1.0 - s))


def merged_weights(idx, ew):
    total = ew
    for r in range(1, idx.shape[0]):
        total = total + jnp.where(pltpu.roll(idx, r, 0) == idx, pltpu.roll(ew, r, 0), 0.0)
    return total.astype(BF)


def edge_columns(idx, ew, start, rows):
    count = idx.shape[0]
    lanes = idx.shape[1]
    position = lax.broadcasted_iota(jnp.int32, (rows, lanes), 0) + start
    position = position.astype(jnp.int16)
    picked = jnp.zeros((rows, lanes), BF)
    for k in range(count):
        picked = jnp.where(idx[k : k + 1, :] == position, ew[k : k + 1, :], picked)
    return picked


def fine_edges(off, ew, s_ref):
    for h in range(TILE // 128):
        lane = slice(128 * h, 128 * (h + 1))
        o = off[:, lane]
        weight = merged_weights(o, ew[:, lane])
        rel = o + lax.broadcasted_iota(jnp.int32, o.shape, 1) + HALO
        rel = rel.astype(jnp.int16)
        for c in range(2 * HALO // 128 + 1):
            s_ref[128 * (h + c) : 128 * (h + c + 1), lane] = edge_columns(
                rel, weight, 128 * c, 128
            )


def clear_corners(s_ref):
    for h in range(TILE // 128):
        lane = slice(128 * h, 128 * (h + 1))
        if h > 0:
            s_ref[: 128 * h, lane] = jnp.zeros((128 * h, 128), BF)
        last = 128 * h + 2 * HALO + 128
        if last < TILE + 2 * HALO:
            s_ref[last:, lane] = jnp.zeros((TILE + 2 * HALO - last, 128), BF)


def forward_weights(w):
    w01 = jnp.concatenate([jnp.transpose(w[0]), jnp.transpose(w[1])], axis=1)
    return w01, jnp.transpose(w[2]), jnp.transpose(w[3])


def pool_matrix(pool, tile_rows):
    lane = lax.broadcasted_iota(jnp.int32, pool.shape, 1) // tile_rows
    values = pool.astype(F32)
    parts = [jnp.where(lane == r, values, 0.0) for r in range(pool.shape[1] // tile_rows)]
    return jnp.concatenate(parts, axis=0).astype(BF)


class Copies:
    def __init__(self, sems):
        self.sems = sems
        self.used = 0
        self.open = {}

    def start(self, source, target):
        copy = pltpu.make_async_copy(source, target, self.sems.at[self.used])
        self.used += 1
        copy.start()
        self.open[id(copy)] = copy
        return copy

    def wait(self, *copies):
        for copy in copies:
            if id(copy) in self.open:
                copy.wait()
                del self.open[id(copy)]

    def finish(self):
        self.wait(*list(self.open.values()))


def shape(dims, dtype=BF):
    return jax.ShapeDtypeStruct(dims, dtype)


def call(kernel, ins, outs, scratch=(), copies=0, us=3, mib=24, aliases={}):
    n_in, n_out = len(ins), len(outs)
    staged_in = [i for i, (_, kind) in enumerate(ins) if kind in "hs012"]
    staged_out = [i for i, (_, kind) in enumerate(outs) if kind in "hs"]
    spaces = {"h": pltpu.VMEM, "s": pltpu.SMEM}
    stage = []
    for i in staged_in:
        array, kind = ins[i]
        dims = array.shape[1:] if kind.isdigit() else array.shape
        stage.append(spaces.get(kind, pltpu.VMEM)(dims, array.dtype))
    stage += [spaces[outs[i][1]](outs[i][0].shape, outs[i][0].dtype) for i in staged_out]
    total = len(staged_in) + len(staged_out) + copies

    def body(*refs):
        in_refs, out_refs = list(refs[:n_in]), list(refs[n_in : n_in + n_out])
        rest = list(refs[n_in + n_out :])
        sems = rest.pop() if total else None
        stages, user = rest[: len(stage)], rest[len(stage) :]
        io = Copies(sems)
        pending = {}
        for i, ref in zip(staged_in, stages):
            kind = ins[i][1]
            source = in_refs[i].at[int(kind)] if kind.isdigit() else in_refs[i]
            pending[i] = io.start(source, ref)
            in_refs[i] = ref
        targets = {}
        for i, ref in zip(staged_out, stages[len(staged_in) :]):
            targets[i] = out_refs[i]
            out_refs[i] = ref

        def need(*which):
            io.wait(*[pending[i] for i in which or pending])

        def flush(*which):
            for i in which:
                io.start(out_refs[i], targets.pop(i))

        kernel(io, need, flush, in_refs, out_refs, *user)
        flush(*list(targets))
        io.finish()

    return pl.pallas_call(
        body,
        out_shape=[
            s if kind == "v" else pltpu.HBM(s.shape, s.dtype) for s, kind in outs
        ],
        in_specs=[VM if kind == "v" else HB for _, kind in ins],
        out_specs=[VM if kind == "v" else HB for _, kind in outs],
        scratch_shapes=stage
        + list(scratch)
        + ([pltpu.SemaphoreType.DMA((total,))] if total else []),
        input_output_aliases=aliases,
        compiler_params=pltpu.CompilerParams(vmem_limit_bytes=mib << 20),
        cost_estimate=pl.CostEstimate(
            flops=0, bytes_accessed=int(us * 3_000_000), transcendentals=0
        ),
    )(*[
        a if kind == "v" else pltpu.with_memory_space_constraint(a, pltpu.HBM)
        for a, kind in ins
    ])


def fine_forward(h_t, agg, weights):
    w01, w2t, w3t = weights
    first = dot(w01, jnp.concatenate([h_t, agg], axis=0))
    middle = silu(first).astype(BF)
    second = dot(w2t, middle)
    outer = silu(second).astype(BF)
    return (h_t.astype(F32) + dot(w3t, outer)).astype(BF)


def outer_tiles(tile_count, per):
    return list(range(per)) + list(range(tile_count - per, tile_count))


def inner_kernel(tile_rows, peers, cap, io, need, flush, ins, outs, feat_t, s_ref, ids, counts):
    off, ew, feat, w, pool, owner, slot, nbrs, cew, cot = ins
    so_ref, win_ref, w01_ref, w2t_ref, w3t_ref, po_ref, spread, ext_ref, agg_ref, place = outs
    rows, d = feat.shape
    block_rows = pool.shape[0]
    n2 = cot.shape[0]
    tiles = rows // TILE
    per = TILE // tile_rows
    tile_count = rows // tile_rows
    for i in range(tiles - 2):
        clear_corners(s_ref.at[i])
    clear_corners(so_ref.at[0])
    clear_corners(so_ref.at[1])
    spread[...] = jnp.zeros(spread.shape, F32)
    ids[...] = jnp.full(ids.shape, -1.0, F32)
    for p in range(peers):
        counts[p] = 0
    need(5, 6)
    lane_slot = lax.broadcasted_iota(jnp.int32, (1, 128), 1) // block_rows
    first_tiles = outer_tiles(tile_count, per)
    for t in first_tiles + [t for t in range(tile_count) if t not in first_tiles]:
        o = owner[t]
        c = counts[o]
        counts[o] = c + 1
        place[t] = o * cap + c
        row = ids[pl.ds(o, 1), :]
        ids[pl.ds(o, 1), :] = jnp.where(lane_slot == c, slot[t].astype(F32), row)
    flush(9)
    need(0, 1)
    for n, i in enumerate((0, tiles - 1)):
        cols = slice(i * TILE, (i + 1) * TILE)
        fine_edges(off[:, cols], ew[:, cols], so_ref.at[n])
    need()
    feat_t[...] = jnp.transpose(feat[...])
    weights = forward_weights(w)
    for i in range(1, tiles - 1):
        cols = slice(i * TILE, (i + 1) * TILE)
        fine_edges(off[:, cols], ew[:, cols], s_ref.at[i - 1])
        around = feat_t[:, i * TILE - HALO : (i + 1) * TILE + HALO]
        agg_ref[:, cols] = dot(around, s_ref[i - 1]).astype(BF)
    for start in range(TILE, rows - TILE, WIDE):
        stop = min(start + WIDE, rows - TILE)
        cols = slice(start, stop)
        fine_out = fine_forward(feat_t[:, cols], agg_ref[:, cols], weights)
        for i in range(start // TILE, stop // TILE):
            at = slice(i * TILE - start, (i + 1) * TILE - start)
            matrix = pool_matrix(pool[:, i * TILE : (i + 1) * TILE], tile_rows)
            blocks = dot_nt(matrix, fine_out[:, at])
            for j in range(per):
                at = pl.ds(pl.multiple_of(place[i * per + j] * block_rows, 8), block_rows)
                spread[at, :] = blocks[j * block_rows : (j + 1) * block_rows, :]
    for n, i in enumerate((0, tiles - 1)):
        po_ref[n] = pool_matrix(pool[:, i * TILE : (i + 1) * TILE], tile_rows)
    win_ref[0] = feat_t[:, : TILE + HALO]
    win_ref[1] = feat_t[:, rows - TILE - HALO :]
    w01_ref[...], w2t_ref[...], w3t_ref[...] = weights
    nb = nbrs[...].astype(F32)
    high = jnp.floor(nb * (1.0 / 256.0))
    ce = cew[...]
    ce_high = ce.astype(BF).astype(F32)
    fields = [high, nb - high * 256.0, ce_high, ce - ce_high]
    fields.append(jnp.zeros((nb.shape[0], 128 - 4 * n2), F32))
    top = jnp.concatenate(fields, axis=1)
    sub = lax.broadcasted_iota(jnp.int32, (8, 128), 0)
    for p in range(peers):
        ext_ref[p, 0:n2, :] = cot[...]
        below = jnp.where(sub == 0, ids[p : p + 1, :], 0.0)
        ext_ref[p, n2 : n2 + 16, :] = jnp.concatenate([top, below], axis=0).astype(BF)


def outer_kernel(
    tile_rows, cap, block_rows, io, need, flush, ins, outs, agg_edge, spread, stage, counts
):
    across, beside, s_in, win, w01, w2t, w3t, pool, spread_in, ext, agg_in, owner = ins
    even = lax.rem(lax.axis_index("nodes"), 2) == 0
    left = jnp.where(even, beside[...], across[...])
    right = jnp.where(even, across[...], beside[...])
    send_ref, agg_ref = outs
    peers, chunk, d = stage.shape
    rows = agg_in.shape[1]
    per = TILE // tile_rows
    io.start(ext, send_ref.at[:, pl.ds(chunk, ext.shape[1]), :])
    inside = pl.ds(TILE, rows - 2 * TILE)
    io.start(agg_in.at[:, inside], agg_ref.at[:, inside])
    spread[...] = spread_in[...]
    for p in range(peers):
        counts[p] = 0
    weights = (w01[...], w2t[...], w3t[...])
    for n in range(2):
        if n == 0:
            window_t = jnp.concatenate([jnp.transpose(left), win[0]], axis=1)
        else:
            window_t = jnp.concatenate([win[1], jnp.transpose(right)], axis=1)
        agg_edge[:, n * TILE : (n + 1) * TILE] = dot(window_t, s_in[n]).astype(BF)
    h_t = jnp.concatenate([win[0, :, :TILE], win[1, :, HALO:]], axis=1)
    fine_out = fine_forward(h_t, agg_edge[...], weights)
    results = [dot_nt(pool[n], fine_out[:, n * TILE : (n + 1) * TILE]) for n in range(2)]
    io.start(agg_edge.at[:, pl.ds(0, TILE)], agg_ref.at[:, pl.ds(0, TILE)])
    io.start(agg_edge.at[:, pl.ds(TILE, TILE)], agg_ref.at[:, pl.ds(rows - TILE, TILE)])
    need()
    for j, t in enumerate(outer_tiles(rows // tile_rows, per)):
        o = owner[t]
        c = counts[o]
        counts[o] = c + 1
        at = pl.ds(pl.multiple_of((o * cap + c) * block_rows, 8), block_rows)
        blocks = results[j // per]
        spread[at, :] = blocks[j % per * block_rows : (j % per + 1) * block_rows, :]
    group = max(1, peers // 4)
    for p in range(peers):
        stage[p] = spread[p * chunk : (p + 1) * chunk, :].astype(BF)
        if p % group == group - 1:
            part = pl.ds(p + 1 - group, group)
            io.start(stage.at[part], send_ref.at[part, pl.ds(0, chunk), :])


def mid_edges(nbrs, ew, s_ref):
    nodes = nbrs.shape[1]
    for c in range(nodes // 128):
        lane = slice(128 * c, 128 * (c + 1))
        idx = nbrs[:, lane]
        weight = merged_weights(idx, ew[:, lane])
        idx = idx.astype(jnp.int16)
        for r in range(nodes // 128):
            s_ref[128 * r : 128 * (r + 1), lane] = edge_columns(idx, weight, 128 * r, 128)


def first_window_kernel(io, need, flush, ins, outs):
    nbrs, ew, w, _ = ins
    smid, w01_ref, w2t_ref, w3t_ref = outs
    need(0, 1)
    mid_edges(nbrs, ew, smid)
    flush(0)
    need()
    w01_ref[...], w2t_ref[...], w3t_ref[...] = forward_weights(w)


def mid_kernel(block_rows, chunk, io, need, flush, ins, outs, blocks, coarse):
    got, smid, w01, w2t, w3t, pool_mid, _ = ins
    send_ref, hid_ref, agg_ref, sel_ref, ext_ref = outs
    peers = got.shape[0]
    nodes = smid.shape[0]
    n2 = pool_mid.shape[0]
    io.start(got.at[:, pl.ds(chunk, n2 + 16), :], ext_ref)
    rows = [got[p, chunk + n2 : chunk + n2 + 16, :].astype(F32)[8:9, :] for p in range(peers)]
    keys = jnp.transpose(jnp.concatenate(rows, axis=0))
    keys = keys * block_rows
    keys = keys + (lax.broadcasted_iota(jnp.int32, keys.shape, 0) % block_rows).astype(F32)
    keys = keys.astype(jnp.int32)
    lane = lax.broadcasted_iota(jnp.int32, (chunk, nodes), 1)
    for p in range(peers):
        sel_ref[p * chunk : (p + 1) * chunk, :] = jnp.where(
            keys[0:chunk, p : p + 1] == lane, 1.0, 0.0
        ).astype(BF)
        blocks[p * chunk : (p + 1) * chunk, :] = got[p, 0:chunk, :]
    flush(3)
    hidden = dot_tn(blocks[...], sel_ref[...]).astype(BF)
    hid_ref[...] = hidden
    need()
    agg = dot(hidden, smid[...]).astype(BF)
    agg_ref[...] = agg
    flush(1, 2)
    middle = silu(dot(w01[...], jnp.concatenate([hidden, agg], axis=0))).astype(BF)
    outer = silu(dot(w2t[...], middle)).astype(BF)
    mid_out = (hidden.astype(F32) + dot(w3t[...], outer)).astype(BF)
    coarse[...] = dot_nt(pool_mid[...], mid_out).astype(BF)
    for p in range(peers):
        io.start(coarse, send_ref.at[p])


def second_window_kernel(io, need, flush, ins, outs, nb_ref, ew_ref):
    ext, hid, agg, mid_cot, w1, w2 = ins
    sco, cot_all, back_ref, w01_ref, w2t_ref, mcot, sl1_ref, sl2_ref = outs
    peers = ext.shape[0]
    n2 = ext.shape[1] - 16
    nodes = peers * n2
    edges = nb_ref.shape[0]
    need()
    for p in range(peers):
        part = ext[p, n2 : n2 + 16, :].astype(F32)[0:edges, :]
        at = slice(p * n2, (p + 1) * n2)
        nb_ref[:, at] = (part[:, 0:n2] * 256.0 + part[:, n2 : 2 * n2]).astype(jnp.int32)
        ew_ref[:, at] = part[:, 2 * n2 : 3 * n2] + part[:, 3 * n2 : 4 * n2]
    cots = jnp.concatenate([ext[p, 0:n2, :] for p in range(peers)], axis=0)
    cot_all[...] = jnp.transpose(cots)
    mcot[...] = jnp.transpose(mid_cot[...])

    def column(c, _):
        lane = pl.ds(pl.multiple_of(c * 128, 128), 128)
        idx = nb_ref[:, lane]
        weight = merged_weights(idx, ew_ref[:, lane])
        idx = idx.astype(jnp.int16)
        for r in range(nodes // 128):
            sco[128 * r : 128 * (r + 1), lane] = edge_columns(idx, weight, 128 * r, 128)
        return 0

    lax.fori_loop(0, nodes // 128, column, 0)
    w01_ref[...], w2t_ref[...], _ = forward_weights(w2)
    back_ref[...] = dot(w2[3], cot_all[...])
    w01, w2t, _ = forward_weights(w1)
    first = dot(w01, jnp.concatenate([hid[...], agg[...]], axis=0))
    s1 = 1.0 / (1.0 + jnp.exp(-first))
    second = dot(w2t, (first * s1).astype(BF))
    s2 = 1.0 / (1.0 + jnp.exp(-second))
    sl1_ref[...] = s1 * (1.0 + first * (1.0 - s1))
    sl2_ref[...] = s2 * (1.0 + second * (1.0 - s2))


def coarse_kernel(io, need, flush, ins, outs):
    got, sco, c01, c2t, cot_all, cot_back, w2, *rest = ins
    cot_my, pool_mid, mcot, w1, msl2, msl1, smid, sel = rest
    send_ref, gmid_ref, sg_ref, fg_ref, cwg_ref = outs
    nodes = got.shape[0]
    n2 = cot_my.shape[0]
    me = lax.axis_index("nodes")
    width = min(TILE, nodes)
    hidden = jnp.transpose(got[...])
    if sco.shape[0] > 512:
        need(1, 2, 3, 4, 5)
    w01, w2t = c01[...], c2t[...]
    mine = pl.ds(pl.multiple_of(me * n2, 16), n2)
    mixed = jnp.zeros((2 * n2, 128), F32)
    grads = [jnp.zeros((128, 128), F32) for _ in range(4)]
    row = lax.broadcasted_iota(jnp.int32, (n2, width), 0) + me * n2
    lane = lax.broadcasted_iota(jnp.int32, (n2, width), 1)
    for i in range(nodes // width):
        cols = slice(i * width, (i + 1) * width)
        h = hidden[:, cols]
        agg = dot(hidden, sco[:, cols]).astype(BF)
        first = dot(w01, jnp.concatenate([h, agg], axis=0))
        s1 = 1.0 / (1.0 + jnp.exp(-first))
        middle = (first * s1).astype(BF)
        second = dot(w2t, middle)
        s2 = 1.0 / (1.0 + jnp.exp(-second))
        outer = (second * s2).astype(BF)
        g = cot_all[:, cols]
        if i == 0:
            need(6)
        sg = (cot_back[:, cols] * (s2 * (1.0 + second * (1.0 - s2)))).astype(BF)
        fg = (dot(w2[2], sg) * (s1 * (1.0 + first * (1.0 - s1)))).astype(BF)
        here = jnp.where(lane + i * width == row, 1.0, 0.0).astype(BF)
        mixed = mixed + dot_nt(jnp.concatenate([here, sco[mine, cols]], axis=0), fg)
        grads = [
            grads[0] + dot_nt(h, fg),
            grads[1] + dot_nt(agg, fg),
            grads[2] + dot_nt(middle, sg),
            grads[3] + dot_nt(outer, g),
        ]
    scale = 1.0 / math.sqrt(nodes)
    for m in range(4):
        cwg_ref[m] = grads[m] * scale
    flush(4)
    need(7, 8, 9, 10, 11, 12)
    mixed = mixed.astype(BF)
    into = jnp.concatenate([mixed[:n2], mixed[n2:]], axis=1)
    back_weights = jnp.concatenate([w2[0], w2[1]], axis=1)
    coarse_grad = (cot_my[...].astype(F32) + dot_nt(into, back_weights)).astype(BF)
    back = dot_tn(coarse_grad, pool_mid[...])
    g = (mcot[...].astype(F32) + back).astype(BF)
    gmid_ref[...] = g
    sg = (dot(w1[3], g) * msl2[...]).astype(BF)
    sg_ref[...] = sg
    fg = (dot(w1[2], sg) * msl1[...]).astype(BF)
    fg_ref[...] = fg
    flush(1, 2, 3)
    spill = dot(w1[1], fg).astype(BF)
    need()
    mid_grad = (g.astype(F32) + dot(w1[0], fg) + dot_nt(spill, smid[...])).astype(BF)
    send_ref[...] = dot_nt(sel[...], mid_grad).astype(BF)


def saved_kernel(tile_rows, io, need, flush, ins, outs):
    feat, agg, w, fine_cot, pool, _ = ins
    hid_ref, mid_ref, outer_ref, sl1_ref, sl2_ref, cot_ref, po_ref = outs
    rows = feat.shape[0]
    need(0, 1, 2)
    hid_ref[...] = jnp.transpose(feat[...])
    flush(0)
    w01, w2t, _ = forward_weights(w)
    for start in range(0, rows, 512):
        cols = slice(start, min(start + 512, rows))
        first = dot(w01, jnp.concatenate([hid_ref[:, cols], agg[:, cols]], axis=0))
        s1 = 1.0 / (1.0 + jnp.exp(-first))
        middle = (first * s1).astype(BF)
        mid_ref[:, cols] = middle
        sl1_ref[:, cols] = s1 * (1.0 + first * (1.0 - s1))
        second = dot(w2t, middle)
        s2 = 1.0 / (1.0 + jnp.exp(-second))
        outer_ref[:, cols] = (second * s2).astype(BF)
        sl2_ref[:, cols] = s2 * (1.0 + second * (1.0 - s2))
    need()
    cot_ref[...] = jnp.transpose(fine_cot[...])
    for i in range(rows // TILE):
        po_ref[i] = pool_matrix(pool[:, i * TILE : (i + 1) * TILE], tile_rows)


def third_window_kernel(mid_scale, io, need, flush, ins, outs):
    mhid, magg, gmid, msg, mfg, w1 = ins
    wg_ref = outs[0]
    d = mhid.shape[0]
    need()
    w01, w2t, _ = forward_weights(w1)
    middle = silu(dot(w01, jnp.concatenate([mhid[...], magg[...]], axis=0))).astype(BF)
    outer = silu(dot(w2t, middle)).astype(BF)
    wg_ref[0:d, :] = (dot_nt(mhid[...], mfg[...]) * mid_scale).astype(BF)
    wg_ref[d : 2 * d, :] = (dot_nt(magg[...], mfg[...]) * mid_scale).astype(BF)
    wg_ref[2 * d : 3 * d, :] = (dot_nt(middle, msg[...]) * mid_scale).astype(BF)
    wg_ref[3 * d : 4 * d, :] = (dot_nt(outer, gmid[...]) * mid_scale).astype(BF)


def pick_kernel(block_rows, io, need, flush, ins, outs):
    place = ins[0]
    pick_ref = outs[0]
    need()
    slots = pick_ref.shape[1]
    lane = lax.broadcasted_iota(jnp.int32, (block_rows, slots), 1)
    lane = lane - lax.broadcasted_iota(jnp.int32, (block_rows, slots), 0)
    for t in range(0, place.shape[0], 2):
        both = [jnp.where(lane == place[t + j] * block_rows, 1.0, 0.0) for j in range(2)]
        pick_ref[t * block_rows : (t + 2) * block_rows, :] = jnp.concatenate(
            both, axis=0
        ).astype(BF)


def add_kernel(io, need, flush, ins, outs):
    mine, other = ins[:2]
    outs[0][...] = (mine[...].astype(F32) + other[...].astype(F32)).astype(BF)


def fine_grad_kernel(scale, io, need, flush, ins, outs, g_ref, fg_ref):
    got, pick, cot, pool, w, slope2, slope1, hid, agg, mid, outer, _ = ins
    send_ref, g_out, fg_out = outs
    d, rows = hid.shape
    if pick.shape[1] > 1024:
        need(1)
    blocks = dot(pick[...], got[...]).astype(BF)
    need(2, 3)
    per = pool.shape[1]
    for i in range(rows // TILE):
        cols = slice(i * TILE, (i + 1) * TILE)
        back = dot_tn(blocks[i * per : (i + 1) * per, :], pool[i])
        g_ref[:, cols] = (cot[:, cols].astype(F32) + back).astype(BF)
    io.start(g_ref, g_out)
    g = g_ref[...]
    need(4, 5, 6)
    sg = (dot(w[3], g) * slope2[...]).astype(BF)
    fg = (dot(w[2], sg) * slope1[...]).astype(BF)
    fg_ref[...] = fg
    io.start(fg_ref, fg_out)
    need()
    for m, (a, b) in enumerate(
        ((hid[...], fg), (agg[...], fg), (mid[...], sg), (outer[...], g))
    ):
        send_ref[m * d : (m + 1) * d, :] = (dot_nt(a, b) * scale).astype(BF)


def fine_spread_kernel(io, need, flush, ins, outs, band, spill, inner):
    off, ew, w, g, fg, _ = ins
    rim_near, rim_far, edge_ref, out_ref = outs
    d, rows = g.shape
    tiles = rows // TILE

    def piece(i, h, c):
        row = 128 * (h + c)
        lane = (2 - row // TILE) * TILE + 128 * h
        return band.at[i + row // TILE, pl.ds(row % TILE, 128), pl.ds(lane, 128)]

    def build(i):
        for h in range(TILE // 128):
            lane = slice(i * TILE + 128 * h, i * TILE + 128 * (h + 1))
            o = off[:, lane]
            weight = merged_weights(o, ew[:, lane])
            rel = o + lax.broadcasted_iota(jnp.int32, o.shape, 1) + HALO
            rel = rel.astype(jnp.int16)
            for c in range(2 * HALO // 128 + 1):
                piece(i, h, c)[...] = edge_columns(rel, weight, 128 * c, 128)

    for i in range(tiles):
        piece(i, 0, 5)[...] = jnp.zeros((128, 128), BF)
        piece(i, 1, -1)[...] = jnp.zeros((128, 128), BF)
    for b in (0, 1, tiles, tiles + 1):
        for j in range(3):
            if not 0 <= b - 2 + j < tiles:
                band[b, :, j * TILE : (j + 1) * TILE] = jnp.zeros((TILE, TILE), BF)
    spill[:, : 2 * TILE] = jnp.zeros((d, 2 * TILE), BF)
    spill[:, 2 * TILE + rows :] = jnp.zeros((d, 2 * TILE), BF)
    even = lax.rem(lax.axis_index("nodes"), 2) == 0
    need(0, 1)
    build(0)
    build(tiles - 1)
    need()
    spill[:, 2 * TILE : 2 * TILE + rows] = dot(w[1], fg[...]).astype(BF)
    low, high = [
        dot_nt(band[b], spill[:, b * TILE : (b + 3) * TILE]).astype(BF) for b in (0, tiles + 1)
    ]
    rim_near[...] = jnp.where(even, high, low)
    rim_far[...] = jnp.where(even, low, high)
    flush(0, 1)
    for i in range(1, tiles - 1):
        build(i)
    for b in range(1, tiles + 1):
        part = dot_nt(band[b], spill[:, b * TILE : (b + 3) * TILE])
        cols = slice((b - 1) * TILE, b * TILE)
        part = part + jnp.transpose(g[:, cols].astype(F32) + dot(w[0], fg[:, cols]))
        if b == 1:
            edge_ref[:TILE, :] = part
        elif b == tiles:
            edge_ref[TILE:, :] = part
        else:
            inner[(b - 2) * TILE : (b - 1) * TILE, :] = part.astype(BF)
    io.start(inner, out_ref.at[pl.ds(TILE, rows - 2 * TILE)])


def sum_kernel(io, need, flush, ins, outs, part):
    got = ins[0]
    send_ref = outs[0]
    peers = got.shape[0]
    need()
    part[...] = sum(got[p].astype(F32) for p in range(peers)).astype(BF)
    for p in range(peers):
        io.start(part, send_ref.at[p])


def join_kernel(io, need, flush, ins, outs, joined):
    edge, across, beside, coarse, _ = ins
    out_ref, wg_ref = outs
    rows = out_ref.shape[0]
    even = lax.rem(lax.axis_index("nodes"), 2) == 0
    from_left = jnp.where(even, beside[...], across[...])
    from_right = jnp.where(even, across[...], beside[...])
    need(0)
    joined[:HALO, :] = (edge[:HALO, :] + from_left.astype(F32)).astype(BF)
    joined[HALO:, :] = (edge[HALO:, :] + from_right.astype(F32)).astype(BF)
    io.start(joined.at[pl.ds(0, HALO)], out_ref.at[pl.ds(0, HALO)])
    io.start(joined.at[pl.ds(HALO, HALO)], out_ref.at[pl.ds(rows - HALO, HALO)])
    need()
    io.start(coarse, wg_ref.at[pl.ds(8, 4)])


def gather_kernel(io, need, flush, ins, outs, wide):
    out_ref = outs[0]
    for half in range(2):
        wide[4 * half : 4 * half + 4] = ins[half][...].astype(F32)
        part = pl.ds(4 * half, 4)
        io.start(wide.at[part], out_ref.at[part])


def exchange(x):
    return lax.all_to_all(x, "nodes", split_axis=0, concat_axis=0, tiled=True)


def per_device(
    features,
    fine_cotangent,
    mid_cotangent,
    coarse_cotangent,
    weights,
    fine_offsets,
    fine_edge_w,
    pool_fine,
    owner_dev,
    coarse_slot,
    mid_nbrs,
    mid_edge_w,
    pool_mid,
    coarse_nbrs,
    coarse_edge_w,
):
    n, d = features.shape
    tile_count = owner_dev.shape[0]
    tile_rows = n // tile_count
    block_rows = pool_fine.shape[0]
    n1 = mid_cotangent.shape[0]
    n2 = coarse_cotangent.shape[0]
    edges = fine_offsets.shape[0]
    peers = lax.axis_size("nodes")
    cap = max(2, 2 * tile_count // peers)
    chunk = cap * block_rows
    window = TILE + 2 * HALO
    per = TILE // tile_rows * block_rows
    ends = peers - 1
    inside_pairs = [(i, i ^ 1) for i in range(peers)]
    between_pairs = [(i, ((i + 1) ^ 1) - 1) for i in range(1, ends)]
    total2 = peers * n2

    odd = lax.rem(lax.axis_index("nodes"), 2)
    near = lax.dynamic_slice_in_dim(features, (1 - odd) * (n - HALO), HALO, 0)
    far = lax.dynamic_slice_in_dim(features, odd * (n - HALO), HALO, 0)
    across = lax.ppermute(near, "nodes", inside_pairs)
    beside = lax.ppermute(far, "nodes", between_pairs)
    owners = owner_dev.reshape(-1)
    s_out, win, w01, w2t, w3t, pool_out, spread, ext, agg_in, place = call(
        functools.partial(inner_kernel, tile_rows, peers, cap),
        [
            (fine_offsets, "h"), (fine_edge_w, "h"), (features, "h"), (weights, "0"),
            (pool_fine, "h"), (owners, "s"), (coarse_slot, "s"), (coarse_nbrs, "h"),
            (coarse_edge_w, "h"), (coarse_cotangent, "h"),
        ],
        [
            (shape((2, window, TILE)), "v"), (shape((2, d, TILE + HALO)), "v"),
            (shape((d, 2 * d)), "v"), (shape((d, d)), "v"), (shape((d, d)), "v"),
            (shape((2, per, TILE)), "v"), (shape((peers * chunk, d), F32), "v"),
            (shape((peers, n2 + 16, d)), "v"), (shape((d, n)), "v"),
            (shape((tile_count,), jnp.int32), "s"),
        ],
        scratch=(
            pltpu.VMEM((d, n), BF),
            pltpu.VMEM((n // TILE - 2, window, TILE), BF),
            pltpu.VMEM((peers, 128), F32),
            pltpu.SMEM((peers,), jnp.int32),
        ),
        us=6,
    )
    send1, agg = call(
        functools.partial(outer_kernel, tile_rows, cap, block_rows),
        [
            (across, "v"), (beside, "v"), (s_out, "v"), (win, "v"), (w01, "v"), (w2t, "v"),
            (w3t, "v"), (pool_out, "v"), (spread, "v"), (ext, "v"), (agg_in, "v"), (owners, "s"),
        ],
        [(shape((peers, chunk + n2 + 16, d)), "r"), (shape((d, n)), "r")],
        scratch=(
            pltpu.VMEM((d, 2 * TILE), BF),
            pltpu.VMEM((peers * chunk, d), F32),
            pltpu.VMEM((peers, chunk, d), BF),
            pltpu.SMEM((peers,), jnp.int32),
        ),
        copies=8,
        us=3,
    )
    got1 = exchange(send1)
    smid, m01, m2t, m3t = call(
        first_window_kernel,
        [(mid_nbrs, "h"), (mid_edge_w, "h"), (weights, "1"), (agg, "r")],
        [
            (shape((n1, n1)), "h"), (shape((d, 2 * d)), "h"), (shape((d, d)), "h"),
            (shape((d, d)), "h"),
        ],
        us=6,
    )
    hid, mid, outer, slope1, slope2, cot, pool_b = call(
        functools.partial(saved_kernel, tile_rows),
        [
            (features, "h"), (agg, "h"), (weights, "0"), (fine_cotangent, "h"),
            (pool_fine, "h"), (m3t, "r"),
        ],
        [
            (shape((d, n)), "h"), (shape((d, n)), "h"), (shape((d, n)), "h"),
            (shape((d, n), F32), "h"), (shape((d, n), F32), "h"), (shape((d, n)), "h"),
            (shape((n // TILE, per, TILE)), "h"),
        ],
        us=4,
    )
    send2, mhid, magg, sel, ext = call(
        functools.partial(mid_kernel, block_rows, chunk),
        [
            (got1, "v"), (smid, "h"), (m01, "h"), (m2t, "h"), (m3t, "h"), (pool_mid, "h"),
            (pool_b, "r"),
        ],
        [
            (shape((peers, n2, d)), "r"), (shape((d, n1)), "h"), (shape((d, n1)), "h"),
            (shape((peers * chunk, n1)), "h"), (shape((peers, n2 + 16, d)), "r"),
        ],
        scratch=(pltpu.VMEM((peers * chunk, d), BF), pltpu.VMEM((n2, d), BF)),
        copies=peers + 1,
        us=3,
    )
    got2 = exchange(send2)
    near = "v" if total2 <= 512 else "h"
    sco, cot_all, cot_back, c01, c2t, mcot, mslope1, mslope2 = call(
        second_window_kernel,
        [
            (ext, "h"), (mhid, "h"), (magg, "h"), (mid_cotangent, "h"), (weights, "1"),
            (weights, "2"),
        ],
        [
            (shape((total2, total2)), near), (shape((d, total2)), near),
            (shape((d, total2), F32), near), (shape((d, 2 * d)), near), (shape((d, d)), near),
            (shape((d, n1)), "h"),
            (shape((d, n1), F32), "h"), (shape((d, n1), F32), "h"),
        ],
        scratch=(pltpu.VMEM((edges, total2), jnp.int32), pltpu.VMEM((edges, total2), F32)),
        us=6,
    )
    send3, gmid, msg, mfg, coarse_wg = call(
        coarse_kernel,
        [
            (got2.reshape(total2, d), "v"), (sco, near), (c01, near), (c2t, near),
            (cot_all, near), (cot_back, near), (weights, "2"),
            (coarse_cotangent, "h"), (pool_mid, "h"), (mcot, "h"), (weights, "1"),
            (mslope2, "h"), (mslope1, "h"), (smid, "h"), (sel, "h"),
        ],
        [
            (shape((peers * chunk, d)), "h"), (shape((d, n1)), "h"), (shape((d, n1)), "h"),
            (shape((d, n1)), "h"), (shape((4, d, d), F32), "h"),
        ],
        us=3,
    )
    got3 = exchange(send3.reshape(peers, chunk, d))
    pick_kind = "v" if peers * chunk <= 1024 else "h"
    (mid_wg,) = call(
        functools.partial(third_window_kernel, 1.0 / math.sqrt(n1 * peers)),
        [
            (mhid, "h"), (magg, "h"), (gmid, "h"), (msg, "h"), (mfg, "h"), (weights, "1"),
        ],
        [(shape((4 * d, d)), "v")],
        us=2,
    )
    reaches = [1 << i for i in range((peers - 1).bit_length())]

    def double(total, reach, *after):
        other = lax.ppermute(total, "nodes", [(i, i ^ reach) for i in range(peers)])
        ins = [(total, "v"), (other, "v")] + [(x, "r") for x in after]
        return call(add_kernel, ins, [(shape((4 * d, d)), "v")], us=1)[0]

    sums = [mid_wg]
    for reach in reaches[:3]:
        sums.append(double(sums[-1], reach))
    (pick,) = call(
        functools.partial(pick_kernel, block_rows),
        [(place, "s"), (sums[1], "v")],
        [(shape((tile_count * block_rows, peers * chunk)), pick_kind)],
        us=1,
    )
    send4, g, fg = call(
        functools.partial(fine_grad_kernel, 1.0 / math.sqrt(n * peers)),
        [
            (got3.reshape(peers * chunk, d), "v"), (pick, pick_kind), (cot, "h"), (pool_b, "h"),
            (weights, "0"), (slope2, "h"), (slope1, "h"), (hid, "h"), (agg, "h"), (mid, "h"),
            (outer, "h"), (sums[2], "v"),
        ],
        [(shape((4 * d, d)), "h"), (shape((d, n)), "r"), (shape((d, n)), "r")],
        scratch=(pltpu.VMEM((d, n), BF), pltpu.VMEM((d, n), BF)),
        copies=2,
        us=4,
    )
    got4 = exchange(send4.reshape(peers, 4 * d // peers, d))
    rim_near, rim_far, edge_sums, inner_grads = call(
        fine_spread_kernel,
        [
            (fine_offsets, "h"), (fine_edge_w, "h"), (weights, "0"), (g, "h"), (fg, "h"),
            (sums[3], "v"),
        ],
        [
            (shape((HALO, d)), "h"), (shape((HALO, d)), "h"), (shape((2 * HALO, d), F32), "h"),
            (shape((n, d)), "r"),
        ],
        scratch=(
            pltpu.VMEM((n // TILE + 2, TILE, window), BF),
            pltpu.VMEM((d, n + 4 * TILE), BF),
            pltpu.VMEM((n - 2 * HALO, d), BF),
        ),
        copies=1,
        us=5,
    )
    sums.append(double(sums[3], reaches[3], rim_near))
    (send5,) = call(
        sum_kernel,
        [(got4, "v"), (rim_near, "r"), (sums[4], "v")],
        [(shape((peers, 4 * d // peers, d)), "r")],
        scratch=(pltpu.VMEM((4 * d // peers, d), BF),),
        copies=peers,
        us=1,
    )
    got5 = exchange(send5)
    for reach in reaches[4:]:
        sums.append(double(sums[-1], reach))
    from_across = lax.ppermute(rim_near, "nodes", inside_pairs)
    from_beside = lax.ppermute(rim_far, "nodes", between_pairs)
    feature_grads, weight_grads = call(
        join_kernel,
        [
            (edge_sums, "h"), (from_across, "v"), (from_beside, "v"), (coarse_wg, "h"),
            (inner_grads, "r"),
        ],
        [(shape((n, d)), "r"), (shape((12, d, d), F32), "r")],
        scratch=(pltpu.VMEM((2 * HALO, d), BF),),
        copies=3,
        aliases={4: 0},
        us=1,
    )
    (weight_grads,) = call(
        gather_kernel,
        [
            (got5.reshape(4, d, d), "v"), (sums[-1].reshape(4, d, d), "v"), (weight_grads, "r"),
        ],
        [(shape((12, d, d), F32), "r")],
        scratch=(pltpu.VMEM((8, d, d), F32),),
        copies=2,
        aliases={2: 0},
        us=1,
    )
    weight_grads = weight_grads.reshape(3, 4, d, d)
    return (feature_grads, weight_grads)


def solution(mesh):
    rows = P(("groups", "nodes"), None)
    cols = P("groups", "nodes")
    in_specs = (
        rows, rows, rows, rows, P(), cols, cols, cols, rows, P(("groups", "nodes")),
        cols, cols, rows, cols, cols,
    )
    out_specs = (rows, P("groups", None, None, None))
    return jax.shard_map(
        per_device, mesh=mesh, in_specs=in_specs, out_specs=out_specs, check_vma=False
    )
```

```python
import functools
import math

import jax
import jax.numpy as jnp
from jax import lax
from jax.experimental import pallas as pl
from jax.experimental.pallas import tpu as pltpu
from jax.sharding import PartitionSpec as P

HALO = 256
TILE = 256
WIDE = 2048
BF = jnp.bfloat16
F32 = jnp.float32

VM = pl.BlockSpec(memory_space=pltpu.VMEM)
HB = pl.BlockSpec(memory_space=pltpu.HBM)


def dot(a, b):
    return jnp.dot(a, b, preferred_element_type=F32)


def dot_nt(a, b):
    return lax.dot_general(a, b, (((1,), (1,)), ((), ())), preferred_element_type=F32)


def dot_tn(a, b):
    return lax.dot_general(a, b, (((0,), (0,)), ((), ())), preferred_element_type=F32)


def silu(v):
    return v / (1.0 + jnp.exp(-v))


def silu_slope(v):
    s = 1.0 / (1.0 + jnp.exp(-v))
    return s * (1.0 + v * (1.0 - s))


def merged_weights(idx, ew):
    total = ew
    for r in range(1, idx.shape[0]):
        total = total + jnp.where(pltpu.roll(idx, r, 0) == idx, pltpu.roll(ew, r, 0), 0.0)
    return total.astype(BF)


def edge_columns(idx, ew, start, rows):
    count = idx.shape[0]
    lanes = idx.shape[1]
    position = lax.broadcasted_iota(jnp.int32, (rows, lanes), 0) + start
    position = position.astype(jnp.int16)
    picked = jnp.zeros((rows, lanes), BF)
    for k in range(count):
        picked = jnp.where(idx[k : k + 1, :] == position, ew[k : k + 1, :], picked)
    return picked


def fine_edges(off, ew, s_ref):
    for h in range(TILE // 128):
        lane = slice(128 * h, 128 * (h + 1))
        o = off[:, lane]
        weight = merged_weights(o, ew[:, lane])
        rel = o + lax.broadcasted_iota(jnp.int32, o.shape, 1) + HALO
        rel = rel.astype(jnp.int16)
        for c in range(2 * HALO // 128 + 1):
            s_ref[128 * (h + c) : 128 * (h + c + 1), lane] = edge_columns(
                rel, weight, 128 * c, 128
            )


def clear_corners(s_ref):
    for h in range(TILE // 128):
        lane = slice(128 * h, 128 * (h + 1))
        if h > 0:
            s_ref[: 128 * h, lane] = jnp.zeros((128 * h, 128), BF)
        last = 128 * h + 2 * HALO + 128
        if last < TILE + 2 * HALO:
            s_ref[last:, lane] = jnp.zeros((TILE + 2 * HALO - last, 128), BF)


def forward_weights(w):
    w01 = jnp.concatenate([jnp.transpose(w[0]), jnp.transpose(w[1])], axis=1)
    return w01, jnp.transpose(w[2]), jnp.transpose(w[3])


def pool_matrix(pool, tile_rows):
    lane = lax.broadcasted_iota(jnp.int32, pool.shape, 1) // tile_rows
    values = pool.astype(F32)
    parts = [jnp.where(lane == r, values, 0.0) for r in range(pool.shape[1] // tile_rows)]
    return jnp.concatenate(parts, axis=0).astype(BF)


class Copies:
    def __init__(self, sems):
        self.sems = sems
        self.used = 0
        self.open = {}

    def start(self, source, target):
        copy = pltpu.make_async_copy(source, target, self.sems.at[self.used])
        self.used += 1
        copy.start()
        self.open[id(copy)] = copy
        return copy

    def wait(self, *copies):
        for copy in copies:
            if id(copy) in self.open:
                copy.wait()
                del self.open[id(copy)]

    def finish(self):
        self.wait(*list(self.open.values()))


def shape(dims, dtype=BF):
    return jax.ShapeDtypeStruct(dims, dtype)


def call(kernel, ins, outs, scratch=(), copies=0, us=3, mib=24, aliases={}):
    n_in, n_out = len(ins), len(outs)
    staged_in = [i for i, (_, kind) in enumerate(ins) if kind in "hs012"]
    staged_out = [i for i, (_, kind) in enumerate(outs) if kind in "hs"]
    spaces = {"h": pltpu.VMEM, "s": pltpu.SMEM}
    stage = []
    for i in staged_in:
        array, kind = ins[i]
        dims = array.shape[1:] if kind.isdigit() else array.shape
        stage.append(spaces.get(kind, pltpu.VMEM)(dims, array.dtype))
    stage += [spaces[outs[i][1]](outs[i][0].shape, outs[i][0].dtype) for i in staged_out]
    total = len(staged_in) + len(staged_out) + copies

    def body(*refs):
        in_refs, out_refs = list(refs[:n_in]), list(refs[n_in : n_in + n_out])
        rest = list(refs[n_in + n_out :])
        sems = rest.pop() if total else None
        stages, user = rest[: len(stage)], rest[len(stage) :]
        io = Copies(sems)
        pending = {}
        for i, ref in zip(staged_in, stages):
            kind = ins[i][1]
            source = in_refs[i].at[int(kind)] if kind.isdigit() else in_refs[i]
            pending[i] = io.start(source, ref)
            in_refs[i] = ref
        targets = {}
        for i, ref in zip(staged_out, stages[len(staged_in) :]):
            targets[i] = out_refs[i]
            out_refs[i] = ref

        def need(*which):
            io.wait(*[pending[i] for i in which or pending])

        def flush(*which):
            for i in which:
                io.start(out_refs[i], targets.pop(i))

        kernel(io, need, flush, in_refs, out_refs, *user)
        flush(*list(targets))
        io.finish()

    return pl.pallas_call(
        body,
        out_shape=[
            s if kind == "v" else pltpu.HBM(s.shape, s.dtype) for s, kind in outs
        ],
        in_specs=[VM if kind == "v" else HB for _, kind in ins],
        out_specs=[VM if kind == "v" else HB for _, kind in outs],
        scratch_shapes=stage
        + list(scratch)
        + ([pltpu.SemaphoreType.DMA((total,))] if total else []),
        input_output_aliases=aliases,
        compiler_params=pltpu.CompilerParams(vmem_limit_bytes=mib << 20),
        cost_estimate=pl.CostEstimate(
            flops=0, bytes_accessed=int(us * 3_000_000), transcendentals=0
        ),
    )(*[
        a if kind == "v" else pltpu.with_memory_space_constraint(a, pltpu.HBM)
        for a, kind in ins
    ])


def fine_forward(h_t, agg, weights):
    w01, w2t, w3t = weights
    first = dot(w01, jnp.concatenate([h_t, agg], axis=0))
    middle = silu(first).astype(BF)
    second = dot(w2t, middle)
    outer = silu(second).astype(BF)
    return (h_t.astype(F32) + dot(w3t, outer)).astype(BF)


def outer_tiles(tile_count, per):
    return list(range(per)) + list(range(tile_count - per, tile_count))


def inner_kernel(tile_rows, peers, cap, io, need, flush, ins, outs, feat_t, s_ref, ids, counts):
    off, ew, feat, w, pool, owner, slot, nbrs, cew, cot = ins
    so_ref, win_ref, w01_ref, w2t_ref, w3t_ref, po_ref, spread, ext_ref, agg_ref, place = outs
    rows, d = feat.shape
    block_rows = pool.shape[0]
    n2 = cot.shape[0]
    tiles = rows // TILE
    per = TILE // tile_rows
    tile_count = rows // tile_rows
    for i in range(tiles - 2):
        clear_corners(s_ref.at[i])
    clear_corners(so_ref.at[0])
    clear_corners(so_ref.at[1])
    spread[...] = jnp.zeros(spread.shape, F32)
    ids[...] = jnp.full(ids.shape, -1.0, F32)
    for p in range(peers):
        counts[p] = 0
    need(5, 6)
    lane_slot = lax.broadcasted_iota(jnp.int32, (1, 128), 1) // block_rows
    first_tiles = outer_tiles(tile_count, per)
    for t in first_tiles + [t for t in range(tile_count) if t not in first_tiles]:
        o = owner[t]
        c = counts[o]
        counts[o] = c + 1
        place[t] = o * cap + c
        row = ids[pl.ds(o, 1), :]
        ids[pl.ds(o, 1), :] = jnp.where(lane_slot == c, slot[t].astype(F32), row)
    flush(9)
    need(0, 1)
    for n, i in enumerate((0, tiles - 1)):
        cols = slice(i * TILE, (i + 1) * TILE)
        fine_edges(off[:, cols], ew[:, cols], so_ref.at[n])
    need()
    feat_t[...] = jnp.transpose(feat[...])
    weights = forward_weights(w)
    for i in range(1, tiles - 1):
        cols = slice(i * TILE, (i + 1) * TILE)
        fine_edges(off[:, cols], ew[:, cols], s_ref.at[i - 1])
        around = feat_t[:, i * TILE - HALO : (i + 1) * TILE + HALO]
        agg_ref[:, cols] = dot(around, s_ref[i - 1]).astype(BF)
    for start in range(TILE, rows - TILE, WIDE):
        stop = min(start + WIDE, rows - TILE)
        cols = slice(start, stop)
        fine_out = fine_forward(feat_t[:, cols], agg_ref[:, cols], weights)
        for i in range(start // TILE, stop // TILE):
            at = slice(i * TILE - start, (i + 1) * TILE - start)
            matrix = pool_matrix(pool[:, i * TILE : (i + 1) * TILE], tile_rows)
            blocks = dot_nt(matrix, fine_out[:, at])
            for j in range(per):
                at = pl.ds(pl.multiple_of(place[i * per + j] * block_rows, 8), block_rows)
                spread[at, :] = blocks[j * block_rows : (j + 1) * block_rows, :]
    for n, i in enumerate((0, tiles - 1)):
        po_ref[n] = pool_matrix(pool[:, i * TILE : (i + 1) * TILE], tile_rows)
    win_ref[0] = feat_t[:, : TILE + HALO]
    win_ref[1] = feat_t[:, rows - TILE - HALO :]
    w01_ref[...], w2t_ref[...], w3t_ref[...] = weights
    nb = nbrs[...].astype(F32)
    high = jnp.floor(nb * (1.0 / 256.0))
    ce = cew[...]
    ce_high = ce.astype(BF).astype(F32)
    fields = [high, nb - high * 256.0, ce_high, ce - ce_high]
    fields.append(jnp.zeros((nb.shape[0], 128 - 4 * n2), F32))
    top = jnp.concatenate(fields, axis=1)
    sub = lax.broadcasted_iota(jnp.int32, (8, 128), 0)
    for p in range(peers):
        ext_ref[p, 0:n2, :] = cot[...]
        below = jnp.where(sub == 0, ids[p : p + 1, :], 0.0)
        ext_ref[p, n2 : n2 + 16, :] = jnp.concatenate([top, below], axis=0).astype(BF)


def outer_kernel(
    tile_rows, cap, block_rows, io, need, flush, ins, outs, agg_edge, spread, stage, counts
):
    across, beside, s_in, win, w01, w2t, w3t, pool, spread_in, ext, agg_in, owner = ins
    even = lax.rem(lax.axis_index("nodes"), 2) == 0
    left = jnp.where(even, beside[...], across[...])
    right = jnp.where(even, across[...], beside[...])
    send_ref, agg_ref = outs
    peers, chunk, d = stage.shape
    rows = agg_in.shape[1]
    per = TILE // tile_rows
    io.start(ext, send_ref.at[:, pl.ds(chunk, ext.shape[1]), :])
    inside = pl.ds(TILE, rows - 2 * TILE)
    io.start(agg_in.at[:, inside], agg_ref.at[:, inside])
    spread[...] = spread_in[...]
    for p in range(peers):
        counts[p] = 0
    weights = (w01[...], w2t[...], w3t[...])
    for n in range(2):
        if n == 0:
            window_t = jnp.concatenate([jnp.transpose(left), win[0]], axis=1)
        else:
            window_t = jnp.concatenate([win[1], jnp.transpose(right)], axis=1)
        agg_edge[:, n * TILE : (n + 1) * TILE] = dot(window_t, s_in[n]).astype(BF)
    h_t = jnp.concatenate([win[0, :, :TILE], win[1, :, HALO:]], axis=1)
    fine_out = fine_forward(h_t, agg_edge[...], weights)
    results = [dot_nt(pool[n], fine_out[:, n * TILE : (n + 1) * TILE]) for n in range(2)]
    io.start(agg_edge.at[:, pl.ds(0, TILE)], agg_ref.at[:, pl.ds(0, TILE)])
    io.start(agg_edge.at[:, pl.ds(TILE, TILE)], agg_ref.at[:, pl.ds(rows - TILE, TILE)])
    need()
    for j, t in enumerate(outer_tiles(rows // tile_rows, per)):
        o = owner[t]
        c = counts[o]
        counts[o] = c + 1
        at = pl.ds(pl.multiple_of((o * cap + c) * block_rows, 8), block_rows)
        blocks = results[j // per]
        spread[at, :] = blocks[j % per * block_rows : (j % per + 1) * block_rows, :]
    group = max(1, peers // 4)
    for p in range(peers):
        stage[p] = spread[p * chunk : (p + 1) * chunk, :].astype(BF)
        if p % group == group - 1:
            part = pl.ds(p + 1 - group, group)
            io.start(stage.at[part], send_ref.at[part, pl.ds(0, chunk), :])


def mid_edges(nbrs, ew, s_ref):
    nodes = nbrs.shape[1]
    for c in range(nodes // 128):
        lane = slice(128 * c, 128 * (c + 1))
        idx = nbrs[:, lane]
        weight = merged_weights(idx, ew[:, lane])
        idx = idx.astype(jnp.int16)
        for r in range(nodes // 128):
            s_ref[128 * r : 128 * (r + 1), lane] = edge_columns(idx, weight, 128 * r, 128)


def first_window_kernel(io, need, flush, ins, outs):
    nbrs, ew, w, _ = ins
    smid, w01_ref, w2t_ref, w3t_ref = outs
    need(0, 1)
    mid_edges(nbrs, ew, smid)
    flush(0)
    need()
    w01_ref[...], w2t_ref[...], w3t_ref[...] = forward_weights(w)


def mid_kernel(block_rows, chunk, io, need, flush, ins, outs, blocks, coarse):
    got, smid, w01, w2t, w3t, pool_mid, _ = ins
    send_ref, hid_ref, agg_ref, sel_ref, ext_ref = outs
    peers = got.shape[0]
    nodes = smid.shape[0]
    n2 = pool_mid.shape[0]
    io.start(got.at[:, pl.ds(chunk, n2 + 16), :], ext_ref)
    rows = [got[p, chunk + n2 : chunk + n2 + 16, :].astype(F32)[8:9, :] for p in range(peers)]
    keys = jnp.transpose(jnp.concatenate(rows, axis=0))
    keys = keys * block_rows
    keys = keys + (lax.broadcasted_iota(jnp.int32, keys.shape, 0) % block_rows).astype(F32)
    keys = keys.astype(jnp.int32)
    lane = lax.broadcasted_iota(jnp.int32, (chunk, nodes), 1)
    for p in range(peers):
        sel_ref[p * chunk : (p + 1) * chunk, :] = jnp.where(
            keys[0:chunk, p : p + 1] == lane, 1.0, 0.0
        ).astype(BF)
        blocks[p * chunk : (p + 1) * chunk, :] = got[p, 0:chunk, :]
    flush(3)
    hidden = dot_tn(blocks[...], sel_ref[...]).astype(BF)
    hid_ref[...] = hidden
    need()
    agg = dot(hidden, smid[...]).astype(BF)
    agg_ref[...] = agg
    flush(1, 2)
    middle = silu(dot(w01[...], jnp.concatenate([hidden, agg], axis=0))).astype(BF)
    outer = silu(dot(w2t[...], middle)).astype(BF)
    mid_out = (hidden.astype(F32) + dot(w3t[...], outer)).astype(BF)
    coarse[...] = dot_nt(pool_mid[...], mid_out).astype(BF)
    for p in range(peers):
        io.start(coarse, send_ref.at[p])


def second_window_kernel(io, need, flush, ins, outs, nb_ref, ew_ref):
    ext, hid, agg, mid_cot, w1, w2 = ins
    sco, cot_all, back_ref, w01_ref, w2t_ref, mcot, sl1_ref, sl2_ref = outs
    peers = ext.shape[0]
    n2 = ext.shape[1] - 16
    nodes = peers * n2
    edges = nb_ref.shape[0]
    need()
    for p in range(peers):
        part = ext[p, n2 : n2 + 16, :].astype(F32)[0:edges, :]
        at = slice(p * n2, (p + 1) * n2)
        nb_ref[:, at] = (part[:, 0:n2] * 256.0 + part[:, n2 : 2 * n2]).astype(jnp.int32)
        ew_ref[:, at] = part[:, 2 * n2 : 3 * n2] + part[:, 3 * n2 : 4 * n2]
    cots = jnp.concatenate([ext[p, 0:n2, :] for p in range(peers)], axis=0)
    cot_all[...] = jnp.transpose(cots)
    mcot[...] = jnp.transpose(mid_cot[...])

    def column(c, _):
        lane = pl.ds(pl.multiple_of(c * 128, 128), 128)
        idx = nb_ref[:, lane]
        weight = merged_weights(idx, ew_ref[:, lane])
        idx = idx.astype(jnp.int16)
        for r in range(nodes // 128):
            sco[128 * r : 128 * (r + 1), lane] = edge_columns(idx, weight, 128 * r, 128)
        return 0

    lax.fori_loop(0, nodes // 128, column, 0)
    w01_ref[...], w2t_ref[...], _ = forward_weights(w2)
    back_ref[...] = dot(w2[3], cot_all[...])
    w01, w2t, _ = forward_weights(w1)
    first = dot(w01, jnp.concatenate([hid[...], agg[...]], axis=0))
    s1 = 1.0 / (1.0 + jnp.exp(-first))
    second = dot(w2t, (first * s1).astype(BF))
    s2 = 1.0 / (1.0 + jnp.exp(-second))
    sl1_ref[...] = s1 * (1.0 + first * (1.0 - s1))
    sl2_ref[...] = s2 * (1.0 + second * (1.0 - s2))


def coarse_kernel(io, need, flush, ins, outs):
    got, sco, c01, c2t, cot_all, cot_back, w2, *rest = ins
    cot_my, pool_mid, mcot, w1, msl2, msl1, smid, sel = rest
    send_ref, gmid_ref, sg_ref, fg_ref, cwg_ref = outs
    nodes = got.shape[0]
    n2 = cot_my.shape[0]
    me = lax.axis_index("nodes")
    width = min(TILE, nodes)
    hidden = jnp.transpose(got[...])
    if sco.shape[0] > 512:
        need(1, 2, 3, 4, 5)
    w01, w2t = c01[...], c2t[...]
    mine = pl.ds(pl.multiple_of(me * n2, 16), n2)
    mixed = jnp.zeros((2 * n2, 128), F32)
    grads = [jnp.zeros((128, 128), F32) for _ in range(4)]
    row = lax.broadcasted_iota(jnp.int32, (n2, width), 0) + me * n2
    lane = lax.broadcasted_iota(jnp.int32, (n2, width), 1)
    for i in range(nodes // width):
        cols = slice(i * width, (i + 1) * width)
        h = hidden[:, cols]
        agg = dot(hidden, sco[:, cols]).astype(BF)
        first = dot(w01, jnp.concatenate([h, agg], axis=0))
        s1 = 1.0 / (1.0 + jnp.exp(-first))
        middle = (first * s1).astype(BF)
        second = dot(w2t, middle)
        s2 = 1.0 / (1.0 + jnp.exp(-second))
        outer = (second * s2).astype(BF)
        g = cot_all[:, cols]
        if i == 0:
            need(6)
        sg = (cot_back[:, cols] * (s2 * (1.0 + second * (1.0 - s2)))).astype(BF)
        fg = (dot(w2[2], sg) * (s1 * (1.0 + first * (1.0 - s1)))).astype(BF)
        here = jnp.where(lane + i * width == row, 1.0, 0.0).astype(BF)
        mixed = mixed + dot_nt(jnp.concatenate([here, sco[mine, cols]], axis=0), fg)
        grads = [
            grads[0] + dot_nt(h, fg),
            grads[1] + dot_nt(agg, fg),
            grads[2] + dot_nt(middle, sg),
            grads[3] + dot_nt(outer, g),
        ]
    scale = 1.0 / math.sqrt(nodes)
    for m in range(4):
        cwg_ref[m] = grads[m] * scale
    flush(4)
    need(7, 8, 9, 10, 11, 12)
    mixed = mixed.astype(BF)
    into = jnp.concatenate([mixed[:n2], mixed[n2:]], axis=1)
    back_weights = jnp.concatenate([w2[0], w2[1]], axis=1)
    coarse_grad = (cot_my[...].astype(F32) + dot_nt(into, back_weights)).astype(BF)
    back = dot_tn(coarse_grad, pool_mid[...])
    g = (mcot[...].astype(F32) + back).astype(BF)
    gmid_ref[...] = g
    sg = (dot(w1[3], g) * msl2[...]).astype(BF)
    sg_ref[...] = sg
    fg = (dot(w1[2], sg) * msl1[...]).astype(BF)
    fg_ref[...] = fg
    flush(1, 2, 3)
    spill = dot(w1[1], fg).astype(BF)
    need()
    mid_grad = (g.astype(F32) + dot(w1[0], fg) + dot_nt(spill, smid[...])).astype(BF)
    send_ref[...] = dot_nt(sel[...], mid_grad).astype(BF)


def saved_kernel(tile_rows, io, need, flush, ins, outs):
    feat, agg, w, fine_cot, pool, _ = ins
    hid_ref, mid_ref, outer_ref, sl1_ref, sl2_ref, cot_ref, po_ref = outs
    rows = feat.shape[0]
    need(0, 1, 2)
    hid_ref[...] = jnp.transpose(feat[...])
    flush(0)
    w01, w2t, _ = forward_weights(w)
    for start in range(0, rows, 512):
        cols = slice(start, min(start + 512, rows))
        first = dot(w01, jnp.concatenate([hid_ref[:, cols], agg[:, cols]], axis=0))
        s1 = 1.0 / (1.0 + jnp.exp(-first))
        middle = (first * s1).astype(BF)
        mid_ref[:, cols] = middle
        sl1_ref[:, cols] = (s1 * (1.0 + first * (1.0 - s1))).astype(BF)
        second = dot(w2t, middle)
        s2 = 1.0 / (1.0 + jnp.exp(-second))
        outer_ref[:, cols] = (second * s2).astype(BF)
        sl2_ref[:, cols] = (s2 * (1.0 + second * (1.0 - s2))).astype(BF)
    need()
    cot_ref[...] = jnp.transpose(fine_cot[...])
    for i in range(rows // TILE):
        po_ref[i] = pool_matrix(pool[:, i * TILE : (i + 1) * TILE], tile_rows)


def third_window_kernel(mid_scale, io, need, flush, ins, outs):
    mhid, magg, gmid, msg, mfg, w1 = ins
    wg_ref = outs[0]
    d = mhid.shape[0]
    need()
    w01, w2t, _ = forward_weights(w1)
    middle = silu(dot(w01, jnp.concatenate([mhid[...], magg[...]], axis=0))).astype(BF)
    outer = silu(dot(w2t, middle)).astype(BF)
    wg_ref[0:d, :] = (dot_nt(mhid[...], mfg[...]) * mid_scale).astype(BF)
    wg_ref[d : 2 * d, :] = (dot_nt(magg[...], mfg[...]) * mid_scale).astype(BF)
    wg_ref[2 * d : 3 * d, :] = (dot_nt(middle, msg[...]) * mid_scale).astype(BF)
    wg_ref[3 * d : 4 * d, :] = (dot_nt(outer, gmid[...]) * mid_scale).astype(BF)


def pick_kernel(block_rows, io, need, flush, ins, outs):
    place = ins[0]
    pick_ref = outs[0]
    need()
    slots = pick_ref.shape[1]
    lane = lax.broadcasted_iota(jnp.int32, (block_rows, slots), 1)
    lane = lane - lax.broadcasted_iota(jnp.int32, (block_rows, slots), 0)
    for t in range(0, place.shape[0], 2):
        both = [jnp.where(lane == place[t + j] * block_rows, 1.0, 0.0) for j in range(2)]
        pick_ref[t * block_rows : (t + 2) * block_rows, :] = jnp.concatenate(
            both, axis=0
        ).astype(BF)


def add_kernel(io, need, flush, ins, outs):
    mine, other = ins[:2]
    outs[0][...] = (mine[...].astype(F32) + other[...].astype(F32)).astype(BF)


def fine_grad_kernel(scale, io, need, flush, ins, outs, g_ref, fg_ref):
    got, pick, cot, pool, w, slope2, slope1, hid, agg, mid, outer, _ = ins
    send_ref, g_out, fg_out = outs
    d, rows = hid.shape
    if pick.shape[1] > 1024:
        need(1)
    blocks = dot(pick[...], got[...]).astype(BF)
    need(2, 3)
    per = pool.shape[1]
    for i in range(rows // TILE):
        cols = slice(i * TILE, (i + 1) * TILE)
        back = dot_tn(blocks[i * per : (i + 1) * per, :], pool[i])
        g_ref[:, cols] = (cot[:, cols].astype(F32) + back).astype(BF)
    io.start(g_ref, g_out)
    g = g_ref[...]
    need(4, 5, 6)
    sg = (dot(w[3], g) * slope2[...].astype(F32)).astype(BF)
    fg = (dot(w[2], sg) * slope1[...].astype(F32)).astype(BF)
    fg_ref[...] = fg
    io.start(fg_ref, fg_out)
    need()
    for m, (a, b) in enumerate(
        ((hid[...], fg), (agg[...], fg), (mid[...], sg), (outer[...], g))
    ):
        send_ref[m * d : (m + 1) * d, :] = (dot_nt(a, b) * scale).astype(BF)


def fine_spread_kernel(io, need, flush, ins, outs, band, spill, inner):
    off, ew, w, g, fg, _ = ins
    rim_near, rim_far, edge_ref, out_ref = outs
    d, rows = g.shape
    tiles = rows // TILE

    def piece(i, h, c):
        row = 128 * (h + c)
        lane = (2 - row // TILE) * TILE + 128 * h
        return band.at[i + row // TILE, pl.ds(row % TILE, 128), pl.ds(lane, 128)]

    def build(i):
        for h in range(TILE // 128):
            lane = slice(i * TILE + 128 * h, i * TILE + 128 * (h + 1))
            o = off[:, lane]
            weight = merged_weights(o, ew[:, lane])
            rel = o + lax.broadcasted_iota(jnp.int32, o.shape, 1) + HALO
            rel = rel.astype(jnp.int16)
            for c in range(2 * HALO // 128 + 1):
                piece(i, h, c)[...] = edge_columns(rel, weight, 128 * c, 128)

    for i in range(tiles):
        piece(i, 0, 5)[...] = jnp.zeros((128, 128), BF)
        piece(i, 1, -1)[...] = jnp.zeros((128, 128), BF)
    for b in (0, 1, tiles, tiles + 1):
        for j in range(3):
            if not 0 <= b - 2 + j < tiles:
                band[b, :, j * TILE : (j + 1) * TILE] = jnp.zeros((TILE, TILE), BF)
    spill[:, : 2 * TILE] = jnp.zeros((d, 2 * TILE), BF)
    spill[:, 2 * TILE + rows :] = jnp.zeros((d, 2 * TILE), BF)
    even = lax.rem(lax.axis_index("nodes"), 2) == 0
    need(0, 1)
    build(0)
    build(tiles - 1)
    need()
    spill[:, 2 * TILE : 2 * TILE + rows] = dot(w[1], fg[...]).astype(BF)
    low, high = [
        dot_nt(band[b], spill[:, b * TILE : (b + 3) * TILE]).astype(BF) for b in (0, tiles + 1)
    ]
    rim_near[...] = jnp.where(even, high, low)
    rim_far[...] = jnp.where(even, low, high)
    flush(0, 1)
    for i in range(1, tiles - 1):
        build(i)
    for b in range(1, tiles + 1):
        part = dot_nt(band[b], spill[:, b * TILE : (b + 3) * TILE])
        cols = slice((b - 1) * TILE, b * TILE)
        part = part + jnp.transpose(g[:, cols].astype(F32) + dot(w[0], fg[:, cols]))
        if b == 1:
            edge_ref[:TILE, :] = part
        elif b == tiles:
            edge_ref[TILE:, :] = part
        else:
            inner[(b - 2) * TILE : (b - 1) * TILE, :] = part.astype(BF)
    io.start(inner, out_ref.at[pl.ds(TILE, rows - 2 * TILE)])


def sum_kernel(io, need, flush, ins, outs, part):
    got = ins[0]
    send_ref = outs[0]
    peers = got.shape[0]
    need()
    part[...] = sum(got[p].astype(F32) for p in range(peers)).astype(BF)
    for p in range(peers):
        io.start(part, send_ref.at[p])


def join_kernel(io, need, flush, ins, outs, joined):
    edge, across, beside, coarse, _ = ins
    out_ref, wg_ref = outs
    rows = out_ref.shape[0]
    even = lax.rem(lax.axis_index("nodes"), 2) == 0
    from_left = jnp.where(even, beside[...], across[...])
    from_right = jnp.where(even, across[...], beside[...])
    need(0)
    joined[:HALO, :] = (edge[:HALO, :] + from_left.astype(F32)).astype(BF)
    joined[HALO:, :] = (edge[HALO:, :] + from_right.astype(F32)).astype(BF)
    io.start(joined.at[pl.ds(0, HALO)], out_ref.at[pl.ds(0, HALO)])
    io.start(joined.at[pl.ds(HALO, HALO)], out_ref.at[pl.ds(rows - HALO, HALO)])
    need()
    io.start(coarse, wg_ref.at[pl.ds(8, 4)])


def gather_kernel(io, need, flush, ins, outs, wide):
    out_ref = outs[0]
    for half in range(2):
        wide[4 * half : 4 * half + 4] = ins[half][...].astype(F32)
        part = pl.ds(4 * half, 4)
        io.start(wide.at[part], out_ref.at[part])


def exchange(x):
    return lax.all_to_all(x, "nodes", split_axis=0, concat_axis=0, tiled=True)


def per_device(
    features,
    fine_cotangent,
    mid_cotangent,
    coarse_cotangent,
    weights,
    fine_offsets,
    fine_edge_w,
    pool_fine,
    owner_dev,
    coarse_slot,
    mid_nbrs,
    mid_edge_w,
    pool_mid,
    coarse_nbrs,
    coarse_edge_w,
):
    n, d = features.shape
    tile_count = owner_dev.shape[0]
    tile_rows = n // tile_count
    block_rows = pool_fine.shape[0]
    n1 = mid_cotangent.shape[0]
    n2 = coarse_cotangent.shape[0]
    edges = fine_offsets.shape[0]
    peers = lax.axis_size("nodes")
    cap = max(2, 2 * tile_count // peers)
    chunk = cap * block_rows
    window = TILE + 2 * HALO
    per = TILE // tile_rows * block_rows
    ends = peers - 1
    inside_pairs = [(i, i ^ 1) for i in range(peers)]
    between_pairs = [(i, ((i + 1) ^ 1) - 1) for i in range(1, ends)]
    total2 = peers * n2

    odd = lax.rem(lax.axis_index("nodes"), 2)
    near = lax.dynamic_slice_in_dim(features, (1 - odd) * (n - HALO), HALO, 0)
    far = lax.dynamic_slice_in_dim(features, odd * (n - HALO), HALO, 0)
    across = lax.ppermute(near, "nodes", inside_pairs)
    beside = lax.ppermute(far, "nodes", between_pairs)
    owners = owner_dev.reshape(-1)
    s_out, win, w01, w2t, w3t, pool_out, spread, ext, agg_in, place = call(
        functools.partial(inner_kernel, tile_rows, peers, cap),
        [
            (fine_offsets, "h"), (fine_edge_w, "h"), (features, "h"), (weights, "0"),
            (pool_fine, "h"), (owners, "s"), (coarse_slot, "s"), (coarse_nbrs, "h"),
            (coarse_edge_w, "h"), (coarse_cotangent, "h"),
        ],
        [
            (shape((2, window, TILE)), "v"), (shape((2, d, TILE + HALO)), "v"),
            (shape((d, 2 * d)), "v"), (shape((d, d)), "v"), (shape((d, d)), "v"),
            (shape((2, per, TILE)), "v"), (shape((peers * chunk, d), F32), "v"),
            (shape((peers, n2 + 16, d)), "v"), (shape((d, n)), "v"),
            (shape((tile_count,), jnp.int32), "s"),
        ],
        scratch=(
            pltpu.VMEM((d, n), BF),
            pltpu.VMEM((n // TILE - 2, window, TILE), BF),
            pltpu.VMEM((peers, 128), F32),
            pltpu.SMEM((peers,), jnp.int32),
        ),
        us=6,
    )
    send1, agg = call(
        functools.partial(outer_kernel, tile_rows, cap, block_rows),
        [
            (across, "v"), (beside, "v"), (s_out, "v"), (win, "v"), (w01, "v"), (w2t, "v"),
            (w3t, "v"), (pool_out, "v"), (spread, "v"), (ext, "v"), (agg_in, "v"), (owners, "s"),
        ],
        [(shape((peers, chunk + n2 + 16, d)), "r"), (shape((d, n)), "r")],
        scratch=(
            pltpu.VMEM((d, 2 * TILE), BF),
            pltpu.VMEM((peers * chunk, d), F32),
            pltpu.VMEM((peers, chunk, d), BF),
            pltpu.SMEM((peers,), jnp.int32),
        ),
        copies=8,
        us=3,
    )
    got1 = exchange(send1)
    smid, m01, m2t, m3t = call(
        first_window_kernel,
        [(mid_nbrs, "h"), (mid_edge_w, "h"), (weights, "1"), (agg, "r")],
        [
            (shape((n1, n1)), "h"), (shape((d, 2 * d)), "h"), (shape((d, d)), "h"),
            (shape((d, d)), "h"),
        ],
        us=6,
    )
    hid, mid, outer, slope1, slope2, cot, pool_b = call(
        functools.partial(saved_kernel, tile_rows),
        [
            (features, "h"), (agg, "h"), (weights, "0"), (fine_cotangent, "h"),
            (pool_fine, "h"), (m3t, "r"),
        ],
        [
            (shape((d, n)), "h"), (shape((d, n)), "h"), (shape((d, n)), "h"),
            (shape((d, n)), "h"), (shape((d, n)), "h"), (shape((d, n)), "h"),
            (shape((n // TILE, per, TILE)), "h"),
        ],
        us=4,
    )
    send2, mhid, magg, sel, ext = call(
        functools.partial(mid_kernel, block_rows, chunk),
        [
            (got1, "v"), (smid, "h"), (m01, "h"), (m2t, "h"), (m3t, "h"), (pool_mid, "h"),
            (pool_b, "r"),
        ],
        [
            (shape((peers, n2, d)), "r"), (shape((d, n1)), "h"), (shape((d, n1)), "h"),
            (shape((peers * chunk, n1)), "h"), (shape((peers, n2 + 16, d)), "r"),
        ],
        scratch=(pltpu.VMEM((peers * chunk, d), BF), pltpu.VMEM((n2, d), BF)),
        copies=peers + 1,
        us=3,
    )
    got2 = exchange(send2)
    near = "v" if total2 <= 512 else "h"
    sco, cot_all, cot_back, c01, c2t, mcot, mslope1, mslope2 = call(
        second_window_kernel,
        [
            (ext, "h"), (mhid, "h"), (magg, "h"), (mid_cotangent, "h"), (weights, "1"),
            (weights, "2"),
        ],
        [
            (shape((total2, total2)), near), (shape((d, total2)), near),
            (shape((d, total2), F32), near), (shape((d, 2 * d)), near), (shape((d, d)), near),
            (shape((d, n1)), "h"),
            (shape((d, n1), F32), "h"), (shape((d, n1), F32), "h"),
        ],
        scratch=(pltpu.VMEM((edges, total2), jnp.int32), pltpu.VMEM((edges, total2), F32)),
        us=6,
    )
    send3, gmid, msg, mfg, coarse_wg = call(
        coarse_kernel,
        [
            (got2.reshape(total2, d), "v"), (sco, near), (c01, near), (c2t, near),
            (cot_all, near), (cot_back, near), (weights, "2"),
            (coarse_cotangent, "h"), (pool_mid, "h"), (mcot, "h"), (weights, "1"),
            (mslope2, "h"), (mslope1, "h"), (smid, "h"), (sel, "h"),
        ],
        [
            (shape((peers * chunk, d)), "h"), (shape((d, n1)), "h"), (shape((d, n1)), "h"),
            (shape((d, n1)), "h"), (shape((4, d, d), F32), "h"),
        ],
        us=3,
    )
    got3 = exchange(send3.reshape(peers, chunk, d))
    pick_kind = "v" if peers * chunk <= 1024 else "h"
    (mid_wg,) = call(
        functools.partial(third_window_kernel, 1.0 / math.sqrt(n1 * peers)),
        [
            (mhid, "h"), (magg, "h"), (gmid, "h"), (msg, "h"), (mfg, "h"), (weights, "1"),
        ],
        [(shape((4 * d, d)), "v")],
        us=2,
    )
    reaches = [1 << i for i in range((peers - 1).bit_length())]
    reaches = reaches[:1] + reaches[-1:] + reaches[1:-1]

    def double(total, reach, *after):
        other = lax.ppermute(total, "nodes", [(i, i ^ reach) for i in range(peers)])
        ins = [(total, "v"), (other, "v")] + [(x, "r") for x in after]
        return call(add_kernel, ins, [(shape((4 * d, d)), "v")], us=1)[0]

    sums = [mid_wg]
    for reach in reaches[:2]:
        sums.append(double(sums[-1], reach))
    (pick,) = call(
        functools.partial(pick_kernel, block_rows),
        [(place, "s"), (sums[1], "v")],
        [(shape((tile_count * block_rows, peers * chunk)), pick_kind)],
        us=1,
    )
    send4, g, fg = call(
        functools.partial(fine_grad_kernel, 1.0 / math.sqrt(n * peers)),
        [
            (got3.reshape(peers * chunk, d), "v"), (pick, pick_kind), (cot, "h"), (pool_b, "h"),
            (weights, "0"), (slope2, "h"), (slope1, "h"), (hid, "h"), (agg, "h"), (mid, "h"),
            (outer, "h"), (sums[1], "v"),
        ],
        [(shape((4 * d, d)), "h"), (shape((d, n)), "r"), (shape((d, n)), "r")],
        scratch=(pltpu.VMEM((d, n), BF), pltpu.VMEM((d, n), BF)),
        copies=2,
        us=4,
    )
    got4 = exchange(send4.reshape(peers, 4 * d // peers, d))
    rim_near, rim_far, edge_sums, inner_grads = call(
        fine_spread_kernel,
        [
            (fine_offsets, "h"), (fine_edge_w, "h"), (weights, "0"), (g, "h"), (fg, "h"),
            (sums[2], "v"),
        ],
        [
            (shape((HALO, d)), "h"), (shape((HALO, d)), "h"), (shape((2 * HALO, d), F32), "h"),
            (shape((n, d)), "r"),
        ],
        scratch=(
            pltpu.VMEM((n // TILE + 2, TILE, window), BF),
            pltpu.VMEM((d, n + 4 * TILE), BF),
            pltpu.VMEM((n - 2 * HALO, d), BF),
        ),
        copies=1,
        us=5,
    )
    sums.append(double(sums[2], reaches[2], rim_near))
    (send5,) = call(
        sum_kernel,
        [(got4, "v"), (rim_near, "r"), (sums[3], "v")],
        [(shape((peers, 4 * d // peers, d)), "r")],
        scratch=(pltpu.VMEM((4 * d // peers, d), BF),),
        copies=peers,
        us=1,
    )
    got5 = exchange(send5)
    for reach in reaches[3:]:
        sums.append(double(sums[-1], reach))
    from_across = lax.ppermute(rim_near, "nodes", inside_pairs)
    from_beside = lax.ppermute(rim_far, "nodes", between_pairs)
    feature_grads, weight_grads = call(
        join_kernel,
        [
            (edge_sums, "h"), (from_across, "v"), (from_beside, "v"), (coarse_wg, "h"),
            (inner_grads, "r"),
        ],
        [(shape((n, d)), "r"), (shape((12, d, d), F32), "r")],
        scratch=(pltpu.VMEM((2 * HALO, d), BF),),
        copies=3,
        aliases={4: 0},
        us=1,
    )
    (weight_grads,) = call(
        gather_kernel,
        [
            (got5.reshape(4, d, d), "v"), (sums[-1].reshape(4, d, d), "v"), (weight_grads, "r"),
        ],
        [(shape((12, d, d), F32), "r")],
        scratch=(pltpu.VMEM((8, d, d), F32),),
        copies=2,
        aliases={2: 0},
        us=1,
    )
    weight_grads = weight_grads.reshape(3, 4, d, d)
    return (feature_grads, weight_grads)


def solution(mesh):
    rows = P(("groups", "nodes"), None)
    cols = P("groups", "nodes")
    in_specs = (
        rows, rows, rows, rows, P(), cols, cols, cols, rows, P(("groups", "nodes")),
        cols, cols, rows, cols, cols,
    )
    out_specs = (rows, P("groups", None, None, None))
    return jax.shard_map(
        per_device, mesh=mesh, in_specs=in_specs, out_specs=out_specs, check_vma=False
    )
```

```python
import functools
import math

import jax
import jax.numpy as jnp
from jax import lax
from jax.experimental import pallas as pl
from jax.experimental.pallas import tpu as pltpu
from jax.sharding import PartitionSpec as P

HALO = 256
TILE = 256
WIDE = 2048
BF = jnp.bfloat16
F32 = jnp.float32

VM = pl.BlockSpec(memory_space=pltpu.VMEM)
HB = pl.BlockSpec(memory_space=pltpu.HBM)


def dot(a, b):
    return jnp.dot(a, b, preferred_element_type=F32)


def dot_nt(a, b):
    return lax.dot_general(a, b, (((1,), (1,)), ((), ())), preferred_element_type=F32)


def dot_tn(a, b):
    return lax.dot_general(a, b, (((0,), (0,)), ((), ())), preferred_element_type=F32)


def silu(v):
    return v / (1.0 + jnp.exp(-v))


def silu_slope(v):
    s = 1.0 / (1.0 + jnp.exp(-v))
    return s * (1.0 + v * (1.0 - s))


def merged_weights(idx, ew):
    total = ew
    for r in range(1, idx.shape[0]):
        total = total + jnp.where(pltpu.roll(idx, r, 0) == idx, pltpu.roll(ew, r, 0), 0.0)
    return total.astype(BF)


def edge_columns(idx, ew, start, rows):
    count = idx.shape[0]
    lanes = idx.shape[1]
    position = lax.broadcasted_iota(jnp.int32, (rows, lanes), 0) + start
    position = position.astype(jnp.int16)
    picked = jnp.zeros((rows, lanes), BF)
    for k in range(count):
        picked = jnp.where(idx[k : k + 1, :] == position, ew[k : k + 1, :], picked)
    return picked


def fine_edges(off, ew, s_ref):
    for h in range(TILE // 128):
        lane = slice(128 * h, 128 * (h + 1))
        o = off[:, lane]
        weight = merged_weights(o, ew[:, lane])
        rel = o + lax.broadcasted_iota(jnp.int32, o.shape, 1) + HALO
        rel = rel.astype(jnp.int16)
        for c in range(2 * HALO // 128 + 1):
            s_ref[128 * (h + c) : 128 * (h + c + 1), lane] = edge_columns(
                rel, weight, 128 * c, 128
            )


def clear_corners(s_ref):
    for h in range(TILE // 128):
        lane = slice(128 * h, 128 * (h + 1))
        if h > 0:
            s_ref[: 128 * h, lane] = jnp.zeros((128 * h, 128), BF)
        last = 128 * h + 2 * HALO + 128
        if last < TILE + 2 * HALO:
            s_ref[last:, lane] = jnp.zeros((TILE + 2 * HALO - last, 128), BF)


def forward_weights(w):
    w01 = jnp.concatenate([jnp.transpose(w[0]), jnp.transpose(w[1])], axis=1)
    return w01, jnp.transpose(w[2]), jnp.transpose(w[3])


def pool_matrix(pool, tile_rows):
    lane = lax.broadcasted_iota(jnp.int32, pool.shape, 1) // tile_rows
    values = pool.astype(F32)
    parts = [jnp.where(lane == r, values, 0.0) for r in range(pool.shape[1] // tile_rows)]
    return jnp.concatenate(parts, axis=0).astype(BF)


class Copies:
    def __init__(self, sems):
        self.sems = sems
        self.used = 0
        self.open = {}

    def start(self, source, target):
        copy = pltpu.make_async_copy(source, target, self.sems.at[self.used])
        self.used += 1
        copy.start()
        self.open[id(copy)] = copy
        return copy

    def wait(self, *copies):
        for copy in copies:
            if id(copy) in self.open:
                copy.wait()
                del self.open[id(copy)]

    def finish(self):
        self.wait(*list(self.open.values()))


def shape(dims, dtype=BF):
    return jax.ShapeDtypeStruct(dims, dtype)


def call(kernel, ins, outs, scratch=(), copies=0, us=3, mib=24, aliases={}):
    n_in, n_out = len(ins), len(outs)
    staged_in = [i for i, (_, kind) in enumerate(ins) if kind in "hs012"]
    staged_out = [i for i, (_, kind) in enumerate(outs) if kind in "hs"]
    spaces = {"h": pltpu.VMEM, "s": pltpu.SMEM}
    stage = []
    for i in staged_in:
        array, kind = ins[i]
        dims = array.shape[1:] if kind.isdigit() else array.shape
        stage.append(spaces.get(kind, pltpu.VMEM)(dims, array.dtype))
    stage += [spaces[outs[i][1]](outs[i][0].shape, outs[i][0].dtype) for i in staged_out]
    total = len(staged_in) + len(staged_out) + copies

    def body(*refs):
        in_refs, out_refs = list(refs[:n_in]), list(refs[n_in : n_in + n_out])
        rest = list(refs[n_in + n_out :])
        sems = rest.pop() if total else None
        stages, user = rest[: len(stage)], rest[len(stage) :]
        io = Copies(sems)
        pending = {}
        for i, ref in zip(staged_in, stages):
            kind = ins[i][1]
            source = in_refs[i].at[int(kind)] if kind.isdigit() else in_refs[i]
            pending[i] = io.start(source, ref)
            in_refs[i] = ref
        targets = {}
        for i, ref in zip(staged_out, stages[len(staged_in) :]):
            targets[i] = out_refs[i]
            out_refs[i] = ref

        def need(*which):
            io.wait(*[pending[i] for i in which or pending])

        def flush(*which):
            for i in which:
                io.start(out_refs[i], targets.pop(i))

        kernel(io, need, flush, in_refs, out_refs, *user)
        flush(*list(targets))
        io.finish()

    return pl.pallas_call(
        body,
        out_shape=[
            s if kind == "v" else pltpu.HBM(s.shape, s.dtype) for s, kind in outs
        ],
        in_specs=[VM if kind == "v" else HB for _, kind in ins],
        out_specs=[VM if kind == "v" else HB for _, kind in outs],
        scratch_shapes=stage
        + list(scratch)
        + ([pltpu.SemaphoreType.DMA((total,))] if total else []),
        input_output_aliases=aliases,
        compiler_params=pltpu.CompilerParams(vmem_limit_bytes=mib << 20),
        cost_estimate=pl.CostEstimate(
            flops=0, bytes_accessed=int(us * 3_000_000), transcendentals=0
        ),
    )(*[
        a if kind == "v" else pltpu.with_memory_space_constraint(a, pltpu.HBM)
        for a, kind in ins
    ])


def fine_forward(h_t, agg, weights):
    w01, w2t, w3t = weights
    first = dot(w01, jnp.concatenate([h_t, agg], axis=0))
    middle = silu(first).astype(BF)
    second = dot(w2t, middle)
    outer = silu(second).astype(BF)
    return (h_t.astype(F32) + dot(w3t, outer)).astype(BF)


def outer_tiles(tile_count, per):
    return list(range(per)) + list(range(tile_count - per, tile_count))


def inner_kernel(tile_rows, peers, cap, io, need, flush, ins, outs, feat_t, s_ref, ids, counts):
    off, ew, feat, w, pool, owner, slot, nbrs, cew, cot = ins
    so_ref, win_ref, w01_ref, w2t_ref, w3t_ref, po_ref, spread, ext_ref, agg_ref, place = outs
    rows, d = feat.shape
    block_rows = pool.shape[0]
    n2 = cot.shape[0]
    tiles = rows // TILE
    per = TILE // tile_rows
    tile_count = rows // tile_rows
    for i in range(tiles - 2):
        clear_corners(s_ref.at[i])
    clear_corners(so_ref.at[0])
    clear_corners(so_ref.at[1])
    spread[...] = jnp.zeros(spread.shape, F32)
    ids[...] = jnp.full(ids.shape, -1.0, F32)
    for p in range(peers):
        counts[p] = 0
    need(5, 6)
    lane_slot = lax.broadcasted_iota(jnp.int32, (1, 128), 1) // block_rows
    first_tiles = outer_tiles(tile_count, per)
    for t in first_tiles + [t for t in range(tile_count) if t not in first_tiles]:
        o = owner[t]
        c = counts[o]
        counts[o] = c + 1
        place[t] = o * cap + c
        row = ids[pl.ds(o, 1), :]
        ids[pl.ds(o, 1), :] = jnp.where(lane_slot == c, slot[t].astype(F32), row)
    flush(9)
    need(0, 1)
    for n, i in enumerate((0, tiles - 1)):
        cols = slice(i * TILE, (i + 1) * TILE)
        fine_edges(off[:, cols], ew[:, cols], so_ref.at[n])
    need()
    feat_t[...] = jnp.transpose(feat[...])
    weights = forward_weights(w)
    for i in range(1, tiles - 1):
        cols = slice(i * TILE, (i + 1) * TILE)
        fine_edges(off[:, cols], ew[:, cols], s_ref.at[i - 1])
        around = feat_t[:, i * TILE - HALO : (i + 1) * TILE + HALO]
        agg_ref[:, cols] = dot(around, s_ref[i - 1]).astype(BF)
    for start in range(TILE, rows - TILE, WIDE):
        stop = min(start + WIDE, rows - TILE)
        cols = slice(start, stop)
        fine_out = fine_forward(feat_t[:, cols], agg_ref[:, cols], weights)
        for i in range(start // TILE, stop // TILE):
            at = slice(i * TILE - start, (i + 1) * TILE - start)
            matrix = pool_matrix(pool[:, i * TILE : (i + 1) * TILE], tile_rows)
            blocks = dot_nt(matrix, fine_out[:, at])
            for j in range(per):
                at = pl.ds(pl.multiple_of(place[i * per + j] * block_rows, 8), block_rows)
                spread[at, :] = blocks[j * block_rows : (j + 1) * block_rows, :]
    for n, i in enumerate((0, tiles - 1)):
        po_ref[n] = pool_matrix(pool[:, i * TILE : (i + 1) * TILE], tile_rows)
    win_ref[0] = feat_t[:, : TILE + HALO]
    win_ref[1] = feat_t[:, rows - TILE - HALO :]
    w01_ref[...], w2t_ref[...], w3t_ref[...] = weights
    nb = nbrs[...].astype(F32)
    high = jnp.floor(nb * (1.0 / 256.0))
    ce = cew[...]
    ce_high = ce.astype(BF).astype(F32)
    fields = [high, nb - high * 256.0, ce_high, ce - ce_high]
    fields.append(jnp.zeros((nb.shape[0], 128 - 4 * n2), F32))
    top = jnp.concatenate(fields, axis=1)
    sub = lax.broadcasted_iota(jnp.int32, (8, 128), 0)
    for p in range(peers):
        ext_ref[p, 0:n2, :] = cot[...]
        below = jnp.where(sub == 0, ids[p : p + 1, :], 0.0)
        ext_ref[p, n2 : n2 + 16, :] = jnp.concatenate([top, below], axis=0).astype(BF)


def outer_kernel(
    tile_rows, cap, block_rows, io, need, flush, ins, outs, agg_edge, spread, stage, counts
):
    across, beside, s_in, win, w01, w2t, w3t, pool, spread_in, ext, agg_in, owner = ins
    even = lax.rem(lax.axis_index("nodes"), 2) == 0
    left = jnp.where(even, beside[...], across[...])
    right = jnp.where(even, across[...], beside[...])
    send_ref, agg_ref = outs
    peers, chunk, d = stage.shape
    rows = agg_in.shape[1]
    per = TILE // tile_rows
    io.start(ext, send_ref.at[:, pl.ds(chunk, ext.shape[1]), :])
    inside = pl.ds(TILE, rows - 2 * TILE)
    io.start(agg_in.at[:, inside], agg_ref.at[:, inside])
    spread[...] = spread_in[...]
    for p in range(peers):
        counts[p] = 0
    weights = (w01[...], w2t[...], w3t[...])
    for n in range(2):
        if n == 0:
            window_t = jnp.concatenate([jnp.transpose(left), win[0]], axis=1)
        else:
            window_t = jnp.concatenate([win[1], jnp.transpose(right)], axis=1)
        agg_edge[:, n * TILE : (n + 1) * TILE] = dot(window_t, s_in[n]).astype(BF)
    h_t = jnp.concatenate([win[0, :, :TILE], win[1, :, HALO:]], axis=1)
    fine_out = fine_forward(h_t, agg_edge[...], weights)
    results = [dot_nt(pool[n], fine_out[:, n * TILE : (n + 1) * TILE]) for n in range(2)]
    io.start(agg_edge.at[:, pl.ds(0, TILE)], agg_ref.at[:, pl.ds(0, TILE)])
    io.start(agg_edge.at[:, pl.ds(TILE, TILE)], agg_ref.at[:, pl.ds(rows - TILE, TILE)])
    need()
    for j, t in enumerate(outer_tiles(rows // tile_rows, per)):
        o = owner[t]
        c = counts[o]
        counts[o] = c + 1
        at = pl.ds(pl.multiple_of((o * cap + c) * block_rows, 8), block_rows)
        blocks = results[j // per]
        spread[at, :] = blocks[j % per * block_rows : (j % per + 1) * block_rows, :]
    group = max(1, peers // 4)
    for p in range(peers):
        stage[p] = spread[p * chunk : (p + 1) * chunk, :].astype(BF)
        if p % group == group - 1:
            part = pl.ds(p + 1 - group, group)
            io.start(stage.at[part], send_ref.at[part, pl.ds(0, chunk), :])


def mid_edges(nbrs, ew, s_ref):
    nodes = nbrs.shape[1]
    for c in range(nodes // 128):
        lane = slice(128 * c, 128 * (c + 1))
        idx = nbrs[:, lane]
        weight = merged_weights(idx, ew[:, lane])
        idx = idx.astype(jnp.int16)
        for r in range(nodes // 128):
            s_ref[128 * r : 128 * (r + 1), lane] = edge_columns(idx, weight, 128 * r, 128)


def first_window_kernel(io, need, flush, ins, outs):
    nbrs, ew, w, _ = ins
    smid, w01_ref, w2t_ref, w3t_ref = outs
    need(0, 1)
    mid_edges(nbrs, ew, smid)
    flush(0)
    need()
    w01_ref[...], w2t_ref[...], w3t_ref[...] = forward_weights(w)


def mid_kernel(block_rows, chunk, io, need, flush, ins, outs, blocks, coarse):
    got, smid, w01, w2t, w3, pool_mid, _ = ins
    send_ref, hid_ref, agg_ref, sel_ref, ext_ref = outs
    peers = got.shape[0]
    nodes = smid.shape[0]
    n2 = pool_mid.shape[0]
    io.start(got.at[:, pl.ds(chunk, n2 + 16), :], ext_ref)
    rows = [got[p, chunk + n2 : chunk + n2 + 16, :].astype(F32)[8:9, :] for p in range(peers)]
    keys = jnp.transpose(jnp.concatenate(rows, axis=0))
    keys = keys * block_rows
    keys = keys + (lax.broadcasted_iota(jnp.int32, keys.shape, 0) % block_rows).astype(F32)
    keys = keys.astype(jnp.int32)
    lane = lax.broadcasted_iota(jnp.int32, (chunk, nodes), 1)
    for p in range(peers):
        sel_ref[p * chunk : (p + 1) * chunk, :] = jnp.where(
            keys[0:chunk, p : p + 1] == lane, 1.0, 0.0
        ).astype(BF)
        blocks[p * chunk : (p + 1) * chunk, :] = got[p, 0:chunk, :]
    flush(3)
    hidden = dot_tn(blocks[...], sel_ref[...]).astype(BF)
    hid_ref[...] = hidden
    need()
    agg = dot(hidden, smid[...]).astype(BF)
    agg_ref[...] = agg
    flush(1, 2)
    middle = silu(dot(w01[...], jnp.concatenate([hidden, agg], axis=0))).astype(BF)
    outer = silu(dot(w2t[...], middle)).astype(BF)
    pooled = dot_nt(pool_mid[...], outer).astype(BF)
    coarse[...] = (dot_nt(pool_mid[...], hidden) + dot(pooled, w3[3])).astype(BF)
    for p in range(peers):
        io.start(coarse, send_ref.at[p])


def second_window_kernel(io, need, flush, ins, outs, nb_ref, ew_ref):
    ext, hid, agg, mid_cot, w1, w2 = ins
    sco, cot_all, back_ref, w01_ref, w2t_ref, mcot, sl1_ref, sl2_ref = outs
    peers = ext.shape[0]
    n2 = ext.shape[1] - 16
    nodes = peers * n2
    edges = nb_ref.shape[0]
    need()
    for p in range(peers):
        part = ext[p, n2 : n2 + 16, :].astype(F32)[0:edges, :]
        at = slice(p * n2, (p + 1) * n2)
        nb_ref[:, at] = (part[:, 0:n2] * 256.0 + part[:, n2 : 2 * n2]).astype(jnp.int32)
        ew_ref[:, at] = part[:, 2 * n2 : 3 * n2] + part[:, 3 * n2 : 4 * n2]
    cots = jnp.concatenate([ext[p, 0:n2, :] for p in range(peers)], axis=0)
    cot_all[...] = jnp.transpose(cots)
    mcot[...] = jnp.transpose(mid_cot[...])

    def column(c, _):
        lane = pl.ds(pl.multiple_of(c * 128, 128), 128)
        idx = nb_ref[:, lane]
        weight = merged_weights(idx, ew_ref[:, lane])
        idx = idx.astype(jnp.int16)
        for r in range(nodes // 128):
            sco[128 * r : 128 * (r + 1), lane] = edge_columns(idx, weight, 128 * r, 128)
        return 0

    lax.fori_loop(0, nodes // 128, column, 0)
    w01_ref[...], w2t_ref[...], _ = forward_weights(w2)
    back_ref[...] = dot(w2[3], cot_all[...])
    w01, w2t, _ = forward_weights(w1)
    first = dot(w01, jnp.concatenate([hid[...], agg[...]], axis=0))
    s1 = 1.0 / (1.0 + jnp.exp(-first))
    second = dot(w2t, (first * s1).astype(BF))
    s2 = 1.0 / (1.0 + jnp.exp(-second))
    sl1_ref[...] = s1 * (1.0 + first * (1.0 - s1))
    sl2_ref[...] = s2 * (1.0 + second * (1.0 - s2))


def coarse_kernel(io, need, flush, ins, outs):
    got, sco, c01, c2t, cot_all, cot_back, w2, *rest = ins
    cot_my, pool_mid, mcot, w1, msl2, msl1, smid, sel = rest
    send_ref, gmid_ref, sg_ref, fg_ref, cwg_ref = outs
    nodes = got.shape[0]
    n2 = cot_my.shape[0]
    me = lax.axis_index("nodes")
    width = min(TILE, nodes)
    hidden = jnp.transpose(got[...])
    if sco.shape[0] > 512:
        need(1, 2, 3, 4, 5)
    w01, w2t = c01[...], c2t[...]
    mine = pl.ds(pl.multiple_of(me * n2, 16), n2)
    mixed = jnp.zeros((2 * n2, 128), F32)
    grads = [jnp.zeros((128, 128), F32) for _ in range(4)]
    row = lax.broadcasted_iota(jnp.int32, (n2, width), 0) + me * n2
    lane = lax.broadcasted_iota(jnp.int32, (n2, width), 1)
    for i in range(nodes // width):
        cols = slice(i * width, (i + 1) * width)
        h = hidden[:, cols]
        agg = dot(hidden, sco[:, cols]).astype(BF)
        first = dot(w01, jnp.concatenate([h, agg], axis=0))
        s1 = 1.0 / (1.0 + jnp.exp(-first))
        middle = (first * s1).astype(BF)
        second = dot(w2t, middle)
        s2 = 1.0 / (1.0 + jnp.exp(-second))
        outer = (second * s2).astype(BF)
        g = cot_all[:, cols]
        if i == 0:
            need(6)
        sg = (cot_back[:, cols] * (s2 * (1.0 + second * (1.0 - s2)))).astype(BF)
        fg = (dot(w2[2], sg) * (s1 * (1.0 + first * (1.0 - s1)))).astype(BF)
        here = jnp.where(lane + i * width == row, 1.0, 0.0).astype(BF)
        mixed = mixed + dot_nt(jnp.concatenate([here, sco[mine, cols]], axis=0), fg)
        grads = [
            grads[0] + dot_nt(h, fg),
            grads[1] + dot_nt(agg, fg),
            grads[2] + dot_nt(middle, sg),
            grads[3] + dot_nt(outer, g),
        ]
    scale = 1.0 / math.sqrt(nodes)
    for m in range(4):
        cwg_ref[m] = grads[m] * scale
    flush(4)
    need(7, 8, 9, 10, 11, 12)
    mixed = mixed.astype(BF)
    into = jnp.concatenate([mixed[:n2], mixed[n2:]], axis=1)
    back_weights = jnp.concatenate([w2[0], w2[1]], axis=1)
    coarse_grad = (cot_my[...].astype(F32) + dot_nt(into, back_weights)).astype(BF)
    back = dot_tn(coarse_grad, pool_mid[...])
    g = (mcot[...].astype(F32) + back).astype(BF)
    gmid_ref[...] = g
    sg = (dot(w1[3], g) * msl2[...]).astype(BF)
    sg_ref[...] = sg
    fg = (dot(w1[2], sg) * msl1[...]).astype(BF)
    fg_ref[...] = fg
    flush(1, 2, 3)
    spill = dot(w1[1], fg).astype(BF)
    need()
    mid_grad = (g.astype(F32) + dot(w1[0], fg) + dot_nt(spill, smid[...])).astype(BF)
    send_ref[...] = dot_nt(sel[...], mid_grad).astype(BF)


def saved_kernel(tile_rows, io, need, flush, ins, outs):
    feat, agg, w, fine_cot, pool, _ = ins
    hid_ref, mid_ref, outer_ref, sl1_ref, sl2_ref, cot_ref, po_ref = outs
    rows = feat.shape[0]
    need(0, 1, 2)
    hid_ref[...] = jnp.transpose(feat[...])
    flush(0)
    w01, w2t, _ = forward_weights(w)
    for start in range(0, rows, 512):
        cols = slice(start, min(start + 512, rows))
        first = dot(w01, jnp.concatenate([hid_ref[:, cols], agg[:, cols]], axis=0))
        s1 = 1.0 / (1.0 + jnp.exp(-first))
        middle = (first * s1).astype(BF)
        mid_ref[:, cols] = middle
        sl1_ref[:, cols] = (s1 * (1.0 + first * (1.0 - s1))).astype(BF)
        second = dot(w2t, middle)
        s2 = 1.0 / (1.0 + jnp.exp(-second))
        outer_ref[:, cols] = (second * s2).astype(BF)
        sl2_ref[:, cols] = (s2 * (1.0 + second * (1.0 - s2))).astype(BF)
    need()
    cot_ref[...] = jnp.transpose(fine_cot[...])
    for i in range(rows // TILE):
        po_ref[i] = pool_matrix(pool[:, i * TILE : (i + 1) * TILE], tile_rows)


def third_window_kernel(mid_scale, io, need, flush, ins, outs):
    mhid, magg, gmid, msg, mfg, w1 = ins
    wg_ref = outs[0]
    d = mhid.shape[0]
    need()
    w01, w2t, _ = forward_weights(w1)
    middle = silu(dot(w01, jnp.concatenate([mhid[...], magg[...]], axis=0))).astype(BF)
    outer = silu(dot(w2t, middle)).astype(BF)
    wg_ref[0:d, :] = (dot_nt(mhid[...], mfg[...]) * mid_scale).astype(BF)
    wg_ref[d : 2 * d, :] = (dot_nt(magg[...], mfg[...]) * mid_scale).astype(BF)
    wg_ref[2 * d : 3 * d, :] = (dot_nt(middle, msg[...]) * mid_scale).astype(BF)
    wg_ref[3 * d : 4 * d, :] = (dot_nt(outer, gmid[...]) * mid_scale).astype(BF)


def pick_kernel(block_rows, io, need, flush, ins, outs):
    place = ins[0]
    pick_ref = outs[0]
    need()
    slots = pick_ref.shape[1]
    lane = lax.broadcasted_iota(jnp.int32, (block_rows, slots), 1)
    lane = lane - lax.broadcasted_iota(jnp.int32, (block_rows, slots), 0)
    for t in range(0, place.shape[0], 2):
        both = [jnp.where(lane == place[t + j] * block_rows, 1.0, 0.0) for j in range(2)]
        pick_ref[t * block_rows : (t + 2) * block_rows, :] = jnp.concatenate(
            both, axis=0
        ).astype(BF)


def fine_grad_kernel(scale, io, need, flush, ins, outs, g_ref, fg_ref):
    got, pick, cot, pool, w, slope2, slope1, hid, agg, mid, outer, mid_wg = ins
    send_ref, g_out, fg_out = outs
    d, rows = hid.shape
    if pick.shape[1] > 1024:
        need(1)
    blocks = dot(pick[...], got[...]).astype(BF)
    send_ref[4 * d : 8 * d, :] = mid_wg[...]
    need(2, 3)
    per = pool.shape[1]
    for i in range(rows // TILE):
        cols = slice(i * TILE, (i + 1) * TILE)
        back = dot_tn(blocks[i * per : (i + 1) * per, :], pool[i])
        g_ref[:, cols] = (cot[:, cols].astype(F32) + back).astype(BF)
    io.start(g_ref, g_out)
    g = g_ref[...]
    need(4, 5, 6)
    sg = (dot(w[3], g) * slope2[...].astype(F32)).astype(BF)
    fg = (dot(w[2], sg) * slope1[...].astype(F32)).astype(BF)
    fg_ref[...] = fg
    io.start(fg_ref, fg_out)
    need()
    for m, (a, b) in enumerate(
        ((hid[...], fg), (agg[...], fg), (mid[...], sg), (outer[...], g))
    ):
        send_ref[m * d : (m + 1) * d, :] = (dot_nt(a, b) * scale).astype(BF)


def fine_spread_kernel(io, need, flush, ins, outs, band, spill, inner):
    off, ew, w, g, fg = ins
    rim_near, rim_far, edge_ref, out_ref = outs
    d, rows = g.shape
    tiles = rows // TILE

    def piece(i, h, c):
        row = 128 * (h + c)
        lane = (2 - row // TILE) * TILE + 128 * h
        return band.at[i + row // TILE, pl.ds(row % TILE, 128), pl.ds(lane, 128)]

    def build(i):
        for h in range(TILE // 128):
            lane = slice(i * TILE + 128 * h, i * TILE + 128 * (h + 1))
            o = off[:, lane]
            weight = merged_weights(o, ew[:, lane])
            rel = o + lax.broadcasted_iota(jnp.int32, o.shape, 1) + HALO
            rel = rel.astype(jnp.int16)
            for c in range(2 * HALO // 128 + 1):
                piece(i, h, c)[...] = edge_columns(rel, weight, 128 * c, 128)

    for i in range(tiles):
        piece(i, 0, 5)[...] = jnp.zeros((128, 128), BF)
        piece(i, 1, -1)[...] = jnp.zeros((128, 128), BF)
    for b in (0, 1, tiles, tiles + 1):
        for j in range(3):
            if not 0 <= b - 2 + j < tiles:
                band[b, :, j * TILE : (j + 1) * TILE] = jnp.zeros((TILE, TILE), BF)
    spill[:, : 2 * TILE] = jnp.zeros((d, 2 * TILE), BF)
    spill[:, 2 * TILE + rows :] = jnp.zeros((d, 2 * TILE), BF)
    even = lax.rem(lax.axis_index("nodes"), 2) == 0
    need(0, 1)
    build(0)
    build(tiles - 1)
    need()
    spill[:, 2 * TILE : 2 * TILE + rows] = dot(w[1], fg[...]).astype(BF)
    low, high = [
        dot_nt(band[b], spill[:, b * TILE : (b + 3) * TILE]).astype(BF) for b in (0, tiles + 1)
    ]
    rim_near[...] = jnp.where(even, high, low)
    rim_far[...] = jnp.where(even, low, high)
    flush(0, 1)
    for i in range(1, tiles - 1):
        build(i)
    for b in range(1, tiles + 1):
        part = dot_nt(band[b], spill[:, b * TILE : (b + 3) * TILE])
        cols = slice((b - 1) * TILE, b * TILE)
        part = part + jnp.transpose(g[:, cols].astype(F32) + dot(w[0], fg[:, cols]))
        if b == 1:
            edge_ref[:TILE, :] = part
        elif b == tiles:
            edge_ref[TILE:, :] = part
        else:
            inner[(b - 2) * TILE : (b - 1) * TILE, :] = part.astype(BF)
    io.start(inner, out_ref.at[pl.ds(TILE, rows - 2 * TILE)])


def sum_kernel(io, need, flush, ins, outs, part):
    got = ins[0]
    send_ref = outs[0]
    peers = got.shape[0]
    need()
    part[...] = sum(got[p].astype(F32) for p in range(peers)).astype(BF)
    for p in range(peers):
        io.start(part, send_ref.at[p])


def join_kernel(io, need, flush, ins, outs, joined):
    edge, across, beside, coarse, _ = ins
    out_ref, wg_ref = outs
    rows = out_ref.shape[0]
    even = lax.rem(lax.axis_index("nodes"), 2) == 0
    from_left = jnp.where(even, beside[...], across[...])
    from_right = jnp.where(even, across[...], beside[...])
    need(0)
    joined[:HALO, :] = (edge[:HALO, :] + from_left.astype(F32)).astype(BF)
    joined[HALO:, :] = (edge[HALO:, :] + from_right.astype(F32)).astype(BF)
    io.start(joined.at[pl.ds(0, HALO)], out_ref.at[pl.ds(0, HALO)])
    io.start(joined.at[pl.ds(HALO, HALO)], out_ref.at[pl.ds(rows - HALO, HALO)])
    need()
    io.start(coarse, wg_ref.at[pl.ds(8, 4)])


def gather_kernel(io, need, flush, ins, outs, wide):
    out_ref = outs[0]
    for half in range(2):
        wide[4 * half : 4 * half + 4] = ins[0][4 * half : 4 * half + 4].astype(F32)
        part = pl.ds(4 * half, 4)
        io.start(wide.at[part], out_ref.at[part])


def exchange(x):
    return lax.all_to_all(x, "nodes", split_axis=0, concat_axis=0, tiled=True)


def per_device(
    features,
    fine_cotangent,
    mid_cotangent,
    coarse_cotangent,
    weights,
    fine_offsets,
    fine_edge_w,
    pool_fine,
    owner_dev,
    coarse_slot,
    mid_nbrs,
    mid_edge_w,
    pool_mid,
    coarse_nbrs,
    coarse_edge_w,
):
    n, d = features.shape
    tile_count = owner_dev.shape[0]
    tile_rows = n // tile_count
    block_rows = pool_fine.shape[0]
    n1 = mid_cotangent.shape[0]
    n2 = coarse_cotangent.shape[0]
    edges = fine_offsets.shape[0]
    peers = lax.axis_size("nodes")
    cap = max(2, 2 * tile_count // peers)
    chunk = cap * block_rows
    window = TILE + 2 * HALO
    per = TILE // tile_rows * block_rows
    ends = peers - 1
    inside_pairs = [(i, i ^ 1) for i in range(peers)]
    between_pairs = [(i, ((i + 1) ^ 1) - 1) for i in range(1, ends)]
    total2 = peers * n2

    odd = lax.rem(lax.axis_index("nodes"), 2)
    near = lax.dynamic_slice_in_dim(features, (1 - odd) * (n - HALO), HALO, 0)
    far = lax.dynamic_slice_in_dim(features, odd * (n - HALO), HALO, 0)
    across = lax.ppermute(near, "nodes", inside_pairs)
    beside = lax.ppermute(far, "nodes", between_pairs)
    owners = owner_dev.reshape(-1)
    s_out, win, w01, w2t, w3t, pool_out, spread, ext, agg_in, place = call(
        functools.partial(inner_kernel, tile_rows, peers, cap),
        [
            (fine_offsets, "h"), (fine_edge_w, "h"), (features, "h"), (weights, "0"),
            (pool_fine, "h"), (owners, "s"), (coarse_slot, "s"), (coarse_nbrs, "h"),
            (coarse_edge_w, "h"), (coarse_cotangent, "h"),
        ],
        [
            (shape((2, window, TILE)), "v"), (shape((2, d, TILE + HALO)), "v"),
            (shape((d, 2 * d)), "v"), (shape((d, d)), "v"), (shape((d, d)), "v"),
            (shape((2, per, TILE)), "v"), (shape((peers * chunk, d), F32), "v"),
            (shape((peers, n2 + 16, d)), "v"), (shape((d, n)), "v"),
            (shape((tile_count,), jnp.int32), "s"),
        ],
        scratch=(
            pltpu.VMEM((d, n), BF),
            pltpu.VMEM((n // TILE - 2, window, TILE), BF),
            pltpu.VMEM((peers, 128), F32),
            pltpu.SMEM((peers,), jnp.int32),
        ),
        us=6,
    )
    send1, agg = call(
        functools.partial(outer_kernel, tile_rows, cap, block_rows),
        [
            (across, "v"), (beside, "v"), (s_out, "v"), (win, "v"), (w01, "v"), (w2t, "v"),
            (w3t, "v"), (pool_out, "v"), (spread, "v"), (ext, "v"), (agg_in, "v"), (owners, "s"),
        ],
        [(shape((peers, chunk + n2 + 16, d)), "r"), (shape((d, n)), "r")],
        scratch=(
            pltpu.VMEM((d, 2 * TILE), BF),
            pltpu.VMEM((peers * chunk, d), F32),
            pltpu.VMEM((peers, chunk, d), BF),
            pltpu.SMEM((peers,), jnp.int32),
        ),
        copies=8,
        us=3,
    )
    got1 = exchange(send1)
    smid, m01, m2t, m3t = call(
        first_window_kernel,
        [(mid_nbrs, "h"), (mid_edge_w, "h"), (weights, "1"), (agg, "r")],
        [
            (shape((n1, n1)), "h"), (shape((d, 2 * d)), "h"), (shape((d, d)), "h"),
            (shape((d, d)), "h"),
        ],
        us=6,
    )
    hid, mid, outer, slope1, slope2, cot, pool_b = call(
        functools.partial(saved_kernel, tile_rows),
        [
            (features, "h"), (agg, "h"), (weights, "0"), (fine_cotangent, "h"),
            (pool_fine, "h"), (m3t, "r"),
        ],
        [
            (shape((d, n)), "h"), (shape((d, n)), "h"), (shape((d, n)), "h"),
            (shape((d, n)), "h"), (shape((d, n)), "h"), (shape((d, n)), "h"),
            (shape((n // TILE, per, TILE)), "h"),
        ],
        us=4,
    )
    send2, mhid, magg, sel, ext = call(
        functools.partial(mid_kernel, block_rows, chunk),
        [
            (got1, "v"), (smid, "h"), (m01, "h"), (m2t, "h"), (weights, "1"), (pool_mid, "h"),
            (pool_b, "r"),
        ],
        [
            (shape((peers, n2, d)), "r"), (shape((d, n1)), "h"), (shape((d, n1)), "h"),
            (shape((peers * chunk, n1)), "h"), (shape((peers, n2 + 16, d)), "r"),
        ],
        scratch=(pltpu.VMEM((peers * chunk, d), BF), pltpu.VMEM((n2, d), BF)),
        copies=peers + 1,
        us=3,
    )
    got2 = exchange(send2)
    near = "v" if total2 <= 512 else "h"
    sco, cot_all, cot_back, c01, c2t, mcot, mslope1, mslope2 = call(
        second_window_kernel,
        [
            (ext, "h"), (mhid, "h"), (magg, "h"), (mid_cotangent, "h"), (weights, "1"),
            (weights, "2"),
        ],
        [
            (shape((total2, total2)), near), (shape((d, total2)), near),
            (shape((d, total2), F32), near), (shape((d, 2 * d)), near), (shape((d, d)), near),
            (shape((d, n1)), "h"),
            (shape((d, n1), F32), "h"), (shape((d, n1), F32), "h"),
        ],
        scratch=(pltpu.VMEM((edges, total2), jnp.int32), pltpu.VMEM((edges, total2), F32)),
        us=6,
    )
    send3, gmid, msg, mfg, coarse_wg = call(
        coarse_kernel,
        [
            (got2.reshape(total2, d), "v"), (sco, near), (c01, near), (c2t, near),
            (cot_all, near), (cot_back, near), (weights, "2"),
            (coarse_cotangent, "h"), (pool_mid, "h"), (mcot, "h"), (weights, "1"),
            (mslope2, "h"), (mslope1, "h"), (smid, "h"), (sel, "h"),
        ],
        [
            (shape((peers * chunk, d)), "h"), (shape((d, n1)), "h"), (shape((d, n1)), "h"),
            (shape((d, n1)), "h"), (shape((4, d, d), F32), "h"),
        ],
        us=3,
    )
    got3 = exchange(send3.reshape(peers, chunk, d))
    pick_kind = "v" if peers * chunk <= 1024 else "h"
    (mid_wg,) = call(
        functools.partial(third_window_kernel, 1.0 / math.sqrt(n1 * peers)),
        [
            (mhid, "h"), (magg, "h"), (gmid, "h"), (msg, "h"), (mfg, "h"), (weights, "1"),
        ],
        [(shape((4 * d, d)), "v")],
        us=2,
    )
    (pick,) = call(
        functools.partial(pick_kernel, block_rows),
        [(place, "s"), (mid_wg, "v")],
        [(shape((tile_count * block_rows, peers * chunk)), pick_kind)],
        us=1,
    )
    send4, g, fg = call(
        functools.partial(fine_grad_kernel, 1.0 / math.sqrt(n * peers)),
        [
            (got3.reshape(peers * chunk, d), "v"), (pick, pick_kind), (cot, "h"), (pool_b, "h"),
            (weights, "0"), (slope2, "h"), (slope1, "h"), (hid, "h"), (agg, "h"), (mid, "h"),
            (outer, "h"), (mid_wg, "v"),
        ],
        [(shape((8 * d, d)), "h"), (shape((d, n)), "r"), (shape((d, n)), "r")],
        scratch=(pltpu.VMEM((d, n), BF), pltpu.VMEM((d, n), BF)),
        copies=2,
        us=4,
    )
    got4 = exchange(send4.reshape(peers, 8 * d // peers, d))
    rim_near, rim_far, edge_sums, inner_grads = call(
        fine_spread_kernel,
        [
            (fine_offsets, "h"), (fine_edge_w, "h"), (weights, "0"), (g, "h"), (fg, "h"),
        ],
        [
            (shape((HALO, d)), "h"), (shape((HALO, d)), "h"), (shape((2 * HALO, d), F32), "h"),
            (shape((n, d)), "r"),
        ],
        scratch=(
            pltpu.VMEM((n // TILE + 2, TILE, window), BF),
            pltpu.VMEM((d, n + 4 * TILE), BF),
            pltpu.VMEM((n - 2 * HALO, d), BF),
        ),
        copies=1,
        us=5,
    )
    (send5,) = call(
        sum_kernel,
        [(got4, "v"), (rim_near, "r")],
        [(shape((peers, 8 * d // peers, d)), "r")],
        scratch=(pltpu.VMEM((8 * d // peers, d), BF),),
        copies=peers,
        us=1,
    )
    got5 = exchange(send5)
    from_across = lax.ppermute(rim_near, "nodes", inside_pairs)
    from_beside = lax.ppermute(rim_far, "nodes", between_pairs)
    feature_grads, weight_grads = call(
        join_kernel,
        [
            (edge_sums, "h"), (from_across, "v"), (from_beside, "v"), (coarse_wg, "h"),
            (inner_grads, "r"),
        ],
        [(shape((n, d)), "r"), (shape((12, d, d), F32), "r")],
        scratch=(pltpu.VMEM((2 * HALO, d), BF),),
        copies=3,
        aliases={4: 0},
        us=1,
    )
    (weight_grads,) = call(
        gather_kernel,
        [
            (got5.reshape(8, d, d), "v"), (weight_grads, "r"),
        ],
        [(shape((12, d, d), F32), "r")],
        scratch=(pltpu.VMEM((8, d, d), F32),),
        copies=2,
        aliases={1: 0},
        us=1,
    )
    weight_grads = weight_grads.reshape(3, 4, d, d)
    return (feature_grads, weight_grads)


def solution(mesh):
    rows = P(("groups", "nodes"), None)
    cols = P("groups", "nodes")
    in_specs = (
        rows, rows, rows, rows, P(), cols, cols, cols, rows, P(("groups", "nodes")),
        cols, cols, rows, cols, cols,
    )
    out_specs = (rows, P("groups", None, None, None))
    return jax.shard_map(
        per_device, mesh=mesh, in_specs=in_specs, out_specs=out_specs, check_vma=False
    )
```

```python
import functools
import math

import jax
import jax.numpy as jnp
from jax import lax
from jax.experimental import pallas as pl
from jax.experimental.pallas import tpu as pltpu
from jax.sharding import PartitionSpec as P

HALO = 256
TILE = 256
WIDE = 2048
BF = jnp.bfloat16
F32 = jnp.float32

VM = pl.BlockSpec(memory_space=pltpu.VMEM)
HB = pl.BlockSpec(memory_space=pltpu.HBM)


def dot(a, b):
    return jnp.dot(a, b, preferred_element_type=F32)


def dot_nt(a, b):
    return lax.dot_general(a, b, (((1,), (1,)), ((), ())), preferred_element_type=F32)


def dot_tn(a, b):
    return lax.dot_general(a, b, (((0,), (0,)), ((), ())), preferred_element_type=F32)


def silu(v):
    return v / (1.0 + jnp.exp(-v))


def silu_slope(v):
    s = 1.0 / (1.0 + jnp.exp(-v))
    return s * (1.0 + v * (1.0 - s))


def merged_weights(idx, ew):
    total = ew
    for r in range(1, idx.shape[0]):
        total = total + jnp.where(pltpu.roll(idx, r, 0) == idx, pltpu.roll(ew, r, 0), 0.0)
    return total.astype(BF)


def edge_columns(idx, ew, start, rows):
    count = idx.shape[0]
    lanes = idx.shape[1]
    position = lax.broadcasted_iota(jnp.int32, (rows, lanes), 0) + start
    position = position.astype(jnp.int16)
    picked = jnp.zeros((rows, lanes), BF)
    for k in range(count):
        picked = jnp.where(idx[k : k + 1, :] == position, ew[k : k + 1, :], picked)
    return picked


def fine_edges(off, ew, s_ref):
    for h in range(TILE // 128):
        lane = slice(128 * h, 128 * (h + 1))
        o = off[:, lane]
        weight = merged_weights(o, ew[:, lane])
        rel = o + lax.broadcasted_iota(jnp.int32, o.shape, 1) + HALO
        rel = rel.astype(jnp.int16)
        for c in range(2 * HALO // 128 + 1):
            s_ref[128 * (h + c) : 128 * (h + c + 1), lane] = edge_columns(
                rel, weight, 128 * c, 128
            )


def clear_corners(s_ref):
    for h in range(TILE // 128):
        lane = slice(128 * h, 128 * (h + 1))
        if h > 0:
            s_ref[: 128 * h, lane] = jnp.zeros((128 * h, 128), BF)
        last = 128 * h + 2 * HALO + 128
        if last < TILE + 2 * HALO:
            s_ref[last:, lane] = jnp.zeros((TILE + 2 * HALO - last, 128), BF)


def forward_weights(w):
    w01 = jnp.concatenate([jnp.transpose(w[0]), jnp.transpose(w[1])], axis=1)
    return w01, jnp.transpose(w[2]), jnp.transpose(w[3])


def pool_matrix(pool, tile_rows):
    lane = lax.broadcasted_iota(jnp.int32, pool.shape, 1) // tile_rows
    values = pool.astype(F32)
    parts = [jnp.where(lane == r, values, 0.0) for r in range(pool.shape[1] // tile_rows)]
    return jnp.concatenate(parts, axis=0).astype(BF)


class Copies:
    def __init__(self, sems):
        self.sems = sems
        self.used = 0
        self.open = {}

    def start(self, source, target):
        copy = pltpu.make_async_copy(source, target, self.sems.at[self.used])
        self.used += 1
        copy.start()
        self.open[id(copy)] = copy
        return copy

    def wait(self, *copies):
        for copy in copies:
            if id(copy) in self.open:
                copy.wait()
                del self.open[id(copy)]

    def finish(self):
        self.wait(*list(self.open.values()))


def shape(dims, dtype=BF):
    return jax.ShapeDtypeStruct(dims, dtype)


def call(kernel, ins, outs, scratch=(), copies=0, us=3, mib=24, aliases={}):
    n_in, n_out = len(ins), len(outs)
    staged_in = [i for i, (_, kind) in enumerate(ins) if kind in "hs012"]
    staged_out = [i for i, (_, kind) in enumerate(outs) if kind in "hs"]
    spaces = {"h": pltpu.VMEM, "s": pltpu.SMEM}
    stage = []
    for i in staged_in:
        array, kind = ins[i]
        dims = array.shape[1:] if kind.isdigit() else array.shape
        stage.append(spaces.get(kind, pltpu.VMEM)(dims, array.dtype))
    stage += [spaces[outs[i][1]](outs[i][0].shape, outs[i][0].dtype) for i in staged_out]
    total = len(staged_in) + len(staged_out) + copies

    def body(*refs):
        in_refs, out_refs = list(refs[:n_in]), list(refs[n_in : n_in + n_out])
        rest = list(refs[n_in + n_out :])
        sems = rest.pop() if total else None
        stages, user = rest[: len(stage)], rest[len(stage) :]
        io = Copies(sems)
        pending = {}
        for i, ref in zip(staged_in, stages):
            kind = ins[i][1]
            source = in_refs[i].at[int(kind)] if kind.isdigit() else in_refs[i]
            pending[i] = io.start(source, ref)
            in_refs[i] = ref
        targets = {}
        for i, ref in zip(staged_out, stages[len(staged_in) :]):
            targets[i] = out_refs[i]
            out_refs[i] = ref

        def need(*which):
            io.wait(*[pending[i] for i in which or pending])

        def flush(*which):
            for i in which:
                io.start(out_refs[i], targets.pop(i))

        kernel(io, need, flush, in_refs, out_refs, *user)
        flush(*list(targets))
        io.finish()

    return pl.pallas_call(
        body,
        out_shape=[
            s if kind == "v" else pltpu.HBM(s.shape, s.dtype) for s, kind in outs
        ],
        in_specs=[VM if kind == "v" else HB for _, kind in ins],
        out_specs=[VM if kind == "v" else HB for _, kind in outs],
        scratch_shapes=stage
        + list(scratch)
        + ([pltpu.SemaphoreType.DMA((total,))] if total else []),
        input_output_aliases=aliases,
        compiler_params=pltpu.CompilerParams(vmem_limit_bytes=mib << 20),
        cost_estimate=pl.CostEstimate(
            flops=0, bytes_accessed=int(us * 3_000_000), transcendentals=0
        ),
    )(*[
        a if kind == "v" else pltpu.with_memory_space_constraint(a, pltpu.HBM)
        for a, kind in ins
    ])


def fine_forward(h_t, agg, weights):
    w01, w2t, w3t = weights
    first = dot(w01, jnp.concatenate([h_t, agg], axis=0))
    middle = silu(first).astype(BF)
    second = dot(w2t, middle)
    outer = silu(second).astype(BF)
    return (h_t.astype(F32) + dot(w3t, outer)).astype(BF)


def outer_tiles(tile_count, per):
    return list(range(per)) + list(range(tile_count - per, tile_count))


def inner_kernel(tile_rows, peers, cap, io, need, flush, ins, outs, feat_t, s_ref, ids, counts):
    off, ew, feat, w, pool, owner, slot, nbrs, cew, cot = ins
    so_ref, win_ref, w01_ref, w2t_ref, w3t_ref, po_ref, spread, ext_ref, agg_ref, place = outs
    rows, d = feat.shape
    block_rows = pool.shape[0]
    n2 = cot.shape[0]
    tiles = rows // TILE
    per = TILE // tile_rows
    tile_count = rows // tile_rows
    for i in range(tiles - 2):
        clear_corners(s_ref.at[i])
    clear_corners(so_ref.at[0])
    clear_corners(so_ref.at[1])
    spread[...] = jnp.zeros(spread.shape, F32)
    ids[...] = jnp.full(ids.shape, -1.0, F32)
    for p in range(peers):
        counts[p] = 0
    need(5, 6)
    lane_slot = lax.broadcasted_iota(jnp.int32, (1, 128), 1) // block_rows
    first_tiles = outer_tiles(tile_count, per)
    for t in first_tiles + [t for t in range(tile_count) if t not in first_tiles]:
        o = owner[t]
        c = counts[o]
        counts[o] = c + 1
        place[t] = o * cap + c
        row = ids[pl.ds(o, 1), :]
        ids[pl.ds(o, 1), :] = jnp.where(lane_slot == c, slot[t].astype(F32), row)
    flush(9)
    need(0, 1)
    for n, i in enumerate((0, tiles - 1)):
        cols = slice(i * TILE, (i + 1) * TILE)
        fine_edges(off[:, cols], ew[:, cols], so_ref.at[n])
    need()
    feat_t[...] = jnp.transpose(feat[...])
    weights = forward_weights(w)
    for i in range(1, tiles - 1):
        cols = slice(i * TILE, (i + 1) * TILE)
        fine_edges(off[:, cols], ew[:, cols], s_ref.at[i - 1])
        around = feat_t[:, i * TILE - HALO : (i + 1) * TILE + HALO]
        agg_ref[:, cols] = dot(around, s_ref[i - 1]).astype(BF)
    for start in range(TILE, rows - TILE, WIDE):
        stop = min(start + WIDE, rows - TILE)
        cols = slice(start, stop)
        fine_out = fine_forward(feat_t[:, cols], agg_ref[:, cols], weights)
        for i in range(start // TILE, stop // TILE):
            at = slice(i * TILE - start, (i + 1) * TILE - start)
            matrix = pool_matrix(pool[:, i * TILE : (i + 1) * TILE], tile_rows)
            blocks = dot_nt(matrix, fine_out[:, at])
            for j in range(per):
                at = pl.ds(pl.multiple_of(place[i * per + j] * block_rows, 8), block_rows)
                spread[at, :] = blocks[j * block_rows : (j + 1) * block_rows, :]
    for n, i in enumerate((0, tiles - 1)):
        po_ref[n] = pool_matrix(pool[:, i * TILE : (i + 1) * TILE], tile_rows)
    win_ref[0] = feat_t[:, : TILE + HALO]
    win_ref[1] = feat_t[:, rows - TILE - HALO :]
    w01_ref[...], w2t_ref[...], w3t_ref[...] = weights
    nb = nbrs[...].astype(F32)
    high = jnp.floor(nb * (1.0 / 256.0))
    ce = cew[...]
    ce_high = ce.astype(BF).astype(F32)
    fields = [high, nb - high * 256.0, ce_high, ce - ce_high]
    fields.append(jnp.zeros((nb.shape[0], 128 - 4 * n2), F32))
    top = jnp.concatenate(fields, axis=1)
    sub = lax.broadcasted_iota(jnp.int32, (8, 128), 0)
    for p in range(peers):
        ext_ref[p, 0:n2, :] = cot[...]
        below = jnp.where(sub == 0, ids[p : p + 1, :], 0.0)
        ext_ref[p, n2 : n2 + 16, :] = jnp.concatenate([top, below], axis=0).astype(BF)


def outer_kernel(
    tile_rows, cap, block_rows, io, need, flush, ins, outs, agg_edge, spread, stage, counts
):
    across, beside, s_in, win, w01, w2t, w3t, pool, spread_in, ext, agg_in, owner = ins
    even = lax.rem(lax.axis_index("nodes"), 2) == 0
    left = jnp.where(even, beside[...], across[...])
    right = jnp.where(even, across[...], beside[...])
    send_ref, agg_ref = outs
    peers, chunk, d = stage.shape
    rows = agg_in.shape[1]
    per = TILE // tile_rows
    io.start(ext, send_ref.at[:, pl.ds(chunk, ext.shape[1]), :])
    inside = pl.ds(TILE, rows - 2 * TILE)
    io.start(agg_in.at[:, inside], agg_ref.at[:, inside])
    spread[...] = spread_in[...]
    for p in range(peers):
        counts[p] = 0
    weights = (w01[...], w2t[...], w3t[...])
    for n in range(2):
        if n == 0:
            window_t = jnp.concatenate([jnp.transpose(left), win[0]], axis=1)
        else:
            window_t = jnp.concatenate([win[1], jnp.transpose(right)], axis=1)
        agg_edge[:, n * TILE : (n + 1) * TILE] = dot(window_t, s_in[n]).astype(BF)
    h_t = jnp.concatenate([win[0, :, :TILE], win[1, :, HALO:]], axis=1)
    fine_out = fine_forward(h_t, agg_edge[...], weights)
    results = [dot_nt(pool[n], fine_out[:, n * TILE : (n + 1) * TILE]) for n in range(2)]
    io.start(agg_edge.at[:, pl.ds(0, TILE)], agg_ref.at[:, pl.ds(0, TILE)])
    io.start(agg_edge.at[:, pl.ds(TILE, TILE)], agg_ref.at[:, pl.ds(rows - TILE, TILE)])
    need()
    for j, t in enumerate(outer_tiles(rows // tile_rows, per)):
        o = owner[t]
        c = counts[o]
        counts[o] = c + 1
        at = pl.ds(pl.multiple_of((o * cap + c) * block_rows, 8), block_rows)
        blocks = results[j // per]
        spread[at, :] = blocks[j % per * block_rows : (j % per + 1) * block_rows, :]
    group = max(1, peers // 4)
    for p in range(peers):
        stage[p] = spread[p * chunk : (p + 1) * chunk, :].astype(BF)
        if p % group == group - 1:
            part = pl.ds(p + 1 - group, group)
            io.start(stage.at[part], send_ref.at[part, pl.ds(0, chunk), :])


def mid_edges(nbrs, ew, s_ref):
    nodes = nbrs.shape[1]
    for c in range(nodes // 128):
        lane = slice(128 * c, 128 * (c + 1))
        idx = nbrs[:, lane]
        weight = merged_weights(idx, ew[:, lane])
        idx = idx.astype(jnp.int16)
        for r in range(nodes // 128):
            s_ref[128 * r : 128 * (r + 1), lane] = edge_columns(idx, weight, 128 * r, 128)


def first_window_kernel(io, need, flush, ins, outs):
    nbrs, ew, w, _ = ins
    smid, w01_ref, w2t_ref, w3t_ref = outs
    need(0, 1)
    mid_edges(nbrs, ew, smid)
    flush(0)
    need()
    w01_ref[...], w2t_ref[...], w3t_ref[...] = forward_weights(w)


def mid_kernel(block_rows, chunk, io, need, flush, ins, outs, blocks, coarse):
    got, smid, w01, w2t, w3, pool_mid, _ = ins
    send_ref, hid_ref, agg_ref, sel_ref, ext_ref = outs
    peers = got.shape[0]
    nodes = smid.shape[0]
    n2 = pool_mid.shape[0]
    io.start(got.at[:, pl.ds(chunk, n2 + 16), :], ext_ref)
    rows = [got[p, chunk + n2 : chunk + n2 + 16, :].astype(F32)[8:9, :] for p in range(peers)]
    keys = jnp.transpose(jnp.concatenate(rows, axis=0))
    keys = keys * block_rows
    keys = keys + (lax.broadcasted_iota(jnp.int32, keys.shape, 0) % block_rows).astype(F32)
    keys = keys.astype(jnp.int32)
    lane = lax.broadcasted_iota(jnp.int32, (chunk, nodes), 1)
    for p in range(peers):
        sel_ref[p * chunk : (p + 1) * chunk, :] = jnp.where(
            keys[0:chunk, p : p + 1] == lane, 1.0, 0.0
        ).astype(BF)
        blocks[p * chunk : (p + 1) * chunk, :] = got[p, 0:chunk, :]
    flush(3)
    hidden = dot_tn(blocks[...], sel_ref[...]).astype(BF)
    hid_ref[...] = hidden
    need()
    agg = dot(hidden, smid[...]).astype(BF)
    agg_ref[...] = agg
    flush(1, 2)
    middle = silu(dot(w01[...], jnp.concatenate([hidden, agg], axis=0))).astype(BF)
    outer = silu(dot(w2t[...], middle)).astype(BF)
    pooled = dot_nt(pool_mid[...], outer).astype(BF)
    coarse[...] = (dot_nt(pool_mid[...], hidden) + dot(pooled, w3[3])).astype(BF)
    for p in range(peers):
        io.start(coarse, send_ref.at[p])


def second_window_kernel(io, need, flush, ins, outs, nb_ref, ew_ref):
    ext, hid, agg, mid_cot, w1, w2 = ins
    sco, cot_all, back_ref, w01_ref, w2t_ref, mcot, sl1_ref, sl2_ref = outs
    peers = ext.shape[0]
    n2 = ext.shape[1] - 16
    nodes = peers * n2
    edges = nb_ref.shape[0]
    need()
    for p in range(peers):
        part = ext[p, n2 : n2 + 16, :].astype(F32)[0:edges, :]
        at = slice(p * n2, (p + 1) * n2)
        nb_ref[:, at] = (part[:, 0:n2] * 256.0 + part[:, n2 : 2 * n2]).astype(jnp.int32)
        ew_ref[:, at] = part[:, 2 * n2 : 3 * n2] + part[:, 3 * n2 : 4 * n2]
    cots = jnp.concatenate([ext[p, 0:n2, :] for p in range(peers)], axis=0)
    cot_all[...] = jnp.transpose(cots)
    mcot[...] = jnp.transpose(mid_cot[...])

    def column(c, _):
        lane = pl.ds(pl.multiple_of(c * 128, 128), 128)
        idx = nb_ref[:, lane]
        weight = merged_weights(idx, ew_ref[:, lane])
        idx = idx.astype(jnp.int16)
        for r in range(nodes // 128):
            sco[128 * r : 128 * (r + 1), lane] = edge_columns(idx, weight, 128 * r, 128)
        return 0

    lax.fori_loop(0, nodes // 128, column, 0)
    w01_ref[...], w2t_ref[...], _ = forward_weights(w2)
    back_ref[...] = dot(w2[3], cot_all[...])
    w01, w2t, _ = forward_weights(w1)
    first = dot(w01, jnp.concatenate([hid[...], agg[...]], axis=0))
    s1 = 1.0 / (1.0 + jnp.exp(-first))
    second = dot(w2t, (first * s1).astype(BF))
    s2 = 1.0 / (1.0 + jnp.exp(-second))
    sl1_ref[...] = s1 * (1.0 + first * (1.0 - s1))
    sl2_ref[...] = s2 * (1.0 + second * (1.0 - s2))


def coarse_kernel(io, need, flush, ins, outs):
    got, sco, c01, c2t, cot_all, cot_back, w2, *rest = ins
    cot_my, pool_mid, mcot, w1, msl2, msl1, smid, sel = rest
    send_ref, gmid_ref, sg_ref, fg_ref, cwg_ref = outs
    nodes = got.shape[0]
    n2 = cot_my.shape[0]
    me = lax.axis_index("nodes")
    width = min(TILE, nodes)
    hidden = jnp.transpose(got[...])
    if sco.shape[0] > 512:
        need(1, 2, 3, 4, 5)
    w01, w2t = c01[...], c2t[...]
    mine = pl.ds(pl.multiple_of(me * n2, 16), n2)
    mixed = jnp.zeros((2 * n2, 128), F32)
    grads = [jnp.zeros((128, 128), F32) for _ in range(4)]
    row = lax.broadcasted_iota(jnp.int32, (n2, width), 0) + me * n2
    lane = lax.broadcasted_iota(jnp.int32, (n2, width), 1)
    for i in range(nodes // width):
        cols = slice(i * width, (i + 1) * width)
        h = hidden[:, cols]
        agg = dot(hidden, sco[:, cols]).astype(BF)
        first = dot(w01, jnp.concatenate([h, agg], axis=0))
        s1 = 1.0 / (1.0 + jnp.exp(-first))
        middle = (first * s1).astype(BF)
        second = dot(w2t, middle)
        s2 = 1.0 / (1.0 + jnp.exp(-second))
        outer = (second * s2).astype(BF)
        g = cot_all[:, cols]
        if i == 0:
            need(6)
        sg = (cot_back[:, cols] * (s2 * (1.0 + second * (1.0 - s2)))).astype(BF)
        fg = (dot(w2[2], sg) * (s1 * (1.0 + first * (1.0 - s1)))).astype(BF)
        here = jnp.where(lane + i * width == row, 1.0, 0.0).astype(BF)
        mixed = mixed + dot_nt(jnp.concatenate([here, sco[mine, cols]], axis=0), fg)
        grads = [
            grads[0] + dot_nt(h, fg),
            grads[1] + dot_nt(agg, fg),
            grads[2] + dot_nt(middle, sg),
            grads[3] + dot_nt(outer, g),
        ]
    scale = 1.0 / math.sqrt(nodes)
    for m in range(4):
        cwg_ref[m] = grads[m] * scale
    flush(4)
    need(7, 8, 9, 10, 11, 12)
    mixed = mixed.astype(BF)
    into = jnp.concatenate([mixed[:n2], mixed[n2:]], axis=1)
    back_weights = jnp.concatenate([w2[0], w2[1]], axis=1)
    coarse_grad = (cot_my[...].astype(F32) + dot_nt(into, back_weights)).astype(BF)
    back = dot_tn(coarse_grad, pool_mid[...])
    g = (mcot[...].astype(F32) + back).astype(BF)
    gmid_ref[...] = g
    sg = (dot(w1[3], g) * msl2[...]).astype(BF)
    sg_ref[...] = sg
    fg = (dot(w1[2], sg) * msl1[...]).astype(BF)
    fg_ref[...] = fg
    flush(1, 2, 3)
    spill = dot(w1[1], fg).astype(BF)
    need()
    mid_grad = (g.astype(F32) + dot(w1[0], fg) + dot_nt(spill, smid[...])).astype(BF)
    send_ref[...] = dot_nt(sel[...], mid_grad).astype(BF)


def saved_kernel(tile_rows, io, need, flush, ins, outs):
    feat, agg, w, fine_cot, pool, _ = ins
    hid_ref, mid_ref, outer_ref, sl1_ref, sl2_ref, cot_ref, po_ref = outs
    rows = feat.shape[0]
    need(0, 1, 2)
    hid_ref[...] = jnp.transpose(feat[...])
    flush(0)
    w01, w2t, _ = forward_weights(w)
    for start in range(0, rows, 512):
        cols = slice(start, min(start + 512, rows))
        first = dot(w01, jnp.concatenate([hid_ref[:, cols], agg[:, cols]], axis=0))
        s1 = 1.0 / (1.0 + jnp.exp(-first))
        middle = (first * s1).astype(BF)
        mid_ref[:, cols] = middle
        sl1_ref[:, cols] = (s1 * (1.0 + first * (1.0 - s1))).astype(BF)
        second = dot(w2t, middle)
        s2 = 1.0 / (1.0 + jnp.exp(-second))
        outer_ref[:, cols] = (second * s2).astype(BF)
        sl2_ref[:, cols] = (s2 * (1.0 + second * (1.0 - s2))).astype(BF)
    need()
    cot_ref[...] = jnp.transpose(fine_cot[...])
    for i in range(rows // TILE):
        po_ref[i] = pool_matrix(pool[:, i * TILE : (i + 1) * TILE], tile_rows)


def third_window_kernel(mid_scale, io, need, flush, ins, outs):
    mhid, magg, gmid, msg, mfg, w1 = ins
    keep_ref, give_ref = outs
    d = mhid.shape[0]
    even = lax.rem(lax.axis_index("nodes"), 2) == 0
    need()
    w01, w2t, _ = forward_weights(w1)
    middle = silu(dot(w01, jnp.concatenate([mhid[...], magg[...]], axis=0))).astype(BF)
    outer = silu(dot(w2t, middle)).astype(BF)
    pairs = ((mhid, mfg), (magg, mfg), (middle, msg), (outer, gmid))
    grads = [(dot_nt(x[...], y[...]) * mid_scale).astype(BF) for x, y in pairs]
    for m in range(2):
        rows = slice(m * d, (m + 1) * d)
        keep_ref[rows, :] = jnp.where(even, grads[m], grads[m + 2])
        give_ref[rows, :] = jnp.where(even, grads[m + 2], grads[m])


def pick_kernel(block_rows, io, need, flush, ins, outs):
    place = ins[0]
    pick_ref = outs[0]
    need()
    slots = pick_ref.shape[1]
    lane = lax.broadcasted_iota(jnp.int32, (block_rows, slots), 1)
    lane = lane - lax.broadcasted_iota(jnp.int32, (block_rows, slots), 0)
    for t in range(0, place.shape[0], 2):
        both = [jnp.where(lane == place[t + j] * block_rows, 1.0, 0.0) for j in range(2)]
        pick_ref[t * block_rows : (t + 2) * block_rows, :] = jnp.concatenate(
            both, axis=0
        ).astype(BF)


def fine_grad_kernel(scale, io, need, flush, ins, outs, g_ref, fg_ref):
    got, pick, cot, pool, w, slope2, slope1, hid, agg, mid, outer, *halves = ins
    send_ref, g_out, fg_out = outs
    d, rows = hid.shape
    if pick.shape[1] > 1024:
        need(1)
    blocks = dot(pick[...], got[...]).astype(BF)
    peers, chunk, _ = send_ref.shape
    fine_rows, mid_rows = chunk * 2 // 3, chunk // 3
    both = (halves[0][...].astype(F32) + halves[1][...].astype(F32)).astype(BF)
    for p in range(peers):
        send_ref[p, fine_rows:, :] = both[p * mid_rows : (p + 1) * mid_rows, :]
    need(2, 3)
    per = pool.shape[1]
    for i in range(rows // TILE):
        cols = slice(i * TILE, (i + 1) * TILE)
        back = dot_tn(blocks[i * per : (i + 1) * per, :], pool[i])
        g_ref[:, cols] = (cot[:, cols].astype(F32) + back).astype(BF)
    io.start(g_ref, g_out)
    g = g_ref[...]
    need(4, 5, 6)
    sg = (dot(w[3], g) * slope2[...].astype(F32)).astype(BF)
    fg = (dot(w[2], sg) * slope1[...].astype(F32)).astype(BF)
    fg_ref[...] = fg
    io.start(fg_ref, fg_out)
    need()
    for m, (a, b) in enumerate(
        ((hid[...], fg), (agg[...], fg), (mid[...], sg), (outer[...], g))
    ):
        grad = (dot_nt(a, b) * scale).astype(BF)
        for q in range(d // fine_rows):
            part = grad[q * fine_rows : (q + 1) * fine_rows, :]
            send_ref[m * d // fine_rows + q, :fine_rows, :] = part


def fine_spread_kernel(io, need, flush, ins, outs, band, spill, inner):
    off, ew, w, g, fg = ins
    rim_near, rim_far, edge_ref, out_ref = outs
    d, rows = g.shape
    tiles = rows // TILE

    def piece(i, h, c):
        row = 128 * (h + c)
        lane = (2 - row // TILE) * TILE + 128 * h
        return band.at[i + row // TILE, pl.ds(row % TILE, 128), pl.ds(lane, 128)]

    def build(i):
        for h in range(TILE // 128):
            lane = slice(i * TILE + 128 * h, i * TILE + 128 * (h + 1))
            o = off[:, lane]
            weight = merged_weights(o, ew[:, lane])
            rel = o + lax.broadcasted_iota(jnp.int32, o.shape, 1) + HALO
            rel = rel.astype(jnp.int16)
            for c in range(2 * HALO // 128 + 1):
                piece(i, h, c)[...] = edge_columns(rel, weight, 128 * c, 128)

    for i in range(tiles):
        piece(i, 0, 5)[...] = jnp.zeros((128, 128), BF)
        piece(i, 1, -1)[...] = jnp.zeros((128, 128), BF)
    for b in (0, 1, tiles, tiles + 1):
        for j in range(3):
            if not 0 <= b - 2 + j < tiles:
                band[b, :, j * TILE : (j + 1) * TILE] = jnp.zeros((TILE, TILE), BF)
    spill[:, : 2 * TILE] = jnp.zeros((d, 2 * TILE), BF)
    spill[:, 2 * TILE + rows :] = jnp.zeros((d, 2 * TILE), BF)
    even = lax.rem(lax.axis_index("nodes"), 2) == 0
    need(0, 1)
    build(0)
    build(tiles - 1)
    need()
    spill[:, 2 * TILE : 2 * TILE + rows] = dot(w[1], fg[...]).astype(BF)
    low, high = [
        dot_nt(band[b], spill[:, b * TILE : (b + 3) * TILE]).astype(BF) for b in (0, tiles + 1)
    ]
    rim_near[...] = jnp.where(even, high, low)
    rim_far[...] = jnp.where(even, low, high)
    flush(0, 1)
    for i in range(1, tiles - 1):
        build(i)
    for b in range(1, tiles + 1):
        part = dot_nt(band[b], spill[:, b * TILE : (b + 3) * TILE])
        cols = slice((b - 1) * TILE, b * TILE)
        part = part + jnp.transpose(g[:, cols].astype(F32) + dot(w[0], fg[:, cols]))
        if b == 1:
            edge_ref[:TILE, :] = part
        elif b == tiles:
            edge_ref[TILE:, :] = part
        else:
            inner[(b - 2) * TILE : (b - 1) * TILE, :] = part.astype(BF)
    io.start(inner, out_ref.at[pl.ds(TILE, rows - 2 * TILE)])


def sum_kernel(io, need, flush, ins, outs, part):
    got = ins[0]
    send_ref = outs[0]
    peers = got.shape[0]
    need()
    fine_rows, mid_rows = got.shape[1] * 2 // 3, got.shape[1] // 3
    fine = sum(got[p, :fine_rows, :].astype(F32) for p in range(peers))
    part[:fine_rows, :] = fine.astype(BF)
    for core in range(2):
        mids = sum(got[p, fine_rows:, :].astype(F32) for p in range(core, peers, 2))
        at = fine_rows + core * mid_rows
        part[at : at + mid_rows, :] = mids.astype(BF)
    for p in range(peers):
        io.start(part, send_ref.at[p])


def join_kernel(io, need, flush, ins, outs, joined):
    edge, across, beside, coarse, _ = ins
    out_ref, wg_ref = outs
    rows = out_ref.shape[0]
    even = lax.rem(lax.axis_index("nodes"), 2) == 0
    from_left = jnp.where(even, beside[...], across[...])
    from_right = jnp.where(even, across[...], beside[...])
    need(0)
    joined[:HALO, :] = (edge[:HALO, :] + from_left.astype(F32)).astype(BF)
    joined[HALO:, :] = (edge[HALO:, :] + from_right.astype(F32)).astype(BF)
    io.start(joined.at[pl.ds(0, HALO)], out_ref.at[pl.ds(0, HALO)])
    io.start(joined.at[pl.ds(HALO, HALO)], out_ref.at[pl.ds(rows - HALO, HALO)])
    need()
    io.start(coarse, wg_ref.at[pl.ds(2 * coarse.shape[0], coarse.shape[0])])


def gather_kernel(io, need, flush, ins, outs, wide):
    summed, out_ref = ins[0], outs[0]
    peers, chunk, _ = summed.shape
    fine_rows, mid_rows = chunk // 2, chunk // 4
    total = wide.shape[0]
    for p in range(peers):
        wide[p * fine_rows : (p + 1) * fine_rows, :] = summed[p, :fine_rows, :].astype(F32)
    io.start(wide.at[pl.ds(0, total // 2)], out_ref.at[pl.ds(0, total // 2)])
    for p in range(peers):
        for core in range(2):
            at = total // 2 + core * total // 4 + p * mid_rows
            rows = slice(fine_rows + core * mid_rows, fine_rows + (core + 1) * mid_rows)
            wide[at : at + mid_rows, :] = summed[p, rows, :].astype(F32)
    rest = pl.ds(total // 2, total // 2)
    io.start(wide.at[rest], out_ref.at[rest])


def exchange(x):
    return lax.all_to_all(x, "nodes", split_axis=0, concat_axis=0, tiled=True)


def per_device(
    features,
    fine_cotangent,
    mid_cotangent,
    coarse_cotangent,
    weights,
    fine_offsets,
    fine_edge_w,
    pool_fine,
    owner_dev,
    coarse_slot,
    mid_nbrs,
    mid_edge_w,
    pool_mid,
    coarse_nbrs,
    coarse_edge_w,
):
    n, d = features.shape
    tile_count = owner_dev.shape[0]
    tile_rows = n // tile_count
    block_rows = pool_fine.shape[0]
    n1 = mid_cotangent.shape[0]
    n2 = coarse_cotangent.shape[0]
    edges = fine_offsets.shape[0]
    peers = lax.axis_size("nodes")
    cap = max(2, 2 * tile_count // peers)
    chunk = cap * block_rows
    window = TILE + 2 * HALO
    per = TILE // tile_rows * block_rows
    ends = peers - 1
    inside_pairs = [(i, i ^ 1) for i in range(peers)]
    between_pairs = [(i, ((i + 1) ^ 1) - 1) for i in range(1, ends)]
    total2 = peers * n2

    odd = lax.rem(lax.axis_index("nodes"), 2)
    near = lax.dynamic_slice_in_dim(features, (1 - odd) * (n - HALO), HALO, 0)
    far = lax.dynamic_slice_in_dim(features, odd * (n - HALO), HALO, 0)
    across = lax.ppermute(near, "nodes", inside_pairs)
    beside = lax.ppermute(far, "nodes", between_pairs)
    owners = owner_dev.reshape(-1)
    s_out, win, w01, w2t, w3t, pool_out, spread, ext, agg_in, place = call(
        functools.partial(inner_kernel, tile_rows, peers, cap),
        [
            (fine_offsets, "h"), (fine_edge_w, "h"), (features, "h"), (weights, "0"),
            (pool_fine, "h"), (owners, "s"), (coarse_slot, "s"), (coarse_nbrs, "h"),
            (coarse_edge_w, "h"), (coarse_cotangent, "h"),
        ],
        [
            (shape((2, window, TILE)), "v"), (shape((2, d, TILE + HALO)), "v"),
            (shape((d, 2 * d)), "v"), (shape((d, d)), "v"), (shape((d, d)), "v"),
            (shape((2, per, TILE)), "v"), (shape((peers * chunk, d), F32), "v"),
            (shape((peers, n2 + 16, d)), "v"), (shape((d, n)), "v"),
            (shape((tile_count,), jnp.int32), "s"),
        ],
        scratch=(
            pltpu.VMEM((d, n), BF),
            pltpu.VMEM((n // TILE - 2, window, TILE), BF),
            pltpu.VMEM((peers, 128), F32),
            pltpu.SMEM((peers,), jnp.int32),
        ),
        us=6,
    )
    send1, agg = call(
        functools.partial(outer_kernel, tile_rows, cap, block_rows),
        [
            (across, "v"), (beside, "v"), (s_out, "v"), (win, "v"), (w01, "v"), (w2t, "v"),
            (w3t, "v"), (pool_out, "v"), (spread, "v"), (ext, "v"), (agg_in, "v"), (owners, "s"),
        ],
        [(shape((peers, chunk + n2 + 16, d)), "r"), (shape((d, n)), "r")],
        scratch=(
            pltpu.VMEM((d, 2 * TILE), BF),
            pltpu.VMEM((peers * chunk, d), F32),
            pltpu.VMEM((peers, chunk, d), BF),
            pltpu.SMEM((peers,), jnp.int32),
        ),
        copies=8,
        us=3,
    )
    got1 = exchange(send1)
    smid, m01, m2t, m3t = call(
        first_window_kernel,
        [(mid_nbrs, "h"), (mid_edge_w, "h"), (weights, "1"), (agg, "r")],
        [
            (shape((n1, n1)), "h"), (shape((d, 2 * d)), "h"), (shape((d, d)), "h"),
            (shape((d, d)), "h"),
        ],
        us=6,
    )
    hid, mid, outer, slope1, slope2, cot, pool_b = call(
        functools.partial(saved_kernel, tile_rows),
        [
            (features, "h"), (agg, "h"), (weights, "0"), (fine_cotangent, "h"),
            (pool_fine, "h"), (m3t, "r"),
        ],
        [
            (shape((d, n)), "h"), (shape((d, n)), "h"), (shape((d, n)), "h"),
            (shape((d, n)), "h"), (shape((d, n)), "h"), (shape((d, n)), "h"),
            (shape((n // TILE, per, TILE)), "h"),
        ],
        us=4,
    )
    send2, mhid, magg, sel, ext = call(
        functools.partial(mid_kernel, block_rows, chunk),
        [
            (got1, "v"), (smid, "h"), (m01, "h"), (m2t, "h"), (weights, "1"), (pool_mid, "h"),
            (pool_b, "r"),
        ],
        [
            (shape((peers, n2, d)), "r"), (shape((d, n1)), "h"), (shape((d, n1)), "h"),
            (shape((peers * chunk, n1)), "h"), (shape((peers, n2 + 16, d)), "r"),
        ],
        scratch=(pltpu.VMEM((peers * chunk, d), BF), pltpu.VMEM((n2, d), BF)),
        copies=peers + 1,
        us=3,
    )
    got2 = exchange(send2)
    near = "v" if total2 <= 512 else "h"
    sco, cot_all, cot_back, c01, c2t, mcot, mslope1, mslope2 = call(
        second_window_kernel,
        [
            (ext, "h"), (mhid, "h"), (magg, "h"), (mid_cotangent, "h"), (weights, "1"),
            (weights, "2"),
        ],
        [
            (shape((total2, total2)), near), (shape((d, total2)), near),
            (shape((d, total2), F32), near), (shape((d, 2 * d)), near), (shape((d, d)), near),
            (shape((d, n1)), "h"),
            (shape((d, n1), F32), "h"), (shape((d, n1), F32), "h"),
        ],
        scratch=(pltpu.VMEM((edges, total2), jnp.int32), pltpu.VMEM((edges, total2), F32)),
        us=6,
    )
    send3, gmid, msg, mfg, coarse_wg = call(
        coarse_kernel,
        [
            (got2.reshape(total2, d), "v"), (sco, near), (c01, near), (c2t, near),
            (cot_all, near), (cot_back, near), (weights, "2"),
            (coarse_cotangent, "h"), (pool_mid, "h"), (mcot, "h"), (weights, "1"),
            (mslope2, "h"), (mslope1, "h"), (smid, "h"), (sel, "h"),
        ],
        [
            (shape((peers * chunk, d)), "h"), (shape((d, n1)), "h"), (shape((d, n1)), "h"),
            (shape((d, n1)), "h"), (shape((4, d, d), F32), "h"),
        ],
        us=3,
    )
    got3 = exchange(send3.reshape(peers, chunk, d))
    pick_kind = "v" if peers * chunk <= 1024 else "h"
    mid_keep, mid_give = call(
        functools.partial(third_window_kernel, 1.0 / math.sqrt(n1 * peers)),
        [
            (mhid, "h"), (magg, "h"), (gmid, "h"), (msg, "h"), (mfg, "h"), (weights, "1"),
        ],
        [(shape((2 * d, d)), "v"), (shape((2 * d, d)), "v")],
        us=2,
    )
    mid_got = lax.ppermute(mid_give, "nodes", inside_pairs)
    (pick,) = call(
        functools.partial(pick_kernel, block_rows),
        [(place, "s"), (mid_keep, "v")],
        [(shape((tile_count * block_rows, peers * chunk)), pick_kind)],
        us=1,
    )
    send4, g, fg = call(
        functools.partial(fine_grad_kernel, 1.0 / math.sqrt(n * peers)),
        [
            (got3.reshape(peers * chunk, d), "v"), (pick, pick_kind), (cot, "h"), (pool_b, "h"),
            (weights, "0"), (slope2, "h"), (slope1, "h"), (hid, "h"), (agg, "h"), (mid, "h"),
            (outer, "h"), (mid_keep, "v"), (mid_got, "v"),
        ],
        [
            (shape((peers, 6 * d // peers, d)), "h"), (shape((d, n)), "r"), (shape((d, n)), "r"),
        ],
        scratch=(pltpu.VMEM((d, n), BF), pltpu.VMEM((d, n), BF)),
        copies=2,
        us=4,
    )
    got4 = exchange(send4)
    rim_near, rim_far, edge_sums, inner_grads = call(
        fine_spread_kernel,
        [
            (fine_offsets, "h"), (fine_edge_w, "h"), (weights, "0"), (g, "h"), (fg, "h"),
        ],
        [
            (shape((HALO, d)), "h"), (shape((HALO, d)), "h"), (shape((2 * HALO, d), F32), "h"),
            (shape((n, d)), "r"),
        ],
        scratch=(
            pltpu.VMEM((n // TILE + 2, TILE, window), BF),
            pltpu.VMEM((d, n + 4 * TILE), BF),
            pltpu.VMEM((n - 2 * HALO, d), BF),
        ),
        copies=1,
        us=5,
    )
    (send5,) = call(
        sum_kernel,
        [(got4, "v"), (rim_near, "r")],
        [(shape((peers, 8 * d // peers, d)), "r")],
        scratch=(pltpu.VMEM((8 * d // peers, d), BF),),
        copies=peers,
        us=1,
    )
    got5 = exchange(send5)
    from_across = lax.ppermute(rim_near, "nodes", inside_pairs)
    from_beside = lax.ppermute(rim_far, "nodes", between_pairs)
    feature_grads, weight_grads = call(
        join_kernel,
        [
            (edge_sums, "h"), (from_across, "v"), (from_beside, "v"), (coarse_wg.reshape(4 * d, d), "h"),
            (inner_grads, "r"),
        ],
        [(shape((n, d)), "r"), (shape((12 * d, d), F32), "r")],
        scratch=(pltpu.VMEM((2 * HALO, d), BF),),
        copies=3,
        aliases={4: 0},
        us=1,
    )
    (weight_grads,) = call(
        gather_kernel,
        [
            (got5, "v"), (weight_grads, "r"),
        ],
        [(shape((12 * d, d), F32), "r")],
        scratch=(pltpu.VMEM((8 * d, d), F32),),
        copies=2,
        aliases={1: 0},
        us=1,
    )
    weight_grads = weight_grads.reshape(3, 4, d, d)
    return (feature_grads, weight_grads)


def solution(mesh):
    rows = P(("groups", "nodes"), None)
    cols = P("groups", "nodes")
    in_specs = (
        rows, rows, rows, rows, P(), cols, cols, cols, rows, P(("groups", "nodes")),
        cols, cols, rows, cols, cols,
    )
    out_specs = (rows, P("groups", None, None, None))
    return jax.shard_map(
        per_device, mesh=mesh, in_specs=in_specs, out_specs=out_specs, check_vma=False
    )
```

```python
import functools
import math

import jax
import jax.numpy as jnp
from jax import lax
from jax.experimental import pallas as pl
from jax.experimental.pallas import tpu as pltpu
from jax.sharding import PartitionSpec as P

HALO = 256
TILE = 256
WIDE = 2048
BF = jnp.bfloat16
F32 = jnp.float32

VM = pl.BlockSpec(memory_space=pltpu.VMEM)
HB = pl.BlockSpec(memory_space=pltpu.HBM)


def dot(a, b):
    return jnp.dot(a, b, preferred_element_type=F32)


def dot_nt(a, b):
    return lax.dot_general(a, b, (((1,), (1,)), ((), ())), preferred_element_type=F32)


def dot_tn(a, b):
    return lax.dot_general(a, b, (((0,), (0,)), ((), ())), preferred_element_type=F32)


def silu(v):
    return v / (1.0 + jnp.exp(-v))


def silu_slope(v):
    s = 1.0 / (1.0 + jnp.exp(-v))
    return s * (1.0 + v * (1.0 - s))


def merged_weights(idx, ew):
    total = ew
    for r in range(1, idx.shape[0]):
        total = total + jnp.where(pltpu.roll(idx, r, 0) == idx, pltpu.roll(ew, r, 0), 0.0)
    return total.astype(BF)


def edge_columns(idx, ew, start, rows):
    count = idx.shape[0]
    lanes = idx.shape[1]
    position = lax.broadcasted_iota(jnp.int32, (rows, lanes), 0) + start
    position = position.astype(jnp.int16)
    picked = jnp.zeros((rows, lanes), BF)
    for k in range(count):
        picked = jnp.where(idx[k : k + 1, :] == position, ew[k : k + 1, :], picked)
    return picked


def fine_edges(off, ew, s_ref):
    for h in range(TILE // 128):
        lane = slice(128 * h, 128 * (h + 1))
        o = off[:, lane]
        weight = merged_weights(o, ew[:, lane])
        rel = o + lax.broadcasted_iota(jnp.int32, o.shape, 1) + HALO
        rel = rel.astype(jnp.int16)
        for c in range(2 * HALO // 128 + 1):
            s_ref[128 * (h + c) : 128 * (h + c + 1), lane] = edge_columns(
                rel, weight, 128 * c, 128
            )


def clear_corners(s_ref):
    for h in range(TILE // 128):
        lane = slice(128 * h, 128 * (h + 1))
        if h > 0:
            s_ref[: 128 * h, lane] = jnp.zeros((128 * h, 128), BF)
        last = 128 * h + 2 * HALO + 128
        if last < TILE + 2 * HALO:
            s_ref[last:, lane] = jnp.zeros((TILE + 2 * HALO - last, 128), BF)


def forward_weights(w):
    w01 = jnp.concatenate([jnp.transpose(w[0]), jnp.transpose(w[1])], axis=1)
    return w01, jnp.transpose(w[2]), jnp.transpose(w[3])


def pool_matrix(pool, tile_rows):
    lane = lax.broadcasted_iota(jnp.int32, pool.shape, 1) // tile_rows
    values = pool.astype(F32)
    parts = [jnp.where(lane == r, values, 0.0) for r in range(pool.shape[1] // tile_rows)]
    return jnp.concatenate(parts, axis=0).astype(BF)


class Copies:
    def __init__(self, sems):
        self.sems = sems
        self.used = 0
        self.open = {}

    def start(self, source, target):
        copy = pltpu.make_async_copy(source, target, self.sems.at[self.used])
        self.used += 1
        copy.start()
        self.open[id(copy)] = copy
        return copy

    def wait(self, *copies):
        for copy in copies:
            if id(copy) in self.open:
                copy.wait()
                del self.open[id(copy)]

    def finish(self):
        self.wait(*list(self.open.values()))


def shape(dims, dtype=BF):
    return jax.ShapeDtypeStruct(dims, dtype)


def call(kernel, ins, outs, scratch=(), copies=0, us=3, mib=24, aliases={}):
    n_in, n_out = len(ins), len(outs)
    staged_in = [i for i, (_, kind) in enumerate(ins) if kind in "hs012"]
    staged_out = [i for i, (_, kind) in enumerate(outs) if kind in "hs"]
    spaces = {"h": pltpu.VMEM, "s": pltpu.SMEM}
    stage = []
    for i in staged_in:
        array, kind = ins[i]
        dims = array.shape[1:] if kind.isdigit() else array.shape
        stage.append(spaces.get(kind, pltpu.VMEM)(dims, array.dtype))
    stage += [spaces[outs[i][1]](outs[i][0].shape, outs[i][0].dtype) for i in staged_out]
    total = len(staged_in) + len(staged_out) + copies

    def body(*refs):
        in_refs, out_refs = list(refs[:n_in]), list(refs[n_in : n_in + n_out])
        rest = list(refs[n_in + n_out :])
        sems = rest.pop() if total else None
        stages, user = rest[: len(stage)], rest[len(stage) :]
        io = Copies(sems)
        pending = {}
        for i, ref in zip(staged_in, stages):
            kind = ins[i][1]
            source = in_refs[i].at[int(kind)] if kind.isdigit() else in_refs[i]
            pending[i] = io.start(source, ref)
            in_refs[i] = ref
        targets = {}
        for i, ref in zip(staged_out, stages[len(staged_in) :]):
            targets[i] = out_refs[i]
            out_refs[i] = ref

        def need(*which):
            io.wait(*[pending[i] for i in which or pending])

        def flush(*which):
            for i in which:
                io.start(out_refs[i], targets.pop(i))

        kernel(io, need, flush, in_refs, out_refs, *user)
        flush(*list(targets))
        io.finish()

    return pl.pallas_call(
        body,
        out_shape=[
            s if kind == "v" else pltpu.HBM(s.shape, s.dtype) for s, kind in outs
        ],
        in_specs=[VM if kind == "v" else HB for _, kind in ins],
        out_specs=[VM if kind == "v" else HB for _, kind in outs],
        scratch_shapes=stage
        + list(scratch)
        + ([pltpu.SemaphoreType.DMA((total,))] if total else []),
        input_output_aliases=aliases,
        compiler_params=pltpu.CompilerParams(vmem_limit_bytes=mib << 20),
        cost_estimate=pl.CostEstimate(
            flops=0, bytes_accessed=int(us * 3_000_000), transcendentals=0
        ),
    )(*[
        a if kind == "v" else pltpu.with_memory_space_constraint(a, pltpu.HBM)
        for a, kind in ins
    ])


def fine_forward(h_t, agg, weights):
    w01, w2t, w3t = weights
    first = dot(w01, jnp.concatenate([h_t, agg], axis=0))
    middle = silu(first).astype(BF)
    second = dot(w2t, middle)
    outer = silu(second).astype(BF)
    return (h_t.astype(F32) + dot(w3t, outer)).astype(BF)


def outer_tiles(tile_count, per):
    return list(range(per)) + list(range(tile_count - per, tile_count))


def inner_kernel(tile_rows, peers, cap, io, need, flush, ins, outs, feat_t, s_ref, ids, counts):
    off, ew, feat, w, pool, owner, slot, nbrs, cew, cot = ins
    so_ref, win_ref, w01_ref, w2t_ref, w3t_ref, po_ref, spread, ext_ref, agg_ref, place = outs
    rows, d = feat.shape
    block_rows = pool.shape[0]
    n2 = cot.shape[0]
    tiles = rows // TILE
    per = TILE // tile_rows
    tile_count = rows // tile_rows
    for i in range(tiles - 2):
        clear_corners(s_ref.at[i])
    clear_corners(so_ref.at[0])
    clear_corners(so_ref.at[1])
    spread[...] = jnp.zeros(spread.shape, F32)
    ids[...] = jnp.full(ids.shape, -1.0, F32)
    for p in range(peers):
        counts[p] = 0
    need(5, 6)
    lane_slot = lax.broadcasted_iota(jnp.int32, (1, 128), 1) // block_rows
    first_tiles = outer_tiles(tile_count, per)
    for t in first_tiles + [t for t in range(tile_count) if t not in first_tiles]:
        o = owner[t]
        c = counts[o]
        counts[o] = c + 1
        place[t] = o * cap + c
        row = ids[pl.ds(o, 1), :]
        ids[pl.ds(o, 1), :] = jnp.where(lane_slot == c, slot[t].astype(F32), row)
    flush(9)
    need(0, 1)
    for n, i in enumerate((0, tiles - 1)):
        cols = slice(i * TILE, (i + 1) * TILE)
        fine_edges(off[:, cols], ew[:, cols], so_ref.at[n])
    need()
    feat_t[...] = jnp.transpose(feat[...])
    weights = forward_weights(w)
    for i in range(1, tiles - 1):
        cols = slice(i * TILE, (i + 1) * TILE)
        fine_edges(off[:, cols], ew[:, cols], s_ref.at[i - 1])
        around = feat_t[:, i * TILE - HALO : (i + 1) * TILE + HALO]
        agg_ref[:, cols] = dot(around, s_ref[i - 1]).astype(BF)
    for start in range(TILE, rows - TILE, WIDE):
        stop = min(start + WIDE, rows - TILE)
        cols = slice(start, stop)
        fine_out = fine_forward(feat_t[:, cols], agg_ref[:, cols], weights)
        for i in range(start // TILE, stop // TILE):
            at = slice(i * TILE - start, (i + 1) * TILE - start)
            matrix = pool_matrix(pool[:, i * TILE : (i + 1) * TILE], tile_rows)
            blocks = dot_nt(matrix, fine_out[:, at])
            for j in range(per):
                at = pl.ds(pl.multiple_of(place[i * per + j] * block_rows, 8), block_rows)
                spread[at, :] = blocks[j * block_rows : (j + 1) * block_rows, :]
    for n, i in enumerate((0, tiles - 1)):
        po_ref[n] = pool_matrix(pool[:, i * TILE : (i + 1) * TILE], tile_rows)
    win_ref[0] = feat_t[:, : TILE + HALO]
    win_ref[1] = feat_t[:, rows - TILE - HALO :]
    w01_ref[...], w2t_ref[...], w3t_ref[...] = weights
    nb = nbrs[...].astype(F32)
    high = jnp.floor(nb * (1.0 / 256.0))
    ce = cew[...]
    ce_high = ce.astype(BF).astype(F32)
    fields = [high, nb - high * 256.0, ce_high, ce - ce_high]
    fields.append(jnp.zeros((nb.shape[0], 128 - 4 * n2), F32))
    top = jnp.concatenate(fields, axis=1)
    sub = lax.broadcasted_iota(jnp.int32, (8, 128), 0)
    for p in range(peers):
        ext_ref[p, 0:n2, :] = cot[...]
        below = jnp.where(sub == 0, ids[p : p + 1, :], 0.0)
        ext_ref[p, n2 : n2 + 16, :] = jnp.concatenate([top, below], axis=0).astype(BF)


def outer_kernel(
    tile_rows, cap, block_rows, io, need, flush, ins, outs, agg_edge, spread, stage, counts
):
    across, beside, s_in, win, w01, w2t, w3t, pool, spread_in, ext, agg_in, owner = ins
    even = lax.rem(lax.axis_index("nodes"), 2) == 0
    left = jnp.where(even, beside[...], across[...])
    right = jnp.where(even, across[...], beside[...])
    send_ref, agg_ref = outs
    peers, chunk, d = stage.shape
    rows = agg_in.shape[1]
    per = TILE // tile_rows
    io.start(ext, send_ref.at[:, pl.ds(chunk, ext.shape[1]), :])
    inside = pl.ds(TILE, rows - 2 * TILE)
    io.start(agg_in.at[:, inside], agg_ref.at[:, inside])
    spread[...] = spread_in[...]
    for p in range(peers):
        counts[p] = 0
    weights = (w01[...], w2t[...], w3t[...])
    for n in range(2):
        if n == 0:
            window_t = jnp.concatenate([jnp.transpose(left), win[0]], axis=1)
        else:
            window_t = jnp.concatenate([win[1], jnp.transpose(right)], axis=1)
        agg_edge[:, n * TILE : (n + 1) * TILE] = dot(window_t, s_in[n]).astype(BF)
    h_t = jnp.concatenate([win[0, :, :TILE], win[1, :, HALO:]], axis=1)
    fine_out = fine_forward(h_t, agg_edge[...], weights)
    results = [dot_nt(pool[n], fine_out[:, n * TILE : (n + 1) * TILE]) for n in range(2)]
    io.start(agg_edge.at[:, pl.ds(0, TILE)], agg_ref.at[:, pl.ds(0, TILE)])
    io.start(agg_edge.at[:, pl.ds(TILE, TILE)], agg_ref.at[:, pl.ds(rows - TILE, TILE)])
    need()
    for j, t in enumerate(outer_tiles(rows // tile_rows, per)):
        o = owner[t]
        c = counts[o]
        counts[o] = c + 1
        at = pl.ds(pl.multiple_of((o * cap + c) * block_rows, 8), block_rows)
        blocks = results[j // per]
        spread[at, :] = blocks[j % per * block_rows : (j % per + 1) * block_rows, :]
    group = max(1, peers // 4)
    for p in range(peers):
        stage[p] = spread[p * chunk : (p + 1) * chunk, :].astype(BF)
        if p % group == group - 1:
            part = pl.ds(p + 1 - group, group)
            io.start(stage.at[part], send_ref.at[part, pl.ds(0, chunk), :])


def mid_edges(nbrs, ew, s_ref):
    nodes = nbrs.shape[1]
    for c in range(nodes // 128):
        lane = slice(128 * c, 128 * (c + 1))
        idx = nbrs[:, lane]
        weight = merged_weights(idx, ew[:, lane])
        idx = idx.astype(jnp.int16)
        for r in range(nodes // 128):
            s_ref[128 * r : 128 * (r + 1), lane] = edge_columns(idx, weight, 128 * r, 128)


def first_window_kernel(io, need, flush, ins, outs):
    nbrs, ew, w, _ = ins
    smid, w01_ref, w2t_ref, w3t_ref = outs
    need(0, 1)
    mid_edges(nbrs, ew, smid)
    flush(0)
    need()
    w01_ref[...], w2t_ref[...], w3t_ref[...] = forward_weights(w)


def mid_kernel(block_rows, chunk, io, need, flush, ins, outs, blocks, coarse):
    got, smid, w01, w2t, w3, pool_mid, _ = ins
    send_ref, hid_ref, agg_ref, sel_ref, ext_ref = outs
    peers = got.shape[0]
    nodes = smid.shape[0]
    n2 = pool_mid.shape[0]
    io.start(got.at[:, pl.ds(chunk, n2 + 16), :], ext_ref)
    rows = [got[p, chunk + n2 : chunk + n2 + 16, :].astype(F32)[8:9, :] for p in range(peers)]
    keys = jnp.transpose(jnp.concatenate(rows, axis=0))
    keys = keys * block_rows
    keys = keys + (lax.broadcasted_iota(jnp.int32, keys.shape, 0) % block_rows).astype(F32)
    keys = keys.astype(jnp.int32)
    lane = lax.broadcasted_iota(jnp.int32, (chunk, nodes), 1)
    for p in range(peers):
        sel_ref[p * chunk : (p + 1) * chunk, :] = jnp.where(
            keys[0:chunk, p : p + 1] == lane, 1.0, 0.0
        ).astype(BF)
        blocks[p * chunk : (p + 1) * chunk, :] = got[p, 0:chunk, :]
    flush(3)
    hidden = dot_tn(blocks[...], sel_ref[...]).astype(BF)
    hid_ref[...] = hidden
    need()
    agg = dot(hidden, smid[...]).astype(BF)
    agg_ref[...] = agg
    flush(1, 2)
    middle = silu(dot(w01[...], jnp.concatenate([hidden, agg], axis=0))).astype(BF)
    outer = silu(dot(w2t[...], middle)).astype(BF)
    pooled = dot_nt(pool_mid[...], outer).astype(BF)
    coarse[...] = (dot_nt(pool_mid[...], hidden) + dot(pooled, w3[3])).astype(BF)
    for p in range(peers):
        io.start(coarse, send_ref.at[p])


def second_window_kernel(io, need, flush, ins, outs, nb_ref, ew_ref):
    ext, hid, agg, mid_cot, w1, w2 = ins
    sco, cot_all, back_ref, w01_ref, w2t_ref, mcot, sl1_ref, sl2_ref = outs
    peers = ext.shape[0]
    n2 = ext.shape[1] - 16
    nodes = peers * n2
    edges = nb_ref.shape[0]
    need()
    for p in range(peers):
        part = ext[p, n2 : n2 + 16, :].astype(F32)[0:edges, :]
        at = slice(p * n2, (p + 1) * n2)
        nb_ref[:, at] = (part[:, 0:n2] * 256.0 + part[:, n2 : 2 * n2]).astype(jnp.int32)
        ew_ref[:, at] = part[:, 2 * n2 : 3 * n2] + part[:, 3 * n2 : 4 * n2]
    cots = jnp.concatenate([ext[p, 0:n2, :] for p in range(peers)], axis=0)
    cot_all[...] = jnp.transpose(cots)
    mcot[...] = jnp.transpose(mid_cot[...])

    def column(c, _):
        lane = pl.ds(pl.multiple_of(c * 128, 128), 128)
        idx = nb_ref[:, lane]
        weight = merged_weights(idx, ew_ref[:, lane])
        idx = idx.astype(jnp.int16)
        for r in range(nodes // 128):
            sco[128 * r : 128 * (r + 1), lane] = edge_columns(idx, weight, 128 * r, 128)
        return 0

    lax.fori_loop(0, nodes // 128, column, 0)
    w01_ref[...], w2t_ref[...], _ = forward_weights(w2)
    back_ref[...] = dot(w2[3], cot_all[...])
    w01, w2t, _ = forward_weights(w1)
    first = dot(w01, jnp.concatenate([hid[...], agg[...]], axis=0))
    s1 = 1.0 / (1.0 + jnp.exp(-first))
    second = dot(w2t, (first * s1).astype(BF))
    s2 = 1.0 / (1.0 + jnp.exp(-second))
    sl1_ref[...] = s1 * (1.0 + first * (1.0 - s1))
    sl2_ref[...] = s2 * (1.0 + second * (1.0 - s2))


def coarse_kernel(io, need, flush, ins, outs):
    got, sco, c01, c2t, cot_all, cot_back, w2, *rest = ins
    cot_my, pool_mid, mcot, w1, msl2, msl1, smid, sel = rest
    send_ref, gmid_ref, sg_ref, fg_ref, cwg_ref = outs
    nodes = got.shape[0]
    n2 = cot_my.shape[0]
    me = lax.axis_index("nodes")
    width = min(TILE, nodes)
    hidden = jnp.transpose(got[...])
    if sco.shape[0] > 512:
        need(1, 2, 3, 4, 5)
    w01, w2t = c01[...], c2t[...]
    mine = pl.ds(pl.multiple_of(me * n2, 16), n2)
    mixed = jnp.zeros((2 * n2, 128), F32)
    grads = [jnp.zeros((128, 128), F32) for _ in range(4)]
    row = lax.broadcasted_iota(jnp.int32, (n2, width), 0) + me * n2
    lane = lax.broadcasted_iota(jnp.int32, (n2, width), 1)
    for i in range(nodes // width):
        cols = slice(i * width, (i + 1) * width)
        h = hidden[:, cols]
        agg = dot(hidden, sco[:, cols]).astype(BF)
        first = dot(w01, jnp.concatenate([h, agg], axis=0))
        s1 = 1.0 / (1.0 + jnp.exp(-first))
        middle = (first * s1).astype(BF)
        second = dot(w2t, middle)
        s2 = 1.0 / (1.0 + jnp.exp(-second))
        outer = (second * s2).astype(BF)
        g = cot_all[:, cols]
        if i == 0:
            need(6)
        sg = (cot_back[:, cols] * (s2 * (1.0 + second * (1.0 - s2)))).astype(BF)
        fg = (dot(w2[2], sg) * (s1 * (1.0 + first * (1.0 - s1)))).astype(BF)
        here = jnp.where(lane + i * width == row, 1.0, 0.0).astype(BF)
        mixed = mixed + dot_nt(jnp.concatenate([here, sco[mine, cols]], axis=0), fg)
        grads = [
            grads[0] + dot_nt(h, fg),
            grads[1] + dot_nt(agg, fg),
            grads[2] + dot_nt(middle, sg),
            grads[3] + dot_nt(outer, g),
        ]
    scale = 1.0 / math.sqrt(nodes)
    for m in range(4):
        cwg_ref[m] = grads[m] * scale
    flush(4)
    need(7, 8, 9, 10, 11, 12)
    mixed = mixed.astype(BF)
    into = jnp.concatenate([mixed[:n2], mixed[n2:]], axis=1)
    back_weights = jnp.concatenate([w2[0], w2[1]], axis=1)
    coarse_grad = (cot_my[...].astype(F32) + dot_nt(into, back_weights)).astype(BF)
    back = dot_tn(coarse_grad, pool_mid[...])
    g = (mcot[...].astype(F32) + back).astype(BF)
    gmid_ref[...] = g
    sg = (dot(w1[3], g) * msl2[...]).astype(BF)
    sg_ref[...] = sg
    fg = (dot(w1[2], sg) * msl1[...]).astype(BF)
    fg_ref[...] = fg
    flush(1, 2, 3)
    spill = dot(w1[1], fg).astype(BF)
    need()
    mid_grad = (g.astype(F32) + dot(w1[0], fg) + dot_nt(spill, smid[...])).astype(BF)
    send_ref[...] = dot_nt(sel[...], mid_grad).astype(BF)


def saved_kernel(tile_rows, io, need, flush, ins, outs):
    feat, agg, w, fine_cot, pool, _ = ins
    hid_ref, mid_ref, outer_ref, sl1_ref, sl2_ref, cot_ref, po_ref = outs
    rows = feat.shape[0]
    need(0, 1, 2)
    hid_ref[...] = jnp.transpose(feat[...])
    flush(0)
    w01, w2t, _ = forward_weights(w)
    for start in range(0, rows, 512):
        cols = slice(start, min(start + 512, rows))
        first = dot(w01, jnp.concatenate([hid_ref[:, cols], agg[:, cols]], axis=0))
        s1 = 1.0 / (1.0 + jnp.exp(-first))
        middle = (first * s1).astype(BF)
        mid_ref[:, cols] = middle
        sl1_ref[:, cols] = (s1 * (1.0 + first * (1.0 - s1))).astype(BF)
        second = dot(w2t, middle)
        s2 = 1.0 / (1.0 + jnp.exp(-second))
        outer_ref[:, cols] = (second * s2).astype(BF)
        sl2_ref[:, cols] = (s2 * (1.0 + second * (1.0 - s2))).astype(BF)
    need()
    cot_ref[...] = jnp.transpose(fine_cot[...])
    for i in range(rows // TILE):
        po_ref[i] = pool_matrix(pool[:, i * TILE : (i + 1) * TILE], tile_rows)


def third_window_kernel(mid_scale, io, need, flush, ins, outs):
    mhid, magg, gmid, msg, mfg, w1 = ins
    keep_ref, give_ref = outs
    d = mhid.shape[0]
    even = lax.rem(lax.axis_index("nodes"), 2) == 0
    need()
    w01, w2t, _ = forward_weights(w1)
    middle = silu(dot(w01, jnp.concatenate([mhid[...], magg[...]], axis=0))).astype(BF)
    outer = silu(dot(w2t, middle)).astype(BF)
    pairs = ((mhid, mfg), (magg, mfg), (middle, msg), (outer, gmid))
    grads = [(dot_nt(x[...], y[...]) * mid_scale).astype(BF) for x, y in pairs]
    for m in range(2):
        rows = slice(m * d, (m + 1) * d)
        keep_ref[rows, :] = jnp.where(even, grads[m], grads[m + 2])
        give_ref[rows, :] = jnp.where(even, grads[m + 2], grads[m])


def pick_kernel(block_rows, io, need, flush, ins, outs):
    place = ins[0]
    pick_ref = outs[0]
    need()
    slots = pick_ref.shape[1]
    lane = lax.broadcasted_iota(jnp.int32, (block_rows, slots), 1)
    lane = lane - lax.broadcasted_iota(jnp.int32, (block_rows, slots), 0)
    for t in range(0, place.shape[0], 2):
        both = [jnp.where(lane == place[t + j] * block_rows, 1.0, 0.0) for j in range(2)]
        pick_ref[t * block_rows : (t + 2) * block_rows, :] = jnp.concatenate(
            both, axis=0
        ).astype(BF)


def fine_grad_kernel(scale, io, need, flush, ins, outs, g_ref, fg_ref, send_ref):
    got, pick, cot, pool, w, slope2, slope1, hid, agg, mid, outer, *halves = ins
    send_out, g_out, fg_out = outs
    d, rows = hid.shape
    if pick.shape[1] > 1024:
        need(1)
    blocks = dot(pick[...], got[...]).astype(BF)
    peers, chunk, _ = send_ref.shape
    fine_rows, mid_rows = chunk * 2 // 3, chunk // 3
    both = (halves[0][...].astype(F32) + halves[1][...].astype(F32)).astype(BF)
    for p in range(peers):
        send_ref[p, fine_rows:, :] = both[p * mid_rows : (p + 1) * mid_rows, :]
    whole_tiles = mid_rows % 16 == 0
    if whole_tiles:
        rows_of_mid = pl.ds(fine_rows, mid_rows)
        io.start(send_ref.at[:, rows_of_mid], send_out.at[:, rows_of_mid])
    need(2, 3)
    per = pool.shape[1]
    for i in range(rows // TILE):
        cols = slice(i * TILE, (i + 1) * TILE)
        back = dot_tn(blocks[i * per : (i + 1) * per, :], pool[i])
        g_ref[:, cols] = (cot[:, cols].astype(F32) + back).astype(BF)
    io.start(g_ref, g_out)
    g = g_ref[...]
    need(4, 5, 6)
    sg = (dot(w[3], g) * slope2[...].astype(F32)).astype(BF)
    fg = (dot(w[2], sg) * slope1[...].astype(F32)).astype(BF)
    fg_ref[...] = fg
    io.start(fg_ref, fg_out)
    need()
    for m, (a, b) in enumerate(
        ((hid[...], fg), (agg[...], fg), (mid[...], sg), (outer[...], g))
    ):
        grad = (dot_nt(a, b) * scale).astype(BF)
        for q in range(d // fine_rows):
            part = grad[q * fine_rows : (q + 1) * fine_rows, :]
            send_ref[m * d // fine_rows + q, :fine_rows, :] = part
        if whole_tiles:
            to = pl.ds(m * d // fine_rows, d // fine_rows)
            rows_of_fine = pl.ds(0, fine_rows)
            io.start(send_ref.at[to, rows_of_fine], send_out.at[to, rows_of_fine])
    if not whole_tiles:
        io.start(send_ref, send_out)


def fine_spread_kernel(io, need, flush, ins, outs, band, spill, inner):
    off, ew, w, g, fg = ins
    rim_near, rim_far, edge_ref, out_ref = outs
    d, rows = g.shape
    tiles = rows // TILE

    def piece(i, h, c):
        row = 128 * (h + c)
        lane = (2 - row // TILE) * TILE + 128 * h
        return band.at[i + row // TILE, pl.ds(row % TILE, 128), pl.ds(lane, 128)]

    def build(i):
        for h in range(TILE // 128):
            lane = slice(i * TILE + 128 * h, i * TILE + 128 * (h + 1))
            o = off[:, lane]
            weight = merged_weights(o, ew[:, lane])
            rel = o + lax.broadcasted_iota(jnp.int32, o.shape, 1) + HALO
            rel = rel.astype(jnp.int16)
            for c in range(2 * HALO // 128 + 1):
                piece(i, h, c)[...] = edge_columns(rel, weight, 128 * c, 128)

    for i in range(tiles):
        piece(i, 0, 5)[...] = jnp.zeros((128, 128), BF)
        piece(i, 1, -1)[...] = jnp.zeros((128, 128), BF)
    for b in (0, 1, tiles, tiles + 1):
        for j in range(3):
            if not 0 <= b - 2 + j < tiles:
                band[b, :, j * TILE : (j + 1) * TILE] = jnp.zeros((TILE, TILE), BF)
    spill[:, : 2 * TILE] = jnp.zeros((d, 2 * TILE), BF)
    spill[:, 2 * TILE + rows :] = jnp.zeros((d, 2 * TILE), BF)
    even = lax.rem(lax.axis_index("nodes"), 2) == 0
    need(0, 1)
    build(0)
    build(tiles - 1)
    need()
    spill[:, 2 * TILE : 2 * TILE + rows] = dot(w[1], fg[...]).astype(BF)
    low, high = [
        dot_nt(band[b], spill[:, b * TILE : (b + 3) * TILE]).astype(BF) for b in (0, tiles + 1)
    ]
    rim_near[...] = jnp.where(even, high, low)
    rim_far[...] = jnp.where(even, low, high)
    flush(0, 1)
    for i in range(1, tiles - 1):
        build(i)
    for b in range(1, tiles + 1):
        part = dot_nt(band[b], spill[:, b * TILE : (b + 3) * TILE])
        cols = slice((b - 1) * TILE, b * TILE)
        part = part + jnp.transpose(g[:, cols].astype(F32) + dot(w[0], fg[:, cols]))
        if b == 1:
            edge_ref[:TILE, :] = part
        elif b == tiles:
            edge_ref[TILE:, :] = part
        else:
            inner[(b - 2) * TILE : (b - 1) * TILE, :] = part.astype(BF)
    io.start(inner, out_ref.at[pl.ds(TILE, rows - 2 * TILE)])


def sum_kernel(io, need, flush, ins, outs, part):
    got = ins[0]
    send_ref = outs[0]
    peers = got.shape[0]
    need()
    fine_rows, mid_rows = got.shape[1] * 2 // 3, got.shape[1] // 3
    fine = sum(got[p, :fine_rows, :].astype(F32) for p in range(peers))
    part[:fine_rows, :] = fine.astype(BF)
    for core in range(2):
        mids = sum(got[p, fine_rows:, :].astype(F32) for p in range(core, peers, 2))
        at = fine_rows + core * mid_rows
        part[at : at + mid_rows, :] = mids.astype(BF)
    for p in range(peers):
        io.start(part, send_ref.at[p])


def join_kernel(io, need, flush, ins, outs, joined):
    edge, across, beside, coarse, _ = ins
    out_ref, wg_ref = outs
    rows = out_ref.shape[0]
    even = lax.rem(lax.axis_index("nodes"), 2) == 0
    from_left = jnp.where(even, beside[...], across[...])
    from_right = jnp.where(even, across[...], beside[...])
    need(0)
    joined[:HALO, :] = (edge[:HALO, :] + from_left.astype(F32)).astype(BF)
    joined[HALO:, :] = (edge[HALO:, :] + from_right.astype(F32)).astype(BF)
    io.start(joined.at[pl.ds(0, HALO)], out_ref.at[pl.ds(0, HALO)])
    io.start(joined.at[pl.ds(HALO, HALO)], out_ref.at[pl.ds(rows - HALO, HALO)])
    need()
    io.start(coarse, wg_ref.at[pl.ds(2 * coarse.shape[0], coarse.shape[0])])


def gather_kernel(io, need, flush, ins, outs, wide):
    summed, out_ref = ins[0], outs[0]
    peers, chunk, _ = summed.shape
    fine_rows, mid_rows = chunk // 2, chunk // 4
    total = wide.shape[0]
    for p in range(peers):
        wide[p * fine_rows : (p + 1) * fine_rows, :] = summed[p, :fine_rows, :].astype(F32)
    io.start(wide.at[pl.ds(0, total // 2)], out_ref.at[pl.ds(0, total // 2)])
    for p in range(peers):
        for core in range(2):
            at = total // 2 + core * total // 4 + p * mid_rows
            rows = slice(fine_rows + core * mid_rows, fine_rows + (core + 1) * mid_rows)
            wide[at : at + mid_rows, :] = summed[p, rows, :].astype(F32)
    rest = pl.ds(total // 2, total // 2)
    io.start(wide.at[rest], out_ref.at[rest])


def exchange(x):
    return lax.all_to_all(x, "nodes", split_axis=0, concat_axis=0, tiled=True)


def per_device(
    features,
    fine_cotangent,
    mid_cotangent,
    coarse_cotangent,
    weights,
    fine_offsets,
    fine_edge_w,
    pool_fine,
    owner_dev,
    coarse_slot,
    mid_nbrs,
    mid_edge_w,
    pool_mid,
    coarse_nbrs,
    coarse_edge_w,
):
    n, d = features.shape
    tile_count = owner_dev.shape[0]
    tile_rows = n // tile_count
    block_rows = pool_fine.shape[0]
    n1 = mid_cotangent.shape[0]
    n2 = coarse_cotangent.shape[0]
    edges = fine_offsets.shape[0]
    peers = lax.axis_size("nodes")
    cap = max(2, 2 * tile_count // peers)
    chunk = cap * block_rows
    window = TILE + 2 * HALO
    per = TILE // tile_rows * block_rows
    ends = peers - 1
    inside_pairs = [(i, i ^ 1) for i in range(peers)]
    between_pairs = [(i, ((i + 1) ^ 1) - 1) for i in range(1, ends)]
    total2 = peers * n2

    odd = lax.rem(lax.axis_index("nodes"), 2)
    near = lax.dynamic_slice_in_dim(features, (1 - odd) * (n - HALO), HALO, 0)
    far = lax.dynamic_slice_in_dim(features, odd * (n - HALO), HALO, 0)
    across = lax.ppermute(near, "nodes", inside_pairs)
    beside = lax.ppermute(far, "nodes", between_pairs)
    owners = owner_dev.reshape(-1)
    s_out, win, w01, w2t, w3t, pool_out, spread, ext, agg_in, place = call(
        functools.partial(inner_kernel, tile_rows, peers, cap),
        [
            (fine_offsets, "h"), (fine_edge_w, "h"), (features, "h"), (weights, "0"),
            (pool_fine, "h"), (owners, "s"), (coarse_slot, "s"), (coarse_nbrs, "h"),
            (coarse_edge_w, "h"), (coarse_cotangent, "h"),
        ],
        [
            (shape((2, window, TILE)), "v"), (shape((2, d, TILE + HALO)), "v"),
            (shape((d, 2 * d)), "v"), (shape((d, d)), "v"), (shape((d, d)), "v"),
            (shape((2, per, TILE)), "v"), (shape((peers * chunk, d), F32), "v"),
            (shape((peers, n2 + 16, d)), "v"), (shape((d, n)), "v"),
            (shape((tile_count,), jnp.int32), "s"),
        ],
        scratch=(
            pltpu.VMEM((d, n), BF),
            pltpu.VMEM((n // TILE - 2, window, TILE), BF),
            pltpu.VMEM((peers, 128), F32),
            pltpu.SMEM((peers,), jnp.int32),
        ),
        us=6,
    )
    send1, agg = call(
        functools.partial(outer_kernel, tile_rows, cap, block_rows),
        [
            (across, "v"), (beside, "v"), (s_out, "v"), (win, "v"), (w01, "v"), (w2t, "v"),
            (w3t, "v"), (pool_out, "v"), (spread, "v"), (ext, "v"), (agg_in, "v"), (owners, "s"),
        ],
        [(shape((peers, chunk + n2 + 16, d)), "r"), (shape((d, n)), "r")],
        scratch=(
            pltpu.VMEM((d, 2 * TILE), BF),
            pltpu.VMEM((peers * chunk, d), F32),
            pltpu.VMEM((peers, chunk, d), BF),
            pltpu.SMEM((peers,), jnp.int32),
        ),
        copies=8,
        us=3,
    )
    got1 = exchange(send1)
    smid, m01, m2t, m3t = call(
        first_window_kernel,
        [(mid_nbrs, "h"), (mid_edge_w, "h"), (weights, "1"), (agg, "r")],
        [
            (shape((n1, n1)), "h"), (shape((d, 2 * d)), "h"), (shape((d, d)), "h"),
            (shape((d, d)), "h"),
        ],
        us=6,
    )
    hid, mid, outer, slope1, slope2, cot, pool_b = call(
        functools.partial(saved_kernel, tile_rows),
        [
            (features, "h"), (agg, "h"), (weights, "0"), (fine_cotangent, "h"),
            (pool_fine, "h"), (m3t, "r"),
        ],
        [
            (shape((d, n)), "h"), (shape((d, n)), "h"), (shape((d, n)), "h"),
            (shape((d, n)), "h"), (shape((d, n)), "h"), (shape((d, n)), "h"),
            (shape((n // TILE, per, TILE)), "h"),
        ],
        us=4,
    )
    send2, mhid, magg, sel, ext = call(
        functools.partial(mid_kernel, block_rows, chunk),
        [
            (got1, "v"), (smid, "h"), (m01, "h"), (m2t, "h"), (weights, "1"), (pool_mid, "h"),
            (pool_b, "r"),
        ],
        [
            (shape((peers, n2, d)), "r"), (shape((d, n1)), "h"), (shape((d, n1)), "h"),
            (shape((peers * chunk, n1)), "h"), (shape((peers, n2 + 16, d)), "r"),
        ],
        scratch=(pltpu.VMEM((peers * chunk, d), BF), pltpu.VMEM((n2, d), BF)),
        copies=peers + 1,
        us=3,
    )
    got2 = exchange(send2)
    near = "v" if total2 <= 512 else "h"
    sco, cot_all, cot_back, c01, c2t, mcot, mslope1, mslope2 = call(
        second_window_kernel,
        [
            (ext, "h"), (mhid, "h"), (magg, "h"), (mid_cotangent, "h"), (weights, "1"),
            (weights, "2"),
        ],
        [
            (shape((total2, total2)), near), (shape((d, total2)), near),
            (shape((d, total2), F32), near), (shape((d, 2 * d)), near), (shape((d, d)), near),
            (shape((d, n1)), "h"),
            (shape((d, n1), F32), "h"), (shape((d, n1), F32), "h"),
        ],
        scratch=(pltpu.VMEM((edges, total2), jnp.int32), pltpu.VMEM((edges, total2), F32)),
        us=6,
    )
    send3, gmid, msg, mfg, coarse_wg = call(
        coarse_kernel,
        [
            (got2.reshape(total2, d), "v"), (sco, near), (c01, near), (c2t, near),
            (cot_all, near), (cot_back, near), (weights, "2"),
            (coarse_cotangent, "h"), (pool_mid, "h"), (mcot, "h"), (weights, "1"),
            (mslope2, "h"), (mslope1, "h"), (smid, "h"), (sel, "h"),
        ],
        [
            (shape((peers * chunk, d)), "h"), (shape((d, n1)), "h"), (shape((d, n1)), "h"),
            (shape((d, n1)), "h"), (shape((4, d, d), F32), "h"),
        ],
        us=3,
    )
    got3 = exchange(send3.reshape(peers, chunk, d))
    pick_kind = "v" if peers * chunk <= 1024 else "h"
    mid_keep, mid_give = call(
        functools.partial(third_window_kernel, 1.0 / math.sqrt(n1 * peers)),
        [
            (mhid, "h"), (magg, "h"), (gmid, "h"), (msg, "h"), (mfg, "h"), (weights, "1"),
        ],
        [(shape((2 * d, d)), "v"), (shape((2 * d, d)), "v")],
        us=2,
    )
    mid_got = lax.ppermute(mid_give, "nodes", inside_pairs)
    (pick,) = call(
        functools.partial(pick_kernel, block_rows),
        [(place, "s"), (mid_keep, "v")],
        [(shape((tile_count * block_rows, peers * chunk)), pick_kind)],
        us=1,
    )
    send4, g, fg = call(
        functools.partial(fine_grad_kernel, 1.0 / math.sqrt(n * peers)),
        [
            (got3.reshape(peers * chunk, d), "v"), (pick, pick_kind), (cot, "h"), (pool_b, "h"),
            (weights, "0"), (slope2, "h"), (slope1, "h"), (hid, "h"), (agg, "h"), (mid, "h"),
            (outer, "h"), (mid_keep, "v"), (mid_got, "v"),
        ],
        [
            (shape((peers, 6 * d // peers, d)), "r"), (shape((d, n)), "r"), (shape((d, n)), "r"),
        ],
        scratch=(
            pltpu.VMEM((d, n), BF),
            pltpu.VMEM((d, n), BF),
            pltpu.VMEM((peers, 6 * d // peers, d), BF),
        ),
        copies=7,
        us=4,
    )
    got4 = exchange(send4)
    rim_near, rim_far, edge_sums, inner_grads = call(
        fine_spread_kernel,
        [
            (fine_offsets, "h"), (fine_edge_w, "h"), (weights, "0"), (g, "h"), (fg, "h"),
        ],
        [
            (shape((HALO, d)), "h"), (shape((HALO, d)), "h"), (shape((2 * HALO, d), F32), "h"),
            (shape((n, d)), "r"),
        ],
        scratch=(
            pltpu.VMEM((n // TILE + 2, TILE, window), BF),
            pltpu.VMEM((d, n + 4 * TILE), BF),
            pltpu.VMEM((n - 2 * HALO, d), BF),
        ),
        copies=1,
        us=5,
    )
    (send5,) = call(
        sum_kernel,
        [(got4, "v"), (rim_near, "r")],
        [(shape((peers, 8 * d // peers, d)), "r")],
        scratch=(pltpu.VMEM((8 * d // peers, d), BF),),
        copies=peers,
        us=1,
    )
    got5 = exchange(send5)
    from_across = lax.ppermute(rim_near, "nodes", inside_pairs)
    from_beside = lax.ppermute(rim_far, "nodes", between_pairs)
    feature_grads, weight_grads = call(
        join_kernel,
        [
            (edge_sums, "h"), (from_across, "v"), (from_beside, "v"), (coarse_wg.reshape(4 * d, d), "h"),
            (inner_grads, "r"),
        ],
        [(shape((n, d)), "r"), (shape((12 * d, d), F32), "r")],
        scratch=(pltpu.VMEM((2 * HALO, d), BF),),
        copies=3,
        aliases={4: 0},
        us=1,
    )
    (weight_grads,) = call(
        gather_kernel,
        [
            (got5, "v"), (weight_grads, "r"),
        ],
        [(shape((12 * d, d), F32), "r")],
        scratch=(pltpu.VMEM((8 * d, d), F32),),
        copies=2,
        aliases={1: 0},
        us=1,
    )
    weight_grads = weight_grads.reshape(3, 4, d, d)
    return (feature_grads, weight_grads)


def solution(mesh):
    rows = P(("groups", "nodes"), None)
    cols = P("groups", "nodes")
    in_specs = (
        rows, rows, rows, rows, P(), cols, cols, cols, rows, P(("groups", "nodes")),
        cols, cols, rows, cols, cols,
    )
    out_specs = (rows, P("groups", None, None, None))
    return jax.shard_map(
        per_device, mesh=mesh, in_specs=in_specs, out_specs=out_specs, check_vma=False
    )
```
